32 devices in a mesh: groups: 2 (over y), mem: 8 (over z, x), lat: 2 (over core).
Axes of the slice: x: 2, y: 2, z: 4, core: 2. Of those that a mesh axis runs over, the one named last changes fastest.
Arguments:
- state: bfloat16 [64, 8, 64, 512], P(('groups', 'mem'), None, 'lat'), parts along dimension 0, may hold values from -6 to 6
- counts: int32 [16], P(('groups', 'mem')), parts along dimension 0, may hold values from 1 to 4, 16 in all
- east_wind: float32 [128, 512], P(('groups', 'lat')), parts along dimension 0, may hold values from -0.48 to 0.48
- north_wind: float32 [128, 512], P(('groups', 'lat')), parts along dimension 0, may hold values from -0.48 to 0.48
- obs_cells: int32 [4, 32768], P(('groups', 'lat')), parts along dimension 0, may hold values from 0 to 16383
- obs_mask: int32 [4, 32768], P(('groups', 'lat')), parts along dimension 0, may hold values 0 or 1
- obs_values: float32 [4, 32768], P(('groups', 'lat')), parts along dimension 0, may hold values from -6 to 6
- obs_error: float32 [4, 32768], P(('groups', 'lat')), parts along dimension 0, may hold values from 0.2 to 2
- relax: float32 [8], replicated, may hold values from 0.3 to 0.9
Outputs:
- new_state: bfloat16 [64, 8, 64, 512], P(('groups', 'mem'), None, 'lat'), parts along dimension 0
- analysis_mean: bfloat16 [16, 64, 512], P('groups', 'lat'), parts along dimension 0
The draws below stay inside these ranges and needn't reach their ends.
There are 2 independent parts, one for each index of `groups`. The reference program is written for one: setup_inputs(seed, part) draws one part's arguments, and reference() takes and returns one part's arrays. A program takes and returns all parts, laid end to end along the dimension named above; an argument that names none is the same for every part. Nothing has to cross between parts.
Inputs may be any that keep to these rules, and one draw needn't show every extreme that they name: counts over the mem axis add up to 16, and some mem index holds 4 members.
All inputs are finite; a program needn't handle non-finite values. No bound on the sum of `counts` or of `obs_mask` on one device may be relied on, other than what follows from the above.
Results may differ from the reference program's by a relative error of at most 0.001.
The reference program's roundings to bfloat16 on the way (of `advected`) count: a program that leaves them out, or rounds other values in their place, can miss the bound.
Values may be sent and summed in bfloat16 or wider, within the bound.
No kernel may reach another device: no remote copies, remote signals or barrier semaphores. Data moves between devices by JAX's collectives and lax.ppermute only.
A program may use at most 128 MiB of HBM per device.

```python
import math
import jax
import jax.numpy as jnp
import numpy as np
from jax import lax

FIELDS = 8
NLON = 512
ROWS = 32
STEPS = 4
SMOOTH = 16
OBS_BAND = 32768
SLOTS = 4
MEMBERS = 16
NLAT = 64
N_MEM = 8
N_LAT = 2


def plant(values, own_key, low, top_value):
    shape = values.shape
    spot = [jax.random.randint(jax.random.fold_in(own_key, axis), (), 0, shape[axis]) for axis in range(len(shape))]
    values = values.at[tuple(spot)].set(low)
    longest = shape.index(max(shape))
    spot[longest] = (spot[longest] + 1) % shape[longest]
    return values.at[tuple(spot)].set(top_value)


def block_levels(key, dims, pieces, low, top_value):
    gain = 1.0
    for position, shards_of in pieces:
        heights = jax.random.uniform(jax.random.fold_in(jax.random.fold_in(key, 6), position), (shards_of,), jnp.float32, low / len(pieces), top_value / len(pieces))
        gain = gain * jnp.repeat(jnp.exp(heights), dims[position] // shards_of).reshape((-1,) + (1,) * (len(dims) - 1 - position))
    return gain


def split_up(number_of, total, most, lean):
    weights = [(1 << 20) // math.isqrt(grade ** lean) + 1 for grade in range(2, number_of + 1)]
    rest, given = total - most - (number_of - 1), [1] * (number_of - 1)
    while rest > 0:
        free = [i for i in range(number_of - 1) if given[i] < most]
        mass, budget = sum([weights[i] for i in free]), rest
        for i in free:
            extra = min(most - given[i], max(1, budget * weights[i] // mass), rest)
            given[i] = given[i] + extra
            rest = rest - extra
    return np.array([most] + given)


def ragged(rng, count, total, bound, slope):
    if count == 2:
        one = jax.random.randint(rng, (), max(1, total - bound), min(bound, total - 1) + 1)
        return jnp.stack([one, total - one])
    tallies = jnp.asarray(split_up(count, total, bound, slope), jnp.int32)
    couples = (count - 1) // 2
    giver, taker = tallies[1:1 + 2 * couples:2], tallies[2:2 + 2 * couples:2]
    slack = jnp.minimum(giver - 1, bound - taker)
    shifted = jax.random.randint(jax.random.fold_in(rng, 1), (couples,), 0, 1 << 20) % (slack + 1)
    tallies = tallies.at[1:1 + 2 * couples:2].set(giver - shifted).at[2:2 + 2 * couples:2].set(taker + shifted)
    return tallies[jax.random.permutation(jax.random.fold_in(rng, 2), count)]


def noise(stream_key, shape, width, limit, pieces=(), held_as=jnp.bfloat16):
    gain = block_levels(stream_key, shape, pieces, -0.22, 0.18) if pieces else 1.0
    values = jax.random.normal(stream_key, shape, jnp.float32) * width * gain
    return jnp.minimum(jnp.maximum(values, -limit), limit).astype(held_as)


def setup_inputs(seed: int = 0, part: int = 0) -> dict:
    seeds = jax.random.split(jax.random.key(seed), 10)
    own_keys = jax.random.split(jax.random.fold_in(seeds[9], part), 10)
    return {
        "state": noise(own_keys[0], (N_MEM * SLOTS, FIELDS, NLAT, NLON), 1.0, 6.0, ((0, 8), (2, 2))),
        "counts": ragged(own_keys[1], N_MEM, MEMBERS, SLOTS, 2).astype(jnp.int32),
        "east_wind": jnp.clip(jax.random.uniform(own_keys[2], (NLAT, NLON), jnp.float32, -0.48, 0.48) * block_levels(own_keys[2], (NLAT, NLON), ((0, 2),), -0.4, 0.0), -0.48, 0.48),
        "north_wind": jnp.clip(jax.random.uniform(own_keys[3], (NLAT, NLON), jnp.float32, -0.48, 0.48) * block_levels(own_keys[3], (NLAT, NLON), ((0, 2),), -0.4, 0.0), -0.48, 0.48),
        "obs_cells": plant(jax.random.randint(own_keys[4], (N_LAT, OBS_BAND), 0, ROWS * NLON), jax.random.fold_in(own_keys[4], 1), 0, (ROWS * NLON) - 1).astype(jnp.int32),
        "obs_mask": plant((jax.random.randint(own_keys[5], (N_LAT, OBS_BAND), 0, 4) < 3).astype(jnp.int32), jax.random.fold_in(own_keys[5], 1), 0, 1),
        "obs_values": noise(own_keys[6], (N_LAT, OBS_BAND), 1.0, 6.0, ((0, 2),), jnp.float32),
        "obs_error": jnp.clip(jnp.exp(math.log(2.0) - 2.3025851 * jax.random.uniform(own_keys[7], (N_LAT, OBS_BAND), jnp.float32) ** block_levels(own_keys[7], (N_LAT, OBS_BAND), ((0, 2),), -0.2, 0.2)), 0.2, 2.0),
        "relax": jnp.clip(jax.random.uniform(seeds[8], (FIELDS,), jnp.float32, 0.3, 0.9), 0.3, 0.9),
    }


LOG_TWO_PI = 1.8378770664093453


def advance(field, east_wind, north_wind):
    centre = field[..., 1:-1, :]
    south_row = field[..., :-2, :]
    north_row = field[..., 2:, :]
    west_cell = jnp.roll(centre, 1, axis=-1)
    east_cell = jnp.roll(centre, -1, axis=-1)
    return (centre - jnp.maximum(east_wind, 0.0) * (centre - west_cell)
            - jnp.minimum(east_wind, 0.0) * (east_cell - centre)
            - jnp.maximum(north_wind, 0.0) * (centre - south_row)
            - jnp.minimum(north_wind, 0.0) * (north_row - centre))


def kernel_matrix(count, reach, periodic):
    index = jnp.arange(count, dtype=jnp.int32)
    offset = jnp.abs(index[:, None] - index[None, :])
    if periodic:
        offset = jnp.minimum(offset, count - offset)
    values = jnp.exp(-(2.0 * offset.astype(jnp.float32) / reach) ** 2)
    return jnp.where(offset <= reach, values, 0.0).astype(jnp.float32)


def band_grids(cells, mask, values, error, count):
    used = mask.astype(jnp.float32)
    inverse = used / (error * error)
    terms = jnp.stack([inverse, inverse * values,
                       inverse * values * values + used * (2.0 * jnp.log(error) + LOG_TWO_PI)])
    return jax.vmap(lambda column: jax.ops.segment_sum(column, cells, num_segments=count))(terms)


def reference(state, counts, east_wind, north_wind, obs_cells, obs_mask, obs_values, obs_error, relax):
    live = (jnp.arange(SLOTS, dtype=jnp.int32)[None, :] < counts[:, None]).reshape(-1)
    grids = jax.vmap(lambda a, b, c, d: band_grids(a, b, c, d, ROWS * NLON))(obs_cells, obs_mask, obs_values, obs_error)
    grids = grids.reshape(N_LAT, 3, ROWS, NLON).transpose(1, 0, 2, 3).reshape(3, NLAT, NLON)
    lat_kernel = kernel_matrix(NLAT, SMOOTH, False)
    lon_kernel = kernel_matrix(NLON, SMOOTH, True)

    def visit(carry, item):
        peak, total, weighted = carry
        member, alive = item
        field = member.astype(jnp.float32)
        for step in range(STEPS):
            padded = jnp.pad(field, ((0, 0), (1, 1), (0, 0)))
            field = advance(padded, east_wind, north_wind)
        advected = field.astype(jnp.bfloat16)
        value = advected[0].astype(jnp.float32)
        loglik = -0.5 * (grids[0] * value * value - 2.0 * grids[1] * value + grids[2])
        smoothed = jnp.dot(lat_kernel, loglik, precision=lax.Precision.HIGHEST, preferred_element_type=jnp.float32)
        scores = jnp.dot(smoothed, lon_kernel, precision=lax.Precision.HIGHEST, preferred_element_type=jnp.float32)
        new_peak = jnp.where(alive, jnp.maximum(peak, scores), peak)
        factor = jnp.exp(peak - new_peak)
        gains = jnp.where(alive, jnp.exp(scores - new_peak), 0.0)
        total = total * factor + gains
        weighted = weighted * factor[None] + gains[None] * advected.astype(jnp.float32)
        return (new_peak, total, weighted), advected

    start = (jnp.full((NLAT, NLON), -jnp.inf, jnp.float32), jnp.zeros((NLAT, NLON), jnp.float32),
             jnp.zeros((FIELDS, NLAT, NLON), jnp.float32))
    (peak, total, weighted), advected_all = lax.scan(visit, start, (state, live))
    merged = weighted / total[None]

    def relax_member(item):
        advected, alive = item
        values = advected.astype(jnp.float32)
        fresh = values + relax[:, None, None] * (merged - values)
        return jnp.where(alive, fresh, 0.0).astype(jnp.bfloat16)

    new_state = lax.map(relax_member, (advected_all, live))
    return new_state, merged.astype(jnp.bfloat16)
```

```python
import functools

import jax
import jax.numpy as jnp
import numpy as np
from jax import lax
from jax.experimental import pallas as pl
from jax.experimental.pallas import tpu as pltpu
from jax.sharding import PartitionSpec as P

STEPS = 4
SMOOTH = 16
LOG_TWO_PI = 1.8378770664093453
LANES = 128
TILE = 8
PARTS = 7
CHUNK_ROWS = 8


VMEM = pl.BlockSpec(memory_space=pltpu.VMEM)
SMEM = pl.BlockSpec(memory_space=pltpu.SMEM)
PARAMS = pltpu.CompilerParams(vmem_limit_bytes=24 * 1024 * 1024)


def kernel_matrix(offset):
    values = np.exp(-((2.0 * offset.astype(np.float32) / SMOOTH) ** 2))
    return np.where(np.abs(offset) <= SMOOTH, values, 0.0).astype(np.float32)


def split_three(x):
    high = x.astype(jnp.bfloat16).astype(jnp.float32)
    rest = x - high
    middle = rest.astype(jnp.bfloat16).astype(jnp.float32)
    return high, middle, rest - middle


def grids_kernel(cells_ref, mask_ref, values_ref, error_ref, grids_ref, acc_ref):
    rows, width = grids_ref.shape[1:]
    half = width // 2
    highs = 2 * rows
    pack = 16
    high_iota = [
        (lax.broadcasted_iota(jnp.int32, (pack, LANES), 0) + pack * i)
        .astype(jnp.float32)
        .astype(jnp.bfloat16)
        for i in range(highs // pack)
    ]
    low_iota = [
        (lax.broadcasted_iota(jnp.int32, (pack, LANES), 0) + pack * i)
        .astype(jnp.float32)
        .astype(jnp.bfloat16)
        for i in range(half // pack)
    ]
    zero = jnp.zeros((pack, LANES), jnp.bfloat16)
    one = jnp.ones((pack, LANES), jnp.bfloat16)
    acc_ref[...] = jnp.zeros_like(acc_ref)

    def body(step, carry):
        here = pl.ds(pl.multiple_of(step * CHUNK_ROWS, CHUNK_ROWS), CHUNK_ROWS)
        cells = cells_ref[here, :]
        used = mask_ref[here, :].astype(jnp.float32)
        values = values_ref[here, :]
        error = error_ref[here, :]
        inverse = used / (error * error)
        first = inverse * values
        second = first * values + used * (2.0 * jnp.log(error) + LOG_TWO_PI)
        row = cells // width
        column = cells % width
        side = column // half
        high = (side * rows + row).astype(jnp.float32)
        low = (column % half).astype(jnp.float32)
        parts = split_three(inverse) + split_three(first) + (second,)
        left, right = [], []
        for r in range(CHUNK_ROWS):

            def spread(x):
                return jnp.broadcast_to(x[r : r + 1, :], (pack, LANES)).astype(jnp.bfloat16)

            high_row, low_row = spread(high), spread(low)
            hit = [iota == high_row for iota in high_iota]
            pieces = []
            for part in parts:
                part_row = spread(part)
                pieces += [jnp.where(h, part_row, zero) for h in hit]
            left.append(jnp.concatenate(pieces, axis=0))
            right.append(
                jnp.concatenate([jnp.where(iota == low_row, one, zero) for iota in low_iota], axis=0)
            )
        acc_ref[...] += lax.dot_general(
            jnp.concatenate(left, axis=1),
            jnp.concatenate(right, axis=1),
            (((1,), (1,)), ((), ())),
            preferred_element_type=jnp.float32,
        )
        return carry

    lax.fori_loop(0, cells_ref.shape[0] // CHUNK_ROWS, body, 0)

    def part_sum(indices):
        total = acc_ref[pl.ds(indices[-1] * highs, highs), :]
        for i in indices[-2::-1]:
            total = total + acc_ref[pl.ds(i * highs, highs), :]
        return total

    for g, indices in enumerate(((0, 1, 2), (3, 4, 5), (6,))):
        total = part_sum(indices)
        grids_ref[g, :, 0:half] = total[0:rows]
        grids_ref[g, :, half:width] = total[rows:highs]


def wind_parts(east_ref, north_ref, wind_halo_ref):
    east = jnp.concatenate([east_ref[...], wind_halo_ref[0]], axis=0)
    north = jnp.concatenate([north_ref[...], wind_halo_ref[1]], axis=0)
    zero = jnp.zeros_like(east)
    return (
        jnp.maximum(east, zero),
        jnp.minimum(east, zero),
        jnp.maximum(north, zero),
        jnp.minimum(north, zero),
    )


def advect(x, winds):
    count, width = x.shape
    east_up, east_down, north_up, north_down = winds
    for _ in range(STEPS):
        west_cell = pltpu.roll(x, 1, 1)
        east_cell = pltpu.roll(x, width - 1, 1)
        south_row = pltpu.roll(x, 1, 0)
        north_row = pltpu.roll(x, count - 1, 0)
        x = (
            x
            - east_up * (x - west_cell)
            - east_down * (east_cell - x)
            - north_up * (x - south_row)
            - north_down * (north_row - x)
        )
    return x


def first_kernel(
    state_ref, halo_ref, east_ref, north_ref, grids_ref, lat_ref, lon_ref, adv_ref, own_ref, send_ref
):
    slots, _, rows, width = state_ref.shape
    fields = state_ref.shape[1]
    winds = wind_parts(east_ref, north_ref, halo_ref.at[pl.ds(slots * fields, 2)])
    inverse, first, second = grids_ref[0], grids_ref[1], grids_ref[2]
    logliks = []
    for s in range(slots):
        x = jnp.concatenate([state_ref[s, 0].astype(jnp.float32), halo_ref[s * fields]], axis=0)
        advected = advect(x, winds)[0:rows].astype(jnp.bfloat16)
        adv_ref[s] = advected
        value = advected.astype(jnp.float32)
        logliks.append(-0.5 * (inverse * value * value - 2.0 * first * value + second))
    smooth = functools.partial(
        jnp.dot, precision=lax.Precision.HIGHEST, preferred_element_type=jnp.float32
    )
    along = smooth(jnp.concatenate(logliks, axis=0), lon_ref[...])
    for s in range(slots):
        scores = smooth(lat_ref[...], along[s * rows : (s + 1) * rows])
        own_ref[s] = scores[0:rows]
        send_ref[s] = scores[rows:]


def rest_kernel(state_ref, halo_ref, east_ref, north_ref, adv_ref, winds_ref):
    slots, fields, rows, width = state_ref.shape
    for i, part in enumerate(
        wind_parts(east_ref, north_ref, halo_ref.at[pl.ds(slots * fields, 2)])
    ):
        winds_ref[i] = part

    def body(i, carry):
        s, f = i // (fields - 1), i % (fields - 1) + 1
        x = jnp.concatenate(
            [state_ref[s, f].astype(jnp.float32), halo_ref[s * fields + f]], axis=0
        )
        winds = [winds_ref[k] for k in range(4)]
        adv_ref[s, f - 1] = advect(x, winds)[0:rows].astype(jnp.bfloat16)
        return carry

    lax.fori_loop(0, slots * (fields - 1), body, 0)


def weigh_kernel(place_ref, counts_ref, own_ref, recv_ref, adv_first_ref, adv_rest_ref, out_ref):
    slots, rows, width = own_ref.shape
    fields = adv_rest_ref.shape[1] + 1
    across = width // LANES

    def store(row_tile, index, value):
        for l in range(across):
            out_ref[row_tile * across + l, index] = value[:, l * LANES : (l + 1) * LANES]

    lower = place_ref[0] == 0
    for t in range(rows // TILE):
        here = slice(t * TILE, (t + 1) * TILE)
        near = (t * TILE) % SMOOTH
        scores = []
        for s in range(slots):
            recv = recv_ref[s, near : near + TILE, :]
            at_this_edge = lower if t * TILE >= rows - SMOOTH else jnp.logical_not(lower)
            score = own_ref[s, here, :] + jnp.where(at_this_edge, recv, 0.0)
            scores.append(jnp.where(s < counts_ref[0], score, -jnp.inf))
        peak = functools.reduce(jnp.maximum, scores)
        gains = [jnp.exp(score - peak) for score in scores]
        store(t, 0, peak)
        store(t, 1, functools.reduce(jnp.add, gains))
        for f in range(fields):
            total = None
            for s in range(slots):
                ref = adv_first_ref.at[s] if f == 0 else adv_rest_ref.at[s, f - 1]
                pair = slice(t // 2 * 2 * TILE, (t // 2 + 1) * 2 * TILE)
                value = ref[pair, :].astype(jnp.float32)[t % 2 * TILE : (t % 2 + 1) * TILE]
                term = gains[s] * value
                total = term if total is None else total + term
            store(t, 2 + f, total)


def merge_kernel(parts_ref, merged_ref):
    count, quantities = parts_ref.shape[:2]
    peak = functools.reduce(jnp.maximum, [parts_ref[d, 0] for d in range(count)])
    factors = [jnp.exp(parts_ref[d, 0] - peak) for d in range(count)]
    total = functools.reduce(jnp.add, [factors[d] * parts_ref[d, 1] for d in range(count)])
    for f in range(quantities - 2):
        weighted = functools.reduce(
            jnp.add, [factors[d] * parts_ref[d, 2 + f] for d in range(count)]
        )
        merged_ref[f] = weighted / total


def relax_kernel(counts_ref, relax_ref, merged_ref, adv_first_ref, adv_rest_ref, new_ref, mean_ref):
    slots, fields, rows, width = new_ref.shape
    across = width // LANES
    for f in range(fields):
        factor = relax_ref[f]
        merged = jnp.concatenate(
            [
                jnp.concatenate(
                    [merged_ref[t * across + l, f] for l in range(across)], axis=1
                )
                for t in range(rows // TILE)
            ],
            axis=0,
        )
        mean_ref[f] = merged.astype(jnp.bfloat16)
        for s in range(slots):
            ref = adv_first_ref.at[s] if f == 0 else adv_rest_ref.at[s, f - 1]
            value = ref[...].astype(jnp.float32)
            fresh = value + factor * (merged - value)
            new_ref[s, f] = jnp.where(s < counts_ref[0], fresh, 0.0).astype(jnp.bfloat16)


def call(kernel, ins, outs, scratch=(), **cost):
    return pl.pallas_call(
        kernel,
        out_shape=[jax.ShapeDtypeStruct(shape, dtype) for shape, dtype in outs],
        in_specs=ins,
        out_specs=[VMEM] * len(outs),
        scratch_shapes=list(scratch),
        compiler_params=PARAMS,
        cost_estimate=pl.CostEstimate(**cost),
    )


def on_device(
    state, counts, east_wind, north_wind, obs_cells, obs_mask, obs_values, obs_error, relax
):
    slots, fields, rows, width = state.shape
    f32, bf16 = jnp.float32, jnp.bfloat16
    place = lax.axis_index("lat")
    swap = [(0, 1), (1, 0)]
    lower = place == 0

    edge = lax.dynamic_slice_in_dim(state, jnp.where(lower, rows - TILE, 0), TILE, axis=2)
    winds = jnp.stack([east_wind, north_wind])
    wind_edge = lax.dynamic_slice_in_dim(winds, jnp.where(lower, rows - TILE, 0), TILE, axis=1)
    message = jnp.concatenate(
        [edge.astype(f32).reshape(slots * fields, TILE, width), wind_edge], axis=0
    )
    near = jnp.arange(TILE) < TILE // 2
    keep = jnp.logical_xor(near, lower)
    message = jnp.where(keep[None, :, None], message, 0.0)
    halo = lax.ppermute(message, "lat", swap)

    observations = obs_cells.shape[1]
    flat = [
        x.reshape(observations // LANES, LANES) for x in (obs_cells, obs_mask, obs_values, obs_error)
    ]
    (grids,) = call(
        grids_kernel,
        [VMEM] * 4,
        [((3, rows, width), f32)],
        [pltpu.VMEM((PARTS * 2 * rows, width // 2), f32)],
        flops=2 * PARTS * rows * width * observations,
        bytes_accessed=16 * observations,
        transcendentals=observations,
    )(*flat)

    index = np.arange(rows)
    own = index[None, :] - index[:, None]
    upper_side = index[None, :] - (index[:SMOOTH, None] + rows)
    lower_side = index[None, :] - (index[rows - SMOOTH :, None] - rows)
    lat_kernel = jnp.where(
        lower,
        jnp.asarray(kernel_matrix(np.concatenate([own, upper_side]))),
        jnp.asarray(kernel_matrix(np.concatenate([own, lower_side]))),
    )
    distance = np.abs(np.arange(width)[:, None] - np.arange(width)[None, :])
    lon_kernel = jnp.asarray(kernel_matrix(np.minimum(distance, width - distance)))

    adv_first, own_scores, edge_scores = call(
        first_kernel,
        [VMEM] * 7,
        [
            ((slots, rows, width), bf16),
            ((slots, rows, width), f32),
            ((slots, SMOOTH, width), f32),
        ],
        flops=12 * slots * rows * width * width,
        bytes_accessed=4 * width * width,
        transcendentals=0,
    )(state, halo, east_wind, north_wind, grids, lat_kernel, lon_kernel)
    received = lax.ppermute(edge_scores, "lat", swap)

    (adv_rest,) = call(
        rest_kernel,
        [VMEM] * 4,
        [((slots, fields - 1, rows, width), bf16)],
        [pltpu.VMEM((4, rows + TILE, width), f32)],
        flops=STEPS * 16 * slots * fields * rows * width,
        bytes_accessed=4 * slots * fields * rows * width,
        transcendentals=0,
    )(state, halo, east_wind, north_wind)

    tiles = rows * width // (TILE * LANES)
    quantities = fields + 2
    (parts,) = call(
        weigh_kernel,
        [SMEM, SMEM] + [VMEM] * 4,
        [((tiles, quantities, TILE, LANES), f32)],
        flops=4 * slots * fields * rows * width,
        bytes_accessed=4 * slots * fields * rows * width,
        transcendentals=slots * rows * width,
    )(place.reshape(1), counts, own_scores, received, adv_first, adv_rest)

    members = lax.axis_size("mem")
    outer = min(members, tiles)
    inner = members // outer
    held = TILE // inner
    depth = tiles // outer
    send = parts.reshape(outer, depth, quantities, inner, held, LANES).transpose(0, 3, 2, 1, 4, 5)
    send = send.reshape(members, quantities, depth * held, LANES)
    got = lax.all_to_all(send, "mem", 0, 0, tiled=True)
    (merged,) = call(
        merge_kernel,
        [VMEM],
        [((fields, depth * held, LANES), f32)],
        flops=4 * members * quantities * depth * held * LANES,
        bytes_accessed=4 * members * quantities * depth * held * LANES,
        transcendentals=members * depth * held * LANES,
    )(got)
    whole = lax.all_gather(merged, "mem", axis=0, tiled=False)
    whole = whole.reshape(outer, inner, fields, depth, held, LANES).transpose(0, 3, 2, 1, 4, 5)
    whole = whole.reshape(tiles, fields, TILE, LANES)

    new_state, mean = call(
        relax_kernel,
        [SMEM, SMEM] + [VMEM] * 3,
        [((slots, fields, rows, width), bf16), ((fields, rows, width), bf16)],
        flops=4 * slots * fields * rows * width,
        bytes_accessed=4 * slots * fields * rows * width,
        transcendentals=0,
    )(counts, relax, whole, adv_first, adv_rest)
    return (new_state, mean)


def solution(mesh):
    return jax.shard_map(
        on_device,
        mesh=mesh,
        in_specs=(
            P(("groups", "mem"), None, "lat", None),
            P(("groups", "mem")),
            P(("groups", "lat"), None),
            P(("groups", "lat"), None),
            P(("groups", "lat"), None),
            P(("groups", "lat"), None),
            P(("groups", "lat"), None),
            P(("groups", "lat"), None),
            P(),
        ),
        out_specs=(P(("groups", "mem"), None, "lat", None), P("groups", "lat", None)),
        check_vma=False,
    )
```

```python
import functools

import jax
import jax.numpy as jnp
import numpy as np
from jax import lax
from jax.experimental import pallas as pl
from jax.experimental.pallas import tpu as pltpu
from jax.sharding import PartitionSpec as P

STEPS = 4
SMOOTH = 16
LOG_TWO_PI = 1.8378770664093453
LANES = 128
TILE = 8
PARTS = 7
CHUNK_ROWS = 8
PAIR = 2
LINE = 4


VMEM = pl.BlockSpec(memory_space=pltpu.VMEM)
SMEM = pl.BlockSpec(memory_space=pltpu.SMEM)
PARAMS = pltpu.CompilerParams(vmem_limit_bytes=24 * 1024 * 1024)


def kernel_matrix(offset):
    values = np.exp(-((2.0 * offset.astype(np.float32) / SMOOTH) ** 2))
    return np.where(np.abs(offset) <= SMOOTH, values, 0.0).astype(np.float32)


def split_three(x):
    high = x.astype(jnp.bfloat16).astype(jnp.float32)
    rest = x - high
    middle = rest.astype(jnp.bfloat16).astype(jnp.float32)
    return high, middle, rest - middle


def grids_kernel(cells_ref, mask_ref, values_ref, error_ref, grids_ref, acc_ref):
    rows, width = grids_ref.shape[1:]
    half = width // 2
    highs = 2 * rows
    pack = 16
    high_iota = [
        (lax.broadcasted_iota(jnp.int32, (pack, LANES), 0) + pack * i)
        .astype(jnp.float32)
        .astype(jnp.bfloat16)
        for i in range(highs // pack)
    ]
    low_iota = [
        (lax.broadcasted_iota(jnp.int32, (pack, LANES), 0) + pack * i)
        .astype(jnp.float32)
        .astype(jnp.bfloat16)
        for i in range(half // pack)
    ]
    zero = jnp.zeros((pack, LANES), jnp.bfloat16)
    one = jnp.ones((pack, LANES), jnp.bfloat16)
    acc_ref[...] = jnp.zeros_like(acc_ref)

    def body(step, carry):
        here = pl.ds(pl.multiple_of(step * CHUNK_ROWS, CHUNK_ROWS), CHUNK_ROWS)
        cells = cells_ref[here, :]
        used = mask_ref[here, :].astype(jnp.float32)
        values = values_ref[here, :]
        error = error_ref[here, :]
        inverse = used / (error * error)
        first = inverse * values
        second = first * values + used * (2.0 * jnp.log(error) + LOG_TWO_PI)
        row = cells // width
        column = cells % width
        side = column // half
        high = (side * rows + row).astype(jnp.float32)
        low = (column % half).astype(jnp.float32)
        parts = split_three(inverse) + split_three(first) + (second,)
        left, right = [], []
        for r in range(CHUNK_ROWS):

            def spread(x):
                return jnp.broadcast_to(x[r : r + 1, :], (pack, LANES)).astype(jnp.bfloat16)

            high_row, low_row = spread(high), spread(low)
            hit = [iota == high_row for iota in high_iota]
            pieces = []
            for part in parts:
                part_row = spread(part)
                pieces += [jnp.where(h, part_row, zero) for h in hit]
            left.append(jnp.concatenate(pieces, axis=0))
            right.append(
                jnp.concatenate([jnp.where(iota == low_row, one, zero) for iota in low_iota], axis=0)
            )
        acc_ref[...] += lax.dot_general(
            jnp.concatenate(left, axis=1),
            jnp.concatenate(right, axis=1),
            (((1,), (1,)), ((), ())),
            preferred_element_type=jnp.float32,
        )
        return carry

    lax.fori_loop(0, cells_ref.shape[0] // CHUNK_ROWS, body, 0)

    def part_sum(indices):
        total = acc_ref[pl.ds(indices[-1] * highs, highs), :]
        for i in indices[-2::-1]:
            total = total + acc_ref[pl.ds(i * highs, highs), :]
        return total

    for g, indices in enumerate(((0, 1, 2), (3, 4, 5), (6,))):
        total = part_sum(indices)
        grids_ref[g, :, 0:half] = total[0:rows]
        grids_ref[g, :, half:width] = total[rows:highs]


def wind_parts(east_ref, north_ref, wind_halo_ref):
    east = jnp.concatenate([east_ref[...], wind_halo_ref[0]], axis=0)
    north = jnp.concatenate([north_ref[...], wind_halo_ref[1]], axis=0)
    zero = jnp.zeros_like(east)
    return (
        jnp.maximum(east, zero),
        jnp.minimum(east, zero),
        jnp.maximum(north, zero),
        jnp.minimum(north, zero),
    )


def advect(x, winds):
    count, width = x.shape
    east_up, east_down, north_up, north_down = winds
    for _ in range(STEPS):
        west_cell = pltpu.roll(x, 1, 1)
        east_cell = pltpu.roll(x, width - 1, 1)
        south_row = pltpu.roll(x, 1, 0)
        north_row = pltpu.roll(x, count - 1, 0)
        x = (
            x
            - east_up * (x - west_cell)
            - east_down * (east_cell - x)
            - north_up * (x - south_row)
            - north_down * (north_row - x)
        )
    return x


def first_kernel(
    state_ref, halo_ref, east_ref, north_ref, grids_ref, lat_ref, lon_ref, adv_ref, own_ref, send_ref
):
    slots, _, rows, width = state_ref.shape
    fields = state_ref.shape[1]
    winds = wind_parts(east_ref, north_ref, halo_ref.at[pl.ds(slots * fields, 2)])
    inverse, first, second = grids_ref[0], grids_ref[1], grids_ref[2]
    logliks = []
    for s in range(slots):
        x = jnp.concatenate([state_ref[s, 0].astype(jnp.float32), halo_ref[s * fields]], axis=0)
        advected = advect(x, winds)[0:rows].astype(jnp.bfloat16)
        adv_ref[s] = advected
        value = advected.astype(jnp.float32)
        logliks.append(-0.5 * (inverse * value * value - 2.0 * first * value + second))
    smooth = functools.partial(
        jnp.dot, precision=lax.Precision.HIGHEST, preferred_element_type=jnp.float32
    )
    along = smooth(jnp.concatenate(logliks, axis=0), lon_ref[...])
    for s in range(slots):
        scores = smooth(lat_ref[...], along[s * rows : (s + 1) * rows])
        own_ref[s] = scores[0:rows]
        send_ref[s] = scores[rows:]


def rest_kernel(state_ref, halo_ref, east_ref, north_ref, adv_ref, winds_ref):
    slots, fields, rows, width = state_ref.shape
    for i, part in enumerate(
        wind_parts(east_ref, north_ref, halo_ref.at[pl.ds(slots * fields, 2)])
    ):
        winds_ref[i] = part

    def body(i, carry):
        s, f = i // (fields - 1), i % (fields - 1) + 1
        x = jnp.concatenate(
            [state_ref[s, f].astype(jnp.float32), halo_ref[s * fields + f]], axis=0
        )
        winds = [winds_ref[k] for k in range(4)]
        adv_ref[s, f - 1] = advect(x, winds)[0:rows].astype(jnp.bfloat16)
        return carry

    lax.fori_loop(0, slots * (fields - 1), body, 0)


def weigh_kernel(
    order_ref, counts_ref, own_ref, recv_ref, adv_first_ref, adv_rest_ref, *refs
):
    out_refs, parts_ref = refs[:-1], refs[-1]
    slots, rows, width = own_ref.shape
    fields = adv_rest_ref.shape[1] + 1
    across = width // LANES
    members, _, held, _ = parts_ref.shape

    def store(row_tile, index, value):
        for l in range(across):
            tile = value[:, l * LANES : (l + 1) * LANES]
            row = (row_tile * across + l) * TILE
            for k in range(0, TILE, min(held, TILE)):
                chunk, at = divmod(row + k, held)
                parts_ref[chunk, index, at : at + min(held, TILE)] = tile[k : k + min(held, TILE)]

    lower = order_ref[0] == 0
    for t in range(rows // TILE):
        here = slice(t * TILE, (t + 1) * TILE)
        near = (t * TILE) % SMOOTH
        scores = []
        for s in range(slots):
            recv = recv_ref[s, near : near + TILE, :]
            at_this_edge = lower if t * TILE >= rows - SMOOTH else jnp.logical_not(lower)
            score = own_ref[s, here, :] + jnp.where(at_this_edge, recv, 0.0)
            scores.append(jnp.where(s < counts_ref[0], score, -jnp.inf))
        peak = functools.reduce(jnp.maximum, scores)
        gains = [jnp.exp(score - peak) for score in scores]
        store(t, 0, peak)
        store(t, 1, functools.reduce(jnp.add, gains))
        for f in range(fields):
            total = None
            for s in range(slots):
                ref = adv_first_ref.at[s] if f == 0 else adv_rest_ref.at[s, f - 1]
                pair = slice(t // 2 * 2 * TILE, (t // 2 + 1) * 2 * TILE)
                value = ref[pair, :].astype(jnp.float32)[t % 2 * TILE : (t % 2 + 1) * TILE]
                term = gains[s] * value
                total = term if total is None else total + term
            store(t, 2 + f, total)
    for i, out_ref in enumerate(out_refs):
        out_ref[...] = parts_ref[order_ref[1 + i]]


def whole_weigh_kernel(*refs):
    weigh_kernel(*refs[:6], refs[6])


def merge_values(refs):
    peak = functools.reduce(jnp.maximum, [ref[0] for ref in refs])
    factors = [jnp.exp(ref[0] - peak) for ref in refs]
    sums = [
        functools.reduce(jnp.add, [factor * ref[q] for factor, ref in zip(factors, refs)])
        for q in range(1, refs[0].shape[0])
    ]
    return peak, sums


def merge_kernel(*refs):
    out_ref = refs[-1]
    peak, sums = merge_values(refs[:-1])
    out_ref[0] = peak
    for q, value in enumerate(sums):
        out_ref[1 + q] = value


def finish_kernel(*refs):
    merged_ref = refs[-1]
    parts = refs[:-1]
    if len(parts) == 1:
        parts = [parts[0].at[d] for d in range(parts[0].shape[0])]
    _, sums = merge_values(parts)
    for f, weighted in enumerate(sums[1:]):
        merged_ref[f] = weighted / sums[0]


def relax_kernel(order_ref, counts_ref, relax_ref, adv_first_ref, adv_rest_ref, *refs):
    merged_refs, (new_ref, mean_ref, whole_ref) = refs[:-3], refs[-3:]
    slots, fields, rows, width = new_ref.shape
    across = width // LANES
    members, _, held, _ = whole_ref.shape
    if len(merged_refs) == 1:
        whole_ref = merged_refs[0]
    else:
        for i, merged_ref in enumerate(merged_refs):
            whole_ref[order_ref[1 + i]] = merged_ref[...]

    def tile(f, row):
        if held >= TILE:
            return whole_ref[row // held, f, row % held : row % held + TILE]
        return jnp.concatenate([whole_ref[(row + k) // held, f] for k in range(0, TILE, held)], axis=0)

    for f in range(fields):
        factor = relax_ref[f]
        merged = jnp.concatenate(
            [
                jnp.concatenate([tile(f, (t * across + l) * TILE) for l in range(across)], axis=1)
                for t in range(rows // TILE)
            ],
            axis=0,
        )
        mean_ref[f] = merged.astype(jnp.bfloat16)
        for s in range(slots):
            ref = adv_first_ref.at[s] if f == 0 else adv_rest_ref.at[s, f - 1]
            value = ref[...].astype(jnp.float32)
            fresh = value + factor * (merged - value)
            new_ref[s, f] = jnp.where(s < counts_ref[0], fresh, 0.0).astype(jnp.bfloat16)


def call(kernel, ins, outs, scratch=(), **cost):
    return pl.pallas_call(
        kernel,
        out_shape=[jax.ShapeDtypeStruct(shape, dtype) for shape, dtype in outs],
        in_specs=ins,
        out_specs=[VMEM] * len(outs),
        scratch_shapes=list(scratch),
        compiler_params=PARAMS,
        cost_estimate=pl.CostEstimate(**cost),
    )


def on_device(
    state, counts, east_wind, north_wind, obs_cells, obs_mask, obs_values, obs_error, relax
):
    slots, fields, rows, width = state.shape
    f32, bf16 = jnp.float32, jnp.bfloat16
    place = lax.axis_index("lat")
    swap = [(0, 1), (1, 0)]
    lower = place == 0

    edge = lax.dynamic_slice_in_dim(state, jnp.where(lower, rows - TILE, 0), TILE, axis=2)
    winds = jnp.stack([east_wind, north_wind])
    wind_edge = lax.dynamic_slice_in_dim(winds, jnp.where(lower, rows - TILE, 0), TILE, axis=1)
    message = jnp.concatenate(
        [edge.astype(f32).reshape(slots * fields, TILE, width), wind_edge], axis=0
    )
    near = jnp.arange(TILE) < TILE // 2
    keep = jnp.logical_xor(near, lower)
    message = jnp.where(keep[None, :, None], message, 0.0)
    halo = lax.ppermute(message, "lat", swap)

    observations = obs_cells.shape[1]
    flat = [
        x.reshape(observations // LANES, LANES) for x in (obs_cells, obs_mask, obs_values, obs_error)
    ]
    (grids,) = call(
        grids_kernel,
        [VMEM] * 4,
        [((3, rows, width), f32)],
        [pltpu.VMEM((PARTS * 2 * rows, width // 2), f32)],
        flops=2 * PARTS * rows * width * observations,
        bytes_accessed=16 * observations,
        transcendentals=observations,
    )(*flat)

    index = np.arange(rows)
    own = index[None, :] - index[:, None]
    upper_side = index[None, :] - (index[:SMOOTH, None] + rows)
    lower_side = index[None, :] - (index[rows - SMOOTH :, None] - rows)
    lat_kernel = jnp.where(
        lower,
        jnp.asarray(kernel_matrix(np.concatenate([own, upper_side]))),
        jnp.asarray(kernel_matrix(np.concatenate([own, lower_side]))),
    )
    distance = np.abs(np.arange(width)[:, None] - np.arange(width)[None, :])
    lon_kernel = jnp.asarray(kernel_matrix(np.minimum(distance, width - distance)))

    adv_first, own_scores, edge_scores = call(
        first_kernel,
        [VMEM] * 7,
        [
            ((slots, rows, width), bf16),
            ((slots, rows, width), f32),
            ((slots, SMOOTH, width), f32),
        ],
        flops=12 * slots * rows * width * width,
        bytes_accessed=4 * width * width,
        transcendentals=0,
    )(state, halo, east_wind, north_wind, grids, lat_kernel, lon_kernel)
    received = lax.ppermute(edge_scores, "lat", swap)

    (adv_rest,) = call(
        rest_kernel,
        [VMEM] * 4,
        [((slots, fields - 1, rows, width), bf16)],
        [pltpu.VMEM((4, rows + TILE, width), f32)],
        flops=STEPS * 16 * slots * fields * rows * width,
        bytes_accessed=4 * slots * fields * rows * width,
        transcendentals=0,
    )(state, halo, east_wind, north_wind)

    members = lax.axis_size("mem")
    member = lax.axis_index("mem")
    held = rows * width // LANES // members
    quantities = fields + 2
    direct = members == PAIR * LINE
    away = [PAIR * j + i for i in range(PAIR) for j in range(LINE)] if direct else []
    order = jnp.stack([place] + [member ^ offset for offset in away]).astype(jnp.int32)

    def swapped(x, offset):
        return lax.ppermute(x, "mem", [(m, m ^ offset) for m in range(members)])

    chunk = ((quantities, held, LANES), f32)
    all_chunks = ((members,) + chunk[0], f32)
    weigh = call(
        weigh_kernel if direct else whole_weigh_kernel,
        [SMEM, SMEM] + [VMEM] * 4,
        [chunk] * len(away) if direct else [all_chunks],
        [pltpu.VMEM(*all_chunks)] if direct else [],
        flops=4 * slots * fields * rows * width,
        bytes_accessed=4 * slots * fields * rows * width,
        transcendentals=slots * rows * width,
    )
    parts = weigh(order, counts, own_scores, received, adv_first, adv_rest)

    def merge(kernel, pieces, out):
        size = quantities * held * LANES * (len(pieces) if direct else members)
        return call(
            kernel,
            [VMEM] * len(pieces),
            [out],
            flops=4 * size,
            bytes_accessed=4 * size,
            transcendentals=size // quantities,
        )(*pieces)[0]

    merged_chunk = ((fields, held, LANES), f32)
    if direct:
        paired = [None] * LINE
        for j in reversed(range(LINE)):
            paired[j] = merge(merge_kernel, [parts[j], swapped(parts[LINE + j], 1)], chunk)
        pieces = [paired[0]] + [swapped(paired[j], PAIR * j) for j in range(1, LINE)]
        merged = merge(finish_kernel, pieces, merged_chunk)
        shares = [merged] + [swapped(merged, PAIR * j) for j in range(1, LINE)]
        shares = shares + [swapped(share, 1) for share in shares]
    else:
        got = lax.all_to_all(parts[0], "mem", 0, 0, tiled=True)
        shares = [lax.all_gather(merge(finish_kernel, [got], merged_chunk), "mem")]

    new_state, mean = call(
        relax_kernel,
        [SMEM] * 3 + [VMEM] * (2 + len(shares)),
        [((slots, fields, rows, width), bf16), ((fields, rows, width), bf16)],
        [pltpu.VMEM((members, fields, held, LANES), f32)],
        flops=4 * slots * fields * rows * width,
        bytes_accessed=4 * slots * fields * rows * width,
        transcendentals=0,
    )(order, counts, relax, adv_first, adv_rest, *shares)
    return (new_state, mean)


def solution(mesh):
    return jax.shard_map(
        on_device,
        mesh=mesh,
        in_specs=(
            P(("groups", "mem"), None, "lat", None),
            P(("groups", "mem")),
            P(("groups", "lat"), None),
            P(("groups", "lat"), None),
            P(("groups", "lat"), None),
            P(("groups", "lat"), None),
            P(("groups", "lat"), None),
            P(("groups", "lat"), None),
            P(),
        ),
        out_specs=(P(("groups", "mem"), None, "lat", None), P("groups", "lat", None)),
        check_vma=False,
    )
```

```python
import functools

import jax
import jax.numpy as jnp
import numpy as np
from jax import lax
from jax.experimental import pallas as pl
from jax.experimental.pallas import tpu as pltpu
from jax.sharding import PartitionSpec as P

STEPS = 4
SMOOTH = 16
LOG_TWO_PI = 1.8378770664093453
LANES = 128
TILE = 8
PARTS = 5
CHUNK_ROWS = 8
PAIR = 2
LINE = 4


VMEM = pl.BlockSpec(memory_space=pltpu.VMEM)
SMEM = pl.BlockSpec(memory_space=pltpu.SMEM)
PARAMS = pltpu.CompilerParams(vmem_limit_bytes=24 * 1024 * 1024)


def kernel_matrix(offset):
    values = np.exp(-((2.0 * offset.astype(np.float32) / SMOOTH) ** 2))
    return np.where(np.abs(offset) <= SMOOTH, values, 0.0).astype(np.float32)


def split_two(x):
    high = x.astype(jnp.bfloat16).astype(jnp.float32)
    return high, x - high


def grids_kernel(cells_ref, mask_ref, values_ref, error_ref, grids_ref, acc_ref):
    rows, width = grids_ref.shape[1:]
    half = width // 2
    highs = 2 * rows
    pack = 16
    high_iota = [
        (lax.broadcasted_iota(jnp.int32, (pack, LANES), 0) + pack * i)
        .astype(jnp.float32)
        .astype(jnp.bfloat16)
        for i in range(highs // pack)
    ]
    low_iota = [
        (lax.broadcasted_iota(jnp.int32, (pack, LANES), 0) + pack * i)
        .astype(jnp.float32)
        .astype(jnp.bfloat16)
        for i in range(half // pack)
    ]
    zero = jnp.zeros((pack, LANES), jnp.bfloat16)
    one = jnp.ones((pack, LANES), jnp.bfloat16)
    acc_ref[...] = jnp.zeros_like(acc_ref)

    def body(step, carry):
        here = pl.ds(pl.multiple_of(step * CHUNK_ROWS, CHUNK_ROWS), CHUNK_ROWS)
        cells = cells_ref[here, :]
        used = mask_ref[here, :].astype(jnp.float32)
        values = values_ref[here, :]
        error = error_ref[here, :]
        inverse = used / (error * error)
        first = inverse * values
        second = first * values + used * (2.0 * jnp.log(error) + LOG_TWO_PI)
        row = cells // width
        column = cells % width
        side = column // half
        high = (side * rows + row).astype(jnp.float32)
        low = (column % half).astype(jnp.float32)
        parts = split_two(inverse) + split_two(first) + (second,)
        left, right = [], []
        for r in range(CHUNK_ROWS):

            def spread(x):
                return jnp.broadcast_to(x[r : r + 1, :], (pack, LANES)).astype(jnp.bfloat16)

            high_row, low_row = spread(high), spread(low)
            hit = [iota == high_row for iota in high_iota]
            pieces = []
            for part in parts:
                part_row = spread(part)
                pieces += [jnp.where(h, part_row, zero) for h in hit]
            left.append(jnp.concatenate(pieces, axis=0))
            right.append(
                jnp.concatenate([jnp.where(iota == low_row, one, zero) for iota in low_iota], axis=0)
            )
        acc_ref[...] += lax.dot_general(
            jnp.concatenate(left, axis=1),
            jnp.concatenate(right, axis=1),
            (((1,), (1,)), ((), ())),
            preferred_element_type=jnp.float32,
        )
        return carry

    lax.fori_loop(0, cells_ref.shape[0] // CHUNK_ROWS, body, 0)

    def part_sum(indices):
        total = acc_ref[pl.ds(indices[-1] * highs, highs), :]
        for i in indices[-2::-1]:
            total = total + acc_ref[pl.ds(i * highs, highs), :]
        return total

    for g, indices in enumerate(((0, 1), (2, 3), (4,))):
        total = part_sum(indices)
        grids_ref[g, :, 0:half] = total[0:rows]
        grids_ref[g, :, half:width] = total[rows:highs]


def wind_parts(east_ref, north_ref, wind_halo_ref):
    east = jnp.concatenate([east_ref[...], wind_halo_ref[0]], axis=0)
    north = jnp.concatenate([north_ref[...], wind_halo_ref[1]], axis=0)
    west, south = jnp.maximum(east, 0.0), jnp.maximum(north, 0.0)
    east, north = -jnp.minimum(east, 0.0), -jnp.minimum(north, 0.0)
    return 1.0 - west - east - south - north, west, east, south, north


def advect(x, winds):
    count, width = x.shape
    centre, west, east, south, north = winds
    for _ in range(STEPS):
        x = (
            centre * x
            + west * pltpu.roll(x, 1, 1)
            + east * pltpu.roll(x, width - 1, 1)
            + south * pltpu.roll(x, 1, 0)
            + north * pltpu.roll(x, count - 1, 0)
        )
    return x


def first_kernel(
    state_ref, halo_ref, east_ref, north_ref, grids_ref, lat_ref, lon_ref, adv_ref, own_ref, send_ref
):
    slots, _, rows, width = state_ref.shape
    fields = state_ref.shape[1]
    winds = wind_parts(east_ref, north_ref, halo_ref.at[pl.ds(slots * fields, 2)])
    inverse, first, second = grids_ref[0], grids_ref[1], grids_ref[2]
    logliks = []
    for s in range(slots):
        x = jnp.concatenate([state_ref[s, 0].astype(jnp.float32), halo_ref[s * fields]], axis=0)
        advected = advect(x, winds)[0:rows].astype(jnp.bfloat16)
        adv_ref[s] = advected
        value = advected.astype(jnp.float32)
        logliks.append(-0.5 * (inverse * value * value - 2.0 * first * value + second))
    smooth = functools.partial(
        jnp.dot, precision=lax.Precision.HIGHEST, preferred_element_type=jnp.float32
    )
    along = smooth(jnp.concatenate(logliks, axis=0), lon_ref[...])
    for s in range(slots):
        scores = smooth(lat_ref[...], along[s * rows : (s + 1) * rows])
        own_ref[s] = scores[0:rows]
        send_ref[s] = scores[rows:]


def rest_kernel(state_ref, halo_ref, east_ref, north_ref, adv_ref, winds_ref):
    slots, fields, rows, width = state_ref.shape
    for i, part in enumerate(
        wind_parts(east_ref, north_ref, halo_ref.at[pl.ds(slots * fields, 2)])
    ):
        winds_ref[i] = part

    def body(i, carry):
        pair, f = i // (fields - 1), i % (fields - 1) + 1
        winds = [winds_ref[k] for k in range(5)]
        for s in (2 * pair, 2 * pair + 1):
            x = jnp.concatenate(
                [state_ref[s, f].astype(jnp.float32), halo_ref[s * fields + f]], axis=0
            )
            adv_ref[s, f - 1] = advect(x, winds)[0:rows].astype(jnp.bfloat16)
        return carry

    lax.fori_loop(0, slots // 2 * (fields - 1), body, 0)


def weigh_kernel(
    order_ref, counts_ref, own_ref, recv_ref, adv_first_ref, adv_rest_ref, *refs
):
    out_refs, parts_ref = refs[:-1], refs[-1]
    slots, rows, width = own_ref.shape
    fields = adv_rest_ref.shape[1] + 1
    across = width // LANES
    members, _, held, _ = parts_ref.shape

    def store(row_tile, index, value):
        for l in range(across):
            tile = value[:, l * LANES : (l + 1) * LANES]
            row = (row_tile * across + l) * TILE
            for k in range(0, TILE, min(held, TILE)):
                chunk, at = divmod(row + k, held)
                parts_ref[chunk, index, at : at + min(held, TILE)] = tile[k : k + min(held, TILE)]

    lower = order_ref[0] == 0
    for t in range(rows // TILE):
        here = slice(t * TILE, (t + 1) * TILE)
        near = (t * TILE) % SMOOTH
        scores = []
        for s in range(slots):
            recv = recv_ref[s, near : near + TILE, :]
            at_this_edge = lower if t * TILE >= rows - SMOOTH else jnp.logical_not(lower)
            score = own_ref[s, here, :] + jnp.where(at_this_edge, recv, 0.0)
            scores.append(jnp.where(s < counts_ref[0], score, -jnp.inf))
        peak = functools.reduce(jnp.maximum, scores)
        gains = [jnp.exp(score - peak) for score in scores]
        store(t, 0, peak)
        store(t, 1, functools.reduce(jnp.add, gains))
        for f in range(fields):
            total = None
            for s in range(slots):
                ref = adv_first_ref.at[s] if f == 0 else adv_rest_ref.at[s, f - 1]
                pair = slice(t // 2 * 2 * TILE, (t // 2 + 1) * 2 * TILE)
                value = ref[pair, :].astype(jnp.float32)[t % 2 * TILE : (t % 2 + 1) * TILE]
                term = gains[s] * value
                total = term if total is None else total + term
            store(t, 2 + f, total)
    for i, out_ref in enumerate(out_refs):
        out_ref[...] = parts_ref[order_ref[1 + i]]


def whole_weigh_kernel(*refs):
    weigh_kernel(*refs[:6], refs[6])


def merge_values(refs):
    peak = functools.reduce(jnp.maximum, [ref[0] for ref in refs])
    factors = [jnp.exp(ref[0] - peak) for ref in refs]
    sums = [
        functools.reduce(jnp.add, [factor * ref[q] for factor, ref in zip(factors, refs)])
        for q in range(1, refs[0].shape[0])
    ]
    return peak, sums


def merge_kernel(*refs):
    out_ref = refs[-1]
    peak, sums = merge_values(refs[:-1])
    out_ref[0] = peak
    for q, value in enumerate(sums):
        out_ref[1 + q] = value


def finish_kernel(*refs):
    merged_ref = refs[-1]
    parts = refs[:-1]
    if len(parts) == 1:
        parts = [parts[0].at[d] for d in range(parts[0].shape[0])]
    _, sums = merge_values(parts)
    for f, weighted in enumerate(sums[1:]):
        merged_ref[f] = weighted / sums[0]


def relax_kernel(order_ref, counts_ref, relax_ref, adv_first_ref, adv_rest_ref, *refs):
    merged_refs, (new_ref, mean_ref, whole_ref) = refs[:-3], refs[-3:]
    slots, fields, rows, width = new_ref.shape
    across = width // LANES
    members, _, held, _ = whole_ref.shape
    if len(merged_refs) == 1:
        whole_ref = merged_refs[0]
    else:
        for i, merged_ref in enumerate(merged_refs):
            whole_ref[order_ref[1 + i]] = merged_ref[...]

    def tile(f, row):
        if held >= TILE:
            return whole_ref[row // held, f, row % held : row % held + TILE]
        return jnp.concatenate([whole_ref[(row + k) // held, f] for k in range(0, TILE, held)], axis=0)

    for f in range(fields):
        factor = relax_ref[f]
        merged = jnp.concatenate(
            [
                jnp.concatenate([tile(f, (t * across + l) * TILE) for l in range(across)], axis=1)
                for t in range(rows // TILE)
            ],
            axis=0,
        )
        mean_ref[f] = merged.astype(jnp.bfloat16)
        for s in range(slots):
            ref = adv_first_ref.at[s] if f == 0 else adv_rest_ref.at[s, f - 1]
            value = ref[...].astype(jnp.float32)
            fresh = value + factor * (merged - value)
            new_ref[s, f] = jnp.where(s < counts_ref[0], fresh, 0.0).astype(jnp.bfloat16)


def call(kernel, ins, outs, scratch=(), **cost):
    return pl.pallas_call(
        kernel,
        out_shape=[jax.ShapeDtypeStruct(shape, dtype) for shape, dtype in outs],
        in_specs=ins,
        out_specs=[VMEM] * len(outs),
        scratch_shapes=list(scratch),
        compiler_params=PARAMS,
        cost_estimate=pl.CostEstimate(**cost),
    )


def on_device(
    state, counts, east_wind, north_wind, obs_cells, obs_mask, obs_values, obs_error, relax
):
    slots, fields, rows, width = state.shape
    f32, bf16 = jnp.float32, jnp.bfloat16
    place = lax.axis_index("lat")
    swap = [(0, 1), (1, 0)]
    lower = place == 0

    edge = lax.dynamic_slice_in_dim(state, jnp.where(lower, rows - TILE, 0), TILE, axis=2)
    winds = jnp.stack([east_wind, north_wind])
    wind_edge = lax.dynamic_slice_in_dim(winds, jnp.where(lower, rows - TILE, 0), TILE, axis=1)
    message = jnp.concatenate(
        [edge.astype(f32).reshape(slots * fields, TILE, width), wind_edge], axis=0
    )
    near = jnp.arange(TILE) < TILE // 2
    keep = jnp.logical_xor(near, lower)
    message = jnp.where(keep[None, :, None], message, 0.0)
    halo = lax.ppermute(message, "lat", swap)

    observations = obs_cells.shape[1]
    flat = [
        x.reshape(observations // LANES, LANES) for x in (obs_cells, obs_mask, obs_values, obs_error)
    ]
    (grids,) = call(
        grids_kernel,
        [VMEM] * 4,
        [((3, rows, width), f32)],
        [pltpu.VMEM((PARTS * 2 * rows, width // 2), f32)],
        flops=2 * PARTS * rows * width * observations,
        bytes_accessed=16 * observations,
        transcendentals=observations,
    )(*flat)

    index = np.arange(rows)
    own = index[None, :] - index[:, None]
    upper_side = index[None, :] - (index[:SMOOTH, None] + rows)
    lower_side = index[None, :] - (index[rows - SMOOTH :, None] - rows)
    lat_kernel = jnp.where(
        lower,
        jnp.asarray(kernel_matrix(np.concatenate([own, upper_side]))),
        jnp.asarray(kernel_matrix(np.concatenate([own, lower_side]))),
    )
    distance = np.abs(np.arange(width)[:, None] - np.arange(width)[None, :])
    lon_kernel = jnp.asarray(kernel_matrix(np.minimum(distance, width - distance)))

    adv_first, own_scores, edge_scores = call(
        first_kernel,
        [VMEM] * 7,
        [
            ((slots, rows, width), bf16),
            ((slots, rows, width), f32),
            ((slots, SMOOTH, width), f32),
        ],
        flops=12 * slots * rows * width * width,
        bytes_accessed=4 * width * width,
        transcendentals=0,
    )(state, halo, east_wind, north_wind, grids, lat_kernel, lon_kernel)
    received = lax.ppermute(edge_scores, "lat", swap)

    (adv_rest,) = call(
        rest_kernel,
        [VMEM] * 4,
        [((slots, fields - 1, rows, width), bf16)],
        [pltpu.VMEM((5, rows + TILE, width), f32)],
        flops=STEPS * 16 * slots * fields * rows * width,
        bytes_accessed=4 * slots * fields * rows * width,
        transcendentals=0,
    )(state, halo, east_wind, north_wind)

    members = lax.axis_size("mem")
    member = lax.axis_index("mem")
    held = rows * width // LANES // members
    quantities = fields + 2
    direct = members == PAIR * LINE
    away = [PAIR * j + i for i in range(PAIR) for j in range(LINE)] if direct else []
    order = jnp.stack([place] + [member ^ offset for offset in away]).astype(jnp.int32)

    def swapped(x, offset):
        return lax.ppermute(x, "mem", [(m, m ^ offset) for m in range(members)])

    chunk = ((quantities, held, LANES), f32)
    all_chunks = ((members,) + chunk[0], f32)
    weigh = call(
        weigh_kernel if direct else whole_weigh_kernel,
        [SMEM, SMEM] + [VMEM] * 4,
        [chunk] * len(away) if direct else [all_chunks],
        [pltpu.VMEM(*all_chunks)] if direct else [],
        flops=4 * slots * fields * rows * width,
        bytes_accessed=4 * slots * fields * rows * width,
        transcendentals=slots * rows * width,
    )
    parts = weigh(order, counts, own_scores, received, adv_first, adv_rest)

    def merge(kernel, pieces, out):
        size = quantities * held * LANES * (len(pieces) if direct else members)
        return call(
            kernel,
            [VMEM] * len(pieces),
            [out],
            flops=4 * size,
            bytes_accessed=4 * size,
            transcendentals=size // quantities,
        )(*pieces)[0]

    merged_chunk = ((fields, held, LANES), f32)
    if direct:
        paired = [None] * LINE
        for j in reversed(range(LINE)):
            paired[j] = merge(merge_kernel, [parts[j], swapped(parts[LINE + j], 1)], chunk)
        pieces = [paired[0]] + [swapped(paired[j], PAIR * j) for j in range(1, LINE)]
        merged = merge(finish_kernel, pieces, merged_chunk)
        shares = [merged] + [swapped(merged, PAIR * j) for j in range(1, LINE)]
        shares = shares + [swapped(share, 1) for share in shares]
    else:
        got = lax.all_to_all(parts[0], "mem", 0, 0, tiled=True)
        shares = [lax.all_gather(merge(finish_kernel, [got], merged_chunk), "mem")]

    new_state, mean = call(
        relax_kernel,
        [SMEM] * 3 + [VMEM] * (2 + len(shares)),
        [((slots, fields, rows, width), bf16), ((fields, rows, width), bf16)],
        [pltpu.VMEM((members, fields, held, LANES), f32)],
        flops=4 * slots * fields * rows * width,
        bytes_accessed=4 * slots * fields * rows * width,
        transcendentals=0,
    )(order, counts, relax, adv_first, adv_rest, *shares)
    return (new_state, mean)


def solution(mesh):
    return jax.shard_map(
        on_device,
        mesh=mesh,
        in_specs=(
            P(("groups", "mem"), None, "lat", None),
            P(("groups", "mem")),
            P(("groups", "lat"), None),
            P(("groups", "lat"), None),
            P(("groups", "lat"), None),
            P(("groups", "lat"), None),
            P(("groups", "lat"), None),
            P(("groups", "lat"), None),
            P(),
        ),
        out_specs=(P(("groups", "mem"), None, "lat", None), P("groups", "lat", None)),
        check_vma=False,
    )
```

```python
import functools

import jax
import jax.numpy as jnp
import numpy as np
from jax import lax
from jax.experimental import pallas as pl
from jax.experimental.pallas import tpu as pltpu
from jax.sharding import PartitionSpec as P

STEPS = 4
SMOOTH = 16
LOG_TWO_PI = 1.8378770664093453
LANES = 128
TILE = 8
PARTS = 5
CHUNK_ROWS = 16
PACK = 16
BEGIN_STEPS = 4
LATER_FIELDS = 2
PAIR = 2
LINE = 4


VMEM = pl.BlockSpec(memory_space=pltpu.VMEM)
SMEM = pl.BlockSpec(memory_space=pltpu.SMEM)
PARAMS = pltpu.CompilerParams(vmem_limit_bytes=24 * 1024 * 1024)


def kernel_matrix(offset):
    values = np.exp(-((2.0 * offset.astype(np.float32) / SMOOTH) ** 2))
    return np.where(np.abs(offset) <= SMOOTH, values, 0.0).astype(np.float32)


def split_two(x):
    high = x.astype(jnp.bfloat16).astype(jnp.float32)
    return high, x - high


def spread_terms(cells_ref, mask_ref, values_ref, error_ref, rows_ref, rows, width):
    half = width // 2
    cells = cells_ref[...]
    used = mask_ref[...].astype(jnp.float32)
    values = values_ref[...]
    error = error_ref[...]
    inverse = used / (error * error)
    first = inverse * values
    second = first * values + used * (2.0 * jnp.log(error) + LOG_TWO_PI)
    row = cells // width
    column = cells % width
    high = (column // half * rows + row).astype(jnp.float32)
    low = (column % half).astype(jnp.float32)
    for k, x in enumerate(split_two(inverse) + split_two(first) + (second, high, low)):
        rows_ref[k] = x


def add_observations(step, rows_ref, acc_ref):
    highs, lows = acc_ref.shape[0] // PARTS, acc_ref.shape[1]

    def steps_of(count):
        base = lax.broadcasted_iota(jnp.int32, (PACK, LANES), 0)
        return [
            (base + PACK * i).astype(jnp.float32).astype(jnp.bfloat16) for i in range(count // PACK)
        ]

    high_iota, low_iota = steps_of(highs), steps_of(lows)
    zero = jnp.zeros((PACK, LANES), jnp.bfloat16)
    one = jnp.ones((PACK, LANES), jnp.bfloat16)
    here = pl.ds(pl.multiple_of(step * CHUNK_ROWS, CHUNK_ROWS), CHUNK_ROWS)
    held = [rows_ref[k, here, :] for k in range(PARTS + 2)]
    left, right = [], []
    for r in range(CHUNK_ROWS):
        spread = [
            jnp.broadcast_to(x[r : r + 1, :], (PACK, LANES)).astype(jnp.bfloat16) for x in held
        ]
        high_row, low_row = spread[PARTS:]
        hit = [iota == high_row for iota in high_iota]
        left.append(
            jnp.concatenate([jnp.where(h, part, zero) for part in spread[:PARTS] for h in hit], axis=0)
        )
        right.append(
            jnp.concatenate([jnp.where(iota == low_row, one, zero) for iota in low_iota], axis=0)
        )
    acc_ref[...] += lax.dot_general(
        jnp.concatenate(left, axis=1),
        jnp.concatenate(right, axis=1),
        (((1,), (1,)), ((), ())),
        preferred_element_type=jnp.float32,
    )


def grids_of(acc_ref, rows):
    highs = 2 * rows

    def part_sum(indices):
        total = acc_ref[pl.ds(indices[-1] * highs, highs), :]
        for i in indices[-2::-1]:
            total = total + acc_ref[pl.ds(i * highs, highs), :]
        return jnp.concatenate([total[0:rows], total[rows:highs]], axis=1)

    return [part_sum(indices) for indices in ((0, 1), (2, 3), (4,))]


def begin_kernel(rows, width, steps, cells_ref, mask_ref, values_ref, error_ref, rows_ref, acc_ref):
    spread_terms(cells_ref, mask_ref, values_ref, error_ref, rows_ref, rows, width)
    acc_ref[...] = jnp.zeros_like(acc_ref)

    def body(step, carry):
        add_observations(step, rows_ref, acc_ref)
        return carry

    lax.fori_loop(0, steps, body, 0)


def wind_parts(east_ref, north_ref, wind_halo_ref):
    east = jnp.concatenate([east_ref[...], wind_halo_ref[0]], axis=0)
    north = jnp.concatenate([north_ref[...], wind_halo_ref[1]], axis=0)
    west, south = jnp.maximum(east, 0.0), jnp.maximum(north, 0.0)
    east, north = -jnp.minimum(east, 0.0), -jnp.minimum(north, 0.0)
    return 1.0 - west - east - south - north, west, east, south, north


def advect(x, winds):
    count, width = x.shape
    centre, west, east, south, north = winds
    for _ in range(STEPS):
        x = (
            centre * x
            + west * pltpu.roll(x, 1, 1)
            + east * pltpu.roll(x, width - 1, 1)
            + south * pltpu.roll(x, 1, 0)
            + north * pltpu.roll(x, count - 1, 0)
        )
    return x


def store_winds(east_ref, north_ref, halo_ref, count, winds_ref):
    for i, part in enumerate(wind_parts(east_ref, north_ref, halo_ref.at[pl.ds(count, 2)])):
        winds_ref[i] = part


def advect_pair(state_ref, halo_ref, winds_ref, pair, f, adv_ref, place):
    fields, rows = state_ref.shape[1:3]
    winds = [winds_ref[k] for k in range(5)]
    for s in (2 * pair, 2 * pair + 1):
        x = jnp.concatenate(
            [state_ref[s, f].astype(jnp.float32), halo_ref[s * fields + f]], axis=0
        )
        adv_ref[s, place] = advect(x, winds)[0:rows].astype(jnp.bfloat16)


def first_kernel(
    steps, state_ref, halo_ref, east_ref, north_ref, terms_ref, acc_in_ref, lat_ref, lon_ref,
    adv_ref, own_ref, send_ref, acc_ref, winds_ref,
):
    slots, fields, rows, width = state_ref.shape
    pairs = slots // 2
    store_winds(east_ref, north_ref, halo_ref, slots * fields, winds_ref)
    acc_ref[...] = acc_in_ref[...]
    held = adv_ref.shape[1]
    total = terms_ref.shape[1] // CHUNK_ROWS

    def body(i, carry):
        add_observations(steps + i, terms_ref, acc_ref)
        advect_pair(state_ref, halo_ref, winds_ref, i % pairs, i // pairs, adv_ref, i // pairs)
        return carry

    def observe(step, carry):
        add_observations(step, terms_ref, acc_ref)
        return carry

    shared = min(pairs * held, total - steps)
    lax.fori_loop(0, shared, body, 0)
    if steps + shared < total:
        lax.fori_loop(steps + shared, total, observe, 0)
    for i in range(shared, pairs * held):
        advect_pair(state_ref, halo_ref, winds_ref, i % pairs, i // pairs, adv_ref, i // pairs)

    inverse, first, second = grids_of(acc_ref, rows)
    logliks = []
    for s in range(slots):
        value = adv_ref[s, 0].astype(jnp.float32)
        logliks.append(-0.5 * (inverse * value * value - 2.0 * first * value + second))
    smooth = functools.partial(
        jnp.dot, precision=lax.Precision.HIGHEST, preferred_element_type=jnp.float32
    )
    along = smooth(jnp.concatenate(logliks, axis=0), lon_ref[...])
    for s in range(slots):
        scores = smooth(lat_ref[...], along[s * rows : (s + 1) * rows])
        own_ref[s] = scores[0:rows]
        send_ref[s] = scores[rows:]


def rest_kernel(state_ref, halo_ref, east_ref, north_ref, adv_ref, winds_ref):
    slots, fields = state_ref.shape[:2]
    pairs = slots // 2
    held = adv_ref.shape[1]
    store_winds(east_ref, north_ref, halo_ref, slots * fields, winds_ref)

    def body(i, carry):
        f = fields - held + i // pairs
        advect_pair(state_ref, halo_ref, winds_ref, i % pairs, f, adv_ref, i // pairs)
        return carry

    lax.fori_loop(0, pairs * held, body, 0)


def field_ref(adv_first_ref, adv_rest_ref, s, f):
    held = adv_first_ref.shape[1]
    return adv_first_ref.at[s, f] if f < held else adv_rest_ref.at[s, f - held]


def weigh_kernel(
    order_ref, counts_ref, own_ref, recv_ref, adv_first_ref, adv_rest_ref, *refs
):
    out_refs, parts_ref = refs[:-1], refs[-1]
    slots, rows, width = own_ref.shape
    fields = adv_first_ref.shape[1] + adv_rest_ref.shape[1]
    across = width // LANES
    members, _, held, _ = parts_ref.shape

    def store(row_tile, index, value):
        for l in range(across):
            tile = value[:, l * LANES : (l + 1) * LANES]
            row = (row_tile * across + l) * TILE
            for k in range(0, TILE, min(held, TILE)):
                chunk, at = divmod(row + k, held)
                parts_ref[chunk, index, at : at + min(held, TILE)] = tile[k : k + min(held, TILE)]

    lower = order_ref[0] == 0
    for t in range(rows // TILE):
        here = slice(t * TILE, (t + 1) * TILE)
        near = (t * TILE) % SMOOTH
        scores = []
        for s in range(slots):
            recv = recv_ref[s, near : near + TILE, :]
            at_this_edge = lower if t * TILE >= rows - SMOOTH else jnp.logical_not(lower)
            score = own_ref[s, here, :] + jnp.where(at_this_edge, recv, 0.0)
            scores.append(jnp.where(s < counts_ref[0], score, -jnp.inf))
        peak = functools.reduce(jnp.maximum, scores)
        gains = [jnp.exp(score - peak) for score in scores]
        store(t, 0, peak)
        store(t, 1, functools.reduce(jnp.add, gains))
        for f in range(fields):
            total = None
            for s in range(slots):
                ref = field_ref(adv_first_ref, adv_rest_ref, s, f)
                pair = slice(t // 2 * 2 * TILE, (t // 2 + 1) * 2 * TILE)
                value = ref[pair, :].astype(jnp.float32)[t % 2 * TILE : (t % 2 + 1) * TILE]
                term = gains[s] * value
                total = term if total is None else total + term
            store(t, 2 + f, total)
    for i, out_ref in enumerate(out_refs):
        out_ref[...] = parts_ref[order_ref[1 + i]]


def whole_weigh_kernel(*refs):
    weigh_kernel(*refs[:6], refs[6])


def merge_values(refs):
    peak = functools.reduce(jnp.maximum, [ref[0] for ref in refs])
    factors = [jnp.exp(ref[0] - peak) for ref in refs]
    sums = [
        functools.reduce(jnp.add, [factor * ref[q] for factor, ref in zip(factors, refs)])
        for q in range(1, refs[0].shape[0])
    ]
    return peak, sums


def merge_kernel(*refs):
    out_ref = refs[-1]
    peak, sums = merge_values(refs[:-1])
    out_ref[0] = peak
    for q, value in enumerate(sums):
        out_ref[1 + q] = value


def finish_kernel(*refs):
    merged_ref = refs[-1]
    parts = refs[:-1]
    if len(parts) == 1:
        parts = [parts[0].at[d] for d in range(parts[0].shape[0])]
    _, sums = merge_values(parts)
    for f, weighted in enumerate(sums[1:]):
        merged_ref[f] = weighted / sums[0]


def relax_kernel(order_ref, counts_ref, relax_ref, adv_first_ref, adv_rest_ref, *refs):
    merged_refs, (new_ref, mean_ref, whole_ref) = refs[:-3], refs[-3:]
    slots, fields, rows, width = new_ref.shape
    across = width // LANES
    members, _, held, _ = whole_ref.shape
    if len(merged_refs) == 1:
        whole_ref = merged_refs[0]
    else:
        for i, merged_ref in enumerate(merged_refs):
            whole_ref[order_ref[1 + i]] = merged_ref[...]

    def tile(f, row):
        if held >= TILE:
            return whole_ref[row // held, f, row % held : row % held + TILE]
        return jnp.concatenate([whole_ref[(row + k) // held, f] for k in range(0, TILE, held)], axis=0)

    for f in range(fields):
        factor = relax_ref[f]
        merged = jnp.concatenate(
            [
                jnp.concatenate([tile(f, (t * across + l) * TILE) for l in range(across)], axis=1)
                for t in range(rows // TILE)
            ],
            axis=0,
        )
        mean_ref[f] = merged.astype(jnp.bfloat16)
        for s in range(slots):
            ref = field_ref(adv_first_ref, adv_rest_ref, s, f)
            value = ref[...].astype(jnp.float32)
            fresh = value + factor * (merged - value)
            new_ref[s, f] = jnp.where(s < counts_ref[0], fresh, 0.0).astype(jnp.bfloat16)


def call(kernel, ins, outs, scratch=(), **cost):
    return pl.pallas_call(
        kernel,
        out_shape=[jax.ShapeDtypeStruct(shape, dtype) for shape, dtype in outs],
        in_specs=ins,
        out_specs=[VMEM] * len(outs),
        scratch_shapes=list(scratch),
        compiler_params=PARAMS,
        cost_estimate=pl.CostEstimate(**cost),
    )


def on_device(
    state, counts, east_wind, north_wind, obs_cells, obs_mask, obs_values, obs_error, relax
):
    slots, fields, rows, width = state.shape
    f32, bf16 = jnp.float32, jnp.bfloat16
    place = lax.axis_index("lat")
    swap = [(0, 1), (1, 0)]
    lower = place == 0

    edge = lax.dynamic_slice_in_dim(state, jnp.where(lower, rows - TILE, 0), TILE, axis=2)
    winds = jnp.stack([east_wind, north_wind])
    wind_edge = lax.dynamic_slice_in_dim(winds, jnp.where(lower, rows - TILE, 0), TILE, axis=1)
    message = jnp.concatenate(
        [edge.astype(f32).reshape(slots * fields, TILE, width), wind_edge], axis=0
    )
    near = jnp.arange(TILE) < TILE // 2
    keep = jnp.logical_xor(near, lower)
    message = jnp.where(keep[None, :, None], message, 0.0)
    halo = lax.ppermute(message, "lat", swap)

    observations = obs_cells.shape[1]
    flat = [
        x.reshape(observations // LANES, LANES) for x in (obs_cells, obs_mask, obs_values, obs_error)
    ]
    acc_shape = (PARTS * 2 * rows, width // 2)
    all_steps = observations // (LANES * CHUNK_ROWS)
    begin_steps = min(BEGIN_STEPS, all_steps)
    observe_flops = 2 * PARTS * rows * width * LANES * CHUNK_ROWS
    terms, begun = call(
        functools.partial(begin_kernel, rows, width, begin_steps),
        [VMEM] * 4,
        [((PARTS + 2, observations // LANES, LANES), f32), (acc_shape, f32)],
        flops=observe_flops * begin_steps,
        bytes_accessed=16 * observations,
        transcendentals=observations,
    )(*flat)

    index = np.arange(rows)
    own = index[None, :] - index[:, None]
    upper_side = index[None, :] - (index[:SMOOTH, None] + rows)
    lower_side = index[None, :] - (index[rows - SMOOTH :, None] - rows)
    lat_kernel = jnp.where(
        lower,
        jnp.asarray(kernel_matrix(np.concatenate([own, upper_side]))),
        jnp.asarray(kernel_matrix(np.concatenate([own, lower_side]))),
    )
    distance = np.abs(np.arange(width)[:, None] - np.arange(width)[None, :])
    lon_kernel = jnp.asarray(kernel_matrix(np.minimum(distance, width - distance)))

    winds_scratch = pltpu.VMEM((5, rows + TILE, width), f32)
    advect_flops = STEPS * 16 * slots * rows * width
    adv_first, own_scores, edge_scores = call(
        functools.partial(first_kernel, begin_steps),
        [VMEM] * 8,
        [
            ((slots, fields - LATER_FIELDS, rows, width), bf16),
            ((slots, rows, width), f32),
            ((slots, SMOOTH, width), f32),
        ],
        [pltpu.VMEM(acc_shape, f32), winds_scratch],
        flops=observe_flops * (all_steps - begin_steps) + advect_flops * (fields - LATER_FIELDS),
        bytes_accessed=4 * width * width,
        transcendentals=0,
    )(state, halo, east_wind, north_wind, terms, begun, lat_kernel, lon_kernel)
    received = lax.ppermute(edge_scores, "lat", swap)

    (adv_rest,) = call(
        rest_kernel,
        [VMEM] * 4,
        [((slots, LATER_FIELDS, rows, width), bf16)],
        [winds_scratch],
        flops=advect_flops * LATER_FIELDS,
        bytes_accessed=4 * slots * fields * rows * width,
        transcendentals=0,
    )(state, halo, east_wind, north_wind)

    members = lax.axis_size("mem")
    member = lax.axis_index("mem")
    held = rows * width // LANES // members
    quantities = fields + 2
    direct = members == PAIR * LINE
    away = [PAIR * j + i for i in range(PAIR) for j in range(LINE)] if direct else []
    order = jnp.stack([place] + [member ^ offset for offset in away]).astype(jnp.int32)

    def swapped(x, offset):
        return lax.ppermute(x, "mem", [(m, m ^ offset) for m in range(members)])

    chunk = ((quantities, held, LANES), f32)
    all_chunks = ((members,) + chunk[0], f32)
    weigh = call(
        weigh_kernel if direct else whole_weigh_kernel,
        [SMEM, SMEM] + [VMEM] * 4,
        [chunk] * len(away) if direct else [all_chunks],
        [pltpu.VMEM(*all_chunks)] if direct else [],
        flops=4 * slots * fields * rows * width,
        bytes_accessed=4 * slots * fields * rows * width,
        transcendentals=slots * rows * width,
    )
    parts = weigh(order, counts, own_scores, received, adv_first, adv_rest)

    def merge(kernel, pieces, out):
        size = quantities * held * LANES * (len(pieces) if direct else members)
        return call(
            kernel,
            [VMEM] * len(pieces),
            [out],
            flops=4 * size,
            bytes_accessed=4 * size,
            transcendentals=size // quantities,
        )(*pieces)[0]

    merged_chunk = ((fields, held, LANES), f32)
    if direct:
        paired = [None] * LINE
        for j in reversed(range(LINE)):
            paired[j] = merge(merge_kernel, [parts[j], swapped(parts[LINE + j], 1)], chunk)
        pieces = [paired[0]] + [swapped(paired[j], PAIR * j) for j in range(1, LINE)]
        merged = merge(finish_kernel, pieces, merged_chunk)
        shares = [merged] + [swapped(merged, PAIR * j) for j in range(1, LINE)]
        shares = shares + [swapped(share, 1) for share in shares]
    else:
        got = lax.all_to_all(parts[0], "mem", 0, 0, tiled=True)
        shares = [lax.all_gather(merge(finish_kernel, [got], merged_chunk), "mem")]

    new_state, mean = call(
        relax_kernel,
        [SMEM] * 3 + [VMEM] * (2 + len(shares)),
        [((slots, fields, rows, width), bf16), ((fields, rows, width), bf16)],
        [pltpu.VMEM((members, fields, held, LANES), f32)],
        flops=4 * slots * fields * rows * width,
        bytes_accessed=4 * slots * fields * rows * width,
        transcendentals=0,
    )(order, counts, relax, adv_first, adv_rest, *shares)
    return (new_state, mean)


def solution(mesh):
    return jax.shard_map(
        on_device,
        mesh=mesh,
        in_specs=(
            P(("groups", "mem"), None, "lat", None),
            P(("groups", "mem")),
            P(("groups", "lat"), None),
            P(("groups", "lat"), None),
            P(("groups", "lat"), None),
            P(("groups", "lat"), None),
            P(("groups", "lat"), None),
            P(("groups", "lat"), None),
            P(),
        ),
        out_specs=(P(("groups", "mem"), None, "lat", None), P("groups", "lat", None)),
        check_vma=False,
    )
```

```python
import functools

import jax
import jax.numpy as jnp
import numpy as np
from jax import lax
from jax.experimental import pallas as pl
from jax.experimental.pallas import tpu as pltpu
from jax.sharding import PartitionSpec as P

STEPS = 4
SMOOTH = 16
LOG_TWO_PI = 1.8378770664093453
LANES = 128
TILE = 8
PARTS = 5
CHUNK_ROWS = 16
PACK = 16
BEGIN_STEPS = 4
LATER_FIELDS = 2
PAIR = 2
LINE = 4
SHARE_ORDER = (6, 7, 4, 1, 2, 3, 5)


VMEM = pl.BlockSpec(memory_space=pltpu.VMEM)
SMEM = pl.BlockSpec(memory_space=pltpu.SMEM)
PARAMS = pltpu.CompilerParams(vmem_limit_bytes=24 * 1024 * 1024)


def kernel_matrix(offset):
    values = np.exp(-((2.0 * offset.astype(np.float32) / SMOOTH) ** 2))
    return np.where(np.abs(offset) <= SMOOTH, values, 0.0).astype(np.float32)


def split_two(x):
    high = x.astype(jnp.bfloat16).astype(jnp.float32)
    return high, x - high


def spread_terms(cells_ref, mask_ref, values_ref, error_ref, rows_ref, rows, width):
    half = width // 2
    cells = cells_ref[...]
    used = mask_ref[...].astype(jnp.float32)
    values = values_ref[...]
    error = error_ref[...]
    inverse = used / (error * error)
    first = inverse * values
    second = first * values + used * (2.0 * jnp.log(error) + LOG_TWO_PI)
    row = cells // width
    column = cells % width
    high = (column // half * rows + row).astype(jnp.float32)
    low = (column % half).astype(jnp.float32)
    for k, x in enumerate(split_two(inverse) + split_two(first) + (second, high, low)):
        rows_ref[k] = x


def add_observations(step, rows_ref, acc_ref):
    highs, lows = acc_ref.shape[0] // PARTS, acc_ref.shape[1]

    def steps_of(count):
        base = lax.broadcasted_iota(jnp.int32, (PACK, LANES), 0)
        return [
            (base + PACK * i).astype(jnp.float32).astype(jnp.bfloat16) for i in range(count // PACK)
        ]

    high_iota, low_iota = steps_of(highs), steps_of(lows)
    zero = jnp.zeros((PACK, LANES), jnp.bfloat16)
    one = jnp.ones((PACK, LANES), jnp.bfloat16)
    here = pl.ds(pl.multiple_of(step * CHUNK_ROWS, CHUNK_ROWS), CHUNK_ROWS)
    held = [rows_ref[k, here, :] for k in range(PARTS + 2)]
    left, right = [], []
    for r in range(CHUNK_ROWS):
        spread = [
            jnp.broadcast_to(x[r : r + 1, :], (PACK, LANES)).astype(jnp.bfloat16) for x in held
        ]
        high_row, low_row = spread[PARTS:]
        hit = [iota == high_row for iota in high_iota]
        left.append(
            jnp.concatenate([jnp.where(h, part, zero) for part in spread[:PARTS] for h in hit], axis=0)
        )
        right.append(
            jnp.concatenate([jnp.where(iota == low_row, one, zero) for iota in low_iota], axis=0)
        )
    acc_ref[...] += lax.dot_general(
        jnp.concatenate(left, axis=1),
        jnp.concatenate(right, axis=1),
        (((1,), (1,)), ((), ())),
        preferred_element_type=jnp.float32,
    )


def grids_of(acc_ref, rows):
    highs = 2 * rows

    def part_sum(indices):
        total = acc_ref[pl.ds(indices[-1] * highs, highs), :]
        for i in indices[-2::-1]:
            total = total + acc_ref[pl.ds(i * highs, highs), :]
        return jnp.concatenate([total[0:rows], total[rows:highs]], axis=1)

    return [part_sum(indices) for indices in ((0, 1), (2, 3), (4,))]


def begin_kernel(rows, width, steps, cells_ref, mask_ref, values_ref, error_ref, rows_ref, acc_ref):
    spread_terms(cells_ref, mask_ref, values_ref, error_ref, rows_ref, rows, width)
    acc_ref[...] = jnp.zeros_like(acc_ref)

    def body(step, carry):
        add_observations(step, rows_ref, acc_ref)
        return carry

    lax.fori_loop(0, steps, body, 0)


def wind_parts(east_ref, north_ref, wind_halo_ref):
    east = jnp.concatenate([east_ref[...], wind_halo_ref[0]], axis=0)
    north = jnp.concatenate([north_ref[...], wind_halo_ref[1]], axis=0)
    west, south = jnp.maximum(east, 0.0), jnp.maximum(north, 0.0)
    east, north = -jnp.minimum(east, 0.0), -jnp.minimum(north, 0.0)
    return 1.0 - west - east - south - north, west, east, south, north


def advect(x, winds):
    count, width = x.shape
    centre, west, east, south, north = winds
    for _ in range(STEPS):
        x = (
            centre * x
            + west * pltpu.roll(x, 1, 1)
            + east * pltpu.roll(x, width - 1, 1)
            + south * pltpu.roll(x, 1, 0)
            + north * pltpu.roll(x, count - 1, 0)
        )
    return x


def store_winds(east_ref, north_ref, halo_ref, count, winds_ref):
    for i, part in enumerate(wind_parts(east_ref, north_ref, halo_ref.at[pl.ds(count, 2)])):
        winds_ref[i] = part


def advect_pair(state_ref, halo_ref, winds_ref, pair, f, adv_ref, place):
    fields, rows = state_ref.shape[1:3]
    winds = [winds_ref[k] for k in range(5)]
    for s in (2 * pair, 2 * pair + 1):
        x = jnp.concatenate(
            [state_ref[s, f].astype(jnp.float32), halo_ref[s * fields + f]], axis=0
        )
        adv_ref[s, place] = advect(x, winds)[0:rows].astype(jnp.bfloat16)


def first_kernel(
    steps, state_ref, halo_ref, east_ref, north_ref, terms_ref, acc_in_ref, lat_ref, lon_ref,
    adv_ref, own_ref, send_ref, acc_ref, winds_ref,
):
    slots, fields, rows, width = state_ref.shape
    pairs = slots // 2
    store_winds(east_ref, north_ref, halo_ref, slots * fields, winds_ref)
    acc_ref[...] = acc_in_ref[...]
    held = adv_ref.shape[1]
    total = terms_ref.shape[1] // CHUNK_ROWS

    def body(i, carry):
        add_observations(steps + i, terms_ref, acc_ref)
        advect_pair(state_ref, halo_ref, winds_ref, i % pairs, i // pairs, adv_ref, i // pairs)
        return carry

    def observe(step, carry):
        add_observations(step, terms_ref, acc_ref)
        return carry

    shared = min(pairs * held, total - steps)
    lax.fori_loop(0, shared, body, 0)
    if steps + shared < total:
        lax.fori_loop(steps + shared, total, observe, 0)
    for i in range(shared, pairs * held):
        advect_pair(state_ref, halo_ref, winds_ref, i % pairs, i // pairs, adv_ref, i // pairs)

    inverse, first, second = grids_of(acc_ref, rows)
    logliks = []
    for s in range(slots):
        value = adv_ref[s, 0].astype(jnp.float32)
        logliks.append(-0.5 * (inverse * value * value - 2.0 * first * value + second))
    smooth = functools.partial(
        jnp.dot, precision=lax.Precision.HIGHEST, preferred_element_type=jnp.float32
    )
    along = smooth(jnp.concatenate(logliks, axis=0), lon_ref[...])
    for s in range(slots):
        scores = smooth(lat_ref[...], along[s * rows : (s + 1) * rows])
        own_ref[s] = scores[0:rows]
        send_ref[s] = scores[rows:]


def rest_kernel(state_ref, halo_ref, east_ref, north_ref, adv_ref, winds_ref):
    slots, fields = state_ref.shape[:2]
    pairs = slots // 2
    held = adv_ref.shape[1]
    store_winds(east_ref, north_ref, halo_ref, slots * fields, winds_ref)

    def body(i, carry):
        f = fields - held + i // pairs
        advect_pair(state_ref, halo_ref, winds_ref, i % pairs, f, adv_ref, i // pairs)
        return carry

    lax.fori_loop(0, pairs * held, body, 0)


def field_ref(adv_first_ref, adv_rest_ref, s, f):
    held = adv_first_ref.shape[1]
    return adv_first_ref.at[s, f] if f < held else adv_rest_ref.at[s, f - held]


def weigh_kernel(
    order_ref, counts_ref, own_ref, recv_ref, adv_first_ref, adv_rest_ref, *refs
):
    out_refs, parts_ref = refs[:-1], refs[-1]
    slots, rows, width = own_ref.shape
    fields = adv_first_ref.shape[1] + adv_rest_ref.shape[1]
    across = width // LANES
    members, _, held, _ = parts_ref.shape

    def store(row_tile, index, value):
        for l in range(across):
            tile = value[:, l * LANES : (l + 1) * LANES]
            row = (row_tile * across + l) * TILE
            for k in range(0, TILE, min(held, TILE)):
                chunk, at = divmod(row + k, held)
                parts_ref[chunk, index, at : at + min(held, TILE)] = tile[k : k + min(held, TILE)]

    lower = order_ref[0] == 0
    for t in range(rows // TILE):
        here = slice(t * TILE, (t + 1) * TILE)
        near = (t * TILE) % SMOOTH
        scores = []
        for s in range(slots):
            recv = recv_ref[s, near : near + TILE, :]
            at_this_edge = lower if t * TILE >= rows - SMOOTH else jnp.logical_not(lower)
            score = own_ref[s, here, :] + jnp.where(at_this_edge, recv, 0.0)
            scores.append(jnp.where(s < counts_ref[0], score, -jnp.inf))
        peak = functools.reduce(jnp.maximum, scores)
        gains = [jnp.exp(score - peak) for score in scores]
        total = functools.reduce(jnp.add, gains)
        store(t, 0, peak + jnp.log(total))
        gains = [gain / total for gain in gains]
        for f in range(fields):
            mean = None
            for s in range(slots):
                ref = field_ref(adv_first_ref, adv_rest_ref, s, f)
                pair = slice(t // 2 * 2 * TILE, (t // 2 + 1) * 2 * TILE)
                value = ref[pair, :].astype(jnp.float32)[t % 2 * TILE : (t % 2 + 1) * TILE]
                term = gains[s] * value
                mean = term if mean is None else mean + term
            store(t, 1 + f, mean)
    for i, out_ref in enumerate(out_refs):
        out_ref[...] = parts_ref[order_ref[1 + i]]


def whole_weigh_kernel(*refs):
    weigh_kernel(*refs[:6], refs[6])


def merge_values(refs):
    peak = functools.reduce(jnp.maximum, [ref[0] for ref in refs])
    weights = [jnp.exp(ref[0] - peak) for ref in refs]
    total = functools.reduce(jnp.add, weights)
    shares = [weight / total for weight in weights]
    means = [
        functools.reduce(jnp.add, [share * ref[q] for share, ref in zip(shares, refs)])
        for q in range(1, refs[0].shape[0])
    ]
    return peak + jnp.log(total), means


def merge_kernel(*refs):
    out_ref = refs[-1]
    log_weight, means = merge_values(refs[:-1])
    out_ref[0] = log_weight
    for f, mean in enumerate(means):
        out_ref[1 + f] = mean


def finish_kernel(*refs):
    merged_ref = refs[-1]
    parts = refs[:-1]
    if len(parts) == 1:
        parts = [parts[0].at[d] for d in range(parts[0].shape[0])]
    for f, mean in enumerate(merge_values(parts)[1]):
        merged_ref[f] = mean


def relax_kernel(order_ref, counts_ref, relax_ref, adv_first_ref, adv_rest_ref, *refs):
    merged_refs, (new_ref, mean_ref, whole_ref) = refs[:-3], refs[-3:]
    slots, fields, rows, width = new_ref.shape
    across = width // LANES
    members, _, held, _ = whole_ref.shape
    if len(merged_refs) == 1:
        whole_ref = merged_refs[0]
    else:
        for i, merged_ref in enumerate(merged_refs):
            whole_ref[order_ref[1 + members + i]] = merged_ref[...]

    def tile(f, row):
        if held >= TILE:
            return whole_ref[row // held, f, row % held : row % held + TILE]
        return jnp.concatenate([whole_ref[(row + k) // held, f] for k in range(0, TILE, held)], axis=0)

    for f in range(fields):
        factor = relax_ref[f]
        merged = jnp.concatenate(
            [
                jnp.concatenate([tile(f, (t * across + l) * TILE) for l in range(across)], axis=1)
                for t in range(rows // TILE)
            ],
            axis=0,
        )
        mean_ref[f] = merged.astype(jnp.bfloat16)
        for s in range(slots):
            ref = field_ref(adv_first_ref, adv_rest_ref, s, f)
            value = ref[...].astype(jnp.float32)
            fresh = value + factor * (merged - value)
            new_ref[s, f] = jnp.where(s < counts_ref[0], fresh, 0.0).astype(jnp.bfloat16)


def call(kernel, ins, outs, scratch=(), **cost):
    return pl.pallas_call(
        kernel,
        out_shape=[jax.ShapeDtypeStruct(shape, dtype) for shape, dtype in outs],
        in_specs=ins,
        out_specs=[VMEM] * len(outs),
        scratch_shapes=list(scratch),
        compiler_params=PARAMS,
        cost_estimate=pl.CostEstimate(**cost),
    )


def on_device(
    state, counts, east_wind, north_wind, obs_cells, obs_mask, obs_values, obs_error, relax
):
    slots, fields, rows, width = state.shape
    f32, bf16 = jnp.float32, jnp.bfloat16
    place = lax.axis_index("lat")
    swap = [(0, 1), (1, 0)]
    lower = place == 0

    edge = lax.dynamic_slice_in_dim(state, jnp.where(lower, rows - TILE, 0), TILE, axis=2)
    winds = jnp.stack([east_wind, north_wind])
    wind_edge = lax.dynamic_slice_in_dim(winds, jnp.where(lower, rows - TILE, 0), TILE, axis=1)
    message = jnp.concatenate(
        [edge.astype(f32).reshape(slots * fields, TILE, width), wind_edge], axis=0
    )
    near = jnp.arange(TILE) < TILE // 2
    keep = jnp.logical_xor(near, lower)
    message = jnp.where(keep[None, :, None], message, 0.0)
    halo = lax.ppermute(message, "lat", swap)

    observations = obs_cells.shape[1]
    flat = [
        x.reshape(observations // LANES, LANES) for x in (obs_cells, obs_mask, obs_values, obs_error)
    ]
    acc_shape = (PARTS * 2 * rows, width // 2)
    all_steps = observations // (LANES * CHUNK_ROWS)
    begin_steps = min(BEGIN_STEPS, all_steps)
    observe_flops = 2 * PARTS * rows * width * LANES * CHUNK_ROWS
    terms, begun = call(
        functools.partial(begin_kernel, rows, width, begin_steps),
        [VMEM] * 4,
        [((PARTS + 2, observations // LANES, LANES), f32), (acc_shape, f32)],
        flops=observe_flops * begin_steps,
        bytes_accessed=16 * observations,
        transcendentals=observations,
    )(*flat)

    index = np.arange(rows)
    own = index[None, :] - index[:, None]
    upper_side = index[None, :] - (index[:SMOOTH, None] + rows)
    lower_side = index[None, :] - (index[rows - SMOOTH :, None] - rows)
    lat_kernel = jnp.where(
        lower,
        jnp.asarray(kernel_matrix(np.concatenate([own, upper_side]))),
        jnp.asarray(kernel_matrix(np.concatenate([own, lower_side]))),
    )
    distance = np.abs(np.arange(width)[:, None] - np.arange(width)[None, :])
    lon_kernel = jnp.asarray(kernel_matrix(np.minimum(distance, width - distance)))

    winds_scratch = pltpu.VMEM((5, rows + TILE, width), f32)
    advect_flops = STEPS * 16 * slots * rows * width
    adv_first, own_scores, edge_scores = call(
        functools.partial(first_kernel, begin_steps),
        [VMEM] * 8,
        [
            ((slots, fields - LATER_FIELDS, rows, width), bf16),
            ((slots, rows, width), f32),
            ((slots, SMOOTH, width), f32),
        ],
        [pltpu.VMEM(acc_shape, f32), winds_scratch],
        flops=observe_flops * (all_steps - begin_steps) + advect_flops * (fields - LATER_FIELDS),
        bytes_accessed=4 * width * width,
        transcendentals=0,
    )(state, halo, east_wind, north_wind, terms, begun, lat_kernel, lon_kernel)
    received = lax.ppermute(edge_scores, "lat", swap)

    (adv_rest,) = call(
        rest_kernel,
        [VMEM] * 4,
        [((slots, LATER_FIELDS, rows, width), bf16)],
        [winds_scratch],
        flops=advect_flops * LATER_FIELDS,
        bytes_accessed=4 * slots * fields * rows * width,
        transcendentals=0,
    )(state, halo, east_wind, north_wind)

    members = lax.axis_size("mem")
    member = lax.axis_index("mem")
    held = rows * width // LANES // members
    quantities = fields + 1
    direct = members == PAIR * LINE
    away = [PAIR * j + i for i in range(PAIR) for j in range(LINE)] if direct else []
    offsets = away + [0] + list(SHARE_ORDER)
    order = jnp.stack([place] + [member ^ offset for offset in offsets]).astype(jnp.int32)

    def swapped(x, offset):
        return lax.ppermute(x, "mem", [(m, m ^ offset) for m in range(members)])

    chunk = ((quantities, held, LANES), f32)
    all_chunks = ((members,) + chunk[0], f32)
    weigh = call(
        weigh_kernel if direct else whole_weigh_kernel,
        [SMEM, SMEM] + [VMEM] * 4,
        [chunk] * len(away) if direct else [all_chunks],
        [pltpu.VMEM(*all_chunks)] if direct else [],
        flops=4 * slots * fields * rows * width,
        bytes_accessed=4 * slots * fields * rows * width,
        transcendentals=slots * rows * width,
    )
    parts = weigh(order, counts, own_scores, received, adv_first, adv_rest)

    def merge(kernel, pieces, out):
        size = quantities * held * LANES * (len(pieces) if direct else members)
        return call(
            kernel,
            [VMEM] * len(pieces),
            [out],
            flops=4 * size,
            bytes_accessed=4 * size,
            transcendentals=size // quantities,
        )(*pieces)[0]

    merged_chunk = ((fields, held, LANES), f32)
    if direct:
        far = LINE - 1
        straight = [swapped(parts[i * LINE + far], PAIR * far + i) for i in range(PAIR)]
        paired = [None] * far
        for j in reversed(range(far)):
            paired[j] = merge(merge_kernel, [parts[j], swapped(parts[LINE + j], 1)], chunk)
        pieces = [paired[0]] + [swapped(paired[j], PAIR * j) for j in range(1, far)]
        merged = merge(finish_kernel, straight + pieces, merged_chunk)
        sent = {0: merged}
        for offset in SHARE_ORDER:
            through = offset ^ 1 if offset % PAIR and offset // PAIR < far else 0
            sent[offset] = swapped(sent[through], offset ^ through)
        shares = [sent[offset] for offset in (0,) + SHARE_ORDER]
    else:
        got = lax.all_to_all(parts[0], "mem", 0, 0, tiled=True)
        shares = [lax.all_gather(merge(finish_kernel, [got], merged_chunk), "mem")]

    new_state, mean = call(
        relax_kernel,
        [SMEM] * 3 + [VMEM] * (2 + len(shares)),
        [((slots, fields, rows, width), bf16), ((fields, rows, width), bf16)],
        [pltpu.VMEM((members, fields, held, LANES), f32)],
        flops=4 * slots * fields * rows * width,
        bytes_accessed=4 * slots * fields * rows * width,
        transcendentals=0,
    )(order, counts, relax, adv_first, adv_rest, *shares)
    return (new_state, mean)


def solution(mesh):
    return jax.shard_map(
        on_device,
        mesh=mesh,
        in_specs=(
            P(("groups", "mem"), None, "lat", None),
            P(("groups", "mem")),
            P(("groups", "lat"), None),
            P(("groups", "lat"), None),
            P(("groups", "lat"), None),
            P(("groups", "lat"), None),
            P(("groups", "lat"), None),
            P(("groups", "lat"), None),
            P(),
        ),
        out_specs=(P(("groups", "mem"), None, "lat", None), P("groups", "lat", None)),
        check_vma=False,
    )
```

```python
import functools

import jax
import jax.numpy as jnp
import numpy as np
from jax import lax
from jax.experimental import pallas as pl
from jax.experimental.pallas import tpu as pltpu
from jax.sharding import PartitionSpec as P

STEPS = 4
SMOOTH = 16
LOG_TWO_PI = 1.8378770664093453
LANES = 128
TILE = 8
PARTS = 5
CHUNK_ROWS = 16
PACK = 16
BEGIN_STEPS = 4
LATER_FIELDS = 2
PAIR = 2
LINE = 4
SHARE_ORDER = (6, 7, 4, 1, 2, 3, 5)


VMEM = pl.BlockSpec(memory_space=pltpu.VMEM)
SMEM = pl.BlockSpec(memory_space=pltpu.SMEM)
PARAMS = pltpu.CompilerParams(vmem_limit_bytes=24 * 1024 * 1024)


def kernel_matrix(offset):
    values = np.exp(-((2.0 * offset.astype(np.float32) / SMOOTH) ** 2))
    return np.where(np.abs(offset) <= SMOOTH, values, 0.0).astype(np.float32)


def split_two(x):
    high = x.astype(jnp.bfloat16).astype(jnp.float32)
    return high, x - high


def spread_terms(cells_ref, mask_ref, values_ref, error_ref, rows_ref, rows, width):
    half = width // 2
    cells = cells_ref[...]
    used = mask_ref[...].astype(jnp.float32)
    values = values_ref[...]
    error = error_ref[...]
    inverse = used / (error * error)
    first = inverse * values
    second = first * values + used * (2.0 * jnp.log(error) + LOG_TWO_PI)
    row = cells // width
    column = cells % width
    high = (column // half * rows + row).astype(jnp.float32)
    low = (column % half).astype(jnp.float32)
    for k, x in enumerate(split_two(inverse) + split_two(first) + (second, high, low)):
        rows_ref[k] = x


def add_observations(step, rows_ref, acc_ref):
    highs, lows = acc_ref.shape[0] // PARTS, acc_ref.shape[1]

    def steps_of(count):
        base = lax.broadcasted_iota(jnp.int32, (PACK, LANES), 0)
        return [
            (base + PACK * i).astype(jnp.float32).astype(jnp.bfloat16) for i in range(count // PACK)
        ]

    high_iota, low_iota = steps_of(highs), steps_of(lows)
    zero = jnp.zeros((PACK, LANES), jnp.bfloat16)
    one = jnp.ones((PACK, LANES), jnp.bfloat16)
    here = pl.ds(pl.multiple_of(step * CHUNK_ROWS, CHUNK_ROWS), CHUNK_ROWS)
    held = [rows_ref[k, here, :] for k in range(PARTS + 2)]
    left, right = [], []
    for r in range(CHUNK_ROWS):
        spread = [
            jnp.broadcast_to(x[r : r + 1, :], (PACK, LANES)).astype(jnp.bfloat16) for x in held
        ]
        high_row, low_row = spread[PARTS:]
        hit = [iota == high_row for iota in high_iota]
        left.append(
            jnp.concatenate([jnp.where(h, part, zero) for part in spread[:PARTS] for h in hit], axis=0)
        )
        right.append(
            jnp.concatenate([jnp.where(iota == low_row, one, zero) for iota in low_iota], axis=0)
        )
    acc_ref[...] += lax.dot_general(
        jnp.concatenate(left, axis=1),
        jnp.concatenate(right, axis=1),
        (((1,), (1,)), ((), ())),
        preferred_element_type=jnp.float32,
    )


def grids_of(acc_ref, rows):
    highs = 2 * rows

    def part_sum(indices):
        total = acc_ref[pl.ds(indices[-1] * highs, highs), :]
        for i in indices[-2::-1]:
            total = total + acc_ref[pl.ds(i * highs, highs), :]
        return jnp.concatenate([total[0:rows], total[rows:highs]], axis=1)

    return [part_sum(indices) for indices in ((0, 1), (2, 3), (4,))]


def begin_kernel(rows, width, steps, cells_ref, mask_ref, values_ref, error_ref, rows_ref, acc_ref):
    spread_terms(cells_ref, mask_ref, values_ref, error_ref, rows_ref, rows, width)
    acc_ref[...] = jnp.zeros_like(acc_ref)

    def body(step, carry):
        add_observations(step, rows_ref, acc_ref)
        return carry

    lax.fori_loop(0, steps, body, 0)


def wind_parts(east_ref, north_ref, wind_halo_ref):
    east = jnp.concatenate([east_ref[...], wind_halo_ref[0]], axis=0)
    north = jnp.concatenate([north_ref[...], wind_halo_ref[1]], axis=0)
    west, south = jnp.maximum(east, 0.0), jnp.maximum(north, 0.0)
    east, north = -jnp.minimum(east, 0.0), -jnp.minimum(north, 0.0)
    return 1.0 - west - east - south - north, west, east, south, north


def advect(x, winds):
    count, width = x.shape
    centre, west, east, south, north = winds
    for _ in range(STEPS):
        x = (
            centre * x
            + west * pltpu.roll(x, 1, 1)
            + east * pltpu.roll(x, width - 1, 1)
            + south * pltpu.roll(x, 1, 0)
            + north * pltpu.roll(x, count - 1, 0)
        )
    return x


def store_winds(east_ref, north_ref, halo_ref, count, winds_ref):
    for i, part in enumerate(wind_parts(east_ref, north_ref, halo_ref.at[pl.ds(count, 2)])):
        winds_ref[i] = part


def advect_pair(state_ref, halo_ref, winds_ref, pair, f, adv_ref, place):
    fields, rows = state_ref.shape[1:3]
    winds = [winds_ref[k] for k in range(5)]
    for s in (2 * pair, 2 * pair + 1):
        x = jnp.concatenate(
            [state_ref[s, f].astype(jnp.float32), halo_ref[s * fields + f]], axis=0
        )
        adv_ref[s, place] = advect(x, winds)[0:rows].astype(jnp.bfloat16)


def first_kernel(
    steps, state_ref, halo_ref, east_ref, north_ref, terms_ref, acc_in_ref, lat_ref, lon_ref,
    adv_ref, own_ref, send_ref, acc_ref, winds_ref,
):
    slots, fields, rows, width = state_ref.shape
    pairs = slots // 2
    store_winds(east_ref, north_ref, halo_ref, slots * fields, winds_ref)
    acc_ref[...] = acc_in_ref[...]
    held = adv_ref.shape[1]
    total = terms_ref.shape[1] // CHUNK_ROWS

    def body(i, carry):
        add_observations(steps + i, terms_ref, acc_ref)
        advect_pair(state_ref, halo_ref, winds_ref, i % pairs, i // pairs, adv_ref, i // pairs)
        return carry

    def observe(step, carry):
        add_observations(step, terms_ref, acc_ref)
        return carry

    shared = min(pairs * held, total - steps)
    lax.fori_loop(0, shared, body, 0)
    if steps + shared < total:
        lax.fori_loop(steps + shared, total, observe, 0)
    for i in range(shared, pairs * held):
        advect_pair(state_ref, halo_ref, winds_ref, i % pairs, i // pairs, adv_ref, i // pairs)

    inverse, first, second = grids_of(acc_ref, rows)
    logliks = []
    for s in range(slots):
        value = adv_ref[s, 0].astype(jnp.float32)
        logliks.append(-0.5 * (inverse * value * value - 2.0 * first * value + second))
    smooth = functools.partial(
        jnp.dot, precision=lax.Precision.HIGHEST, preferred_element_type=jnp.float32
    )
    along = smooth(jnp.concatenate(logliks, axis=0), lon_ref[...])
    for s in range(slots):
        scores = smooth(lat_ref[...], along[s * rows : (s + 1) * rows])
        own_ref[s] = scores[0:rows]
        send_ref[s] = scores[rows:]


def rest_kernel(state_ref, halo_ref, east_ref, north_ref, adv_ref, winds_ref):
    slots, fields = state_ref.shape[:2]
    pairs = slots // 2
    held = adv_ref.shape[1]
    store_winds(east_ref, north_ref, halo_ref, slots * fields, winds_ref)

    def body(i, carry):
        f = fields - held + i // pairs
        advect_pair(state_ref, halo_ref, winds_ref, i % pairs, f, adv_ref, i // pairs)
        return carry

    lax.fori_loop(0, pairs * held, body, 0)


def field_ref(adv_first_ref, adv_rest_ref, s, f):
    held = adv_first_ref.shape[1]
    return adv_first_ref.at[s, f] if f < held else adv_rest_ref.at[s, f - held]


def weigh_all_kernel(
    where_ref, counts_ref, own_ref, recv_ref, adv_first_ref, adv_rest_ref, parts_ref
):
    slots, rows, width = own_ref.shape
    fields = adv_first_ref.shape[1] + adv_rest_ref.shape[1]
    across = width // LANES
    members, _, held, _ = parts_ref.shape

    def store(row_tile, index, value):
        for l in range(across):
            tile = value[:, l * LANES : (l + 1) * LANES]
            row = (row_tile * across + l) * TILE
            for k in range(0, TILE, min(held, TILE)):
                chunk, at = divmod(row + k, held)
                parts_ref[chunk, index, at : at + min(held, TILE)] = tile[k : k + min(held, TILE)]

    lower = where_ref[0] == 0
    for t in range(rows // TILE):
        here = slice(t * TILE, (t + 1) * TILE)
        near = (t * TILE) % SMOOTH
        scores = []
        for s in range(slots):
            recv = recv_ref[s, near : near + TILE, :]
            at_this_edge = lower if t * TILE >= rows - SMOOTH else jnp.logical_not(lower)
            score = own_ref[s, here, :] + jnp.where(at_this_edge, recv, 0.0)
            scores.append(jnp.where(s < counts_ref[0], score, -jnp.inf))
        peak = functools.reduce(jnp.maximum, scores)
        gains = [jnp.exp(score - peak) for score in scores]
        total = functools.reduce(jnp.add, gains)
        store(t, 0, peak + jnp.log(total))
        gains = [gain / total for gain in gains]
        for f in range(fields):
            mean = None
            for s in range(slots):
                ref = field_ref(adv_first_ref, adv_rest_ref, s, f)
                pair = slice(t // 2 * 2 * TILE, (t // 2 + 1) * 2 * TILE)
                value = ref[pair, :].astype(jnp.float32)[t % 2 * TILE : (t % 2 + 1) * TILE]
                term = gains[s] * value
                mean = term if mean is None else mean + term
            store(t, 1 + f, mean)


def weigh_kernel(
    distances, where_ref, counts_ref, own_ref, recv_ref, adv_first_ref, adv_rest_ref, *refs
):
    out_refs = refs[len(refs) - 2 * len(distances) :]
    slots, rows, width = own_ref.shape
    fields = adv_first_ref.shape[1] + adv_rest_ref.shape[1]
    half = width // PAIR
    lower = where_ref[0] == 0
    even_side = where_ref[1] % PAIR == 0
    for n, distance in enumerate(distances):
        tile = (where_ref[1] // PAIR) ^ distance
        here = pl.ds(pl.multiple_of(tile * TILE, TILE), TILE)
        near = pl.ds(pl.multiple_of(tile % 2 * TILE, TILE), TILE)
        pair = pl.ds(pl.multiple_of(tile // 2 * (2 * TILE), 2 * TILE), 2 * TILE)
        even_tile = tile % 2 == 0
        at_edge = lower == (tile * TILE >= rows - SMOOTH)
        keep_ref, send_ref = out_refs[2 * n], out_refs[2 * n + 1]

        def store(index, value):
            left, right = value[:, 0:half], value[:, half:width]
            keep_ref[index] = jnp.where(even_side, left, right)
            send_ref[index] = jnp.where(even_side, right, left)

        scores = []
        for s in range(slots):
            score = own_ref[s, here, :] + jnp.where(at_edge, recv_ref[s, near, :], 0.0)
            scores.append(jnp.where(s < counts_ref[0], score, -jnp.inf))
        peak = functools.reduce(jnp.maximum, scores)
        gains = [jnp.exp(score - peak) for score in scores]
        total = functools.reduce(jnp.add, gains)
        store(0, peak + jnp.log(total))
        gains = [gain / total for gain in gains]
        for f in range(fields):
            mean = None
            for s in range(slots):
                ref = field_ref(adv_first_ref, adv_rest_ref, s, f)
                value = ref[pair, :].astype(jnp.float32)
                term = gains[s] * jnp.where(even_tile, value[0:TILE], value[TILE:])
                mean = term if mean is None else mean + term
            store(1 + f, mean)


def merge_values(refs):
    peak = functools.reduce(jnp.maximum, [ref[0] for ref in refs])
    weights = [jnp.exp(ref[0] - peak) for ref in refs]
    total = functools.reduce(jnp.add, weights)
    shares = [weight / total for weight in weights]
    means = [
        functools.reduce(jnp.add, [share * ref[q] for share, ref in zip(shares, refs)])
        for q in range(1, refs[0].shape[0])
    ]
    return peak + jnp.log(total), means


def merge_kernel(*refs):
    out_ref = refs[-1]
    log_weight, means = merge_values(refs[:-1])
    out_ref[0] = log_weight
    for f, mean in enumerate(means):
        out_ref[1 + f] = mean


def finish_kernel(*refs):
    merged_ref = refs[-1]
    parts = refs[:-1]
    if len(parts) == 1:
        parts = [parts[0].at[d] for d in range(parts[0].shape[0])]
    for f, mean in enumerate(merge_values(parts)[1]):
        merged_ref[f] = mean


def relax_field(f, merged, factor, counts_ref, adv_first_ref, adv_rest_ref, new_ref, mean_ref):
    mean_ref[f] = merged.astype(jnp.bfloat16)
    for s in range(new_ref.shape[0]):
        value = field_ref(adv_first_ref, adv_rest_ref, s, f)[...].astype(jnp.float32)
        fresh = value + factor * (merged - value)
        new_ref[s, f] = jnp.where(s < counts_ref[0], fresh, 0.0).astype(jnp.bfloat16)


def relax_all_kernel(
    counts_ref, relax_ref, adv_first_ref, adv_rest_ref, whole_ref, new_ref, mean_ref
):
    _, fields, rows, width = new_ref.shape
    across = width // LANES
    held = whole_ref.shape[2]

    def tile(f, row):
        if held >= TILE:
            return whole_ref[row // held, f, row % held : row % held + TILE]
        return jnp.concatenate([whole_ref[(row + k) // held, f] for k in range(0, TILE, held)], axis=0)

    for f in range(fields):
        merged = jnp.concatenate(
            [
                jnp.concatenate([tile(f, (t * across + l) * TILE) for l in range(across)], axis=1)
                for t in range(rows // TILE)
            ],
            axis=0,
        )
        relax_field(
            f, merged, relax_ref[f], counts_ref, adv_first_ref, adv_rest_ref, new_ref, mean_ref
        )


def relax_kernel(
    distance, where_ref, counts_ref, relax_ref, adv_first_ref, adv_rest_ref,
    near_same, near_other, far_same, far_other, *refs,
):
    new_ref, mean_ref = refs[-2:]
    even_side = where_ref[1] % PAIR == 0
    even_tile = ((where_ref[1] // PAIR) ^ distance) % 2 == 0
    for f in range(new_ref.shape[1]):
        tiles = []
        for same_ref, other_ref in ((near_same, near_other), (far_same, far_other)):
            same, other = same_ref[f], other_ref[f]
            left = jnp.where(even_side, same, other)
            right = jnp.where(even_side, other, same)
            tiles.append(jnp.concatenate([left, right], axis=1))
        top = jnp.where(even_tile, tiles[0], tiles[1])
        bottom = jnp.where(even_tile, tiles[1], tiles[0])
        merged = jnp.concatenate([top, bottom], axis=0)
        relax_field(
            f, merged, relax_ref[f], counts_ref, adv_first_ref, adv_rest_ref, new_ref, mean_ref
        )


def call(kernel, ins, outs, scratch=(), **cost):
    return pl.pallas_call(
        kernel,
        out_shape=[jax.ShapeDtypeStruct(shape, dtype) for shape, dtype in outs],
        in_specs=ins,
        out_specs=[VMEM] * len(outs),
        scratch_shapes=list(scratch),
        compiler_params=PARAMS,
        cost_estimate=pl.CostEstimate(**cost),
    )


def on_device(
    state, counts, east_wind, north_wind, obs_cells, obs_mask, obs_values, obs_error, relax
):
    slots, fields, rows, width = state.shape
    f32, bf16 = jnp.float32, jnp.bfloat16
    place = lax.axis_index("lat")
    swap = [(0, 1), (1, 0)]
    lower = place == 0

    edge = lax.dynamic_slice_in_dim(state, jnp.where(lower, rows - TILE, 0), TILE, axis=2)
    winds = jnp.stack([east_wind, north_wind])
    wind_edge = lax.dynamic_slice_in_dim(winds, jnp.where(lower, rows - TILE, 0), TILE, axis=1)
    message = jnp.concatenate(
        [edge.astype(f32).reshape(slots * fields, TILE, width), wind_edge], axis=0
    )
    near = jnp.arange(TILE) < TILE // 2
    keep = jnp.logical_xor(near, lower)
    message = jnp.where(keep[None, :, None], message, 0.0)
    halo = lax.ppermute(message, "lat", swap)

    observations = obs_cells.shape[1]
    flat = [
        x.reshape(observations // LANES, LANES) for x in (obs_cells, obs_mask, obs_values, obs_error)
    ]
    acc_shape = (PARTS * 2 * rows, width // 2)
    all_steps = observations // (LANES * CHUNK_ROWS)
    begin_steps = min(BEGIN_STEPS, all_steps)
    observe_flops = 2 * PARTS * rows * width * LANES * CHUNK_ROWS
    terms, begun = call(
        functools.partial(begin_kernel, rows, width, begin_steps),
        [VMEM] * 4,
        [((PARTS + 2, observations // LANES, LANES), f32), (acc_shape, f32)],
        flops=observe_flops * begin_steps,
        bytes_accessed=16 * observations,
        transcendentals=observations,
    )(*flat)

    index = np.arange(rows)
    own = index[None, :] - index[:, None]
    upper_side = index[None, :] - (index[:SMOOTH, None] + rows)
    lower_side = index[None, :] - (index[rows - SMOOTH :, None] - rows)
    lat_kernel = jnp.where(
        lower,
        jnp.asarray(kernel_matrix(np.concatenate([own, upper_side]))),
        jnp.asarray(kernel_matrix(np.concatenate([own, lower_side]))),
    )
    distance = np.abs(np.arange(width)[:, None] - np.arange(width)[None, :])
    lon_kernel = jnp.asarray(kernel_matrix(np.minimum(distance, width - distance)))

    winds_scratch = pltpu.VMEM((5, rows + TILE, width), f32)
    advect_flops = STEPS * 16 * slots * rows * width
    adv_first, own_scores, edge_scores = call(
        functools.partial(first_kernel, begin_steps),
        [VMEM] * 8,
        [
            ((slots, fields - LATER_FIELDS, rows, width), bf16),
            ((slots, rows, width), f32),
            ((slots, SMOOTH, width), f32),
        ],
        [pltpu.VMEM(acc_shape, f32), winds_scratch],
        flops=observe_flops * (all_steps - begin_steps) + advect_flops * (fields - LATER_FIELDS),
        bytes_accessed=4 * width * width,
        transcendentals=0,
    )(state, halo, east_wind, north_wind, terms, begun, lat_kernel, lon_kernel)
    received = lax.ppermute(edge_scores, "lat", swap)

    (adv_rest,) = call(
        rest_kernel,
        [VMEM] * 4,
        [((slots, LATER_FIELDS, rows, width), bf16)],
        [winds_scratch],
        flops=advect_flops * LATER_FIELDS,
        bytes_accessed=4 * slots * fields * rows * width,
        transcendentals=0,
    )(state, halo, east_wind, north_wind)

    members = lax.axis_size("mem")
    member = lax.axis_index("mem")
    where = jnp.stack([place, member]).astype(jnp.int32)
    quantities = fields + 1
    direct = (members, rows, width % (PAIR * LANES)) == (PAIR * LINE, LINE * TILE, 0)
    chunk = (TILE, width // PAIR) if direct else (rows * width // LANES // members, LANES)
    cells = chunk[0] * chunk[1]

    def weigh(kernel, share, outs, after=()):
        return call(
            kernel,
            [SMEM, SMEM] + [VMEM] * 4 + [pl.BlockSpec(memory_space=pl.ANY)] * len(after),
            outs,
            flops=4 * slots * fields * share,
            bytes_accessed=4 * slots * fields * share,
            transcendentals=slots * share,
        )(where, counts, own_scores, received, adv_first, adv_rest, *after)

    def merge(kernel, pieces, out):
        size = quantities * cells * (len(pieces) if direct else members)
        return call(
            kernel,
            [VMEM] * len(pieces),
            [out],
            flops=4 * size,
            bytes_accessed=4 * size,
            transcendentals=size // quantities,
        )(*pieces)[0]

    def swapped(x, offset):
        return lax.ppermute(x, "mem", [(m, m ^ offset) for m in range(members)])

    merged_chunk = ((fields,) + chunk, f32)
    new_shape, mean_shape = (slots, fields, rows, width), (fields, rows, width)
    outs = [(new_shape, bf16), (mean_shape, bf16)]
    if direct:
        piece = ((quantities,) + chunk, f32)
        far = LINE - 1
        first = functools.partial(weigh_kernel, (far,))
        parts = {far: weigh(first, PAIR * cells, [piece] * PAIR)}
        straight = [swapped(parts[far][i], PAIR * far + i) for i in range(PAIR)]
        straight = merge(merge_kernel, straight, piece)
        later = tuple(reversed(range(far)))
        rest = functools.partial(weigh_kernel, later)
        pieces = weigh(rest, PAIR * cells * far, [piece] * (PAIR * far), parts[far][:1])
        paired = {}
        for n, j in enumerate(later):
            keep, send = pieces[2 * n : 2 * n + 2]
            got = swapped(send, 1)
            if j == 1:
                got, straight = lax.optimization_barrier((got, straight))
            paired[j] = merge(merge_kernel, [keep, got], piece)
        pieces = [swapped(paired[j], PAIR * j) for j in range(far - 1, 0, -1)] + [paired[0]]
        merged = merge(finish_kernel, [straight] + pieces, merged_chunk)
        sent = {0: merged}
        for offset in SHARE_ORDER:
            through = offset ^ 1 if offset % PAIR and offset // PAIR < far else 0
            sent[offset] = swapped(sent[through], offset ^ through)

        def relax_rows(distance, done, after=()):
            block = 2 * TILE

            def at(i, place_ref):
                return (0, 0, (place_ref[1] // PAIR ^ distance) // 2, 0)

            shares = [sent[PAIR * distance + i] for i in range(2 * PAIR)]
            size = slots * fields * block * width
            return pl.pallas_call(
                functools.partial(relax_kernel, distance),
                out_shape=[jax.ShapeDtypeStruct(*out) for out in outs],
                grid_spec=pltpu.PrefetchScalarGridSpec(
                    num_scalar_prefetch=1,
                    grid=(1,),
                    in_specs=[SMEM, SMEM]
                    + [
                        pl.BlockSpec((slots, x.shape[1], block, width), at)
                        for x in (adv_first, adv_rest)
                    ]
                    + [VMEM] * len(shares)
                    + [pl.BlockSpec(memory_space=pl.ANY)] * (len(done) + len(after)),
                    out_specs=[
                        pl.BlockSpec((slots, fields, block, width), at),
                        pl.BlockSpec((fields, block, width), lambda i, w: at(i, w)[1:]),
                    ],
                ),
                input_output_aliases={5 + len(shares) + i: i for i in range(len(done))},
                compiler_params=PARAMS,
                cost_estimate=pl.CostEstimate(
                    flops=4 * size, bytes_accessed=4 * size, transcendentals=0
                ),
            )(where, counts, relax, adv_first, adv_rest, *shares, *done, *after)

        done = relax_rows(0, [], [sent[PAIR * far + i] for i in range(PAIR)])
        new_state, mean = relax_rows(2, done)
    else:
        (parts,) = weigh(weigh_all_kernel, rows * width, [((members, quantities) + chunk, f32)])
        got = lax.all_to_all(parts, "mem", 0, 0, tiled=True)
        whole = lax.all_gather(merge(finish_kernel, [got], merged_chunk), "mem")
        new_state, mean = call(
            relax_all_kernel,
            [SMEM] * 2 + [VMEM] * 3,
            outs,
            flops=4 * slots * fields * rows * width,
            bytes_accessed=4 * slots * fields * rows * width,
            transcendentals=0,
        )(counts, relax, adv_first, adv_rest, whole)
    return (new_state, mean)


def solution(mesh):
    return jax.shard_map(
        on_device,
        mesh=mesh,
        in_specs=(
            P(("groups", "mem"), None, "lat", None),
            P(("groups", "mem")),
            P(("groups", "lat"), None),
            P(("groups", "lat"), None),
            P(("groups", "lat"), None),
            P(("groups", "lat"), None),
            P(("groups", "lat"), None),
            P(("groups", "lat"), None),
            P(),
        ),
        out_specs=(P(("groups", "mem"), None, "lat", None), P("groups", "lat", None)),
        check_vma=False,
    )
```

```python
import functools

import jax
import jax.numpy as jnp
import numpy as np
from jax import lax
from jax.experimental import pallas as pl
from jax.experimental.pallas import tpu as pltpu
from jax.sharding import PartitionSpec as P

STEPS = 4
SMOOTH = 16
LOG_TWO_PI = 1.8378770664093453
LANES = 128
TILE = 8
PARTS = 5
CHUNK_ROWS = 16
PACK = 16
BEGIN_STEPS = 4
LATER_FIELDS = 2
PAIR = 2
LINE = 4
SHARE_ORDER = (0, 6, 7, 4, 1, 2, 3, 5)


VMEM = pl.BlockSpec(memory_space=pltpu.VMEM)
SMEM = pl.BlockSpec(memory_space=pltpu.SMEM)
PARAMS = pltpu.CompilerParams(vmem_limit_bytes=24 * 1024 * 1024)


def kernel_matrix(offset):
    values = np.exp(-((2.0 * offset.astype(np.float32) / SMOOTH) ** 2))
    return np.where(np.abs(offset) <= SMOOTH, values, 0.0).astype(np.float32)


def split_two(x):
    high = x.astype(jnp.bfloat16).astype(jnp.float32)
    return high, x - high


def spread_terms(cells_ref, mask_ref, values_ref, error_ref, rows_ref, rows, width):
    half = width // 2
    cells = cells_ref[...]
    used = mask_ref[...].astype(jnp.float32)
    values = values_ref[...]
    error = error_ref[...]
    inverse = used / (error * error)
    first = inverse * values
    second = first * values + used * (2.0 * jnp.log(error) + LOG_TWO_PI)
    row = cells // width
    column = cells % width
    high = (column // half * rows + row).astype(jnp.float32)
    low = (column % half).astype(jnp.float32)
    for k, x in enumerate(split_two(inverse) + split_two(first) + (second, high, low)):
        rows_ref[k] = x


def add_observations(step, rows_ref, acc_ref):
    highs, lows = acc_ref.shape[0] // PARTS, acc_ref.shape[1]

    def steps_of(count):
        base = lax.broadcasted_iota(jnp.int32, (PACK, LANES), 0)
        return [
            (base + PACK * i).astype(jnp.float32).astype(jnp.bfloat16) for i in range(count // PACK)
        ]

    high_iota, low_iota = steps_of(highs), steps_of(lows)
    zero = jnp.zeros((PACK, LANES), jnp.bfloat16)
    one = jnp.ones((PACK, LANES), jnp.bfloat16)
    here = pl.ds(pl.multiple_of(step * CHUNK_ROWS, CHUNK_ROWS), CHUNK_ROWS)
    held = [rows_ref[k, here, :] for k in range(PARTS + 2)]
    left, right = [], []
    for r in range(CHUNK_ROWS):
        spread = [
            jnp.broadcast_to(x[r : r + 1, :], (PACK, LANES)).astype(jnp.bfloat16) for x in held
        ]
        high_row, low_row = spread[PARTS:]
        hit = [iota == high_row for iota in high_iota]
        left.append(
            jnp.concatenate([jnp.where(h, part, zero) for part in spread[:PARTS] for h in hit], axis=0)
        )
        right.append(
            jnp.concatenate([jnp.where(iota == low_row, one, zero) for iota in low_iota], axis=0)
        )
    acc_ref[...] += lax.dot_general(
        jnp.concatenate(left, axis=1),
        jnp.concatenate(right, axis=1),
        (((1,), (1,)), ((), ())),
        preferred_element_type=jnp.float32,
    )


def grids_of(acc_ref, rows):
    highs = 2 * rows

    def part_sum(indices):
        total = acc_ref[pl.ds(indices[-1] * highs, highs), :]
        for i in indices[-2::-1]:
            total = total + acc_ref[pl.ds(i * highs, highs), :]
        return jnp.concatenate([total[0:rows], total[rows:highs]], axis=1)

    return [part_sum(indices) for indices in ((0, 1), (2, 3), (4,))]


def begin_kernel(rows, width, steps, cells_ref, mask_ref, values_ref, error_ref, rows_ref, acc_ref):
    spread_terms(cells_ref, mask_ref, values_ref, error_ref, rows_ref, rows, width)
    acc_ref[...] = jnp.zeros_like(acc_ref)

    def body(step, carry):
        add_observations(step, rows_ref, acc_ref)
        return carry

    lax.fori_loop(0, steps, body, 0)


def wind_parts(east_ref, north_ref, wind_halo_ref):
    east = jnp.concatenate([east_ref[...], wind_halo_ref[0]], axis=0)
    north = jnp.concatenate([north_ref[...], wind_halo_ref[1]], axis=0)
    west, south = jnp.maximum(east, 0.0), jnp.maximum(north, 0.0)
    east, north = -jnp.minimum(east, 0.0), -jnp.minimum(north, 0.0)
    return 1.0 - west - east - south - north, west, east, south, north


def advect(x, winds):
    count, width = x.shape
    centre, west, east, south, north = winds
    for _ in range(STEPS):
        x = (
            centre * x
            + west * pltpu.roll(x, 1, 1)
            + east * pltpu.roll(x, width - 1, 1)
            + south * pltpu.roll(x, 1, 0)
            + north * pltpu.roll(x, count - 1, 0)
        )
    return x


def store_winds(east_ref, north_ref, halo_ref, count, winds_ref):
    for i, part in enumerate(wind_parts(east_ref, north_ref, halo_ref.at[pl.ds(count, 2)])):
        winds_ref[i] = part


def advect_pair(state_ref, halo_ref, winds_ref, pair, f, adv_ref, place):
    fields, rows = state_ref.shape[1:3]
    winds = [winds_ref[k] for k in range(5)]
    for s in (2 * pair, 2 * pair + 1):
        x = jnp.concatenate(
            [state_ref[s, f].astype(jnp.float32), halo_ref[s * fields + f]], axis=0
        )
        adv_ref[s, place] = advect(x, winds)[0:rows].astype(jnp.bfloat16)


def first_kernel(
    steps, state_ref, halo_ref, east_ref, north_ref, terms_ref, acc_in_ref, lat_ref, lon_ref,
    adv_ref, own_ref, send_ref, acc_ref, winds_ref,
):
    slots, fields, rows, width = state_ref.shape
    pairs = slots // 2
    store_winds(east_ref, north_ref, halo_ref, slots * fields, winds_ref)
    acc_ref[...] = acc_in_ref[...]
    held = adv_ref.shape[1]
    total = terms_ref.shape[1] // CHUNK_ROWS

    def body(i, carry):
        add_observations(steps + i, terms_ref, acc_ref)
        advect_pair(state_ref, halo_ref, winds_ref, i % pairs, i // pairs, adv_ref, i // pairs)
        return carry

    def observe(step, carry):
        add_observations(step, terms_ref, acc_ref)
        return carry

    shared = min(pairs * held, total - steps)
    lax.fori_loop(0, shared, body, 0)
    if steps + shared < total:
        lax.fori_loop(steps + shared, total, observe, 0)
    for i in range(shared, pairs * held):
        advect_pair(state_ref, halo_ref, winds_ref, i % pairs, i // pairs, adv_ref, i // pairs)

    inverse, first, second = grids_of(acc_ref, rows)
    logliks = []
    for s in range(slots):
        value = adv_ref[s, 0].astype(jnp.float32)
        logliks.append(-0.5 * (inverse * value * value - 2.0 * first * value + second))
    smooth = functools.partial(
        jnp.dot, precision=lax.Precision.HIGHEST, preferred_element_type=jnp.float32
    )
    along = smooth(jnp.concatenate(logliks, axis=0), lon_ref[...])
    for s in range(slots):
        scores = smooth(lat_ref[...], along[s * rows : (s + 1) * rows])
        own_ref[s] = scores[0:rows]
        send_ref[s] = scores[rows:]


def rest_kernel(state_ref, halo_ref, east_ref, north_ref, adv_ref, winds_ref):
    slots, fields = state_ref.shape[:2]
    pairs = slots // 2
    held = adv_ref.shape[1]
    store_winds(east_ref, north_ref, halo_ref, slots * fields, winds_ref)

    def body(i, carry):
        f = fields - held + i // pairs
        advect_pair(state_ref, halo_ref, winds_ref, i % pairs, f, adv_ref, i // pairs)
        return carry

    lax.fori_loop(0, pairs * held, body, 0)


def field_ref(adv_first_ref, adv_rest_ref, s, f):
    held = adv_first_ref.shape[1]
    return adv_first_ref.at[s, f] if f < held else adv_rest_ref.at[s, f - held]


def weigh_all_kernel(
    place_ref, member_ref, counts_ref, own_ref, recv_ref, adv_first_ref, adv_rest_ref, parts_ref
):
    slots, rows, width = own_ref.shape
    fields = adv_first_ref.shape[1] + adv_rest_ref.shape[1]
    across = width // LANES
    members, _, held, _ = parts_ref.shape

    def store(row_tile, index, value):
        for l in range(across):
            tile = value[:, l * LANES : (l + 1) * LANES]
            row = (row_tile * across + l) * TILE
            for k in range(0, TILE, min(held, TILE)):
                chunk, at = divmod(row + k, held)
                parts_ref[chunk, index, at : at + min(held, TILE)] = tile[k : k + min(held, TILE)]

    lower = place_ref[0] == 0
    for t in range(rows // TILE):
        here = slice(t * TILE, (t + 1) * TILE)
        near = (t * TILE) % SMOOTH
        scores = []
        for s in range(slots):
            recv = recv_ref[s, near : near + TILE, :]
            at_this_edge = lower if t * TILE >= rows - SMOOTH else jnp.logical_not(lower)
            score = own_ref[s, here, :] + jnp.where(at_this_edge, recv, 0.0)
            scores.append(jnp.where(s < counts_ref[0], score, -jnp.inf))
        peak = functools.reduce(jnp.maximum, scores)
        gains = [jnp.exp(score - peak) for score in scores]
        total = functools.reduce(jnp.add, gains)
        store(t, 0, peak + jnp.log(total))
        gains = [gain / total for gain in gains]
        for f in range(fields):
            mean = None
            for s in range(slots):
                ref = field_ref(adv_first_ref, adv_rest_ref, s, f)
                pair = slice(t // 2 * 2 * TILE, (t // 2 + 1) * 2 * TILE)
                value = ref[pair, :].astype(jnp.float32)[t % 2 * TILE : (t % 2 + 1) * TILE]
                term = gains[s] * value
                mean = term if mean is None else mean + term
            store(t, 1 + f, mean)


def weigh_kernel(
    place_ref, member_ref, counts_ref, own_ref, recv_ref, adv_first_ref, adv_rest_ref, *out_refs
):
    slots, rows, width = own_ref.shape
    fields = adv_first_ref.shape[1] + adv_rest_ref.shape[1]
    half = width // PAIR
    lower = place_ref[0] == 0
    even_side = member_ref[0] % PAIR == 0
    for distance in range(LINE):
        tile = (member_ref[0] // PAIR) ^ distance
        here = pl.ds(pl.multiple_of(tile * TILE, TILE), TILE)
        near = pl.ds(pl.multiple_of(tile % 2 * TILE, TILE), TILE)
        pair = pl.ds(pl.multiple_of(tile // 2 * (2 * TILE), 2 * TILE), 2 * TILE)
        even_tile = tile % 2 == 0
        at_edge = lower == (tile * TILE >= rows - SMOOTH)
        keep_ref, send_ref = out_refs[distance], out_refs[LINE + distance]

        def store(index, value):
            left, right = value[:, 0:half], value[:, half:width]
            keep_ref[index] = jnp.where(even_side, left, right)
            send_ref[index] = jnp.where(even_side, right, left)

        scores = []
        for s in range(slots):
            score = own_ref[s, here, :] + jnp.where(at_edge, recv_ref[s, near, :], 0.0)
            scores.append(jnp.where(s < counts_ref[0], score, -jnp.inf))
        peak = functools.reduce(jnp.maximum, scores)
        gains = [jnp.exp(score - peak) for score in scores]
        total = functools.reduce(jnp.add, gains)
        store(0, peak + jnp.log(total))
        gains = [gain / total for gain in gains]
        for f in range(fields):
            mean = None
            for s in range(slots):
                ref = field_ref(adv_first_ref, adv_rest_ref, s, f)
                value = ref[pair, :].astype(jnp.float32)
                term = gains[s] * jnp.where(even_tile, value[0:TILE], value[TILE:])
                mean = term if mean is None else mean + term
            store(1 + f, mean)


def merge_values(refs):
    peak = functools.reduce(jnp.maximum, [ref[0] for ref in refs])
    weights = [jnp.exp(ref[0] - peak) for ref in refs]
    total = functools.reduce(jnp.add, weights)
    shares = [weight / total for weight in weights]
    means = [
        functools.reduce(jnp.add, [share * ref[q] for share, ref in zip(shares, refs)])
        for q in range(1, refs[0].shape[0])
    ]
    return peak + jnp.log(total), means


def merge_kernel(*refs):
    out_ref = refs[-1]
    log_weight, means = merge_values(refs[:-1])
    out_ref[0] = log_weight
    for f, mean in enumerate(means):
        out_ref[1 + f] = mean


def finish_kernel(*refs):
    merged_ref = refs[-1]
    parts = refs[:-1]
    if len(parts) == 1:
        parts = [parts[0].at[d] for d in range(parts[0].shape[0])]
    for f, mean in enumerate(merge_values(parts)[1]):
        merged_ref[f] = mean


def relaxed(value, merged, factor, live):
    value = value.astype(jnp.float32)
    return jnp.where(live, value + factor * (merged - value), 0.0).astype(jnp.bfloat16)


def relax_all_kernel(
    counts_ref, relax_ref, adv_first_ref, adv_rest_ref, whole_ref, new_ref, mean_ref
):
    _, fields, rows, width = new_ref.shape
    across = width // LANES
    held = whole_ref.shape[2]

    def tile(f, row):
        if held >= TILE:
            return whole_ref[row // held, f, row % held : row % held + TILE]
        return jnp.concatenate([whole_ref[(row + k) // held, f] for k in range(0, TILE, held)], axis=0)

    for f in range(fields):
        merged = jnp.concatenate(
            [
                jnp.concatenate([tile(f, (t * across + l) * TILE) for l in range(across)], axis=1)
                for t in range(rows // TILE)
            ],
            axis=0,
        )
        mean_ref[f] = merged.astype(jnp.bfloat16)
        for s in range(new_ref.shape[0]):
            value = field_ref(adv_first_ref, adv_rest_ref, s, f)[...]
            new_ref[s, f] = relaxed(value, merged, relax_ref[f], s < counts_ref[0])


def relax_kernel(member_ref, counts_ref, relax_ref, adv_first_ref, adv_rest_ref, *refs):
    share_refs, (new_out, mean_out, merged_ref, new_ref, mean_ref, sems) = refs[:-6], refs[-6:]
    slots, fields, rows, width = new_ref.shape
    share_of = dict(zip(SHARE_ORDER, share_refs))
    even_side = member_ref[0] % PAIR == 0
    copies = []
    for f in range(fields):
        for distance in range(LINE):
            tile = (member_ref[0] // PAIR) ^ distance
            same = share_of[PAIR * distance][f]
            other = share_of[PAIR * distance + 1][f]
            left = jnp.where(even_side, same, other)
            right = jnp.where(even_side, other, same)
            merged_ref[f, pl.ds(pl.multiple_of(tile * TILE, TILE), TILE), :] = jnp.concatenate(
                [left, right], axis=1
            )
        merged = merged_ref[f]
        mean_ref[f] = merged.astype(jnp.bfloat16)
        for s in range(slots):
            value = field_ref(adv_first_ref, adv_rest_ref, s, f)[...]
            new_ref[s, f] = relaxed(value, merged, relax_ref[f], s < counts_ref[0])
        copies.append(pltpu.make_async_copy(new_ref.at[:, f], new_out.at[:, f], sems.at[0, f]))
        copies.append(pltpu.make_async_copy(mean_ref.at[f], mean_out.at[f], sems.at[1, f]))
        for copy in copies[-2:]:
            copy.start()
    for copy in copies:
        copy.wait()


def call(kernel, ins, outs, scratch=(), **cost):
    return pl.pallas_call(
        kernel,
        out_shape=[jax.ShapeDtypeStruct(shape, dtype) for shape, dtype in outs],
        in_specs=ins,
        out_specs=[VMEM] * len(outs),
        scratch_shapes=list(scratch),
        compiler_params=PARAMS,
        cost_estimate=pl.CostEstimate(**cost),
    )


def on_device(
    state, counts, east_wind, north_wind, obs_cells, obs_mask, obs_values, obs_error, relax
):
    slots, fields, rows, width = state.shape
    f32, bf16 = jnp.float32, jnp.bfloat16
    place = lax.axis_index("lat")
    swap = [(0, 1), (1, 0)]
    lower = place == 0

    edge = lax.dynamic_slice_in_dim(state, jnp.where(lower, rows - TILE, 0), TILE, axis=2)
    winds = jnp.stack([east_wind, north_wind])
    wind_edge = lax.dynamic_slice_in_dim(winds, jnp.where(lower, rows - TILE, 0), TILE, axis=1)
    message = jnp.concatenate(
        [edge.astype(f32).reshape(slots * fields, TILE, width), wind_edge], axis=0
    )
    near = jnp.arange(TILE) < TILE // 2
    keep = jnp.logical_xor(near, lower)
    message = jnp.where(keep[None, :, None], message, 0.0)
    halo = lax.ppermute(message, "lat", swap)

    observations = obs_cells.shape[1]
    flat = [
        x.reshape(observations // LANES, LANES) for x in (obs_cells, obs_mask, obs_values, obs_error)
    ]
    acc_shape = (PARTS * 2 * rows, width // 2)
    all_steps = observations // (LANES * CHUNK_ROWS)
    begin_steps = min(BEGIN_STEPS, all_steps)
    observe_flops = 2 * PARTS * rows * width * LANES * CHUNK_ROWS
    terms, begun = call(
        functools.partial(begin_kernel, rows, width, begin_steps),
        [VMEM] * 4,
        [((PARTS + 2, observations // LANES, LANES), f32), (acc_shape, f32)],
        flops=observe_flops * begin_steps,
        bytes_accessed=16 * observations,
        transcendentals=observations,
    )(*flat)

    index = np.arange(rows)
    own = index[None, :] - index[:, None]
    upper_side = index[None, :] - (index[:SMOOTH, None] + rows)
    lower_side = index[None, :] - (index[rows - SMOOTH :, None] - rows)
    lat_kernel = jnp.where(
        lower,
        jnp.asarray(kernel_matrix(np.concatenate([own, upper_side]))),
        jnp.asarray(kernel_matrix(np.concatenate([own, lower_side]))),
    )
    distance = np.abs(np.arange(width)[:, None] - np.arange(width)[None, :])
    lon_kernel = jnp.asarray(kernel_matrix(np.minimum(distance, width - distance)))

    winds_scratch = pltpu.VMEM((5, rows + TILE, width), f32)
    advect_flops = STEPS * 16 * slots * rows * width
    adv_first, own_scores, edge_scores = call(
        functools.partial(first_kernel, begin_steps),
        [VMEM] * 8,
        [
            ((slots, fields - LATER_FIELDS, rows, width), bf16),
            ((slots, rows, width), f32),
            ((slots, SMOOTH, width), f32),
        ],
        [pltpu.VMEM(acc_shape, f32), winds_scratch],
        flops=observe_flops * (all_steps - begin_steps) + advect_flops * (fields - LATER_FIELDS),
        bytes_accessed=4 * width * width,
        transcendentals=0,
    )(state, halo, east_wind, north_wind, terms, begun, lat_kernel, lon_kernel)
    received = lax.ppermute(edge_scores, "lat", swap)

    (adv_rest,) = call(
        rest_kernel,
        [VMEM] * 4,
        [((slots, LATER_FIELDS, rows, width), bf16)],
        [winds_scratch],
        flops=advect_flops * LATER_FIELDS,
        bytes_accessed=4 * slots * fields * rows * width,
        transcendentals=0,
    )(state, halo, east_wind, north_wind)

    members = lax.axis_size("mem")
    member = lax.axis_index("mem")
    place_of, member_of = place.reshape(1), member.reshape(1)
    factors = jnp.broadcast_to(relax[:, None, None], (fields, 1, width))
    quantities = fields + 1
    direct = (members, rows, width % (PAIR * LANES)) == (PAIR * LINE, LINE * TILE, 0)
    chunk = (TILE, width // PAIR) if direct else (rows * width // LANES // members, LANES)
    cells = chunk[0] * chunk[1]

    def weigh(kernel, outs):
        return call(
            kernel,
            [SMEM] * 3 + [VMEM] * 4,
            outs,
            flops=4 * slots * fields * rows * width,
            bytes_accessed=4 * slots * fields * rows * width,
            transcendentals=slots * rows * width,
        )(place_of, member_of, counts, own_scores, received, adv_first, adv_rest)

    def merge(kernel, pieces, out):
        size = quantities * cells * (len(pieces) if direct else members)
        return call(
            kernel,
            [VMEM] * len(pieces),
            [out],
            flops=4 * size,
            bytes_accessed=4 * size,
            transcendentals=size // quantities,
        )(*pieces)[0]

    def swapped(x, offset):
        return lax.ppermute(x, "mem", [(m, m ^ offset) for m in range(members)])

    merged_chunk = ((fields,) + chunk, f32)
    new_shape, mean_shape = (slots, fields, rows, width), (fields, rows, width)
    outs = [(new_shape, bf16), (mean_shape, bf16)]
    if direct:
        piece = ((quantities,) + chunk, f32)
        parts = weigh(weigh_kernel, [piece] * (PAIR * LINE))
        paired = [None] * LINE
        for j in reversed(range(LINE)):
            paired[j] = merge(merge_kernel, [parts[j], swapped(parts[LINE + j], 1)], piece)
        pieces = [paired[0]] + [swapped(paired[j], PAIR * j) for j in range(1, LINE)]
        merged = merge(finish_kernel, pieces, merged_chunk)
        far = LINE - 1
        sent = {0: merged}
        for offset in SHARE_ORDER[1:]:
            through = offset ^ 1 if offset % PAIR and offset // PAIR < far else 0
            sent[offset] = swapped(sent[through], offset ^ through)
        size = slots * fields * rows * width
        new_state, mean = pl.pallas_call(
            relax_kernel,
            out_shape=[jax.ShapeDtypeStruct(*out) for out in outs],
            in_specs=[SMEM] * 2 + [VMEM] * (3 + len(sent)),
            out_specs=[pl.BlockSpec(memory_space=pl.ANY)] * 2,
            scratch_shapes=[
                pltpu.VMEM((fields, rows, width), f32),
                pltpu.VMEM(new_shape, bf16),
                pltpu.VMEM(mean_shape, bf16),
                pltpu.SemaphoreType.DMA((2, fields)),
            ],
            compiler_params=PARAMS,
            cost_estimate=pl.CostEstimate(flops=4 * size, bytes_accessed=4 * size, transcendentals=0),
        )(member_of, counts, factors, adv_first, adv_rest, *[sent[i] for i in SHARE_ORDER])
    else:
        (parts,) = weigh(weigh_all_kernel, [((members, quantities) + chunk, f32)])
        got = lax.all_to_all(parts, "mem", 0, 0, tiled=True)
        whole = lax.all_gather(merge(finish_kernel, [got], merged_chunk), "mem")
        new_state, mean = call(
            relax_all_kernel,
            [SMEM] + [VMEM] * 4,
            outs,
            flops=4 * slots * fields * rows * width,
            bytes_accessed=4 * slots * fields * rows * width,
            transcendentals=0,
        )(counts, factors, adv_first, adv_rest, whole)
    return (new_state, mean)


def solution(mesh):
    return jax.shard_map(
        on_device,
        mesh=mesh,
        in_specs=(
            P(("groups", "mem"), None, "lat", None),
            P(("groups", "mem")),
            P(("groups", "lat"), None),
            P(("groups", "lat"), None),
            P(("groups", "lat"), None),
            P(("groups", "lat"), None),
            P(("groups", "lat"), None),
            P(("groups", "lat"), None),
            P(),
        ),
        out_specs=(P(("groups", "mem"), None, "lat", None), P("groups", "lat", None)),
        check_vma=False,
    )
```

```python
import functools

import jax
import jax.numpy as jnp
import numpy as np
from jax import lax
from jax.experimental import pallas as pl
from jax.experimental.pallas import tpu as pltpu
from jax.sharding import PartitionSpec as P

STEPS = 4
SMOOTH = 16
LOG_TWO_PI = 1.8378770664093453
LANES = 128
TILE = 8
PARTS = 5
CHUNK_ROWS = 16
PACK = 16
BEGIN_STEPS = 4
LATER_FIELDS = 2
PAIR = 2
LINE = 4
SHARE_ORDER = (0, 6, 7, 4, 1, 2, 3, 5)


VMEM = pl.BlockSpec(memory_space=pltpu.VMEM)
SMEM = pl.BlockSpec(memory_space=pltpu.SMEM)
PARAMS = pltpu.CompilerParams(vmem_limit_bytes=24 * 1024 * 1024)
EDGE_VMEM = 63 * 1024 * 1024


def kernel_matrix(offset):
    values = np.exp(-((2.0 * offset.astype(np.float32) / SMOOTH) ** 2))
    return np.where(np.abs(offset) <= SMOOTH, values, 0.0).astype(np.float32)


def split_two(x):
    high = x.astype(jnp.bfloat16).astype(jnp.float32)
    return high, x - high


def spread_terms(cells_ref, mask_ref, values_ref, error_ref, rows_ref, rows, width):
    half = width // 2
    cells = cells_ref[...]
    used = mask_ref[...].astype(jnp.float32)
    values = values_ref[...]
    error = error_ref[...]
    inverse = used / (error * error)
    first = inverse * values
    second = first * values + used * (2.0 * jnp.log(error) + LOG_TWO_PI)
    row = cells // width
    column = cells % width
    high = (column // half * rows + row).astype(jnp.float32)
    low = (column % half).astype(jnp.float32)
    for k, x in enumerate(split_two(inverse) + split_two(first) + (second, high, low)):
        rows_ref[k] = x


def add_observations(step, rows_ref, acc_ref):
    highs, lows = acc_ref.shape[0] // PARTS, acc_ref.shape[1]

    def steps_of(count):
        base = lax.broadcasted_iota(jnp.int32, (PACK, LANES), 0)
        return [
            (base + PACK * i).astype(jnp.float32).astype(jnp.bfloat16) for i in range(count // PACK)
        ]

    high_iota, low_iota = steps_of(highs), steps_of(lows)
    zero = jnp.zeros((PACK, LANES), jnp.bfloat16)
    one = jnp.ones((PACK, LANES), jnp.bfloat16)
    here = pl.ds(pl.multiple_of(step * CHUNK_ROWS, CHUNK_ROWS), CHUNK_ROWS)
    held = [rows_ref[k, here, :] for k in range(PARTS + 2)]
    left, right = [], []
    for r in range(CHUNK_ROWS):
        spread = [
            jnp.broadcast_to(x[r : r + 1, :], (PACK, LANES)).astype(jnp.bfloat16) for x in held
        ]
        high_row, low_row = spread[PARTS:]
        hit = [iota == high_row for iota in high_iota]
        left.append(
            jnp.concatenate([jnp.where(h, part, zero) for part in spread[:PARTS] for h in hit], axis=0)
        )
        right.append(
            jnp.concatenate([jnp.where(iota == low_row, one, zero) for iota in low_iota], axis=0)
        )
    acc_ref[...] += lax.dot_general(
        jnp.concatenate(left, axis=1),
        jnp.concatenate(right, axis=1),
        (((1,), (1,)), ((), ())),
        preferred_element_type=jnp.float32,
    )


def grids_of(acc_ref, rows):
    highs = 2 * rows

    def part_sum(indices):
        total = acc_ref[pl.ds(indices[-1] * highs, highs), :]
        for i in indices[-2::-1]:
            total = total + acc_ref[pl.ds(i * highs, highs), :]
        return jnp.concatenate([total[0:rows], total[rows:highs]], axis=1)

    return [part_sum(indices) for indices in ((0, 1), (2, 3), (4,))]


def begin_kernel(rows, width, steps, cells_ref, mask_ref, values_ref, error_ref, rows_ref, acc_ref):
    spread_terms(cells_ref, mask_ref, values_ref, error_ref, rows_ref, rows, width)
    acc_ref[...] = jnp.zeros_like(acc_ref)

    def body(step, carry):
        add_observations(step, rows_ref, acc_ref)
        return carry

    lax.fori_loop(0, steps, body, 0)


def wind_parts(east_ref, north_ref, wind_halo_ref):
    east = jnp.concatenate([east_ref[...], wind_halo_ref[0]], axis=0)
    north = jnp.concatenate([north_ref[...], wind_halo_ref[1]], axis=0)
    west, south = jnp.maximum(east, 0.0), jnp.maximum(north, 0.0)
    east, north = -jnp.minimum(east, 0.0), -jnp.minimum(north, 0.0)
    return 1.0 - west - east - south - north, west, east, south, north


def advect(x, winds):
    count, width = x.shape
    centre, west, east, south, north = winds
    for _ in range(STEPS):
        x = (
            centre * x
            + west * pltpu.roll(x, 1, 1)
            + east * pltpu.roll(x, width - 1, 1)
            + south * pltpu.roll(x, 1, 0)
            + north * pltpu.roll(x, count - 1, 0)
        )
    return x


def edge_kernel(place_ref, state_in, east_in, north_in, out_ref, state_ref, wind_ref, sems):
    slots, fields, rows, width = state_in.shape
    lower = place_ref[0] == 0
    start = pl.multiple_of((1 - place_ref[0]) * (rows - 2 * TILE), 2 * TILE)
    here = pl.ds(start, 2 * TILE)
    copies = [
        pltpu.make_async_copy(state_in.at[:, :, here], state_ref, sems.at[0]),
        pltpu.make_async_copy(east_in.at[here], wind_ref.at[0], sems.at[1]),
        pltpu.make_async_copy(north_in.at[here], wind_ref.at[1], sems.at[2]),
    ]
    for copy in copies:
        copy.start()
    low_row = lax.broadcasted_iota(jnp.int32, (TILE, width), 0) < TILE // 2
    keep = low_row != lower

    def edge(block):
        return jnp.where(keep, jnp.where(lower, block[TILE:], block[0:TILE]), 0.0)

    for copy in copies:
        copy.wait()
    for s in range(slots):
        for f in range(fields):
            out_ref[s * fields + f] = edge(state_ref[s, f].astype(jnp.float32))
    for i in range(2):
        out_ref[slots * fields + i] = edge(wind_ref[i])


def store_winds(east_ref, north_ref, halo_ref, count, winds_ref):
    for i, part in enumerate(wind_parts(east_ref, north_ref, halo_ref.at[pl.ds(count, 2)])):
        winds_ref[i] = part


def advect_pair(state_ref, halo_ref, winds_ref, pair, f, adv_ref, place):
    fields, rows = state_ref.shape[1:3]
    winds = [winds_ref[k] for k in range(5)]
    for s in (2 * pair, 2 * pair + 1):
        x = jnp.concatenate(
            [state_ref[s, f].astype(jnp.float32), halo_ref[s * fields + f]], axis=0
        )
        adv_ref[s, place] = advect(x, winds)[0:rows].astype(jnp.bfloat16)


def first_kernel(
    steps, state_ref, halo_ref, east_ref, north_ref, terms_ref, acc_in_ref, lat_ref, lon_ref,
    adv_ref, own_ref, send_ref, acc_ref, winds_ref,
):
    slots, fields, rows, width = state_ref.shape
    pairs = slots // 2
    store_winds(east_ref, north_ref, halo_ref, slots * fields, winds_ref)
    acc_ref[...] = acc_in_ref[...]
    held = adv_ref.shape[1]
    total = terms_ref.shape[1] // CHUNK_ROWS

    def body(i, carry):
        add_observations(steps + i, terms_ref, acc_ref)
        advect_pair(state_ref, halo_ref, winds_ref, i % pairs, i // pairs, adv_ref, i // pairs)
        return carry

    def observe(step, carry):
        add_observations(step, terms_ref, acc_ref)
        return carry

    shared = min(pairs * held, total - steps)
    lax.fori_loop(0, shared, body, 0)
    if steps + shared < total:
        lax.fori_loop(steps + shared, total, observe, 0)
    for i in range(shared, pairs * held):
        advect_pair(state_ref, halo_ref, winds_ref, i % pairs, i // pairs, adv_ref, i // pairs)

    inverse, first, second = grids_of(acc_ref, rows)
    logliks = []
    for s in range(slots):
        value = adv_ref[s, 0].astype(jnp.float32)
        logliks.append(-0.5 * (inverse * value * value - 2.0 * first * value + second))
    smooth = functools.partial(
        jnp.dot, precision=lax.Precision.HIGHEST, preferred_element_type=jnp.float32
    )
    along = smooth(jnp.concatenate(logliks, axis=0), lon_ref[...])
    for s in range(slots):
        scores = smooth(lat_ref[...], along[s * rows : (s + 1) * rows])
        own_ref[s] = scores[0:rows]
        send_ref[s] = scores[rows:]


def rest_kernel(state_ref, halo_ref, east_ref, north_ref, adv_ref, winds_ref):
    slots, fields = state_ref.shape[:2]
    pairs = slots // 2
    held = adv_ref.shape[1]
    store_winds(east_ref, north_ref, halo_ref, slots * fields, winds_ref)

    def body(i, carry):
        f = fields - held + i // pairs
        advect_pair(state_ref, halo_ref, winds_ref, i % pairs, f, adv_ref, i // pairs)
        return carry

    lax.fori_loop(0, pairs * held, body, 0)


def field_ref(adv_first_ref, adv_rest_ref, s, f):
    held = adv_first_ref.shape[1]
    return adv_first_ref.at[s, f] if f < held else adv_rest_ref.at[s, f - held]


def weigh_all_kernel(
    place_ref, member_ref, counts_ref, own_ref, recv_ref, adv_first_ref, adv_rest_ref, parts_ref
):
    slots, rows, width = own_ref.shape
    fields = adv_first_ref.shape[1] + adv_rest_ref.shape[1]
    across = width // LANES
    members, _, held, _ = parts_ref.shape

    def store(row_tile, index, value):
        for l in range(across):
            tile = value[:, l * LANES : (l + 1) * LANES]
            row = (row_tile * across + l) * TILE
            for k in range(0, TILE, min(held, TILE)):
                chunk, at = divmod(row + k, held)
                parts_ref[chunk, index, at : at + min(held, TILE)] = tile[k : k + min(held, TILE)]

    lower = place_ref[0] == 0
    for t in range(rows // TILE):
        here = slice(t * TILE, (t + 1) * TILE)
        near = (t * TILE) % SMOOTH
        scores = []
        for s in range(slots):
            recv = recv_ref[s, near : near + TILE, :]
            at_this_edge = lower if t * TILE >= rows - SMOOTH else jnp.logical_not(lower)
            score = own_ref[s, here, :] + jnp.where(at_this_edge, recv, 0.0)
            scores.append(jnp.where(s < counts_ref[0], score, -jnp.inf))
        peak = functools.reduce(jnp.maximum, scores)
        gains = [jnp.exp(score - peak) for score in scores]
        total = functools.reduce(jnp.add, gains)
        store(t, 0, peak + jnp.log(total))
        gains = [gain / total for gain in gains]
        for f in range(fields):
            mean = None
            for s in range(slots):
                ref = field_ref(adv_first_ref, adv_rest_ref, s, f)
                pair = slice(t // 2 * 2 * TILE, (t // 2 + 1) * 2 * TILE)
                value = ref[pair, :].astype(jnp.float32)[t % 2 * TILE : (t % 2 + 1) * TILE]
                term = gains[s] * value
                mean = term if mean is None else mean + term
            store(t, 1 + f, mean)


def weigh_kernel(
    place_ref, member_ref, counts_ref, own_ref, recv_ref, adv_first_ref, adv_rest_ref, *out_refs
):
    slots, rows, width = own_ref.shape
    fields = adv_first_ref.shape[1] + adv_rest_ref.shape[1]
    half = width // PAIR
    lower = place_ref[0] == 0
    even_side = member_ref[0] % PAIR == 0
    for distance in range(LINE):
        tile = (member_ref[0] // PAIR) ^ distance
        here = pl.ds(pl.multiple_of(tile * TILE, TILE), TILE)
        near = pl.ds(pl.multiple_of(tile % 2 * TILE, TILE), TILE)
        pair = pl.ds(pl.multiple_of(tile // 2 * (2 * TILE), 2 * TILE), 2 * TILE)
        even_tile = tile % 2 == 0
        at_edge = lower == (tile * TILE >= rows - SMOOTH)
        keep_ref, send_ref = out_refs[distance], out_refs[LINE + distance]

        def store(index, value):
            left, right = value[:, 0:half], value[:, half:width]
            keep_ref[index] = jnp.where(even_side, left, right)
            send_ref[index] = jnp.where(even_side, right, left)

        scores = []
        for s in range(slots):
            score = own_ref[s, here, :] + jnp.where(at_edge, recv_ref[s, near, :], 0.0)
            scores.append(jnp.where(s < counts_ref[0], score, -jnp.inf))
        peak = functools.reduce(jnp.maximum, scores)
        gains = [jnp.exp(score - peak) for score in scores]
        total = functools.reduce(jnp.add, gains)
        store(0, peak + jnp.log(total))
        gains = [gain / total for gain in gains]
        for f in range(fields):
            mean = None
            for s in range(slots):
                ref = field_ref(adv_first_ref, adv_rest_ref, s, f)
                value = ref[pair, :].astype(jnp.float32)
                term = gains[s] * jnp.where(even_tile, value[0:TILE], value[TILE:])
                mean = term if mean is None else mean + term
            store(1 + f, mean)


def merge_values(refs):
    peak = functools.reduce(jnp.maximum, [ref[0] for ref in refs])
    weights = [jnp.exp(ref[0] - peak) for ref in refs]
    total = functools.reduce(jnp.add, weights)
    shares = [weight / total for weight in weights]
    means = [
        functools.reduce(jnp.add, [share * ref[q] for share, ref in zip(shares, refs)])
        for q in range(1, refs[0].shape[0])
    ]
    return peak + jnp.log(total), means


def merge_kernel(*refs):
    out_ref = refs[-1]
    log_weight, means = merge_values(refs[:-1])
    out_ref[0] = log_weight
    for f, mean in enumerate(means):
        out_ref[1 + f] = mean


def finish_kernel(*refs):
    merged_ref = refs[-1]
    parts = refs[:-1]
    if len(parts) == 1:
        parts = [parts[0].at[d] for d in range(parts[0].shape[0])]
    for f, mean in enumerate(merge_values(parts)[1]):
        merged_ref[f] = mean


def relaxed(value, merged, factor, live):
    value = value.astype(jnp.float32)
    return jnp.where(live, value + factor * (merged - value), 0.0).astype(jnp.bfloat16)


def relax_all_kernel(
    counts_ref, relax_ref, adv_first_ref, adv_rest_ref, whole_ref, new_ref, mean_ref
):
    _, fields, rows, width = new_ref.shape
    across = width // LANES
    held = whole_ref.shape[2]

    def tile(f, row):
        if held >= TILE:
            return whole_ref[row // held, f, row % held : row % held + TILE]
        return jnp.concatenate([whole_ref[(row + k) // held, f] for k in range(0, TILE, held)], axis=0)

    for f in range(fields):
        merged = jnp.concatenate(
            [
                jnp.concatenate([tile(f, (t * across + l) * TILE) for l in range(across)], axis=1)
                for t in range(rows // TILE)
            ],
            axis=0,
        )
        mean_ref[f] = merged.astype(jnp.bfloat16)
        for s in range(new_ref.shape[0]):
            value = field_ref(adv_first_ref, adv_rest_ref, s, f)[...]
            new_ref[s, f] = relaxed(value, merged, relax_ref[f], s < counts_ref[0])


def relax_kernel(member_ref, counts_ref, relax_ref, adv_first_ref, adv_rest_ref, *refs):
    share_refs, (new_out, mean_out, merged_ref, new_ref, mean_ref, sems) = refs[:-6], refs[-6:]
    slots, fields, rows, width = new_ref.shape
    share_of = dict(zip(SHARE_ORDER, share_refs))
    even_side = member_ref[0] % PAIR == 0
    copies = []
    for f in range(fields):
        for distance in range(LINE):
            tile = (member_ref[0] // PAIR) ^ distance
            same = share_of[PAIR * distance][f]
            other = share_of[PAIR * distance + 1][f]
            left = jnp.where(even_side, same, other)
            right = jnp.where(even_side, other, same)
            merged_ref[f, pl.ds(pl.multiple_of(tile * TILE, TILE), TILE), :] = jnp.concatenate(
                [left, right], axis=1
            )
        merged = merged_ref[f]
        mean_ref[f] = merged.astype(jnp.bfloat16)
        for s in range(slots):
            value = field_ref(adv_first_ref, adv_rest_ref, s, f)[...]
            new_ref[s, f] = relaxed(value, merged, relax_ref[f], s < counts_ref[0])
        copies.append(pltpu.make_async_copy(new_ref.at[:, f], new_out.at[:, f], sems.at[0, f]))
        copies.append(pltpu.make_async_copy(mean_ref.at[f], mean_out.at[f], sems.at[1, f]))
        for copy in copies[-2:]:
            copy.start()
    for copy in copies:
        copy.wait()


def call(kernel, ins, outs, scratch=(), **cost):
    return pl.pallas_call(
        kernel,
        out_shape=[jax.ShapeDtypeStruct(shape, dtype) for shape, dtype in outs],
        in_specs=ins,
        out_specs=[VMEM] * len(outs),
        scratch_shapes=list(scratch),
        compiler_params=PARAMS,
        cost_estimate=pl.CostEstimate(**cost),
    )


def on_device(
    state, counts, east_wind, north_wind, obs_cells, obs_mask, obs_values, obs_error, relax
):
    slots, fields, rows, width = state.shape
    f32, bf16 = jnp.float32, jnp.bfloat16
    place = lax.axis_index("lat")
    swap = [(0, 1), (1, 0)]
    lower = place == 0

    (message,) = pl.pallas_call(
        edge_kernel,
        out_shape=[jax.ShapeDtypeStruct((slots * fields + 2, TILE, width), f32)],
        in_specs=[SMEM] + [pl.BlockSpec(memory_space=pltpu.HBM)] * 3,
        out_specs=[VMEM],
        scratch_shapes=[
            pltpu.VMEM((slots, fields, 2 * TILE, width), bf16),
            pltpu.VMEM((2, 2 * TILE, width), f32),
            pltpu.SemaphoreType.DMA((3,)),
        ],
        compiler_params=pltpu.CompilerParams(vmem_limit_bytes=EDGE_VMEM),
        cost_estimate=pl.CostEstimate(
            flops=0, bytes_accessed=6 * slots * fields * TILE * width, transcendentals=0
        ),
    )(place.reshape(1), state, east_wind, north_wind)
    halo = lax.ppermute(message, "lat", swap)

    observations = obs_cells.shape[1]
    flat = [
        x.reshape(observations // LANES, LANES) for x in (obs_cells, obs_mask, obs_values, obs_error)
    ]
    acc_shape = (PARTS * 2 * rows, width // 2)
    all_steps = observations // (LANES * CHUNK_ROWS)
    begin_steps = min(BEGIN_STEPS, all_steps)
    observe_flops = 2 * PARTS * rows * width * LANES * CHUNK_ROWS
    terms, begun = call(
        functools.partial(begin_kernel, rows, width, begin_steps),
        [VMEM] * 4,
        [((PARTS + 2, observations // LANES, LANES), f32), (acc_shape, f32)],
        flops=observe_flops * begin_steps,
        bytes_accessed=16 * observations,
        transcendentals=observations,
    )(*flat)

    index = np.arange(rows)
    own = index[None, :] - index[:, None]
    upper_side = index[None, :] - (index[:SMOOTH, None] + rows)
    lower_side = index[None, :] - (index[rows - SMOOTH :, None] - rows)
    lat_kernel = jnp.where(
        lower,
        jnp.asarray(kernel_matrix(np.concatenate([own, upper_side]))),
        jnp.asarray(kernel_matrix(np.concatenate([own, lower_side]))),
    )
    distance = np.abs(np.arange(width)[:, None] - np.arange(width)[None, :])
    lon_kernel = jnp.asarray(kernel_matrix(np.minimum(distance, width - distance)))

    winds_scratch = pltpu.VMEM((5, rows + TILE, width), f32)
    advect_flops = STEPS * 16 * slots * rows * width
    adv_first, own_scores, edge_scores = call(
        functools.partial(first_kernel, begin_steps),
        [VMEM] * 8,
        [
            ((slots, fields - LATER_FIELDS, rows, width), bf16),
            ((slots, rows, width), f32),
            ((slots, SMOOTH, width), f32),
        ],
        [pltpu.VMEM(acc_shape, f32), winds_scratch],
        flops=observe_flops * (all_steps - begin_steps) + advect_flops * (fields - LATER_FIELDS),
        bytes_accessed=4 * width * width,
        transcendentals=0,
    )(state, halo, east_wind, north_wind, terms, begun, lat_kernel, lon_kernel)
    received = lax.ppermute(edge_scores, "lat", swap)

    (adv_rest,) = call(
        rest_kernel,
        [VMEM] * 4,
        [((slots, LATER_FIELDS, rows, width), bf16)],
        [winds_scratch],
        flops=advect_flops * LATER_FIELDS,
        bytes_accessed=4 * slots * fields * rows * width,
        transcendentals=0,
    )(state, halo, east_wind, north_wind)

    members = lax.axis_size("mem")
    member = lax.axis_index("mem")
    place_of, member_of = place.reshape(1), member.reshape(1)
    factors = jnp.broadcast_to(relax[:, None, None], (fields, 1, width))
    quantities = fields + 1
    direct = (members, rows, width % (PAIR * LANES)) == (PAIR * LINE, LINE * TILE, 0)
    chunk = (TILE, width // PAIR) if direct else (rows * width // LANES // members, LANES)
    cells = chunk[0] * chunk[1]

    def weigh(kernel, outs):
        return call(
            kernel,
            [SMEM] * 3 + [VMEM] * 4,
            outs,
            flops=4 * slots * fields * rows * width,
            bytes_accessed=4 * slots * fields * rows * width,
            transcendentals=slots * rows * width,
        )(place_of, member_of, counts, own_scores, received, adv_first, adv_rest)

    def merge(kernel, pieces, out):
        size = quantities * cells * (len(pieces) if direct else members)
        return call(
            kernel,
            [VMEM] * len(pieces),
            [out],
            flops=4 * size,
            bytes_accessed=4 * size,
            transcendentals=size // quantities,
        )(*pieces)[0]

    def swapped(x, offset):
        return lax.ppermute(x, "mem", [(m, m ^ offset) for m in range(members)])

    merged_chunk = ((fields,) + chunk, f32)
    new_shape, mean_shape = (slots, fields, rows, width), (fields, rows, width)
    outs = [(new_shape, bf16), (mean_shape, bf16)]
    if direct:
        piece = ((quantities,) + chunk, f32)
        parts = weigh(weigh_kernel, [piece] * (PAIR * LINE))
        paired, got = [None] * LINE, [None] * LINE
        for j in reversed(range(LINE)):
            send = parts[LINE + j]
            if j < LINE - 1:
                ahead = max(j + 1, LINE - 1 if j else LINE - 2)
                got[ahead], send = lax.optimization_barrier((got[ahead], send))
            got[j] = swapped(send, 1)
        for j in reversed(range(LINE)):
            paired[j] = merge(merge_kernel, [parts[j], got[j]], piece)
        pieces = [paired[0]] + [swapped(paired[j], PAIR * j) for j in range(1, LINE)]
        merged = merge(finish_kernel, pieces, merged_chunk)
        far = LINE - 1
        sent = {0: merged}
        for offset in SHARE_ORDER[1:]:
            through = offset ^ 1 if offset % PAIR and offset // PAIR < far else 0
            sent[offset] = swapped(sent[through], offset ^ through)
        size = slots * fields * rows * width
        new_state, mean = pl.pallas_call(
            relax_kernel,
            out_shape=[jax.ShapeDtypeStruct(*out) for out in outs],
            in_specs=[SMEM] * 2 + [VMEM] * (3 + len(sent)),
            out_specs=[pl.BlockSpec(memory_space=pl.ANY)] * 2,
            scratch_shapes=[
                pltpu.VMEM((fields, rows, width), f32),
                pltpu.VMEM(new_shape, bf16),
                pltpu.VMEM(mean_shape, bf16),
                pltpu.SemaphoreType.DMA((2, fields)),
            ],
            compiler_params=PARAMS,
            cost_estimate=pl.CostEstimate(flops=4 * size, bytes_accessed=4 * size, transcendentals=0),
        )(member_of, counts, factors, adv_first, adv_rest, *[sent[i] for i in SHARE_ORDER])
    else:
        (parts,) = weigh(weigh_all_kernel, [((members, quantities) + chunk, f32)])
        got = lax.all_to_all(parts, "mem", 0, 0, tiled=True)
        whole = lax.all_gather(merge(finish_kernel, [got], merged_chunk), "mem")
        new_state, mean = call(
            relax_all_kernel,
            [SMEM] + [VMEM] * 4,
            outs,
            flops=4 * slots * fields * rows * width,
            bytes_accessed=4 * slots * fields * rows * width,
            transcendentals=0,
        )(counts, factors, adv_first, adv_rest, whole)
    return (new_state, mean)


def solution(mesh):
    return jax.shard_map(
        on_device,
        mesh=mesh,
        in_specs=(
            P(("groups", "mem"), None, "lat", None),
            P(("groups", "mem")),
            P(("groups", "lat"), None),
            P(("groups", "lat"), None),
            P(("groups", "lat"), None),
            P(("groups", "lat"), None),
            P(("groups", "lat"), None),
            P(("groups", "lat"), None),
            P(),
        ),
        out_specs=(P(("groups", "mem"), None, "lat", None), P("groups", "lat", None)),
        check_vma=False,
    )
```

```python
import functools

import jax
import jax.numpy as jnp
import numpy as np
from jax import lax
from jax.experimental import pallas as pl
from jax.experimental.pallas import tpu as pltpu
from jax.sharding import PartitionSpec as P

STEPS = 4
SMOOTH = 16
LOG_TWO_PI = 1.8378770664093453
LANES = 128
TILE = 8
PARTS = 5
CHUNK_ROWS = 16
PACK = 16
BEGIN_STEPS = 4
LATER_FIELDS = 2
PAIR = 2
LINE = 4
SHARE_ORDER = (0, 6, 7, 4, 1, 2, 3, 5)


VMEM = pl.BlockSpec(memory_space=pltpu.VMEM)
SMEM = pl.BlockSpec(memory_space=pltpu.SMEM)
PARAMS = pltpu.CompilerParams(vmem_limit_bytes=24 * 1024 * 1024)


def kernel_matrix(offset):
    values = np.exp(-((2.0 * offset.astype(np.float32) / SMOOTH) ** 2))
    return np.where(np.abs(offset) <= SMOOTH, values, 0.0).astype(np.float32)


def split_two(x):
    high = x.astype(jnp.bfloat16).astype(jnp.float32)
    return high, x - high


def spread_terms(cells_ref, mask_ref, values_ref, error_ref, rows_ref, rows, width):
    half = width // 2
    cells = cells_ref[...]
    used = mask_ref[...].astype(jnp.float32)
    values = values_ref[...]
    error = error_ref[...]
    inverse = used / (error * error)
    first = inverse * values
    second = first * values + used * (2.0 * jnp.log(error) + LOG_TWO_PI)
    row = cells // width
    column = cells % width
    high = (column // half * rows + row).astype(jnp.float32)
    low = (column % half).astype(jnp.float32)
    for k, x in enumerate(split_two(inverse) + split_two(first) + (second, high, low)):
        rows_ref[k] = x


def add_observations(step, rows_ref, acc_ref):
    highs, lows = acc_ref.shape[0] // PARTS, acc_ref.shape[1]

    def steps_of(count):
        base = lax.broadcasted_iota(jnp.int32, (PACK, LANES), 0)
        return [
            (base + PACK * i).astype(jnp.float32).astype(jnp.bfloat16) for i in range(count // PACK)
        ]

    high_iota, low_iota = steps_of(highs), steps_of(lows)
    zero = jnp.zeros((PACK, LANES), jnp.bfloat16)
    one = jnp.ones((PACK, LANES), jnp.bfloat16)
    here = pl.ds(pl.multiple_of(step * CHUNK_ROWS, CHUNK_ROWS), CHUNK_ROWS)
    held = [rows_ref[k, here, :] for k in range(PARTS + 2)]
    left, right = [], []
    for r in range(CHUNK_ROWS):
        spread = [
            jnp.broadcast_to(x[r : r + 1, :], (PACK, LANES)).astype(jnp.bfloat16) for x in held
        ]
        high_row, low_row = spread[PARTS:]
        hit = [iota == high_row for iota in high_iota]
        left.append(
            jnp.concatenate([jnp.where(h, part, zero) for part in spread[:PARTS] for h in hit], axis=0)
        )
        right.append(
            jnp.concatenate([jnp.where(iota == low_row, one, zero) for iota in low_iota], axis=0)
        )
    acc_ref[...] += lax.dot_general(
        jnp.concatenate(left, axis=1),
        jnp.concatenate(right, axis=1),
        (((1,), (1,)), ((), ())),
        preferred_element_type=jnp.float32,
    )


def grids_of(acc_ref, rows):
    highs = 2 * rows

    def part_sum(indices):
        total = acc_ref[pl.ds(indices[-1] * highs, highs), :]
        for i in indices[-2::-1]:
            total = total + acc_ref[pl.ds(i * highs, highs), :]
        return jnp.concatenate([total[0:rows], total[rows:highs]], axis=1)

    return [part_sum(indices) for indices in ((0, 1), (2, 3), (4,))]


def begin_kernel(rows, width, steps, cells_ref, mask_ref, values_ref, error_ref, rows_ref, acc_ref):
    spread_terms(cells_ref, mask_ref, values_ref, error_ref, rows_ref, rows, width)
    acc_ref[...] = jnp.zeros_like(acc_ref)

    def body(step, carry):
        add_observations(step, rows_ref, acc_ref)
        return carry

    lax.fori_loop(0, steps, body, 0)


def wind_parts(east_ref, north_ref, wind_halo_ref):
    east = jnp.concatenate([east_ref[...], wind_halo_ref[0]], axis=0)
    north = jnp.concatenate([north_ref[...], wind_halo_ref[1]], axis=0)
    west, south = jnp.maximum(east, 0.0), jnp.maximum(north, 0.0)
    east, north = -jnp.minimum(east, 0.0), -jnp.minimum(north, 0.0)
    return 1.0 - west - east - south - north, west, east, south, north


def put_rows(buffer_ref, start, rows):
    for l in range(buffer_ref.shape[0]):
        here = pl.ds(start, rows.shape[0])
        buffer_ref[l, here, :] = rows[:, l * LANES : (l + 1) * LANES]


def row_groups(buffer_ref):
    across, rows = buffer_ref.shape[:2]
    count = rows // TILE
    return [
        jnp.concatenate(
            [buffer_ref[l, pl.ds(v, TILE, stride=count), :] for l in range(across)], axis=1
        )
        for v in range(count)
    ]


def put_row_groups(buffer_ref, groups):
    for v, group in enumerate(groups):
        for l in range(buffer_ref.shape[0]):
            here = pl.ds(v, TILE, stride=len(groups))
            buffer_ref[l, here, :] = group[:, l * LANES : (l + 1) * LANES]


def advect(groups, winds_ref, as_written):
    count, width = len(groups), groups[0].shape[1]
    for _ in range(STEPS):
        south = [pltpu.roll(groups[-1], 1, 0)] + groups[:-1]
        north = groups[1:] + [pltpu.roll(groups[0], TILE - 1, 0)]
        stepped = []
        for v, x in enumerate(groups):
            centre, *winds = [winds_ref[i, v] for i in range(5)]
            cells = [pltpu.roll(x, 1, 1), pltpu.roll(x, width - 1, 1), south[v], north[v]]
            if as_written:
                x = (
                    x
                    - winds[0] * (x - cells[0])
                    + winds[1] * (cells[1] - x)
                    - winds[2] * (x - cells[2])
                    + winds[3] * (cells[3] - x)
                )
            else:
                x = centre * x
                for wind, cell in zip(winds, cells):
                    x = x + wind * cell
            stepped.append(x)
        groups = stepped
    return groups


def store_winds(east_ref, north_ref, halo_ref, count, winds_ref, buffer_ref):
    for i, part in enumerate(wind_parts(east_ref, north_ref, halo_ref.at[pl.ds(count, 2)])):
        put_rows(buffer_ref.at[0], 0, part)
        for v, group in enumerate(row_groups(buffer_ref.at[0])):
            winds_ref[i, v] = group


def advect_pair(
    state_ref, halo_ref, winds_ref, buffer_ref, pair, f, adv_ref, place, as_written=False
):
    fields, rows = state_ref.shape[1:3]
    for k in range(2):
        s = 2 * pair + k
        buffer = buffer_ref.at[k]
        put_rows(buffer, 0, state_ref[s, f].astype(jnp.float32))
        put_rows(buffer, rows, halo_ref[s * fields + f])
        put_row_groups(buffer, advect(row_groups(buffer), winds_ref, as_written))
        advected = [buffer[l, 0:rows, :] for l in range(buffer.shape[0])]
        adv_ref[s, place] = jnp.concatenate(advected, axis=1).astype(jnp.bfloat16)


def first_kernel(
    steps, state_ref, halo_ref, east_ref, north_ref, terms_ref, acc_in_ref, lat_ref, lon_ref,
    adv_ref, own_ref, send_ref, acc_ref, winds_ref, buffer_ref,
):
    slots, fields, rows, width = state_ref.shape
    pairs = slots // 2
    store_winds(east_ref, north_ref, halo_ref, slots * fields, winds_ref, buffer_ref)
    acc_ref[...] = acc_in_ref[...]
    held = adv_ref.shape[1]
    total = terms_ref.shape[1] // CHUNK_ROWS

    def advect_next(i, as_written):
        f = i // pairs
        advect_pair(
            state_ref, halo_ref, winds_ref, buffer_ref, i % pairs, f, adv_ref, f, as_written
        )

    def both(as_written):
        def body(i, carry):
            add_observations(steps + i, terms_ref, acc_ref)
            advect_next(i, as_written)
            return carry

        return body

    def observe(step, carry):
        add_observations(step, terms_ref, acc_ref)
        return carry

    shared = min(pairs * held, total - steps)
    lax.fori_loop(0, min(pairs, shared), both(True), 0)
    if pairs < shared:
        lax.fori_loop(pairs, shared, both(False), 0)
    if steps + shared < total:
        lax.fori_loop(steps + shared, total, observe, 0)
    for i in range(shared, pairs * held):
        advect_next(i, i < pairs)

    inverse, first, second = grids_of(acc_ref, rows)
    logliks = []
    for s in range(slots):
        value = adv_ref[s, 0].astype(jnp.float32)
        logliks.append(-0.5 * (inverse * value * value - 2.0 * first * value + second))
    smooth = functools.partial(
        jnp.dot, precision=lax.Precision.HIGHEST, preferred_element_type=jnp.float32
    )
    along = smooth(jnp.concatenate(logliks, axis=0), lon_ref[...])
    for s in range(slots):
        scores = smooth(lat_ref[...], along[s * rows : (s + 1) * rows])
        own_ref[s] = scores[0:rows]
        send_ref[s] = scores[rows:]


def rest_kernel(
    state_ref, halo_ref, east_ref, north_ref, adv_ref, winds_ref, buffer_ref
):
    slots, fields = state_ref.shape[:2]
    pairs = slots // 2
    held = adv_ref.shape[1]
    store_winds(east_ref, north_ref, halo_ref, slots * fields, winds_ref, buffer_ref)

    def body(i, carry):
        f = fields - held + i // pairs
        advect_pair(state_ref, halo_ref, winds_ref, buffer_ref, i % pairs, f, adv_ref, i // pairs)
        return carry

    lax.fori_loop(0, pairs * held, body, 0)


def field_ref(adv_first_ref, adv_rest_ref, s, f):
    held = adv_first_ref.shape[1]
    return adv_first_ref.at[s, f] if f < held else adv_rest_ref.at[s, f - held]


def weigh_all_kernel(
    place_ref, member_ref, counts_ref, own_ref, recv_ref, adv_first_ref, adv_rest_ref, parts_ref
):
    slots, rows, width = own_ref.shape
    fields = adv_first_ref.shape[1] + adv_rest_ref.shape[1]
    across = width // LANES
    members, _, held, _ = parts_ref.shape

    def store(row_tile, index, value):
        for l in range(across):
            tile = value[:, l * LANES : (l + 1) * LANES]
            row = (row_tile * across + l) * TILE
            for k in range(0, TILE, min(held, TILE)):
                chunk, at = divmod(row + k, held)
                parts_ref[chunk, index, at : at + min(held, TILE)] = tile[k : k + min(held, TILE)]

    lower = place_ref[0] == 0
    for t in range(rows // TILE):
        here = slice(t * TILE, (t + 1) * TILE)
        near = (t * TILE) % SMOOTH
        scores = []
        for s in range(slots):
            recv = recv_ref[s, near : near + TILE, :]
            at_this_edge = lower if t * TILE >= rows - SMOOTH else jnp.logical_not(lower)
            score = own_ref[s, here, :] + jnp.where(at_this_edge, recv, 0.0)
            scores.append(jnp.where(s < counts_ref[0], score, -jnp.inf))
        peak = functools.reduce(jnp.maximum, scores)
        gains = [jnp.exp(score - peak) for score in scores]
        total = functools.reduce(jnp.add, gains)
        store(t, 0, peak + jnp.log(total))
        gains = [gain / total for gain in gains]
        for f in range(fields):
            mean = None
            for s in range(slots):
                ref = field_ref(adv_first_ref, adv_rest_ref, s, f)
                pair = slice(t // 2 * 2 * TILE, (t // 2 + 1) * 2 * TILE)
                value = ref[pair, :].astype(jnp.float32)[t % 2 * TILE : (t % 2 + 1) * TILE]
                term = gains[s] * value
                mean = term if mean is None else mean + term
            store(t, 1 + f, mean)


def weigh_kernel(
    place_ref, member_ref, counts_ref, own_ref, recv_ref, adv_first_ref, adv_rest_ref, *out_refs
):
    slots, rows, width = own_ref.shape
    fields = adv_first_ref.shape[1] + adv_rest_ref.shape[1]
    half = width // PAIR
    lower = place_ref[0] == 0
    even_side = member_ref[0] % PAIR == 0
    for distance in range(LINE):
        tile = (member_ref[0] // PAIR) ^ distance
        here = pl.ds(pl.multiple_of(tile * TILE, TILE), TILE)
        near = pl.ds(pl.multiple_of(tile % 2 * TILE, TILE), TILE)
        pair = pl.ds(pl.multiple_of(tile // 2 * (2 * TILE), 2 * TILE), 2 * TILE)
        even_tile = tile % 2 == 0
        at_edge = lower == (tile * TILE >= rows - SMOOTH)
        keep_ref, send_ref = out_refs[distance], out_refs[LINE + distance]

        def store(index, value):
            left, right = value[:, 0:half], value[:, half:width]
            keep_ref[index] = jnp.where(even_side, left, right)
            send_ref[index] = jnp.where(even_side, right, left)

        scores = []
        for s in range(slots):
            score = own_ref[s, here, :] + jnp.where(at_edge, recv_ref[s, near, :], 0.0)
            scores.append(jnp.where(s < counts_ref[0], score, -jnp.inf))
        peak = functools.reduce(jnp.maximum, scores)
        gains = [jnp.exp(score - peak) for score in scores]
        total = functools.reduce(jnp.add, gains)
        store(0, peak + jnp.log(total))
        gains = [gain / total for gain in gains]
        for f in range(fields):
            mean = None
            for s in range(slots):
                ref = field_ref(adv_first_ref, adv_rest_ref, s, f)
                value = ref[pair, :].astype(jnp.float32)
                term = gains[s] * jnp.where(even_tile, value[0:TILE], value[TILE:])
                mean = term if mean is None else mean + term
            store(1 + f, mean)


def merge_values(refs):
    peak = functools.reduce(jnp.maximum, [ref[0] for ref in refs])
    weights = [jnp.exp(ref[0] - peak) for ref in refs]
    total = functools.reduce(jnp.add, weights)
    shares = [weight / total for weight in weights]
    means = [
        functools.reduce(jnp.add, [share * ref[q] for share, ref in zip(shares, refs)])
        for q in range(1, refs[0].shape[0])
    ]
    return peak + jnp.log(total), means


def merge_kernel(*refs):
    out_ref = refs[-1]
    log_weight, means = merge_values(refs[:-1])
    out_ref[0] = log_weight
    for f, mean in enumerate(means):
        out_ref[1 + f] = mean


def finish_kernel(*refs):
    merged_ref = refs[-1]
    parts = refs[:-1]
    if len(parts) == 1:
        parts = [parts[0].at[d] for d in range(parts[0].shape[0])]
    for f, mean in enumerate(merge_values(parts)[1]):
        merged_ref[f] = mean


def relaxed(value, merged, factor, live):
    value = value.astype(jnp.float32)
    return jnp.where(live, value + factor * (merged - value), 0.0).astype(jnp.bfloat16)


def relax_all_kernel(
    counts_ref, relax_ref, adv_first_ref, adv_rest_ref, whole_ref, new_ref, mean_ref
):
    _, fields, rows, width = new_ref.shape
    across = width // LANES
    held = whole_ref.shape[2]

    def tile(f, row):
        if held >= TILE:
            return whole_ref[row // held, f, row % held : row % held + TILE]
        return jnp.concatenate([whole_ref[(row + k) // held, f] for k in range(0, TILE, held)], axis=0)

    for f in range(fields):
        merged = jnp.concatenate(
            [
                jnp.concatenate([tile(f, (t * across + l) * TILE) for l in range(across)], axis=1)
                for t in range(rows // TILE)
            ],
            axis=0,
        )
        mean_ref[f] = merged.astype(jnp.bfloat16)
        for s in range(new_ref.shape[0]):
            value = field_ref(adv_first_ref, adv_rest_ref, s, f)[...]
            new_ref[s, f] = relaxed(value, merged, relax_ref[f], s < counts_ref[0])


def relax_kernel(member_ref, counts_ref, relax_ref, adv_first_ref, adv_rest_ref, *refs):
    share_refs, (new_out, mean_out, merged_ref, new_ref, mean_ref, sems) = refs[:-6], refs[-6:]
    slots, fields, rows, width = new_ref.shape
    share_of = dict(zip(SHARE_ORDER, share_refs))
    even_side = member_ref[0] % PAIR == 0
    copies = []
    for f in range(fields):
        for distance in range(LINE):
            tile = (member_ref[0] // PAIR) ^ distance
            same = share_of[PAIR * distance][f]
            other = share_of[PAIR * distance + 1][f]
            left = jnp.where(even_side, same, other)
            right = jnp.where(even_side, other, same)
            merged_ref[f, pl.ds(pl.multiple_of(tile * TILE, TILE), TILE), :] = jnp.concatenate(
                [left, right], axis=1
            )
        merged = merged_ref[f]
        mean_ref[f] = merged.astype(jnp.bfloat16)
        for s in range(slots):
            value = field_ref(adv_first_ref, adv_rest_ref, s, f)[...]
            new_ref[s, f] = relaxed(value, merged, relax_ref[f], s < counts_ref[0])
        copies.append(pltpu.make_async_copy(new_ref.at[:, f], new_out.at[:, f], sems.at[0, f]))
        copies.append(pltpu.make_async_copy(mean_ref.at[f], mean_out.at[f], sems.at[1, f]))
        for copy in copies[-2:]:
            copy.start()
    for copy in copies:
        copy.wait()


def call(kernel, ins, outs, scratch=(), **cost):
    return pl.pallas_call(
        kernel,
        out_shape=[jax.ShapeDtypeStruct(shape, dtype) for shape, dtype in outs],
        in_specs=ins,
        out_specs=[VMEM] * len(outs),
        scratch_shapes=list(scratch),
        compiler_params=PARAMS,
        cost_estimate=pl.CostEstimate(**cost),
    )


def on_device(
    state, counts, east_wind, north_wind, obs_cells, obs_mask, obs_values, obs_error, relax
):
    slots, fields, rows, width = state.shape
    f32, bf16 = jnp.float32, jnp.bfloat16
    place = lax.axis_index("lat")
    swap = [(0, 1), (1, 0)]
    lower = place == 0

    edge = lax.dynamic_slice_in_dim(state, jnp.where(lower, rows - TILE, 0), TILE, axis=2)
    winds = jnp.stack([east_wind, north_wind])
    wind_edge = lax.dynamic_slice_in_dim(winds, jnp.where(lower, rows - TILE, 0), TILE, axis=1)
    message = jnp.concatenate(
        [edge.astype(f32).reshape(slots * fields, TILE, width), wind_edge], axis=0
    )
    near = jnp.arange(TILE) < TILE // 2
    keep = jnp.logical_xor(near, lower)
    message = jnp.where(keep[None, :, None], message, 0.0)
    halo = lax.ppermute(message, "lat", swap)

    observations = obs_cells.shape[1]
    flat = [
        x.reshape(observations // LANES, LANES) for x in (obs_cells, obs_mask, obs_values, obs_error)
    ]
    acc_shape = (PARTS * 2 * rows, width // 2)
    all_steps = observations // (LANES * CHUNK_ROWS)
    begin_steps = min(BEGIN_STEPS, all_steps)
    observe_flops = 2 * PARTS * rows * width * LANES * CHUNK_ROWS
    terms, begun = call(
        functools.partial(begin_kernel, rows, width, begin_steps),
        [VMEM] * 4,
        [((PARTS + 2, observations // LANES, LANES), f32), (acc_shape, f32)],
        flops=observe_flops * begin_steps,
        bytes_accessed=16 * observations,
        transcendentals=observations,
    )(*flat)

    index = np.arange(rows)
    own = index[None, :] - index[:, None]
    upper_side = index[None, :] - (index[:SMOOTH, None] + rows)
    lower_side = index[None, :] - (index[rows - SMOOTH :, None] - rows)
    lat_kernel = jnp.where(
        lower,
        jnp.asarray(kernel_matrix(np.concatenate([own, upper_side]))),
        jnp.asarray(kernel_matrix(np.concatenate([own, lower_side]))),
    )
    distance = np.abs(np.arange(width)[:, None] - np.arange(width)[None, :])
    lon_kernel = jnp.asarray(kernel_matrix(np.minimum(distance, width - distance)))

    row_groups_of = (rows + TILE) // TILE
    advect_scratch = [
        pltpu.VMEM((5, row_groups_of, TILE, width), f32),
        pltpu.VMEM((2, width // LANES, rows + TILE, LANES), f32),
    ]
    advect_flops = STEPS * 16 * slots * rows * width
    adv_first, own_scores, edge_scores = call(
        functools.partial(first_kernel, begin_steps),
        [VMEM] * 8,
        [
            ((slots, fields - LATER_FIELDS, rows, width), bf16),
            ((slots, rows, width), f32),
            ((slots, SMOOTH, width), f32),
        ],
        [pltpu.VMEM(acc_shape, f32)] + advect_scratch,
        flops=observe_flops * (all_steps - begin_steps) + advect_flops * (fields - LATER_FIELDS),
        bytes_accessed=4 * width * width,
        transcendentals=0,
    )(state, halo, east_wind, north_wind, terms, begun, lat_kernel, lon_kernel)
    received = lax.ppermute(edge_scores, "lat", swap)

    (adv_rest,) = call(
        rest_kernel,
        [VMEM] * 4,
        [((slots, LATER_FIELDS, rows, width), bf16)],
        advect_scratch,
        flops=advect_flops * LATER_FIELDS,
        bytes_accessed=4 * slots * fields * rows * width,
        transcendentals=0,
    )(state, halo, east_wind, north_wind)

    members = lax.axis_size("mem")
    member = lax.axis_index("mem")
    place_of, member_of = place.reshape(1), member.reshape(1)
    factors = jnp.broadcast_to(relax[:, None, None], (fields, 1, width))
    quantities = fields + 1
    direct = (members, rows, width % (PAIR * LANES)) == (PAIR * LINE, LINE * TILE, 0)
    chunk = (TILE, width // PAIR) if direct else (rows * width // LANES // members, LANES)
    cells = chunk[0] * chunk[1]

    def weigh(kernel, outs):
        return call(
            kernel,
            [SMEM] * 3 + [VMEM] * 4,
            outs,
            flops=4 * slots * fields * rows * width,
            bytes_accessed=4 * slots * fields * rows * width,
            transcendentals=slots * rows * width,
        )(place_of, member_of, counts, own_scores, received, adv_first, adv_rest)

    def merge(kernel, pieces, out):
        size = quantities * cells * (len(pieces) if direct else members)
        return call(
            kernel,
            [VMEM] * len(pieces),
            [out],
            flops=4 * size,
            bytes_accessed=4 * size,
            transcendentals=size // quantities,
        )(*pieces)[0]

    def swapped(x, offset):
        return lax.ppermute(x, "mem", [(m, m ^ offset) for m in range(members)])

    merged_chunk = ((fields,) + chunk, f32)
    new_shape, mean_shape = (slots, fields, rows, width), (fields, rows, width)
    outs = [(new_shape, bf16), (mean_shape, bf16)]
    if direct:
        piece = ((quantities,) + chunk, f32)
        parts = weigh(weigh_kernel, [piece] * (PAIR * LINE))
        paired = [None] * LINE
        for j in reversed(range(LINE)):
            paired[j] = merge(merge_kernel, [parts[j], swapped(parts[LINE + j], 1)], piece)
        pieces = [paired[0]] + [swapped(paired[j], PAIR * j) for j in range(1, LINE)]
        merged = merge(finish_kernel, pieces, merged_chunk)
        far = LINE - 1
        sent = {0: merged}
        for offset in SHARE_ORDER[1:]:
            through = offset ^ 1 if offset % PAIR and offset // PAIR < far else 0
            sent[offset] = swapped(sent[through], offset ^ through)
        size = slots * fields * rows * width
        new_state, mean = pl.pallas_call(
            relax_kernel,
            out_shape=[jax.ShapeDtypeStruct(*out) for out in outs],
            in_specs=[SMEM] * 2 + [VMEM] * (3 + len(sent)),
            out_specs=[pl.BlockSpec(memory_space=pl.ANY)] * 2,
            scratch_shapes=[
                pltpu.VMEM((fields, rows, width), f32),
                pltpu.VMEM(new_shape, bf16),
                pltpu.VMEM(mean_shape, bf16),
                pltpu.SemaphoreType.DMA((2, fields)),
            ],
            compiler_params=PARAMS,
            cost_estimate=pl.CostEstimate(flops=4 * size, bytes_accessed=4 * size, transcendentals=0),
        )(member_of, counts, factors, adv_first, adv_rest, *[sent[i] for i in SHARE_ORDER])
    else:
        (parts,) = weigh(weigh_all_kernel, [((members, quantities) + chunk, f32)])
        got = lax.all_to_all(parts, "mem", 0, 0, tiled=True)
        whole = lax.all_gather(merge(finish_kernel, [got], merged_chunk), "mem")
        new_state, mean = call(
            relax_all_kernel,
            [SMEM] + [VMEM] * 4,
            outs,
            flops=4 * slots * fields * rows * width,
            bytes_accessed=4 * slots * fields * rows * width,
            transcendentals=0,
        )(counts, factors, adv_first, adv_rest, whole)
    return (new_state, mean)


def solution(mesh):
    return jax.shard_map(
        on_device,
        mesh=mesh,
        in_specs=(
            P(("groups", "mem"), None, "lat", None),
            P(("groups", "mem")),
            P(("groups", "lat"), None),
            P(("groups", "lat"), None),
            P(("groups", "lat"), None),
            P(("groups", "lat"), None),
            P(("groups", "lat"), None),
            P(("groups", "lat"), None),
            P(),
        ),
        out_specs=(P(("groups", "mem"), None, "lat", None), P("groups", "lat", None)),
        check_vma=False,
    )
```

```python
import functools

import jax
import jax.numpy as jnp
import numpy as np
from jax import lax
from jax.experimental import pallas as pl
from jax.experimental.pallas import tpu as pltpu
from jax.sharding import PartitionSpec as P

STEPS = 4
SMOOTH = 16
LOG_TWO_PI = 1.8378770664093453
LANES = 128
TILE = 8
PARTS = 5
CHUNK_ROWS = 32
PACK = 16
BEGIN_STEPS = 2
LATER_FIELDS = 2
PAIR = 2
LINE = 4
SHARE_ORDER = (0, 6, 7, 4, 1, 2, 3, 5)


VMEM = pl.BlockSpec(memory_space=pltpu.VMEM)
SMEM = pl.BlockSpec(memory_space=pltpu.SMEM)
PARAMS = pltpu.CompilerParams(vmem_limit_bytes=24 * 1024 * 1024)


def kernel_matrix(offset):
    values = np.exp(-((2.0 * offset.astype(np.float32) / SMOOTH) ** 2))
    return np.where(np.abs(offset) <= SMOOTH, values, 0.0).astype(np.float32)


def split_two(x):
    high = x.astype(jnp.bfloat16).astype(jnp.float32)
    return high, x - high


def spread_terms(cells_ref, mask_ref, values_ref, error_ref, rows_ref, rows, width):
    half = width // 2
    cells = cells_ref[...]
    used = mask_ref[...].astype(jnp.float32)
    values = values_ref[...]
    error = error_ref[...]
    inverse = used / (error * error)
    first = inverse * values
    second = first * values + used * (2.0 * jnp.log(error) + LOG_TWO_PI)
    row = cells // width
    column = cells % width
    high = (column // half * rows + row).astype(jnp.float32)
    low = (column % half).astype(jnp.float32)
    for k, x in enumerate(split_two(inverse) + split_two(first) + (second, high, low)):
        rows_ref[k] = x


def add_observations(step, rows_ref, acc_ref):
    highs, lows = acc_ref.shape[0] // PARTS, acc_ref.shape[1]

    def steps_of(count):
        base = lax.broadcasted_iota(jnp.int32, (PACK, LANES), 0)
        return [
            (base + PACK * i).astype(jnp.float32).astype(jnp.bfloat16) for i in range(count // PACK)
        ]

    high_iota, low_iota = steps_of(highs), steps_of(lows)
    zero = jnp.zeros((PACK, LANES), jnp.bfloat16)
    one = jnp.ones((PACK, LANES), jnp.bfloat16)
    here = pl.ds(pl.multiple_of(step * CHUNK_ROWS, CHUNK_ROWS), CHUNK_ROWS)
    held = [rows_ref[k, here, :] for k in range(PARTS + 2)]
    left, right = [], []
    for r in range(CHUNK_ROWS):
        spread = [
            jnp.broadcast_to(x[r : r + 1, :], (PACK, LANES)).astype(jnp.bfloat16) for x in held
        ]
        high_row, low_row = spread[PARTS:]
        hit = [iota == high_row for iota in high_iota]
        left.append(
            jnp.concatenate([jnp.where(h, part, zero) for part in spread[:PARTS] for h in hit], axis=0)
        )
        right.append(
            jnp.concatenate([jnp.where(iota == low_row, one, zero) for iota in low_iota], axis=0)
        )
    acc_ref[...] += lax.dot_general(
        jnp.concatenate(left, axis=1),
        jnp.concatenate(right, axis=1),
        (((1,), (1,)), ((), ())),
        preferred_element_type=jnp.float32,
    )


def grids_of(acc_ref, rows):
    highs = 2 * rows

    def part_sum(indices):
        total = acc_ref[pl.ds(indices[-1] * highs, highs), :]
        for i in indices[-2::-1]:
            total = total + acc_ref[pl.ds(i * highs, highs), :]
        return jnp.concatenate([total[0:rows], total[rows:highs]], axis=1)

    return [part_sum(indices) for indices in ((0, 1), (2, 3), (4,))]


def begin_kernel(rows, width, steps, cells_ref, mask_ref, values_ref, error_ref, rows_ref, acc_ref):
    spread_terms(cells_ref, mask_ref, values_ref, error_ref, rows_ref, rows, width)
    acc_ref[...] = jnp.zeros_like(acc_ref)

    def body(step, carry):
        add_observations(step, rows_ref, acc_ref)
        return carry

    lax.fori_loop(0, steps, body, 0)


def wind_parts(east_ref, north_ref, wind_halo_ref):
    east = jnp.concatenate([east_ref[...], wind_halo_ref[0]], axis=0)
    north = jnp.concatenate([north_ref[...], wind_halo_ref[1]], axis=0)
    west, south = jnp.maximum(east, 0.0), jnp.maximum(north, 0.0)
    east, north = -jnp.minimum(east, 0.0), -jnp.minimum(north, 0.0)
    return 1.0 - west - east - south - north, west, east, south, north


def advect(x, winds, as_written):
    count, width = x.shape
    centre, west, east, south, north = winds
    for _ in range(STEPS):
        west_cell, east_cell = pltpu.roll(x, 1, 1), pltpu.roll(x, width - 1, 1)
        south_row, north_row = pltpu.roll(x, 1, 0), pltpu.roll(x, count - 1, 0)
        if as_written:
            x = (
                x
                - west * (x - west_cell)
                + east * (east_cell - x)
                - south * (x - south_row)
                + north * (north_row - x)
            )
        else:
            x = (
                centre * x
                + west * west_cell
                + east * east_cell
                + south * south_row
                + north * north_row
            )
    return x


def store_winds(east_ref, north_ref, halo_ref, count, winds_ref):
    for i, part in enumerate(wind_parts(east_ref, north_ref, halo_ref.at[pl.ds(count, 2)])):
        winds_ref[i] = part


def advect_field(state_ref, halo_ref, winds_ref, f, adv_ref, place, as_written=False):
    slots, fields, rows = state_ref.shape[:3]
    winds = [winds_ref[k] for k in range(5)]
    for s in range(slots):
        x = jnp.concatenate(
            [state_ref[s, f].astype(jnp.float32), halo_ref[s * fields + f]], axis=0
        )
        adv_ref[s, place] = advect(x, winds, as_written)[0:rows].astype(jnp.bfloat16)


def first_kernel(
    steps, state_ref, halo_ref, east_ref, north_ref, terms_ref, acc_in_ref, lat_ref, lon_ref,
    adv_ref, own_ref, send_ref, acc_ref, winds_ref,
):
    slots, fields, rows, width = state_ref.shape
    store_winds(east_ref, north_ref, halo_ref, slots * fields, winds_ref)
    acc_ref[...] = acc_in_ref[...]
    held = adv_ref.shape[1]
    total = terms_ref.shape[1] // CHUNK_ROWS

    def both(as_written):
        def body(i, carry):
            add_observations(steps + i, terms_ref, acc_ref)
            advect_field(state_ref, halo_ref, winds_ref, i, adv_ref, i, as_written)
            return carry

        return body

    def observe(step, carry):
        add_observations(step, terms_ref, acc_ref)
        return carry

    shared = min(held, total - steps)
    if shared:
        lax.fori_loop(0, 1, both(True), 0)
        lax.fori_loop(1, shared, both(False), 0)
    if steps + shared < total:
        lax.fori_loop(steps + shared, total, observe, 0)
    for f in range(shared, held):
        advect_field(state_ref, halo_ref, winds_ref, f, adv_ref, f, f == 0)

    inverse, first, second = grids_of(acc_ref, rows)
    logliks = []
    for s in range(slots):
        value = adv_ref[s, 0].astype(jnp.float32)
        logliks.append(-0.5 * (inverse * value * value - 2.0 * first * value + second))
    smooth = functools.partial(
        jnp.dot, precision=lax.Precision.HIGHEST, preferred_element_type=jnp.float32
    )
    along = smooth(jnp.concatenate(logliks, axis=0), lon_ref[...])
    for s in range(slots):
        scores = smooth(lat_ref[...], along[s * rows : (s + 1) * rows])
        own_ref[s] = scores[0:rows]
        send_ref[s] = scores[rows:]


def rest_kernel(state_ref, halo_ref, east_ref, north_ref, adv_ref, winds_ref):
    slots, fields = state_ref.shape[:2]
    held = adv_ref.shape[1]
    store_winds(east_ref, north_ref, halo_ref, slots * fields, winds_ref)

    def body(i, carry):
        advect_field(state_ref, halo_ref, winds_ref, fields - held + i, adv_ref, i)
        return carry

    lax.fori_loop(0, held, body, 0)


def field_ref(adv_first_ref, adv_rest_ref, s, f):
    held = adv_first_ref.shape[1]
    return adv_first_ref.at[s, f] if f < held else adv_rest_ref.at[s, f - held]


def weigh_all_kernel(
    place_ref, member_ref, counts_ref, own_ref, recv_ref, adv_first_ref, adv_rest_ref, parts_ref
):
    slots, rows, width = own_ref.shape
    fields = adv_first_ref.shape[1] + adv_rest_ref.shape[1]
    across = width // LANES
    members, _, held, _ = parts_ref.shape

    def store(row_tile, index, value):
        for l in range(across):
            tile = value[:, l * LANES : (l + 1) * LANES]
            row = (row_tile * across + l) * TILE
            for k in range(0, TILE, min(held, TILE)):
                chunk, at = divmod(row + k, held)
                parts_ref[chunk, index, at : at + min(held, TILE)] = tile[k : k + min(held, TILE)]

    lower = place_ref[0] == 0
    for t in range(rows // TILE):
        here = slice(t * TILE, (t + 1) * TILE)
        near = (t * TILE) % SMOOTH
        scores = []
        for s in range(slots):
            recv = recv_ref[s, near : near + TILE, :]
            at_this_edge = lower if t * TILE >= rows - SMOOTH else jnp.logical_not(lower)
            score = own_ref[s, here, :] + jnp.where(at_this_edge, recv, 0.0)
            scores.append(jnp.where(s < counts_ref[0], score, -jnp.inf))
        peak = functools.reduce(jnp.maximum, scores)
        gains = [jnp.exp(score - peak) for score in scores]
        total = functools.reduce(jnp.add, gains)
        store(t, 0, peak + jnp.log(total))
        gains = [gain / total for gain in gains]
        for f in range(fields):
            mean = None
            for s in range(slots):
                ref = field_ref(adv_first_ref, adv_rest_ref, s, f)
                pair = slice(t // 2 * 2 * TILE, (t // 2 + 1) * 2 * TILE)
                value = ref[pair, :].astype(jnp.float32)[t % 2 * TILE : (t % 2 + 1) * TILE]
                term = gains[s] * value
                mean = term if mean is None else mean + term
            store(t, 1 + f, mean)


def weigh_kernel(
    place_ref, member_ref, counts_ref, own_ref, recv_ref, adv_first_ref, adv_rest_ref, *out_refs
):
    slots, rows, width = own_ref.shape
    fields = adv_first_ref.shape[1] + adv_rest_ref.shape[1]
    half = width // PAIR
    lower = place_ref[0] == 0
    even_side = member_ref[0] % PAIR == 0
    for distance in range(LINE):
        tile = (member_ref[0] // PAIR) ^ distance
        here = pl.ds(pl.multiple_of(tile * TILE, TILE), TILE)
        near = pl.ds(pl.multiple_of(tile % 2 * TILE, TILE), TILE)
        pair = pl.ds(pl.multiple_of(tile // 2 * (2 * TILE), 2 * TILE), 2 * TILE)
        even_tile = tile % 2 == 0
        at_edge = lower == (tile * TILE >= rows - SMOOTH)
        keep_ref, send_ref = out_refs[distance], out_refs[LINE + distance]

        def store(index, value):
            left, right = value[:, 0:half], value[:, half:width]
            keep_ref[index] = jnp.where(even_side, left, right)
            send_ref[index] = jnp.where(even_side, right, left)

        scores = []
        for s in range(slots):
            score = own_ref[s, here, :] + jnp.where(at_edge, recv_ref[s, near, :], 0.0)
            scores.append(jnp.where(s < counts_ref[0], score, -jnp.inf))
        peak = functools.reduce(jnp.maximum, scores)
        gains = [jnp.exp(score - peak) for score in scores]
        total = functools.reduce(jnp.add, gains)
        store(0, peak + jnp.log(total))
        gains = [gain / total for gain in gains]
        for f in range(fields):
            mean = None
            for s in range(slots):
                ref = field_ref(adv_first_ref, adv_rest_ref, s, f)
                value = ref[pair, :].astype(jnp.float32)
                term = gains[s] * jnp.where(even_tile, value[0:TILE], value[TILE:])
                mean = term if mean is None else mean + term
            store(1 + f, mean)


def merge_values(refs):
    peak = functools.reduce(jnp.maximum, [ref[0] for ref in refs])
    weights = [jnp.exp(ref[0] - peak) for ref in refs]
    total = functools.reduce(jnp.add, weights)
    shares = [weight / total for weight in weights]
    means = [
        functools.reduce(jnp.add, [share * ref[q] for share, ref in zip(shares, refs)])
        for q in range(1, refs[0].shape[0])
    ]
    return peak + jnp.log(total), means


def merge_kernel(*refs):
    out_ref = refs[-1]
    log_weight, means = merge_values(refs[:-1])
    out_ref[0] = log_weight
    for f, mean in enumerate(means):
        out_ref[1 + f] = mean


def finish_kernel(*refs):
    merged_ref = refs[-1]
    parts = refs[:-1]
    if len(parts) == 1:
        parts = [parts[0].at[d] for d in range(parts[0].shape[0])]
    for f, mean in enumerate(merge_values(parts)[1]):
        merged_ref[f] = mean


def relaxed(value, merged, factor, live):
    value = value.astype(jnp.float32)
    return jnp.where(live, value + factor * (merged - value), 0.0).astype(jnp.bfloat16)


def relax_all_kernel(
    counts_ref, relax_ref, adv_first_ref, adv_rest_ref, whole_ref, new_ref, mean_ref
):
    _, fields, rows, width = new_ref.shape
    across = width // LANES
    held = whole_ref.shape[2]

    def tile(f, row):
        if held >= TILE:
            return whole_ref[row // held, f, row % held : row % held + TILE]
        return jnp.concatenate([whole_ref[(row + k) // held, f] for k in range(0, TILE, held)], axis=0)

    for f in range(fields):
        merged = jnp.concatenate(
            [
                jnp.concatenate([tile(f, (t * across + l) * TILE) for l in range(across)], axis=1)
                for t in range(rows // TILE)
            ],
            axis=0,
        )
        mean_ref[f] = merged.astype(jnp.bfloat16)
        for s in range(new_ref.shape[0]):
            value = field_ref(adv_first_ref, adv_rest_ref, s, f)[...]
            new_ref[s, f] = relaxed(value, merged, relax_ref[f], s < counts_ref[0])


def relax_kernel(member_ref, counts_ref, relax_ref, adv_first_ref, adv_rest_ref, *refs):
    share_refs, (new_out, mean_out, merged_ref, new_ref, mean_ref, sems) = refs[:-6], refs[-6:]
    slots, fields, rows, width = new_ref.shape
    share_of = dict(zip(SHARE_ORDER, share_refs))
    even_side = member_ref[0] % PAIR == 0
    copies = []
    for f in range(fields):
        for distance in range(LINE):
            tile = (member_ref[0] // PAIR) ^ distance
            same = share_of[PAIR * distance][f]
            other = share_of[PAIR * distance + 1][f]
            left = jnp.where(even_side, same, other)
            right = jnp.where(even_side, other, same)
            merged_ref[f, pl.ds(pl.multiple_of(tile * TILE, TILE), TILE), :] = jnp.concatenate(
                [left, right], axis=1
            )
        merged = merged_ref[f]
        mean_ref[f] = merged.astype(jnp.bfloat16)
        for s in range(slots):
            value = field_ref(adv_first_ref, adv_rest_ref, s, f)[...]
            new_ref[s, f] = relaxed(value, merged, relax_ref[f], s < counts_ref[0])
        copies.append(pltpu.make_async_copy(new_ref.at[:, f], new_out.at[:, f], sems.at[0, f]))
        copies.append(pltpu.make_async_copy(mean_ref.at[f], mean_out.at[f], sems.at[1, f]))
        for copy in copies[-2:]:
            copy.start()
    for copy in copies:
        copy.wait()


def call(kernel, ins, outs, scratch=(), **cost):
    return pl.pallas_call(
        kernel,
        out_shape=[jax.ShapeDtypeStruct(shape, dtype) for shape, dtype in outs],
        in_specs=ins,
        out_specs=[VMEM] * len(outs),
        scratch_shapes=list(scratch),
        compiler_params=PARAMS,
        cost_estimate=pl.CostEstimate(**cost),
    )


def on_device(
    state, counts, east_wind, north_wind, obs_cells, obs_mask, obs_values, obs_error, relax
):
    slots, fields, rows, width = state.shape
    f32, bf16 = jnp.float32, jnp.bfloat16
    place = lax.axis_index("lat")
    swap = [(0, 1), (1, 0)]
    lower = place == 0

    edge = lax.dynamic_slice_in_dim(state, jnp.where(lower, rows - TILE, 0), TILE, axis=2)
    winds = jnp.stack([east_wind, north_wind])
    wind_edge = lax.dynamic_slice_in_dim(winds, jnp.where(lower, rows - TILE, 0), TILE, axis=1)
    message = jnp.concatenate(
        [edge.astype(f32).reshape(slots * fields, TILE, width), wind_edge], axis=0
    )
    near = jnp.arange(TILE) < TILE // 2
    keep = jnp.logical_xor(near, lower)
    message = jnp.where(keep[None, :, None], message, 0.0)
    halo = lax.ppermute(message, "lat", swap)

    observations = obs_cells.shape[1]
    flat = [
        x.reshape(observations // LANES, LANES) for x in (obs_cells, obs_mask, obs_values, obs_error)
    ]
    acc_shape = (PARTS * 2 * rows, width // 2)
    all_steps = observations // (LANES * CHUNK_ROWS)
    begin_steps = min(BEGIN_STEPS, all_steps)
    observe_flops = 2 * PARTS * rows * width * LANES * CHUNK_ROWS
    terms, begun = call(
        functools.partial(begin_kernel, rows, width, begin_steps),
        [VMEM] * 4,
        [((PARTS + 2, observations // LANES, LANES), f32), (acc_shape, f32)],
        flops=observe_flops * begin_steps,
        bytes_accessed=16 * observations,
        transcendentals=observations,
    )(*flat)

    index = np.arange(rows)
    own = index[None, :] - index[:, None]
    upper_side = index[None, :] - (index[:SMOOTH, None] + rows)
    lower_side = index[None, :] - (index[rows - SMOOTH :, None] - rows)
    lat_kernel = jnp.where(
        lower,
        jnp.asarray(kernel_matrix(np.concatenate([own, upper_side]))),
        jnp.asarray(kernel_matrix(np.concatenate([own, lower_side]))),
    )
    distance = np.abs(np.arange(width)[:, None] - np.arange(width)[None, :])
    lon_kernel = jnp.asarray(kernel_matrix(np.minimum(distance, width - distance)))

    winds_scratch = pltpu.VMEM((5, rows + TILE, width), f32)
    advect_flops = STEPS * 16 * slots * rows * width
    adv_first, own_scores, edge_scores = call(
        functools.partial(first_kernel, begin_steps),
        [VMEM] * 8,
        [
            ((slots, fields - LATER_FIELDS, rows, width), bf16),
            ((slots, rows, width), f32),
            ((slots, SMOOTH, width), f32),
        ],
        [pltpu.VMEM(acc_shape, f32), winds_scratch],
        flops=observe_flops * (all_steps - begin_steps) + advect_flops * (fields - LATER_FIELDS),
        bytes_accessed=4 * width * width,
        transcendentals=0,
    )(state, halo, east_wind, north_wind, terms, begun, lat_kernel, lon_kernel)
    received = lax.ppermute(edge_scores, "lat", swap)

    (adv_rest,) = call(
        rest_kernel,
        [VMEM] * 4,
        [((slots, LATER_FIELDS, rows, width), bf16)],
        [winds_scratch],
        flops=advect_flops * LATER_FIELDS,
        bytes_accessed=4 * slots * fields * rows * width,
        transcendentals=0,
    )(state, halo, east_wind, north_wind)

    members = lax.axis_size("mem")
    member = lax.axis_index("mem")
    place_of, member_of = place.reshape(1), member.reshape(1)
    factors = jnp.broadcast_to(relax[:, None, None], (fields, 1, width))
    quantities = fields + 1
    direct = (members, rows, width % (PAIR * LANES)) == (PAIR * LINE, LINE * TILE, 0)
    chunk = (TILE, width // PAIR) if direct else (rows * width // LANES // members, LANES)
    cells = chunk[0] * chunk[1]

    def weigh(kernel, outs):
        return call(
            kernel,
            [SMEM] * 3 + [VMEM] * 4,
            outs,
            flops=4 * slots * fields * rows * width,
            bytes_accessed=4 * slots * fields * rows * width,
            transcendentals=slots * rows * width,
        )(place_of, member_of, counts, own_scores, received, adv_first, adv_rest)

    def merge(kernel, pieces, out):
        size = quantities * cells * (len(pieces) if direct else members)
        return call(
            kernel,
            [VMEM] * len(pieces),
            [out],
            flops=4 * size,
            bytes_accessed=4 * size,
            transcendentals=size // quantities,
        )(*pieces)[0]

    def swapped(x, offset):
        return lax.ppermute(x, "mem", [(m, m ^ offset) for m in range(members)])

    merged_chunk = ((fields,) + chunk, f32)
    new_shape, mean_shape = (slots, fields, rows, width), (fields, rows, width)
    outs = [(new_shape, bf16), (mean_shape, bf16)]
    if direct:
        piece = ((quantities,) + chunk, f32)
        parts = weigh(weigh_kernel, [piece] * (PAIR * LINE))
        paired = [None] * LINE
        for j in reversed(range(LINE)):
            paired[j] = merge(merge_kernel, [parts[j], swapped(parts[LINE + j], 1)], piece)
        pieces = [paired[0]] + [swapped(paired[j], PAIR * j) for j in range(1, LINE)]
        merged = merge(finish_kernel, pieces, merged_chunk)
        far = LINE - 1
        sent = {0: merged}
        for offset in SHARE_ORDER[1:]:
            through = offset ^ 1 if offset % PAIR and offset // PAIR < far else 0
            sent[offset] = swapped(sent[through], offset ^ through)
        size = slots * fields * rows * width
        new_state, mean = pl.pallas_call(
            relax_kernel,
            out_shape=[jax.ShapeDtypeStruct(*out) for out in outs],
            in_specs=[SMEM] * 2 + [VMEM] * (3 + len(sent)),
            out_specs=[pl.BlockSpec(memory_space=pl.ANY)] * 2,
            scratch_shapes=[
                pltpu.VMEM((fields, rows, width), f32),
                pltpu.VMEM(new_shape, bf16),
                pltpu.VMEM(mean_shape, bf16),
                pltpu.SemaphoreType.DMA((2, fields)),
            ],
            compiler_params=PARAMS,
            cost_estimate=pl.CostEstimate(flops=4 * size, bytes_accessed=4 * size, transcendentals=0),
        )(member_of, counts, factors, adv_first, adv_rest, *[sent[i] for i in SHARE_ORDER])
    else:
        (parts,) = weigh(weigh_all_kernel, [((members, quantities) + chunk, f32)])
        got = lax.all_to_all(parts, "mem", 0, 0, tiled=True)
        whole = lax.all_gather(merge(finish_kernel, [got], merged_chunk), "mem")
        new_state, mean = call(
            relax_all_kernel,
            [SMEM] + [VMEM] * 4,
            outs,
            flops=4 * slots * fields * rows * width,
            bytes_accessed=4 * slots * fields * rows * width,
            transcendentals=0,
        )(counts, factors, adv_first, adv_rest, whole)
    return (new_state, mean)


def solution(mesh):
    return jax.shard_map(
        on_device,
        mesh=mesh,
        in_specs=(
            P(("groups", "mem"), None, "lat", None),
            P(("groups", "mem")),
            P(("groups", "lat"), None),
            P(("groups", "lat"), None),
            P(("groups", "lat"), None),
            P(("groups", "lat"), None),
            P(("groups", "lat"), None),
            P(("groups", "lat"), None),
            P(),
        ),
        out_specs=(P(("groups", "mem"), None, "lat", None), P("groups", "lat", None)),
        check_vma=False,
    )
```

```python
import functools

import jax
import jax.numpy as jnp
import numpy as np
from jax import lax
from jax.experimental import pallas as pl
from jax.experimental.pallas import tpu as pltpu
from jax.sharding import PartitionSpec as P

STEPS = 4
SMOOTH = 16
LOG_TWO_PI = 1.8378770664093453
LANES = 128
TILE = 8
PARTS = 5
CHUNK_ROWS = 16
PACK = 16
BEGIN_CHUNK = 32
BEGIN_STEPS = 2
LATER_FIELDS = 2
PAIR = 2
LINE = 4
SHARE_ORDER = (0, 6, 7, 4, 1, 2, 3, 5)


VMEM = pl.BlockSpec(memory_space=pltpu.VMEM)
PARAMS = pltpu.CompilerParams(vmem_limit_bytes=24 * 1024 * 1024)
EDGE_VMEM = 63 * 1024 * 1024


def kernel_matrix(offset):
    values = np.exp(-((2.0 * offset.astype(np.float32) / SMOOTH) ** 2))
    return np.where(np.abs(offset) <= SMOOTH, values, 0.0).astype(np.float32)


def split_two(x):
    high = x.astype(jnp.bfloat16).astype(jnp.float32)
    return high, x - high


def spread_terms(cells_ref, mask_ref, values_ref, error_ref, rows_ref, rows, width):
    half = width // 2
    cells = cells_ref[...]
    used = mask_ref[...].astype(jnp.float32)
    values = values_ref[...]
    error = error_ref[...]
    inverse = used / (error * error)
    first = inverse * values
    second = first * values + used * (2.0 * jnp.log(error) + LOG_TWO_PI)
    row = cells // width
    column = cells % width
    high = (column // half * rows + row).astype(jnp.float32)
    low = (column % half).astype(jnp.float32)
    for k, x in enumerate(split_two(inverse) + split_two(first) + (second, high, low)):
        rows_ref[k] = x


def add_observations(step, size, rows_ref, acc_ref):
    highs, lows = acc_ref.shape[0] // PARTS, acc_ref.shape[1]

    def steps_of(count):
        base = lax.broadcasted_iota(jnp.int32, (PACK, LANES), 0)
        return [
            (base + PACK * i).astype(jnp.float32).astype(jnp.bfloat16) for i in range(count // PACK)
        ]

    high_iota, low_iota = steps_of(highs), steps_of(lows)
    zero = jnp.zeros((PACK, LANES), jnp.bfloat16)
    one = jnp.ones((PACK, LANES), jnp.bfloat16)
    here = pl.ds(pl.multiple_of(step * size, size), size)
    held = [rows_ref[k, here, :] for k in range(PARTS + 2)]
    left, right = [], []
    for r in range(size):
        spread = [
            jnp.broadcast_to(x[r : r + 1, :], (PACK, LANES)).astype(jnp.bfloat16) for x in held
        ]
        high_row, low_row = spread[PARTS:]
        hit = [iota == high_row for iota in high_iota]
        left.append(
            jnp.concatenate([jnp.where(h, part, zero) for part in spread[:PARTS] for h in hit], axis=0)
        )
        right.append(
            jnp.concatenate([jnp.where(iota == low_row, one, zero) for iota in low_iota], axis=0)
        )
    acc_ref[...] += lax.dot_general(
        jnp.concatenate(left, axis=1),
        jnp.concatenate(right, axis=1),
        (((1,), (1,)), ((), ())),
        preferred_element_type=jnp.float32,
    )


def grids_of(acc_ref, rows):
    highs = 2 * rows

    def part_sum(indices):
        total = acc_ref[pl.ds(indices[-1] * highs, highs), :]
        for i in indices[-2::-1]:
            total = total + acc_ref[pl.ds(i * highs, highs), :]
        return jnp.concatenate([total[0:rows], total[rows:highs]], axis=1)

    return [part_sum(indices) for indices in ((0, 1), (2, 3), (4,))]


def begin_kernel(rows, width, steps, cells_ref, mask_ref, values_ref, error_ref, rows_ref, acc_ref):
    spread_terms(cells_ref, mask_ref, values_ref, error_ref, rows_ref, rows, width)
    acc_ref[...] = jnp.zeros_like(acc_ref)

    def body(step, carry):
        add_observations(step, BEGIN_CHUNK, rows_ref, acc_ref)
        return carry

    lax.fori_loop(0, steps, body, 0)


def wind_parts(east_ref, north_ref, wind_halo_ref):
    east = jnp.concatenate([east_ref[...], wind_halo_ref[0]], axis=0)
    north = jnp.concatenate([north_ref[...], wind_halo_ref[1]], axis=0)
    west, south = jnp.maximum(east, 0.0), jnp.maximum(north, 0.0)
    east, north = -jnp.minimum(east, 0.0), -jnp.minimum(north, 0.0)
    return 1.0 - west - east - south - north, west, east, south, north


def advect(x, winds, as_written):
    count, width = x.shape
    centre, west, east, south, north = winds
    for _ in range(STEPS):
        west_cell, east_cell = pltpu.roll(x, 1, 1), pltpu.roll(x, width - 1, 1)
        south_row, north_row = pltpu.roll(x, 1, 0), pltpu.roll(x, count - 1, 0)
        if as_written:
            x = (
                x
                - west * (x - west_cell)
                + east * (east_cell - x)
                - south * (x - south_row)
                + north * (north_row - x)
            )
        else:
            x = (
                centre * x
                + west * west_cell
                + east * east_cell
                + south * south_row
                + north * north_row
            )
    return x


def edge_kernel(state_in, east_in, north_in, out_ref, state_ref, wind_ref, sems):
    slots, fields, rows, width = state_in.shape
    place = lax.axis_index("lat")
    lower = place == 0
    here = pl.ds(pl.multiple_of((1 - place) * (rows - 2 * TILE), 2 * TILE), 2 * TILE)
    copies = [
        pltpu.make_async_copy(state_in.at[:, :, here], state_ref, sems.at[0]),
        pltpu.make_async_copy(east_in.at[here], wind_ref.at[0], sems.at[1]),
        pltpu.make_async_copy(north_in.at[here], wind_ref.at[1], sems.at[2]),
    ]
    for copy in copies:
        copy.start()
    low_row = lax.broadcasted_iota(jnp.int32, (TILE, width), 0) < TILE // 2
    keep = low_row != lower

    def edge(block):
        return jnp.where(keep, jnp.where(lower, block[TILE:], block[0:TILE]), 0.0)

    for copy in copies:
        copy.wait()
    for s in range(slots):
        for f in range(fields):
            out_ref[s * fields + f] = edge(state_ref[s, f].astype(jnp.float32))
    for i in range(2):
        out_ref[slots * fields + i] = edge(wind_ref[i])


def store_winds(east_ref, north_ref, halo_ref, count, winds_ref):
    for i, part in enumerate(wind_parts(east_ref, north_ref, halo_ref.at[pl.ds(count, 2)])):
        winds_ref[i] = part


def advect_pair(state_ref, halo_ref, winds_ref, i, f, adv_ref, place, as_written=False):
    slots, fields, rows = state_ref.shape[:3]
    winds = [winds_ref[k] for k in range(5)]
    for k in range(2):
        s = 2 * (i % (slots // 2)) + k
        x = jnp.concatenate(
            [state_ref[s, f].astype(jnp.float32), halo_ref[s * fields + f]], axis=0
        )
        adv_ref[s, place] = advect(x, winds, as_written)[0:rows].astype(jnp.bfloat16)


def first_kernel(
    steps, state_ref, halo_ref, east_ref, north_ref, terms_ref, acc_in_ref, lat_ref, lon_ref,
    adv_ref, own_ref, send_ref, acc_ref, winds_ref,
):
    slots, fields, rows, width = state_ref.shape
    store_winds(east_ref, north_ref, halo_ref, slots * fields, winds_ref)
    acc_ref[...] = acc_in_ref[...]
    pairs, held = slots // 2, adv_ref.shape[1]
    total = terms_ref.shape[1] // CHUNK_ROWS

    def advect_next(i, as_written):
        f = i // pairs
        advect_pair(state_ref, halo_ref, winds_ref, i, f, adv_ref, f, as_written)

    def both(as_written):
        def body(i, carry):
            add_observations(steps + i, CHUNK_ROWS, terms_ref, acc_ref)
            advect_next(i, as_written)
            return carry

        return body

    def observe(step, carry):
        add_observations(step, CHUNK_ROWS, terms_ref, acc_ref)
        return carry

    shared = min(pairs * held, total - steps)
    lax.fori_loop(0, min(pairs, shared), both(True), 0)
    if pairs < shared:
        lax.fori_loop(pairs, shared, both(False), 0)
    if steps + shared < total:
        lax.fori_loop(steps + shared, total, observe, 0)
    for i in range(shared, pairs * held):
        advect_next(i, i < pairs)

    inverse, first, second = grids_of(acc_ref, rows)
    logliks = []
    for s in range(slots):
        value = adv_ref[s, 0].astype(jnp.float32)
        logliks.append(-0.5 * (inverse * value * value - 2.0 * first * value + second))
    smooth = functools.partial(
        jnp.dot, precision=lax.Precision.HIGHEST, preferred_element_type=jnp.float32
    )
    edge = rows + jnp.where(lax.axis_index("lat") == 0, 0, SMOOTH)
    lat_rows = jnp.concatenate(
        [lat_ref[0:rows], lat_ref[pl.ds(pl.multiple_of(edge, SMOOTH), SMOOTH)]], axis=0
    )
    along = smooth(jnp.concatenate(logliks, axis=0), lon_ref[...])
    for s in range(slots):
        scores = smooth(lat_rows, along[s * rows : (s + 1) * rows])
        own_ref[s] = scores[0:rows]
        send_ref[s] = scores[rows:]


def rest_kernel(state_ref, halo_ref, east_ref, north_ref, adv_ref, winds_ref):
    slots, fields = state_ref.shape[:2]
    held = adv_ref.shape[1]
    store_winds(east_ref, north_ref, halo_ref, slots * fields, winds_ref)

    pairs = slots // 2

    def body(i, carry):
        f = i // pairs
        advect_pair(state_ref, halo_ref, winds_ref, i, fields - held + f, adv_ref, f)
        return carry

    lax.fori_loop(0, pairs * held, body, 0)


def field_ref(adv_first_ref, adv_rest_ref, s, f):
    held = adv_first_ref.shape[1]
    return adv_first_ref.at[s, f] if f < held else adv_rest_ref.at[s, f - held]


def weigh_all_kernel(
    counts_ref, own_ref, recv_ref, adv_first_ref, adv_rest_ref, parts_ref
):
    slots, rows, width = own_ref.shape
    fields = adv_first_ref.shape[1] + adv_rest_ref.shape[1]
    across = width // LANES
    members, _, held, _ = parts_ref.shape

    def store(row_tile, index, value):
        for l in range(across):
            tile = value[:, l * LANES : (l + 1) * LANES]
            row = (row_tile * across + l) * TILE
            for k in range(0, TILE, min(held, TILE)):
                chunk, at = divmod(row + k, held)
                parts_ref[chunk, index, at : at + min(held, TILE)] = tile[k : k + min(held, TILE)]

    lower = lax.axis_index("lat") == 0
    for t in range(rows // TILE):
        here = slice(t * TILE, (t + 1) * TILE)
        near = (t * TILE) % SMOOTH
        scores = []
        for s in range(slots):
            recv = recv_ref[s, near : near + TILE, :]
            at_this_edge = lower if t * TILE >= rows - SMOOTH else jnp.logical_not(lower)
            score = own_ref[s, here, :] + jnp.where(at_this_edge, recv, 0.0)
            scores.append(jnp.where(s < counts_ref[0:1, 0:1], score, -jnp.inf))
        peak = functools.reduce(jnp.maximum, scores)
        gains = [jnp.exp(score - peak) for score in scores]
        total = functools.reduce(jnp.add, gains)
        store(t, 0, peak + jnp.log(total))
        gains = [gain / total for gain in gains]
        for f in range(fields):
            mean = None
            for s in range(slots):
                ref = field_ref(adv_first_ref, adv_rest_ref, s, f)
                pair = slice(t // 2 * 2 * TILE, (t // 2 + 1) * 2 * TILE)
                value = ref[pair, :].astype(jnp.float32)[t % 2 * TILE : (t % 2 + 1) * TILE]
                term = gains[s] * value
                mean = term if mean is None else mean + term
            store(t, 1 + f, mean)


def weigh_kernel(
    counts_ref, own_ref, recv_ref, adv_first_ref, adv_rest_ref, *out_refs
):
    slots, rows, width = own_ref.shape
    fields = adv_first_ref.shape[1] + adv_rest_ref.shape[1]
    half = width // PAIR
    lower = lax.axis_index("lat") == 0
    member = lax.axis_index("mem")
    even_side = member % PAIR == 0
    for distance in range(LINE):
        tile = (member // PAIR) ^ distance
        here = pl.ds(pl.multiple_of(tile * TILE, TILE), TILE)
        near = pl.ds(pl.multiple_of(tile % 2 * TILE, TILE), TILE)
        pair = pl.ds(pl.multiple_of(tile // 2 * (2 * TILE), 2 * TILE), 2 * TILE)
        even_tile = tile % 2 == 0
        at_edge = lower == (tile * TILE >= rows - SMOOTH)
        keep_ref, send_ref = out_refs[distance], out_refs[LINE + distance]

        def store(index, value):
            left, right = value[:, 0:half], value[:, half:width]
            keep_ref[index] = jnp.where(even_side, left, right)
            send_ref[index] = jnp.where(even_side, right, left)

        scores = []
        for s in range(slots):
            score = own_ref[s, here, :] + jnp.where(at_edge, recv_ref[s, near, :], 0.0)
            scores.append(jnp.where(s < counts_ref[0:1, 0:1], score, -jnp.inf))
        peak = functools.reduce(jnp.maximum, scores)
        gains = [jnp.exp(score - peak) for score in scores]
        total = functools.reduce(jnp.add, gains)
        store(0, peak + jnp.log(total))
        gains = [gain / total for gain in gains]
        for f in range(fields):
            mean = None
            for s in range(slots):
                ref = field_ref(adv_first_ref, adv_rest_ref, s, f)
                value = ref[pair, :].astype(jnp.float32)
                term = gains[s] * jnp.where(even_tile, value[0:TILE], value[TILE:])
                mean = term if mean is None else mean + term
            store(1 + f, mean)


def merge_values(refs):
    peak = functools.reduce(jnp.maximum, [ref[0] for ref in refs])
    weights = [jnp.exp(ref[0] - peak) for ref in refs]
    total = functools.reduce(jnp.add, weights)
    shares = [weight / total for weight in weights]
    means = [
        functools.reduce(jnp.add, [share * ref[q] for share, ref in zip(shares, refs)])
        for q in range(1, refs[0].shape[0])
    ]
    return peak + jnp.log(total), means


def merge_kernel(*refs):
    out_ref = refs[-1]
    log_weight, means = merge_values(refs[:-1])
    out_ref[0] = log_weight
    for f, mean in enumerate(means):
        out_ref[1 + f] = mean


def finish_kernel(*refs):
    merged_ref = refs[-1]
    parts = refs[:-1]
    if len(parts) == 1:
        parts = [parts[0].at[d] for d in range(parts[0].shape[0])]
    for f, mean in enumerate(merge_values(parts)[1]):
        merged_ref[f] = mean


def relaxed(value, merged, factor, live):
    value = value.astype(jnp.float32)
    return jnp.where(live, value + factor * (merged - value), 0.0).astype(jnp.bfloat16)


def relax_all_kernel(
    counts_ref, relax_ref, adv_first_ref, adv_rest_ref, whole_ref, new_ref, mean_ref
):
    _, fields, rows, width = new_ref.shape
    across = width // LANES
    held = whole_ref.shape[2]

    def tile(f, row):
        if held >= TILE:
            return whole_ref[row // held, f, row % held : row % held + TILE]
        return jnp.concatenate([whole_ref[(row + k) // held, f] for k in range(0, TILE, held)], axis=0)

    for f in range(fields):
        merged = jnp.concatenate(
            [
                jnp.concatenate([tile(f, (t * across + l) * TILE) for l in range(across)], axis=1)
                for t in range(rows // TILE)
            ],
            axis=0,
        )
        mean_ref[f] = merged.astype(jnp.bfloat16)
        for s in range(new_ref.shape[0]):
            value = field_ref(adv_first_ref, adv_rest_ref, s, f)[...]
            new_ref[s, f] = relaxed(value, merged, relax_ref[f], s < counts_ref[0:1, 0:1])


def relax_kernel(counts_ref, relax_ref, adv_first_ref, adv_rest_ref, *refs):
    share_refs, (new_out, mean_out, merged_ref, new_ref, mean_ref, sems) = refs[:-6], refs[-6:]
    slots, fields, rows, width = new_ref.shape
    share_of = dict(zip(SHARE_ORDER, share_refs))
    member = lax.axis_index("mem")
    even_side = member % PAIR == 0
    copies = []
    for f in range(fields):
        for distance in range(LINE):
            tile = (member // PAIR) ^ distance
            same = share_of[PAIR * distance][f]
            other = share_of[PAIR * distance + 1][f]
            left = jnp.where(even_side, same, other)
            right = jnp.where(even_side, other, same)
            merged_ref[f, pl.ds(pl.multiple_of(tile * TILE, TILE), TILE), :] = jnp.concatenate(
                [left, right], axis=1
            )
        merged = merged_ref[f]
        mean_ref[f] = merged.astype(jnp.bfloat16)
        for s in range(slots):
            value = field_ref(adv_first_ref, adv_rest_ref, s, f)[...]
            new_ref[s, f] = relaxed(value, merged, relax_ref[f], s < counts_ref[0:1, 0:1])
        copies.append(pltpu.make_async_copy(new_ref.at[:, f], new_out.at[:, f], sems.at[0, f]))
        copies.append(pltpu.make_async_copy(mean_ref.at[f], mean_out.at[f], sems.at[1, f]))
        for copy in copies[-2:]:
            copy.start()
    for copy in copies:
        copy.wait()


def call(kernel, ins, outs, scratch=(), **cost):
    return pl.pallas_call(
        kernel,
        out_shape=[jax.ShapeDtypeStruct(shape, dtype) for shape, dtype in outs],
        in_specs=ins,
        out_specs=[VMEM] * len(outs),
        scratch_shapes=list(scratch),
        compiler_params=PARAMS,
        cost_estimate=pl.CostEstimate(**cost),
    )


def on_device(
    state, counts, east_wind, north_wind, obs_cells, obs_mask, obs_values, obs_error, relax
):
    slots, fields, rows, width = state.shape
    f32, bf16 = jnp.float32, jnp.bfloat16
    swap = [(0, 1), (1, 0)]
    (message,) = pl.pallas_call(
        edge_kernel,
        out_shape=[jax.ShapeDtypeStruct((slots * fields + 2, TILE, width), f32)],
        in_specs=[pl.BlockSpec(memory_space=pltpu.HBM)] * 3,
        out_specs=[VMEM],
        scratch_shapes=[
            pltpu.VMEM((slots, fields, 2 * TILE, width), bf16),
            pltpu.VMEM((2, 2 * TILE, width), f32),
            pltpu.SemaphoreType.DMA((3,)),
        ],
        compiler_params=pltpu.CompilerParams(vmem_limit_bytes=EDGE_VMEM),
        cost_estimate=pl.CostEstimate(
            flops=0, bytes_accessed=6 * slots * fields * TILE * width, transcendentals=0
        ),
    )(state, east_wind, north_wind)
    halo = lax.ppermute(message, "lat", swap)

    observations = obs_cells.shape[1]
    flat = [
        x.reshape(observations // LANES, LANES) for x in (obs_cells, obs_mask, obs_values, obs_error)
    ]
    acc_shape = (PARTS * 2 * rows, width // 2)
    all_steps = observations // (LANES * CHUNK_ROWS)
    begin_steps = min(BEGIN_STEPS * BEGIN_CHUNK // CHUNK_ROWS, all_steps)
    observe_flops = 2 * PARTS * rows * width * LANES * CHUNK_ROWS
    terms, begun = call(
        functools.partial(begin_kernel, rows, width, begin_steps * CHUNK_ROWS // BEGIN_CHUNK),
        [VMEM] * 4,
        [((PARTS + 2, observations // LANES, LANES), f32), (acc_shape, f32)],
        flops=observe_flops * begin_steps,
        bytes_accessed=16 * observations,
        transcendentals=observations,
    )(*flat)

    index = np.arange(rows)
    own = index[None, :] - index[:, None]
    upper_side = index[None, :] - (index[:SMOOTH, None] + rows)
    lower_side = index[None, :] - (index[rows - SMOOTH :, None] - rows)
    lat_kernel = jnp.asarray(
        kernel_matrix(np.concatenate([own, upper_side, lower_side])), dtype=f32
    )
    distance = np.abs(np.arange(width)[:, None] - np.arange(width)[None, :])
    lon_kernel = jnp.asarray(kernel_matrix(np.minimum(distance, width - distance)))

    winds_scratch = pltpu.VMEM((5, rows + TILE, width), f32)
    advect_flops = STEPS * 16 * slots * rows * width
    adv_first, own_scores, edge_scores = call(
        functools.partial(first_kernel, begin_steps),
        [VMEM] * 8,
        [
            ((slots, fields - LATER_FIELDS, rows, width), bf16),
            ((slots, rows, width), f32),
            ((slots, SMOOTH, width), f32),
        ],
        [pltpu.VMEM(acc_shape, f32), winds_scratch],
        flops=observe_flops * (all_steps - begin_steps) + advect_flops * (fields - LATER_FIELDS),
        bytes_accessed=4 * width * width,
        transcendentals=0,
    )(state, halo, east_wind, north_wind, terms, begun, lat_kernel, lon_kernel)
    received = lax.ppermute(edge_scores, "lat", swap)

    (adv_rest,) = call(
        rest_kernel,
        [VMEM] * 4,
        [((slots, LATER_FIELDS, rows, width), bf16)],
        [winds_scratch],
        flops=advect_flops * LATER_FIELDS,
        bytes_accessed=4 * slots * fields * rows * width,
        transcendentals=0,
    )(state, halo, east_wind, north_wind)

    members = lax.axis_size("mem")
    counts = jnp.broadcast_to(jnp.clip(counts, 1, slots)[0], (TILE, LANES))
    factors = jnp.broadcast_to(relax[:, None, None], (fields, 1, width))
    quantities = fields + 1
    direct = (members, rows, width % (PAIR * LANES)) == (PAIR * LINE, LINE * TILE, 0)
    chunk = (TILE, width // PAIR) if direct else (rows * width // LANES // members, LANES)
    cells = chunk[0] * chunk[1]

    def weigh(kernel, outs):
        return call(
            kernel,
            [VMEM] * 5,
            outs,
            flops=4 * slots * fields * rows * width,
            bytes_accessed=4 * slots * fields * rows * width,
            transcendentals=slots * rows * width,
        )(counts, own_scores, received, adv_first, adv_rest)

    def merge(kernel, pieces, out):
        size = quantities * cells * (len(pieces) if direct else members)
        return call(
            kernel,
            [VMEM] * len(pieces),
            [out],
            flops=4 * size,
            bytes_accessed=4 * size,
            transcendentals=size // quantities,
        )(*pieces)[0]

    def swapped(x, offset):
        return lax.ppermute(x, "mem", [(m, m ^ offset) for m in range(members)])

    merged_chunk = ((fields,) + chunk, f32)
    new_shape, mean_shape = (slots, fields, rows, width), (fields, rows, width)
    outs = [(new_shape, bf16), (mean_shape, bf16)]
    if direct:
        piece = ((quantities,) + chunk, f32)
        parts = weigh(weigh_kernel, [piece] * (PAIR * LINE))
        paired = [None] * LINE
        for j in reversed(range(LINE)):
            paired[j] = merge(merge_kernel, [parts[j], swapped(parts[LINE + j], 1)], piece)
        pieces = [paired[0]] + [swapped(paired[j], PAIR * j) for j in range(1, LINE)]
        merged = merge(finish_kernel, pieces, merged_chunk)
        far = LINE - 1
        sent = {0: merged}
        for offset in SHARE_ORDER[1:]:
            through = offset ^ 1 if offset % PAIR and offset // PAIR < far else 0
            sent[offset] = swapped(sent[through], offset ^ through)
        size = slots * fields * rows * width
        new_state, mean = pl.pallas_call(
            relax_kernel,
            out_shape=[jax.ShapeDtypeStruct(*out) for out in outs],
            in_specs=[VMEM] * (4 + len(sent)),
            out_specs=[pl.BlockSpec(memory_space=pl.ANY)] * 2,
            scratch_shapes=[
                pltpu.VMEM((fields, rows, width), f32),
                pltpu.VMEM(new_shape, bf16),
                pltpu.VMEM(mean_shape, bf16),
                pltpu.SemaphoreType.DMA((2, fields)),
            ],
            compiler_params=PARAMS,
            cost_estimate=pl.CostEstimate(flops=4 * size, bytes_accessed=4 * size, transcendentals=0),
        )(counts, factors, adv_first, adv_rest, *[sent[i] for i in SHARE_ORDER])
    else:
        (parts,) = weigh(weigh_all_kernel, [((members, quantities) + chunk, f32)])
        got = lax.all_to_all(parts, "mem", 0, 0, tiled=True)
        whole = lax.all_gather(merge(finish_kernel, [got], merged_chunk), "mem")
        new_state, mean = call(
            relax_all_kernel,
            [VMEM] * 5,
            outs,
            flops=4 * slots * fields * rows * width,
            bytes_accessed=4 * slots * fields * rows * width,
            transcendentals=0,
        )(counts, factors, adv_first, adv_rest, whole)
    return (new_state, mean)


def solution(mesh):
    return jax.shard_map(
        on_device,
        mesh=mesh,
        in_specs=(
            P(("groups", "mem"), None, "lat", None),
            P(("groups", "mem")),
            P(("groups", "lat"), None),
            P(("groups", "lat"), None),
            P(("groups", "lat"), None),
            P(("groups", "lat"), None),
            P(("groups", "lat"), None),
            P(("groups", "lat"), None),
            P(),
        ),
        out_specs=(P(("groups", "mem"), None, "lat", None), P("groups", "lat", None)),
        check_vma=False,
    )
```

```python
import functools

import jax
import jax.numpy as jnp
import numpy as np
from jax import lax
from jax.experimental import pallas as pl
from jax.experimental.pallas import tpu as pltpu
from jax.sharding import PartitionSpec as P

STEPS = 4
SMOOTH = 16
LOG_TWO_PI = 1.8378770664093453
LANES = 128
TILE = 8
PARTS = 5
CHUNK_ROWS = 16
PACK = 16
BEGIN_CHUNK = 32
BEGIN_STEPS = 2
LATER_FIELDS = 1
PAIR = 2
LINE = 4
SHARE_ORDER = (0, 6, 7, 4, 1, 2, 3, 5)


VMEM = pl.BlockSpec(memory_space=pltpu.VMEM)
PARAMS = pltpu.CompilerParams(vmem_limit_bytes=24 * 1024 * 1024)
EDGE_VMEM = 63 * 1024 * 1024


def kernel_matrix(offset):
    values = np.exp(-((2.0 * offset.astype(np.float32) / SMOOTH) ** 2))
    return np.where(np.abs(offset) <= SMOOTH, values, 0.0).astype(np.float32)


def split_two(x):
    high = x.astype(jnp.bfloat16).astype(jnp.float32)
    return high, x - high


def spread_terms(cells_ref, mask_ref, values_ref, error_ref, rows_ref, rows, width):
    half = width // 2
    cells = cells_ref[...]
    used = mask_ref[...].astype(jnp.float32)
    values = values_ref[...]
    error = error_ref[...]
    inverse = used / (error * error)
    first = inverse * values
    second = first * values + used * (2.0 * jnp.log(error) + LOG_TWO_PI)
    row = cells // width
    column = cells % width
    high = (column // half * rows + row).astype(jnp.float32)
    low = (column % half).astype(jnp.float32)
    for k, x in enumerate(split_two(inverse) + split_two(first) + (second, high, low)):
        rows_ref[k] = x


def add_observations(step, size, rows_ref, acc_ref):
    highs, lows = acc_ref.shape[0] // PARTS, acc_ref.shape[1]

    def steps_of(count):
        base = lax.broadcasted_iota(jnp.int32, (PACK, LANES), 0)
        return [
            (base + PACK * i).astype(jnp.float32).astype(jnp.bfloat16) for i in range(count // PACK)
        ]

    high_iota, low_iota = steps_of(highs), steps_of(lows)
    zero = jnp.zeros((PACK, LANES), jnp.bfloat16)
    one = jnp.ones((PACK, LANES), jnp.bfloat16)
    here = pl.ds(pl.multiple_of(step * size, size), size)
    held = [rows_ref[k, here, :] for k in range(PARTS + 2)]
    left, right = [], []
    for r in range(size):
        spread = [
            jnp.broadcast_to(x[r : r + 1, :], (PACK, LANES)).astype(jnp.bfloat16) for x in held
        ]
        high_row, low_row = spread[PARTS:]
        hit = [iota == high_row for iota in high_iota]
        left.append(
            jnp.concatenate([jnp.where(h, part, zero) for part in spread[:PARTS] for h in hit], axis=0)
        )
        right.append(
            jnp.concatenate([jnp.where(iota == low_row, one, zero) for iota in low_iota], axis=0)
        )
    acc_ref[...] += lax.dot_general(
        jnp.concatenate(left, axis=1),
        jnp.concatenate(right, axis=1),
        (((1,), (1,)), ((), ())),
        preferred_element_type=jnp.float32,
    )


def grids_of(acc_ref, rows):
    highs = 2 * rows

    def part_sum(indices):
        total = acc_ref[pl.ds(indices[-1] * highs, highs), :]
        for i in indices[-2::-1]:
            total = total + acc_ref[pl.ds(i * highs, highs), :]
        return jnp.concatenate([total[0:rows], total[rows:highs]], axis=1)

    return [part_sum(indices) for indices in ((0, 1), (2, 3), (4,))]


def begin_kernel(rows, width, steps, cells_ref, mask_ref, values_ref, error_ref, rows_ref, acc_ref):
    spread_terms(cells_ref, mask_ref, values_ref, error_ref, rows_ref, rows, width)
    acc_ref[...] = jnp.zeros_like(acc_ref)

    def body(step, carry):
        add_observations(step, BEGIN_CHUNK, rows_ref, acc_ref)
        return carry

    lax.fori_loop(0, steps, body, 0)


def wind_parts(east_ref, north_ref, wind_halo_ref):
    east = jnp.concatenate([east_ref[...], wind_halo_ref[0]], axis=0)
    north = jnp.concatenate([north_ref[...], wind_halo_ref[1]], axis=0)
    west, south = jnp.maximum(east, 0.0), jnp.maximum(north, 0.0)
    east, north = -jnp.minimum(east, 0.0), -jnp.minimum(north, 0.0)
    return 1.0 - west - east - south - north, west, east, south, north


def advect(x, winds, as_written):
    count, width = x.shape
    centre, west, east, south, north = winds
    for _ in range(STEPS):
        west_cell, east_cell = pltpu.roll(x, 1, 1), pltpu.roll(x, width - 1, 1)
        south_row, north_row = pltpu.roll(x, 1, 0), pltpu.roll(x, count - 1, 0)
        if as_written:
            x = (
                x
                - west * (x - west_cell)
                + east * (east_cell - x)
                - south * (x - south_row)
                + north * (north_row - x)
            )
        else:
            x = (
                centre * x
                + west * west_cell
                + east * east_cell
                + south * south_row
                + north * north_row
            )
    return x


def edge_kernel(state_in, east_in, north_in, out_ref, state_ref, wind_ref, sems):
    slots, fields, rows, width = state_in.shape
    place = lax.axis_index("lat")
    lower = place == 0
    here = pl.ds(pl.multiple_of((1 - place) * (rows - 2 * TILE), 2 * TILE), 2 * TILE)
    copies = [
        pltpu.make_async_copy(state_in.at[:, :, here], state_ref, sems.at[0]),
        pltpu.make_async_copy(east_in.at[here], wind_ref.at[0], sems.at[1]),
        pltpu.make_async_copy(north_in.at[here], wind_ref.at[1], sems.at[2]),
    ]
    for copy in copies:
        copy.start()
    low_row = lax.broadcasted_iota(jnp.int32, (TILE, width), 0) < TILE // 2
    keep = low_row != lower

    def edge(block):
        return jnp.where(keep, jnp.where(lower, block[TILE:], block[0:TILE]), 0.0)

    for copy in copies:
        copy.wait()
    for s in range(slots):
        for f in range(fields):
            out_ref[s * fields + f] = edge(state_ref[s, f].astype(jnp.float32))
    for i in range(2):
        out_ref[slots * fields + i] = edge(wind_ref[i])


def store_winds(east_ref, north_ref, halo_ref, count, winds_ref):
    for i, part in enumerate(wind_parts(east_ref, north_ref, halo_ref.at[pl.ds(count, 2)])):
        winds_ref[i] = part


def advect_pair(state_ref, halo_ref, winds_ref, i, f, adv_ref, place, as_written=False):
    slots, fields, rows = state_ref.shape[:3]
    winds = [winds_ref[k] for k in range(5)]
    for k in range(2):
        s = 2 * (i % (slots // 2)) + k
        x = jnp.concatenate(
            [state_ref[s, f].astype(jnp.float32), halo_ref[s * fields + f]], axis=0
        )
        adv_ref[s, place] = advect(x, winds, as_written)[0:rows].astype(jnp.bfloat16)


def first_kernel(
    steps, state_ref, halo_ref, east_ref, north_ref, terms_ref, acc_in_ref, lat_ref, lon_ref,
    adv_ref, own_ref, send_ref, acc_ref, winds_ref,
):
    slots, fields, rows, width = state_ref.shape
    store_winds(east_ref, north_ref, halo_ref, slots * fields, winds_ref)
    acc_ref[...] = acc_in_ref[...]
    pairs, held = slots // 2, adv_ref.shape[1]
    total = terms_ref.shape[1] // CHUNK_ROWS

    def advect_next(i, as_written):
        f = i // pairs
        advect_pair(state_ref, halo_ref, winds_ref, i, f, adv_ref, f, as_written)

    def both(as_written):
        def body(i, carry):
            add_observations(steps + i, CHUNK_ROWS, terms_ref, acc_ref)
            advect_next(i, as_written)
            return carry

        return body

    def observe(step, carry):
        add_observations(step, CHUNK_ROWS, terms_ref, acc_ref)
        return carry

    shared = min(pairs * held, total - steps)
    lax.fori_loop(0, min(pairs, shared), both(True), 0)
    if pairs < shared:
        lax.fori_loop(pairs, shared, both(False), 0)
    if steps + shared < total:
        lax.fori_loop(steps + shared, total, observe, 0)
    for i in range(shared, pairs * held):
        advect_next(i, i < pairs)

    inverse, first, second = grids_of(acc_ref, rows)
    logliks = []
    for s in range(slots):
        value = adv_ref[s, 0].astype(jnp.float32)
        logliks.append(-0.5 * (inverse * value * value - 2.0 * first * value + second))
    smooth = functools.partial(
        jnp.dot, precision=lax.Precision.HIGHEST, preferred_element_type=jnp.float32
    )
    edge = rows + jnp.where(lax.axis_index("lat") == 0, 0, SMOOTH)
    lat_rows = jnp.concatenate(
        [lat_ref[0:rows], lat_ref[pl.ds(pl.multiple_of(edge, SMOOTH), SMOOTH)]], axis=0
    )
    along = smooth(jnp.concatenate(logliks, axis=0), lon_ref[...])
    for s in range(slots):
        scores = smooth(lat_rows, along[s * rows : (s + 1) * rows])
        own_ref[s] = scores[0:rows]
        send_ref[s] = scores[rows:]


def rest_kernel(state_ref, halo_ref, east_ref, north_ref, adv_ref, winds_ref):
    slots, fields = state_ref.shape[:2]
    held = adv_ref.shape[1]
    store_winds(east_ref, north_ref, halo_ref, slots * fields, winds_ref)

    pairs = slots // 2

    def body(i, carry):
        f = i // pairs
        advect_pair(state_ref, halo_ref, winds_ref, i, fields - held + f, adv_ref, f)
        return carry

    lax.fori_loop(0, pairs * held, body, 0)


def field_ref(adv_first_ref, adv_rest_ref, s, f):
    held = adv_first_ref.shape[1]
    return adv_first_ref.at[s, f] if f < held else adv_rest_ref.at[s, f - held]


def weigh_all_kernel(
    counts_ref, own_ref, recv_ref, adv_first_ref, adv_rest_ref, parts_ref
):
    slots, rows, width = own_ref.shape
    fields = adv_first_ref.shape[1] + adv_rest_ref.shape[1]
    across = width // LANES
    members, _, held, _ = parts_ref.shape

    def store(row_tile, index, value):
        for l in range(across):
            tile = value[:, l * LANES : (l + 1) * LANES]
            row = (row_tile * across + l) * TILE
            for k in range(0, TILE, min(held, TILE)):
                chunk, at = divmod(row + k, held)
                parts_ref[chunk, index, at : at + min(held, TILE)] = tile[k : k + min(held, TILE)]

    lower = lax.axis_index("lat") == 0
    for t in range(rows // TILE):
        here = slice(t * TILE, (t + 1) * TILE)
        near = (t * TILE) % SMOOTH
        scores = []
        for s in range(slots):
            recv = recv_ref[s, near : near + TILE, :]
            at_this_edge = lower if t * TILE >= rows - SMOOTH else jnp.logical_not(lower)
            score = own_ref[s, here, :] + jnp.where(at_this_edge, recv, 0.0)
            scores.append(jnp.where(s < counts_ref[0:1, 0:1], score, -jnp.inf))
        peak = functools.reduce(jnp.maximum, scores)
        gains = [jnp.exp(score - peak) for score in scores]
        total = functools.reduce(jnp.add, gains)
        store(t, 0, peak + jnp.log(total))
        gains = [gain / total for gain in gains]
        for f in range(fields):
            mean = None
            for s in range(slots):
                ref = field_ref(adv_first_ref, adv_rest_ref, s, f)
                pair = slice(t // 2 * 2 * TILE, (t // 2 + 1) * 2 * TILE)
                value = ref[pair, :].astype(jnp.float32)[t % 2 * TILE : (t % 2 + 1) * TILE]
                term = gains[s] * value
                mean = term if mean is None else mean + term
            store(t, 1 + f, mean)


def weigh_kernel(
    counts_ref, own_ref, recv_ref, adv_first_ref, adv_rest_ref, *out_refs
):
    slots, rows, width = own_ref.shape
    fields = adv_first_ref.shape[1] + adv_rest_ref.shape[1]
    half = width // PAIR
    lower = lax.axis_index("lat") == 0
    member = lax.axis_index("mem")
    even_side = member % PAIR == 0
    for distance in range(LINE):
        tile = (member // PAIR) ^ distance
        here = pl.ds(pl.multiple_of(tile * TILE, TILE), TILE)
        near = pl.ds(pl.multiple_of(tile % 2 * TILE, TILE), TILE)
        pair = pl.ds(pl.multiple_of(tile // 2 * (2 * TILE), 2 * TILE), 2 * TILE)
        even_tile = tile % 2 == 0
        at_edge = lower == (tile * TILE >= rows - SMOOTH)
        keep_ref, send_ref = out_refs[distance], out_refs[LINE + distance]

        def store(index, value):
            left, right = value[:, 0:half], value[:, half:width]
            keep_ref[index] = jnp.where(even_side, left, right)
            send_ref[index] = jnp.where(even_side, right, left)

        scores = []
        for s in range(slots):
            score = own_ref[s, here, :] + jnp.where(at_edge, recv_ref[s, near, :], 0.0)
            scores.append(jnp.where(s < counts_ref[0:1, 0:1], score, -jnp.inf))
        peak = functools.reduce(jnp.maximum, scores)
        gains = [jnp.exp(score - peak) for score in scores]
        total = functools.reduce(jnp.add, gains)
        store(0, peak + jnp.log(total))
        gains = [gain / total for gain in gains]
        for f in range(fields):
            mean = None
            for s in range(slots):
                ref = field_ref(adv_first_ref, adv_rest_ref, s, f)
                value = ref[pair, :].astype(jnp.float32)
                term = gains[s] * jnp.where(even_tile, value[0:TILE], value[TILE:])
                mean = term if mean is None else mean + term
            store(1 + f, mean)


def merge_values(refs):
    peak = functools.reduce(jnp.maximum, [ref[0] for ref in refs])
    weights = [jnp.exp(ref[0] - peak) for ref in refs]
    total = functools.reduce(jnp.add, weights)
    shares = [weight / total for weight in weights]
    means = [
        functools.reduce(jnp.add, [share * ref[q] for share, ref in zip(shares, refs)])
        for q in range(1, refs[0].shape[0])
    ]
    return peak + jnp.log(total), means


def merge_kernel(*refs):
    out_ref = refs[-1]
    log_weight, means = merge_values(refs[:-1])
    out_ref[0] = log_weight
    for f, mean in enumerate(means):
        out_ref[1 + f] = mean


def finish_kernel(*refs):
    merged_ref = refs[-1]
    parts = refs[:-1]
    if len(parts) == 1:
        parts = [parts[0].at[d] for d in range(parts[0].shape[0])]
    for f, mean in enumerate(merge_values(parts)[1]):
        merged_ref[f] = mean


def relaxed(value, merged, factor, live):
    value = value.astype(jnp.float32)
    return jnp.where(live, value + factor * (merged - value), 0.0).astype(jnp.bfloat16)


def relax_all_kernel(
    counts_ref, relax_ref, adv_first_ref, adv_rest_ref, whole_ref, new_ref, mean_ref
):
    _, fields, rows, width = new_ref.shape
    across = width // LANES
    held = whole_ref.shape[2]

    def tile(f, row):
        if held >= TILE:
            return whole_ref[row // held, f, row % held : row % held + TILE]
        return jnp.concatenate([whole_ref[(row + k) // held, f] for k in range(0, TILE, held)], axis=0)

    for f in range(fields):
        merged = jnp.concatenate(
            [
                jnp.concatenate([tile(f, (t * across + l) * TILE) for l in range(across)], axis=1)
                for t in range(rows // TILE)
            ],
            axis=0,
        )
        mean_ref[f] = merged.astype(jnp.bfloat16)
        for s in range(new_ref.shape[0]):
            value = field_ref(adv_first_ref, adv_rest_ref, s, f)[...]
            new_ref[s, f] = relaxed(value, merged, relax_ref[f], s < counts_ref[0:1, 0:1])


def relax_kernel(counts_ref, relax_ref, adv_first_ref, adv_rest_ref, *refs):
    share_refs, (new_out, mean_out, merged_ref, new_ref, mean_ref, sems) = refs[:-6], refs[-6:]
    slots, fields, rows, width = new_ref.shape
    share_of = dict(zip(SHARE_ORDER, share_refs))
    member = lax.axis_index("mem")
    even_side = member % PAIR == 0
    copies = []
    for f in range(fields):
        for distance in range(LINE):
            tile = (member // PAIR) ^ distance
            same = share_of[PAIR * distance][f]
            other = share_of[PAIR * distance + 1][f]
            left = jnp.where(even_side, same, other)
            right = jnp.where(even_side, other, same)
            merged_ref[f, pl.ds(pl.multiple_of(tile * TILE, TILE), TILE), :] = jnp.concatenate(
                [left, right], axis=1
            )
        merged = merged_ref[f]
        mean_ref[f] = merged.astype(jnp.bfloat16)
        for s in range(slots):
            value = field_ref(adv_first_ref, adv_rest_ref, s, f)[...]
            new_ref[s, f] = relaxed(value, merged, relax_ref[f], s < counts_ref[0:1, 0:1])
        copies.append(pltpu.make_async_copy(new_ref.at[:, f], new_out.at[:, f], sems.at[0, f]))
        copies.append(pltpu.make_async_copy(mean_ref.at[f], mean_out.at[f], sems.at[1, f]))
        for copy in copies[-2:]:
            copy.start()
    for copy in copies:
        copy.wait()


def call(kernel, ins, outs, scratch=(), **cost):
    return pl.pallas_call(
        kernel,
        out_shape=[jax.ShapeDtypeStruct(shape, dtype) for shape, dtype in outs],
        in_specs=ins,
        out_specs=[VMEM] * len(outs),
        scratch_shapes=list(scratch),
        compiler_params=PARAMS,
        cost_estimate=pl.CostEstimate(**cost),
    )


def on_device(
    state, counts, east_wind, north_wind, obs_cells, obs_mask, obs_values, obs_error, relax
):
    slots, fields, rows, width = state.shape
    f32, bf16 = jnp.float32, jnp.bfloat16
    swap = [(0, 1), (1, 0)]
    (message,) = pl.pallas_call(
        edge_kernel,
        out_shape=[jax.ShapeDtypeStruct((slots * fields + 2, TILE, width), f32)],
        in_specs=[pl.BlockSpec(memory_space=pltpu.HBM)] * 3,
        out_specs=[VMEM],
        scratch_shapes=[
            pltpu.VMEM((slots, fields, 2 * TILE, width), bf16),
            pltpu.VMEM((2, 2 * TILE, width), f32),
            pltpu.SemaphoreType.DMA((3,)),
        ],
        compiler_params=pltpu.CompilerParams(vmem_limit_bytes=EDGE_VMEM),
        cost_estimate=pl.CostEstimate(
            flops=0, bytes_accessed=6 * slots * fields * TILE * width, transcendentals=0
        ),
    )(state, east_wind, north_wind)
    halo = lax.ppermute(message, "lat", swap)

    observations = obs_cells.shape[1]
    flat = [
        x.reshape(observations // LANES, LANES) for x in (obs_cells, obs_mask, obs_values, obs_error)
    ]
    acc_shape = (PARTS * 2 * rows, width // 2)
    all_steps = observations // (LANES * CHUNK_ROWS)
    begin_steps = min(BEGIN_STEPS * BEGIN_CHUNK // CHUNK_ROWS, all_steps)
    observe_flops = 2 * PARTS * rows * width * LANES * CHUNK_ROWS
    terms, begun = call(
        functools.partial(begin_kernel, rows, width, begin_steps * CHUNK_ROWS // BEGIN_CHUNK),
        [VMEM] * 4,
        [((PARTS + 2, observations // LANES, LANES), f32), (acc_shape, f32)],
        flops=observe_flops * begin_steps,
        bytes_accessed=16 * observations,
        transcendentals=observations,
    )(*flat)

    index = np.arange(rows)
    own = index[None, :] - index[:, None]
    upper_side = index[None, :] - (index[:SMOOTH, None] + rows)
    lower_side = index[None, :] - (index[rows - SMOOTH :, None] - rows)
    lat_kernel = jnp.asarray(
        kernel_matrix(np.concatenate([own, upper_side, lower_side])), dtype=f32
    )
    distance = np.abs(np.arange(width)[:, None] - np.arange(width)[None, :])
    lon_kernel = jnp.asarray(kernel_matrix(np.minimum(distance, width - distance)))

    winds_scratch = pltpu.VMEM((5, rows + TILE, width), f32)
    advect_flops = STEPS * 16 * slots * rows * width
    adv_first, own_scores, edge_scores = call(
        functools.partial(first_kernel, begin_steps),
        [VMEM] * 8,
        [
            ((slots, fields - LATER_FIELDS, rows, width), bf16),
            ((slots, rows, width), f32),
            ((slots, SMOOTH, width), f32),
        ],
        [pltpu.VMEM(acc_shape, f32), winds_scratch],
        flops=observe_flops * (all_steps - begin_steps) + advect_flops * (fields - LATER_FIELDS),
        bytes_accessed=4 * width * width,
        transcendentals=0,
    )(state, halo, east_wind, north_wind, terms, begun, lat_kernel, lon_kernel)
    received = lax.ppermute(edge_scores, "lat", swap)

    (adv_rest,) = call(
        rest_kernel,
        [VMEM] * 4,
        [((slots, LATER_FIELDS, rows, width), bf16)],
        [winds_scratch],
        flops=advect_flops * LATER_FIELDS,
        bytes_accessed=4 * slots * fields * rows * width,
        transcendentals=0,
    )(state, halo, east_wind, north_wind)

    members = lax.axis_size("mem")
    counts = jnp.broadcast_to(jnp.clip(counts, 1, slots)[0], (TILE, LANES))
    factors = jnp.broadcast_to(relax[:, None, None], (fields, 1, width))
    quantities = fields + 1
    direct = (members, rows, width % (PAIR * LANES)) == (PAIR * LINE, LINE * TILE, 0)
    chunk = (TILE, width // PAIR) if direct else (rows * width // LANES // members, LANES)
    cells = chunk[0] * chunk[1]

    def weigh(kernel, outs):
        return call(
            kernel,
            [VMEM] * 5,
            outs,
            flops=4 * slots * fields * rows * width,
            bytes_accessed=4 * slots * fields * rows * width,
            transcendentals=slots * rows * width,
        )(counts, own_scores, received, adv_first, adv_rest)

    def merge(kernel, pieces, out):
        size = quantities * cells * (len(pieces) if direct else members)
        return call(
            kernel,
            [VMEM] * len(pieces),
            [out],
            flops=4 * size,
            bytes_accessed=4 * size,
            transcendentals=size // quantities,
        )(*pieces)[0]

    def swapped(x, offset):
        return lax.ppermute(x, "mem", [(m, m ^ offset) for m in range(members)])

    merged_chunk = ((fields,) + chunk, f32)
    new_shape, mean_shape = (slots, fields, rows, width), (fields, rows, width)
    outs = [(new_shape, bf16), (mean_shape, bf16)]
    if direct:
        piece = ((quantities,) + chunk, f32)
        parts = weigh(weigh_kernel, [piece] * (PAIR * LINE))
        paired = [None] * LINE
        for j in reversed(range(LINE)):
            paired[j] = merge(merge_kernel, [parts[j], swapped(parts[LINE + j], 1)], piece)
        pieces = [paired[0]] + [swapped(paired[j], PAIR * j) for j in range(1, LINE)]
        merged = merge(finish_kernel, pieces, merged_chunk)
        far = LINE - 1
        sent = {0: merged}
        for offset in SHARE_ORDER[1:]:
            through = offset ^ 1 if offset % PAIR and offset // PAIR < far else 0
            sent[offset] = swapped(sent[through], offset ^ through)
        size = slots * fields * rows * width
        new_state, mean = pl.pallas_call(
            relax_kernel,
            out_shape=[jax.ShapeDtypeStruct(*out) for out in outs],
            in_specs=[VMEM] * (4 + len(sent)),
            out_specs=[pl.BlockSpec(memory_space=pl.ANY)] * 2,
            scratch_shapes=[
                pltpu.VMEM((fields, rows, width), f32),
                pltpu.VMEM(new_shape, bf16),
                pltpu.VMEM(mean_shape, bf16),
                pltpu.SemaphoreType.DMA((2, fields)),
            ],
            compiler_params=PARAMS,
            cost_estimate=pl.CostEstimate(flops=4 * size, bytes_accessed=4 * size, transcendentals=0),
        )(counts, factors, adv_first, adv_rest, *[sent[i] for i in SHARE_ORDER])
    else:
        (parts,) = weigh(weigh_all_kernel, [((members, quantities) + chunk, f32)])
        got = lax.all_to_all(parts, "mem", 0, 0, tiled=True)
        whole = lax.all_gather(merge(finish_kernel, [got], merged_chunk), "mem")
        new_state, mean = call(
            relax_all_kernel,
            [VMEM] * 5,
            outs,
            flops=4 * slots * fields * rows * width,
            bytes_accessed=4 * slots * fields * rows * width,
            transcendentals=0,
        )(counts, factors, adv_first, adv_rest, whole)
    return (new_state, mean)


def solution(mesh):
    return jax.shard_map(
        on_device,
        mesh=mesh,
        in_specs=(
            P(("groups", "mem"), None, "lat", None),
            P(("groups", "mem")),
            P(("groups", "lat"), None),
            P(("groups", "lat"), None),
            P(("groups", "lat"), None),
            P(("groups", "lat"), None),
            P(("groups", "lat"), None),
            P(("groups", "lat"), None),
            P(),
        ),
        out_specs=(P(("groups", "mem"), None, "lat", None), P("groups", "lat", None)),
        check_vma=False,
    )
```

```python
import functools

import jax
import jax.numpy as jnp
import numpy as np
from jax import lax
from jax.experimental import pallas as pl
from jax.experimental.pallas import tpu as pltpu
from jax.sharding import PartitionSpec as P

STEPS = 4
SMOOTH = 16
LOG_TWO_PI = 1.8378770664093453
LANES = 128
TILE = 8
PARTS = 5
CHUNK_ROWS = 16
PACK = 16
BEGIN_CHUNK = 32
BEGIN_STEPS = 2
LATER_FIELDS = 1
PAIR = 2
LINE = 4
SHARE_ORDER = (0, 6, 7, 4, 1, 2, 3, 5)


VMEM = pl.BlockSpec(memory_space=pltpu.VMEM)
PARAMS = pltpu.CompilerParams(vmem_limit_bytes=24 * 1024 * 1024)
EDGE_VMEM = 63 * 1024 * 1024


def kernel_matrix(offset):
    values = np.exp(-((2.0 * offset.astype(np.float32) / SMOOTH) ** 2))
    return np.where(np.abs(offset) <= SMOOTH, values, 0.0).astype(np.float32)


def split_two(x):
    high = x.astype(jnp.bfloat16).astype(jnp.float32)
    return high, x - high


def spread_terms(cells_ref, mask_ref, values_ref, error_ref, rows_ref, rows, width):
    half = width // 2
    cells = cells_ref[...]
    used = mask_ref[...].astype(jnp.float32)
    values = values_ref[...]
    error = error_ref[...]
    inverse = used / (error * error)
    first = inverse * values
    second = first * values + used * (2.0 * jnp.log(error) + LOG_TWO_PI)
    row = cells // width
    column = cells % width
    high = (column // half * rows + row).astype(jnp.float32)
    low = (column % half).astype(jnp.float32)
    for k, x in enumerate(split_two(inverse) + split_two(first) + (second, high, low)):
        rows_ref[k] = x


def add_observations(step, size, rows_ref, acc_ref):
    highs, lows = acc_ref.shape[0] // PARTS, acc_ref.shape[1]

    def steps_of(count):
        base = lax.broadcasted_iota(jnp.int32, (PACK, LANES), 0)
        return [
            (base + PACK * i).astype(jnp.float32).astype(jnp.bfloat16) for i in range(count // PACK)
        ]

    high_iota, low_iota = steps_of(highs), steps_of(lows)
    zero = jnp.zeros((PACK, LANES), jnp.bfloat16)
    one = jnp.ones((PACK, LANES), jnp.bfloat16)
    here = pl.ds(pl.multiple_of(step * size, size), size)
    held = [rows_ref[k, here, :] for k in range(PARTS + 2)]
    left, right = [], []
    for r in range(size):
        spread = [
            jnp.broadcast_to(x[r : r + 1, :], (PACK, LANES)).astype(jnp.bfloat16) for x in held
        ]
        high_row, low_row = spread[PARTS:]
        hit = [iota == high_row for iota in high_iota]
        left.append(
            jnp.concatenate([jnp.where(h, part, zero) for part in spread[:PARTS] for h in hit], axis=0)
        )
        right.append(
            jnp.concatenate([jnp.where(iota == low_row, one, zero) for iota in low_iota], axis=0)
        )
    acc_ref[...] += lax.dot_general(
        jnp.concatenate(left, axis=1),
        jnp.concatenate(right, axis=1),
        (((1,), (1,)), ((), ())),
        preferred_element_type=jnp.float32,
    )


def grids_of(acc_ref, rows):
    highs = 2 * rows

    def part_sum(indices):
        total = acc_ref[pl.ds(indices[-1] * highs, highs), :]
        for i in indices[-2::-1]:
            total = total + acc_ref[pl.ds(i * highs, highs), :]
        return jnp.concatenate([total[0:rows], total[rows:highs]], axis=1)

    return [part_sum(indices) for indices in ((0, 1), (2, 3), (4,))]


def begin_kernel(rows, width, steps, cells_ref, mask_ref, values_ref, error_ref, rows_ref, acc_ref):
    spread_terms(cells_ref, mask_ref, values_ref, error_ref, rows_ref, rows, width)
    acc_ref[...] = jnp.zeros_like(acc_ref)

    def body(step, carry):
        add_observations(step, BEGIN_CHUNK, rows_ref, acc_ref)
        return carry

    lax.fori_loop(0, steps, body, 0)


def wind_parts(east_ref, north_ref, wind_halo_ref):
    east = jnp.concatenate([east_ref[...], wind_halo_ref[0]], axis=0)
    north = jnp.concatenate([north_ref[...], wind_halo_ref[1]], axis=0)
    west, south = jnp.maximum(east, 0.0), jnp.maximum(north, 0.0)
    east, north = -jnp.minimum(east, 0.0), -jnp.minimum(north, 0.0)
    return 1.0 - west - east - south - north, west, east, south, north


def edge_kernel(state_in, east_in, north_in, out_ref, state_ref, wind_ref, sems):
    slots, fields, rows, width = state_in.shape
    place = lax.axis_index("lat")
    lower = place == 0
    here = pl.ds(pl.multiple_of((1 - place) * (rows - 2 * TILE), 2 * TILE), 2 * TILE)
    copies = [
        pltpu.make_async_copy(state_in.at[:, :, here], state_ref, sems.at[0]),
        pltpu.make_async_copy(east_in.at[here], wind_ref.at[0], sems.at[1]),
        pltpu.make_async_copy(north_in.at[here], wind_ref.at[1], sems.at[2]),
    ]
    for copy in copies:
        copy.start()
    low_row = lax.broadcasted_iota(jnp.int32, (TILE, width), 0) < TILE // 2
    keep = low_row != lower

    def edge(block):
        return jnp.where(keep, jnp.where(lower, block[TILE:], block[0:TILE]), 0.0)

    for copy in copies:
        copy.wait()
    for s in range(slots):
        for f in range(fields):
            out_ref[s * fields + f] = edge(state_ref[s, f].astype(jnp.float32))
    for i in range(2):
        out_ref[slots * fields + i] = edge(wind_ref[i])


def store_winds(east_ref, north_ref, halo_ref, count, winds_ref):
    for i, part in enumerate(wind_parts(east_ref, north_ref, halo_ref.at[pl.ds(count, 2)])):
        winds_ref[i] = part


def advect_pair(
    state_ref, halo_ref, winds_ref, buffer_ref, i, f, adv_ref, place, as_written=False
):
    slots, fields, rows, width = state_ref.shape
    across, band_tiles = width // LANES, rows // TILE
    tiles = band_tiles + 1
    members = [2 * (i % (slots // 2)) + k for k in range(2)]
    lane = lax.broadcasted_iota(jnp.int32, (TILE, LANES), 1)
    first, last = lane == 0, lane == LANES - 1

    def columns(l):
        return slice(l * LANES, (l + 1) * LANES)

    def put(side, k, l, v, value):
        copies = [v + 1] + ([0] if v == tiles - 1 else []) + ([tiles + 1] if v == 0 else [])
        for at in copies:
            buffer_ref[side, k, l, at * TILE : (at + 1) * TILE, :] = value

    for k, s in enumerate(members):
        x = state_ref[s, f].astype(jnp.float32)
        halo = halo_ref[s * fields + f]
        for l in range(across):
            for v in range(band_tiles):
                put(0, k, l, v, x[v * TILE : (v + 1) * TILE, columns(l)])
            put(0, k, l, band_tiles, halo[:, columns(l)])

    done = [[], []]
    for step in range(STEPS):
        side = step % 2
        ends = step == STEPS - 1
        for v in range(band_tiles if ends else tiles):
            cells = []
            for k in range(2):

                def row_tile(offset):
                    start = (v + 1) * TILE + offset
                    return [buffer_ref[side, k, l, start : start + TILE, :] for l in range(across)]

                x = row_tile(0)
                west = [pltpu.roll(value, 1, 1) for value in x]
                east = [pltpu.roll(value, LANES - 1, 1) for value in x]
                cells.append(
                    (
                        x,
                        [jnp.where(first, west[l - 1], west[l]) for l in range(across)],
                        [jnp.where(last, east[(l + 1) % across], east[l]) for l in range(across)],
                        row_tile(-1),
                        row_tile(1),
                    )
                )
            stepped = [[], []]
            for l in range(across):
                here = slice(v * TILE, (v + 1) * TILE)
                centre, *winds = [winds_ref[c, here, columns(l)] for c in range(5)]
                for k in range(2):
                    x, west, east, south, north = [values[l] for values in cells[k]]
                    if as_written:
                        x = (
                            x
                            - winds[0] * (x - west)
                            + winds[1] * (east - x)
                            - winds[2] * (x - south)
                            + winds[3] * (north - x)
                        )
                    else:
                        x = (
                            centre * x
                            + winds[0] * west
                            + winds[1] * east
                            + winds[2] * south
                            + winds[3] * north
                        )
                    if ends:
                        stepped[k].append(x)
                    else:
                        put(1 - side, k, l, v, x)
            if ends:
                for k in range(2):
                    done[k].append(jnp.concatenate(stepped[k], axis=1))
    for k, s in enumerate(members):
        for v in range(0, band_tiles, 2):
            block = jnp.concatenate(done[k][v : v + 2], axis=0)
            adv_ref[s, place, v * TILE : (v + 2) * TILE, :] = block.astype(jnp.bfloat16)


def first_kernel(
    steps, state_ref, halo_ref, east_ref, north_ref, terms_ref, acc_in_ref, lat_ref, lon_ref,
    adv_ref, own_ref, send_ref, acc_ref, winds_ref, buffer_ref,
):
    slots, fields, rows, width = state_ref.shape
    store_winds(east_ref, north_ref, halo_ref, slots * fields, winds_ref)
    acc_ref[...] = acc_in_ref[...]
    pairs, held = slots // 2, adv_ref.shape[1]
    total = terms_ref.shape[1] // CHUNK_ROWS

    def advect_next(i, as_written):
        f = i // pairs
        advect_pair(state_ref, halo_ref, winds_ref, buffer_ref, i, f, adv_ref, f, as_written)

    def both(as_written):
        def body(i, carry):
            add_observations(steps + i, CHUNK_ROWS, terms_ref, acc_ref)
            advect_next(i, as_written)
            return carry

        return body

    def observe(step, carry):
        add_observations(step, CHUNK_ROWS, terms_ref, acc_ref)
        return carry

    shared = min(pairs * held, total - steps)
    lax.fori_loop(0, min(pairs, shared), both(True), 0)
    if pairs < shared:
        lax.fori_loop(pairs, shared, both(False), 0)
    if steps + shared < total:
        lax.fori_loop(steps + shared, total, observe, 0)
    for i in range(shared, pairs * held):
        advect_next(i, i < pairs)

    inverse, first, second = grids_of(acc_ref, rows)
    logliks = []
    for s in range(slots):
        value = adv_ref[s, 0].astype(jnp.float32)
        logliks.append(-0.5 * (inverse * value * value - 2.0 * first * value + second))
    smooth = functools.partial(
        jnp.dot, precision=lax.Precision.HIGHEST, preferred_element_type=jnp.float32
    )
    edge = rows + jnp.where(lax.axis_index("lat") == 0, 0, SMOOTH)
    lat_rows = jnp.concatenate(
        [lat_ref[0:rows], lat_ref[pl.ds(pl.multiple_of(edge, SMOOTH), SMOOTH)]], axis=0
    )
    along = smooth(jnp.concatenate(logliks, axis=0), lon_ref[...])
    for s in range(slots):
        scores = smooth(lat_rows, along[s * rows : (s + 1) * rows])
        own_ref[s] = scores[0:rows]
        send_ref[s] = scores[rows:]


def rest_kernel(
    state_ref, halo_ref, east_ref, north_ref, adv_ref, winds_ref, buffer_ref
):
    slots, fields = state_ref.shape[:2]
    held = adv_ref.shape[1]
    store_winds(east_ref, north_ref, halo_ref, slots * fields, winds_ref)

    pairs = slots // 2

    def body(i, carry):
        f = i // pairs
        here = fields - held + f
        advect_pair(state_ref, halo_ref, winds_ref, buffer_ref, i, here, adv_ref, f)
        return carry

    lax.fori_loop(0, pairs * held, body, 0)


def field_ref(adv_first_ref, adv_rest_ref, s, f):
    held = adv_first_ref.shape[1]
    return adv_first_ref.at[s, f] if f < held else adv_rest_ref.at[s, f - held]


def weigh_all_kernel(
    counts_ref, own_ref, recv_ref, adv_first_ref, adv_rest_ref, parts_ref
):
    slots, rows, width = own_ref.shape
    fields = adv_first_ref.shape[1] + adv_rest_ref.shape[1]
    across = width // LANES
    members, _, held, _ = parts_ref.shape

    def store(row_tile, index, value):
        for l in range(across):
            tile = value[:, l * LANES : (l + 1) * LANES]
            row = (row_tile * across + l) * TILE
            for k in range(0, TILE, min(held, TILE)):
                chunk, at = divmod(row + k, held)
                parts_ref[chunk, index, at : at + min(held, TILE)] = tile[k : k + min(held, TILE)]

    lower = lax.axis_index("lat") == 0
    for t in range(rows // TILE):
        here = slice(t * TILE, (t + 1) * TILE)
        near = (t * TILE) % SMOOTH
        scores = []
        for s in range(slots):
            recv = recv_ref[s, near : near + TILE, :]
            at_this_edge = lower if t * TILE >= rows - SMOOTH else jnp.logical_not(lower)
            score = own_ref[s, here, :] + jnp.where(at_this_edge, recv, 0.0)
            scores.append(jnp.where(s < counts_ref[0:1, 0:1], score, -jnp.inf))
        peak = functools.reduce(jnp.maximum, scores)
        gains = [jnp.exp(score - peak) for score in scores]
        total = functools.reduce(jnp.add, gains)
        store(t, 0, peak + jnp.log(total))
        gains = [gain / total for gain in gains]
        for f in range(fields):
            mean = None
            for s in range(slots):
                ref = field_ref(adv_first_ref, adv_rest_ref, s, f)
                pair = slice(t // 2 * 2 * TILE, (t // 2 + 1) * 2 * TILE)
                value = ref[pair, :].astype(jnp.float32)[t % 2 * TILE : (t % 2 + 1) * TILE]
                term = gains[s] * value
                mean = term if mean is None else mean + term
            store(t, 1 + f, mean)


def weigh_kernel(
    counts_ref, own_ref, recv_ref, adv_first_ref, adv_rest_ref, *out_refs
):
    slots, rows, width = own_ref.shape
    fields = adv_first_ref.shape[1] + adv_rest_ref.shape[1]
    half = width // PAIR
    lower = lax.axis_index("lat") == 0
    member = lax.axis_index("mem")
    even_side = member % PAIR == 0
    for distance in range(LINE):
        tile = (member // PAIR) ^ distance
        here = pl.ds(pl.multiple_of(tile * TILE, TILE), TILE)
        near = pl.ds(pl.multiple_of(tile % 2 * TILE, TILE), TILE)
        pair = pl.ds(pl.multiple_of(tile // 2 * (2 * TILE), 2 * TILE), 2 * TILE)
        even_tile = tile % 2 == 0
        at_edge = lower == (tile * TILE >= rows - SMOOTH)
        keep_ref, send_ref = out_refs[distance], out_refs[LINE + distance]

        def store(index, value):
            left, right = value[:, 0:half], value[:, half:width]
            keep_ref[index] = jnp.where(even_side, left, right)
            send_ref[index] = jnp.where(even_side, right, left)

        scores = []
        for s in range(slots):
            score = own_ref[s, here, :] + jnp.where(at_edge, recv_ref[s, near, :], 0.0)
            scores.append(jnp.where(s < counts_ref[0:1, 0:1], score, -jnp.inf))
        peak = functools.reduce(jnp.maximum, scores)
        gains = [jnp.exp(score - peak) for score in scores]
        total = functools.reduce(jnp.add, gains)
        store(0, peak + jnp.log(total))
        gains = [gain / total for gain in gains]
        for f in range(fields):
            mean = None
            for s in range(slots):
                ref = field_ref(adv_first_ref, adv_rest_ref, s, f)
                value = ref[pair, :].astype(jnp.float32)
                term = gains[s] * jnp.where(even_tile, value[0:TILE], value[TILE:])
                mean = term if mean is None else mean + term
            store(1 + f, mean)


def merge_values(refs):
    peak = functools.reduce(jnp.maximum, [ref[0] for ref in refs])
    weights = [jnp.exp(ref[0] - peak) for ref in refs]
    total = functools.reduce(jnp.add, weights)
    shares = [weight / total for weight in weights]
    means = [
        functools.reduce(jnp.add, [share * ref[q] for share, ref in zip(shares, refs)])
        for q in range(1, refs[0].shape[0])
    ]
    return peak + jnp.log(total), means


def merge_kernel(*refs):
    out_ref = refs[-1]
    log_weight, means = merge_values(refs[:-1])
    out_ref[0] = log_weight
    for f, mean in enumerate(means):
        out_ref[1 + f] = mean


def finish_kernel(*refs):
    merged_ref = refs[-1]
    parts = refs[:-1]
    if len(parts) == 1:
        parts = [parts[0].at[d] for d in range(parts[0].shape[0])]
    for f, mean in enumerate(merge_values(parts)[1]):
        merged_ref[f] = mean


def relaxed(value, merged, factor, live):
    value = value.astype(jnp.float32)
    return jnp.where(live, value + factor * (merged - value), 0.0).astype(jnp.bfloat16)


def relax_all_kernel(
    counts_ref, relax_ref, adv_first_ref, adv_rest_ref, whole_ref, new_ref, mean_ref
):
    _, fields, rows, width = new_ref.shape
    across = width // LANES
    held = whole_ref.shape[2]

    def tile(f, row):
        if held >= TILE:
            return whole_ref[row // held, f, row % held : row % held + TILE]
        return jnp.concatenate([whole_ref[(row + k) // held, f] for k in range(0, TILE, held)], axis=0)

    for f in range(fields):
        merged = jnp.concatenate(
            [
                jnp.concatenate([tile(f, (t * across + l) * TILE) for l in range(across)], axis=1)
                for t in range(rows // TILE)
            ],
            axis=0,
        )
        mean_ref[f] = merged.astype(jnp.bfloat16)
        for s in range(new_ref.shape[0]):
            value = field_ref(adv_first_ref, adv_rest_ref, s, f)[...]
            new_ref[s, f] = relaxed(value, merged, relax_ref[f], s < counts_ref[0:1, 0:1])


def relax_kernel(counts_ref, relax_ref, adv_first_ref, adv_rest_ref, *refs):
    share_refs, (new_out, mean_out, merged_ref, new_ref, mean_ref, sems) = refs[:-6], refs[-6:]
    slots, fields, rows, width = new_ref.shape
    share_of = dict(zip(SHARE_ORDER, share_refs))
    member = lax.axis_index("mem")
    even_side = member % PAIR == 0
    copies = []
    for f in range(fields):
        for distance in range(LINE):
            tile = (member // PAIR) ^ distance
            same = share_of[PAIR * distance][f]
            other = share_of[PAIR * distance + 1][f]
            left = jnp.where(even_side, same, other)
            right = jnp.where(even_side, other, same)
            merged_ref[f, pl.ds(pl.multiple_of(tile * TILE, TILE), TILE), :] = jnp.concatenate(
                [left, right], axis=1
            )
        merged = merged_ref[f]
        mean_ref[f] = merged.astype(jnp.bfloat16)
        for s in range(slots):
            value = field_ref(adv_first_ref, adv_rest_ref, s, f)[...]
            new_ref[s, f] = relaxed(value, merged, relax_ref[f], s < counts_ref[0:1, 0:1])
        copies.append(pltpu.make_async_copy(new_ref.at[:, f], new_out.at[:, f], sems.at[0, f]))
        copies.append(pltpu.make_async_copy(mean_ref.at[f], mean_out.at[f], sems.at[1, f]))
        for copy in copies[-2:]:
            copy.start()
    for copy in copies:
        copy.wait()


def call(kernel, ins, outs, scratch=(), **cost):
    return pl.pallas_call(
        kernel,
        out_shape=[jax.ShapeDtypeStruct(shape, dtype) for shape, dtype in outs],
        in_specs=ins,
        out_specs=[VMEM] * len(outs),
        scratch_shapes=list(scratch),
        compiler_params=PARAMS,
        cost_estimate=pl.CostEstimate(**cost),
    )


def on_device(
    state, counts, east_wind, north_wind, obs_cells, obs_mask, obs_values, obs_error, relax
):
    slots, fields, rows, width = state.shape
    f32, bf16 = jnp.float32, jnp.bfloat16
    swap = [(0, 1), (1, 0)]
    (message,) = pl.pallas_call(
        edge_kernel,
        out_shape=[jax.ShapeDtypeStruct((slots * fields + 2, TILE, width), f32)],
        in_specs=[pl.BlockSpec(memory_space=pltpu.HBM)] * 3,
        out_specs=[VMEM],
        scratch_shapes=[
            pltpu.VMEM((slots, fields, 2 * TILE, width), bf16),
            pltpu.VMEM((2, 2 * TILE, width), f32),
            pltpu.SemaphoreType.DMA((3,)),
        ],
        compiler_params=pltpu.CompilerParams(vmem_limit_bytes=EDGE_VMEM),
        cost_estimate=pl.CostEstimate(
            flops=0, bytes_accessed=6 * slots * fields * TILE * width, transcendentals=0
        ),
    )(state, east_wind, north_wind)
    halo = lax.ppermute(message, "lat", swap)

    observations = obs_cells.shape[1]
    flat = [
        x.reshape(observations // LANES, LANES) for x in (obs_cells, obs_mask, obs_values, obs_error)
    ]
    acc_shape = (PARTS * 2 * rows, width // 2)
    all_steps = observations // (LANES * CHUNK_ROWS)
    begin_steps = min(BEGIN_STEPS * BEGIN_CHUNK // CHUNK_ROWS, all_steps)
    observe_flops = 2 * PARTS * rows * width * LANES * CHUNK_ROWS
    terms, begun = call(
        functools.partial(begin_kernel, rows, width, begin_steps * CHUNK_ROWS // BEGIN_CHUNK),
        [VMEM] * 4,
        [((PARTS + 2, observations // LANES, LANES), f32), (acc_shape, f32)],
        flops=observe_flops * begin_steps,
        bytes_accessed=16 * observations,
        transcendentals=observations,
    )(*flat)

    index = np.arange(rows)
    own = index[None, :] - index[:, None]
    upper_side = index[None, :] - (index[:SMOOTH, None] + rows)
    lower_side = index[None, :] - (index[rows - SMOOTH :, None] - rows)
    lat_kernel = jnp.asarray(
        kernel_matrix(np.concatenate([own, upper_side, lower_side])), dtype=f32
    )
    distance = np.abs(np.arange(width)[:, None] - np.arange(width)[None, :])
    lon_kernel = jnp.asarray(kernel_matrix(np.minimum(distance, width - distance)))

    advect_scratch = [
        pltpu.VMEM((5, rows + TILE, width), f32),
        pltpu.VMEM((2, 2, width // LANES, rows + 3 * TILE, LANES), f32),
    ]
    advect_flops = STEPS * 16 * slots * rows * width
    adv_first, own_scores, edge_scores = call(
        functools.partial(first_kernel, begin_steps),
        [VMEM] * 8,
        [
            ((slots, fields - LATER_FIELDS, rows, width), bf16),
            ((slots, rows, width), f32),
            ((slots, SMOOTH, width), f32),
        ],
        [pltpu.VMEM(acc_shape, f32)] + advect_scratch,
        flops=observe_flops * (all_steps - begin_steps) + advect_flops * (fields - LATER_FIELDS),
        bytes_accessed=4 * width * width,
        transcendentals=0,
    )(state, halo, east_wind, north_wind, terms, begun, lat_kernel, lon_kernel)
    received = lax.ppermute(edge_scores, "lat", swap)

    (adv_rest,) = call(
        rest_kernel,
        [VMEM] * 4,
        [((slots, LATER_FIELDS, rows, width), bf16)],
        advect_scratch,
        flops=advect_flops * LATER_FIELDS,
        bytes_accessed=4 * slots * fields * rows * width,
        transcendentals=0,
    )(state, halo, east_wind, north_wind)

    members = lax.axis_size("mem")
    counts = jnp.broadcast_to(jnp.clip(counts, 1, slots)[0], (TILE, LANES))
    factors = jnp.broadcast_to(relax[:, None, None], (fields, 1, width))
    quantities = fields + 1
    direct = (members, rows, width % (PAIR * LANES)) == (PAIR * LINE, LINE * TILE, 0)
    chunk = (TILE, width // PAIR) if direct else (rows * width // LANES // members, LANES)
    cells = chunk[0] * chunk[1]

    def weigh(kernel, outs):
        return call(
            kernel,
            [VMEM] * 5,
            outs,
            flops=4 * slots * fields * rows * width,
            bytes_accessed=4 * slots * fields * rows * width,
            transcendentals=slots * rows * width,
        )(counts, own_scores, received, adv_first, adv_rest)

    def merge(kernel, pieces, out):
        size = quantities * cells * (len(pieces) if direct else members)
        return call(
            kernel,
            [VMEM] * len(pieces),
            [out],
            flops=4 * size,
            bytes_accessed=4 * size,
            transcendentals=size // quantities,
        )(*pieces)[0]

    def swapped(x, offset):
        return lax.ppermute(x, "mem", [(m, m ^ offset) for m in range(members)])

    merged_chunk = ((fields,) + chunk, f32)
    new_shape, mean_shape = (slots, fields, rows, width), (fields, rows, width)
    outs = [(new_shape, bf16), (mean_shape, bf16)]
    if direct:
        piece = ((quantities,) + chunk, f32)
        parts = weigh(weigh_kernel, [piece] * (PAIR * LINE))
        paired = [None] * LINE
        for j in reversed(range(LINE)):
            paired[j] = merge(merge_kernel, [parts[j], swapped(parts[LINE + j], 1)], piece)
        pieces = [paired[0]] + [swapped(paired[j], PAIR * j) for j in range(1, LINE)]
        merged = merge(finish_kernel, pieces, merged_chunk)
        far = LINE - 1
        sent = {0: merged}
        for offset in SHARE_ORDER[1:]:
            through = offset ^ 1 if offset % PAIR and offset // PAIR < far else 0
            sent[offset] = swapped(sent[through], offset ^ through)
        size = slots * fields * rows * width
        new_state, mean = pl.pallas_call(
            relax_kernel,
            out_shape=[jax.ShapeDtypeStruct(*out) for out in outs],
            in_specs=[VMEM] * (4 + len(sent)),
            out_specs=[pl.BlockSpec(memory_space=pl.ANY)] * 2,
            scratch_shapes=[
                pltpu.VMEM((fields, rows, width), f32),
                pltpu.VMEM(new_shape, bf16),
                pltpu.VMEM(mean_shape, bf16),
                pltpu.SemaphoreType.DMA((2, fields)),
            ],
            compiler_params=PARAMS,
            cost_estimate=pl.CostEstimate(flops=4 * size, bytes_accessed=4 * size, transcendentals=0),
        )(counts, factors, adv_first, adv_rest, *[sent[i] for i in SHARE_ORDER])
    else:
        (parts,) = weigh(weigh_all_kernel, [((members, quantities) + chunk, f32)])
        got = lax.all_to_all(parts, "mem", 0, 0, tiled=True)
        whole = lax.all_gather(merge(finish_kernel, [got], merged_chunk), "mem")
        new_state, mean = call(
            relax_all_kernel,
            [VMEM] * 5,
            outs,
            flops=4 * slots * fields * rows * width,
            bytes_accessed=4 * slots * fields * rows * width,
            transcendentals=0,
        )(counts, factors, adv_first, adv_rest, whole)
    return (new_state, mean)


def solution(mesh):
    return jax.shard_map(
        on_device,
        mesh=mesh,
        in_specs=(
            P(("groups", "mem"), None, "lat", None),
            P(("groups", "mem")),
            P(("groups", "lat"), None),
            P(("groups", "lat"), None),
            P(("groups", "lat"), None),
            P(("groups", "lat"), None),
            P(("groups", "lat"), None),
            P(("groups", "lat"), None),
            P(),
        ),
        out_specs=(P(("groups", "mem"), None, "lat", None), P("groups", "lat", None)),
        check_vma=False,
    )
```

```python
import functools

import jax
import jax.numpy as jnp
import numpy as np
from jax import lax
from jax.experimental import pallas as pl
from jax.experimental.pallas import tpu as pltpu
from jax.sharding import PartitionSpec as P

STEPS = 4
SMOOTH = 16
LOG_TWO_PI = 1.8378770664093453
LANES = 128
TILE = 8
PARTS = 5
CHUNK_ROWS = 32
PACK = 16
BEGIN_STEPS = 2
LATER_FIELDS = 1
PAIR = 2
LINE = 4
SHARE_ORDER = (0, 6, 7, 4, 1, 2, 3, 5)


VMEM = pl.BlockSpec(memory_space=pltpu.VMEM)
PARAMS = pltpu.CompilerParams(vmem_limit_bytes=24 * 1024 * 1024)
EDGE_VMEM = 63 * 1024 * 1024


def kernel_matrix(offset):
    values = np.exp(-((2.0 * offset.astype(np.float32) / SMOOTH) ** 2))
    return np.where(np.abs(offset) <= SMOOTH, values, 0.0).astype(np.float32)


def split_two(x):
    high = x.astype(jnp.bfloat16).astype(jnp.float32)
    return high, x - high


def spread_terms(cells_ref, mask_ref, values_ref, error_ref, rows_ref, rows, width):
    half = width // 2
    cells = cells_ref[...]
    used = mask_ref[...].astype(jnp.float32)
    values = values_ref[...]
    error = error_ref[...]
    inverse = used / (error * error)
    first = inverse * values
    second = first * values + used * (2.0 * jnp.log(error) + LOG_TWO_PI)
    row = cells // width
    column = cells % width
    high = (column // half * rows + row).astype(jnp.float32)
    low = (column % half).astype(jnp.float32)
    for k, x in enumerate(split_two(inverse) + split_two(first) + (second, high, low)):
        rows_ref[k] = x


def add_observations(step, size, rows_ref, acc_ref):
    highs, lows = acc_ref.shape[0] // PARTS, acc_ref.shape[1]

    def steps_of(count):
        base = lax.broadcasted_iota(jnp.int32, (PACK, LANES), 0)
        return [
            (base + PACK * i).astype(jnp.float32).astype(jnp.bfloat16) for i in range(count // PACK)
        ]

    high_iota, low_iota = steps_of(highs), steps_of(lows)
    zero = jnp.zeros((PACK, LANES), jnp.bfloat16)
    one = jnp.ones((PACK, LANES), jnp.bfloat16)
    here = pl.ds(pl.multiple_of(step * size, size), size)
    held = [rows_ref[k, here, :] for k in range(PARTS + 2)]
    left, right = [], []
    for r in range(size):
        spread = [
            jnp.broadcast_to(x[r : r + 1, :], (PACK, LANES)).astype(jnp.bfloat16) for x in held
        ]
        high_row, low_row = spread[PARTS:]
        hit = [iota == high_row for iota in high_iota]
        left.append(
            jnp.concatenate([jnp.where(h, part, zero) for part in spread[:PARTS] for h in hit], axis=0)
        )
        right.append(
            jnp.concatenate([jnp.where(iota == low_row, one, zero) for iota in low_iota], axis=0)
        )
    acc_ref[...] += lax.dot_general(
        jnp.concatenate(left, axis=1),
        jnp.concatenate(right, axis=1),
        (((1,), (1,)), ((), ())),
        preferred_element_type=jnp.float32,
    )


def grids_of(acc_ref, rows):
    highs = 2 * rows

    def part_sum(indices):
        total = acc_ref[pl.ds(indices[-1] * highs, highs), :]
        for i in indices[-2::-1]:
            total = total + acc_ref[pl.ds(i * highs, highs), :]
        return jnp.concatenate([total[0:rows], total[rows:highs]], axis=1)

    return [part_sum(indices) for indices in ((0, 1), (2, 3), (4,))]


def begin_kernel(rows, width, steps, cells_ref, mask_ref, values_ref, error_ref, rows_ref, acc_ref):
    spread_terms(cells_ref, mask_ref, values_ref, error_ref, rows_ref, rows, width)
    acc_ref[...] = jnp.zeros_like(acc_ref)

    def body(step, carry):
        add_observations(step, CHUNK_ROWS, rows_ref, acc_ref)
        return carry

    lax.fori_loop(0, steps, body, 0)


def wind_parts(east_ref, north_ref, wind_halo_ref):
    east = jnp.concatenate([east_ref[...], wind_halo_ref[0]], axis=0)
    north = jnp.concatenate([north_ref[...], wind_halo_ref[1]], axis=0)
    west, south = jnp.maximum(east, 0.0), jnp.maximum(north, 0.0)
    east, north = -jnp.minimum(east, 0.0), -jnp.minimum(north, 0.0)
    return 1.0 - west - east - south - north, west, east, south, north


def edge_kernel(state_in, east_in, north_in, out_ref, state_ref, wind_ref, sems):
    slots, fields, rows, width = state_in.shape
    place = lax.axis_index("lat")
    lower = place == 0
    here = pl.ds(pl.multiple_of((1 - place) * (rows - 2 * TILE), 2 * TILE), 2 * TILE)
    copies = [
        pltpu.make_async_copy(state_in.at[:, :, here], state_ref, sems.at[0]),
        pltpu.make_async_copy(east_in.at[here], wind_ref.at[0], sems.at[1]),
        pltpu.make_async_copy(north_in.at[here], wind_ref.at[1], sems.at[2]),
    ]
    for copy in copies:
        copy.start()
    low_row = lax.broadcasted_iota(jnp.int32, (TILE, width), 0) < TILE // 2
    keep = low_row != lower

    def edge(block):
        return jnp.where(keep, jnp.where(lower, block[TILE:], block[0:TILE]), 0.0)

    for copy in copies:
        copy.wait()
    for s in range(slots):
        for f in range(fields):
            out_ref[s * fields + f] = edge(state_ref[s, f].astype(jnp.float32))
    for i in range(2):
        out_ref[slots * fields + i] = edge(wind_ref[i])


def store_winds(east_ref, north_ref, halo_ref, count, winds_ref):
    for i, part in enumerate(wind_parts(east_ref, north_ref, halo_ref.at[pl.ds(count, 2)])):
        winds_ref[i] = part


def advect_field(state_ref, halo_ref, winds_ref, buffer_ref, f, adv_ref, place, as_written=False):
    slots, fields, rows, width = state_ref.shape
    across, band_tiles = width // LANES, rows // TILE
    tiles = band_tiles + 1
    lane = lax.broadcasted_iota(jnp.int32, (TILE, LANES), 1)
    first, last = lane == 0, lane == LANES - 1

    def columns(l):
        return slice(l * LANES, (l + 1) * LANES)

    def put(side, k, l, v, value):
        copies = [v + 1] + ([0] if v == tiles - 1 else []) + ([tiles + 1] if v == 0 else [])
        for at in copies:
            buffer_ref[side, k, l, at * TILE : (at + 1) * TILE, :] = value

    for k in range(slots):
        x = state_ref[k, f].astype(jnp.float32)
        halo = halo_ref[k * fields + f]
        for l in range(across):
            for v in range(band_tiles):
                put(0, k, l, v, x[v * TILE : (v + 1) * TILE, columns(l)])
            put(0, k, l, band_tiles, halo[:, columns(l)])

    done = [[] for _ in range(slots)]
    for step in range(STEPS):
        side = step % 2
        ends = step == STEPS - 1
        for v in range(band_tiles if ends else tiles):
            cells = []
            for k in range(slots):

                def row_tile(offset):
                    start = (v + 1) * TILE + offset
                    return [buffer_ref[side, k, l, start : start + TILE, :] for l in range(across)]

                x = row_tile(0)
                west = [pltpu.roll(value, 1, 1) for value in x]
                east = [pltpu.roll(value, LANES - 1, 1) for value in x]
                cells.append(
                    (
                        x,
                        [jnp.where(first, west[l - 1], west[l]) for l in range(across)],
                        [jnp.where(last, east[(l + 1) % across], east[l]) for l in range(across)],
                        row_tile(-1),
                        row_tile(1),
                    )
                )
            stepped = [[] for _ in range(slots)]
            for l in range(across):
                here = slice(v * TILE, (v + 1) * TILE)
                centre, *winds = [winds_ref[c, here, columns(l)] for c in range(5)]
                for k in range(slots):
                    x, west, east, south, north = [values[l] for values in cells[k]]
                    if as_written:
                        x = (
                            x
                            - winds[0] * (x - west)
                            + winds[1] * (east - x)
                            - winds[2] * (x - south)
                            + winds[3] * (north - x)
                        )
                    else:
                        x = (
                            centre * x
                            + winds[0] * west
                            + winds[1] * east
                            + winds[2] * south
                            + winds[3] * north
                        )
                    if ends:
                        stepped[k].append(x)
                    else:
                        put(1 - side, k, l, v, x)
            if ends:
                for k in range(slots):
                    done[k].append(jnp.concatenate(stepped[k], axis=1))
    for k in range(slots):
        for v in range(0, band_tiles, 2):
            block = jnp.concatenate(done[k][v : v + 2], axis=0)
            adv_ref[k, place, v * TILE : (v + 2) * TILE, :] = block.astype(jnp.bfloat16)


def first_kernel(
    steps, state_ref, halo_ref, east_ref, north_ref, terms_ref, acc_in_ref, lat_ref, lon_ref,
    adv_ref, own_ref, send_ref, acc_ref, winds_ref, buffer_ref,
):
    slots, fields, rows, width = state_ref.shape
    store_winds(east_ref, north_ref, halo_ref, slots * fields, winds_ref)
    acc_ref[...] = acc_in_ref[...]
    held = adv_ref.shape[1]
    total = terms_ref.shape[1] // CHUNK_ROWS

    def advect_next(f, as_written):
        advect_field(state_ref, halo_ref, winds_ref, buffer_ref, f, adv_ref, f, as_written)

    def both(as_written):
        def body(i, carry):
            add_observations(steps + i, CHUNK_ROWS, terms_ref, acc_ref)
            advect_next(i, as_written)
            return carry

        return body

    def observe(step, carry):
        add_observations(step, CHUNK_ROWS, terms_ref, acc_ref)
        return carry

    shared = min(held, total - steps)
    if shared:
        lax.fori_loop(0, 1, both(True), 0)
        lax.fori_loop(1, shared, both(False), 0)
    if steps + shared < total:
        lax.fori_loop(steps + shared, total, observe, 0)
    for f in range(shared, held):
        advect_next(f, f == 0)

    inverse, first, second = grids_of(acc_ref, rows)
    logliks = []
    for s in range(slots):
        value = adv_ref[s, 0].astype(jnp.float32)
        logliks.append(-0.5 * (inverse * value * value - 2.0 * first * value + second))
    smooth = functools.partial(
        jnp.dot, precision=lax.Precision.HIGHEST, preferred_element_type=jnp.float32
    )
    edge = rows + jnp.where(lax.axis_index("lat") == 0, 0, SMOOTH)
    lat_rows = jnp.concatenate(
        [lat_ref[0:rows], lat_ref[pl.ds(pl.multiple_of(edge, SMOOTH), SMOOTH)]], axis=0
    )
    along = smooth(jnp.concatenate(logliks, axis=0), lon_ref[...])
    for s in range(slots):
        scores = smooth(lat_rows, along[s * rows : (s + 1) * rows])
        own_ref[s] = scores[0:rows]
        send_ref[s] = scores[rows:]


def rest_kernel(
    state_ref, halo_ref, east_ref, north_ref, adv_ref, winds_ref, buffer_ref
):
    slots, fields = state_ref.shape[:2]
    held = adv_ref.shape[1]
    store_winds(east_ref, north_ref, halo_ref, slots * fields, winds_ref)


    def body(i, carry):
        f = fields - held + i
        advect_field(state_ref, halo_ref, winds_ref, buffer_ref, f, adv_ref, i)
        return carry

    lax.fori_loop(0, held, body, 0)


def field_ref(adv_first_ref, adv_rest_ref, s, f):
    held = adv_first_ref.shape[1]
    return adv_first_ref.at[s, f] if f < held else adv_rest_ref.at[s, f - held]


def weigh_all_kernel(
    counts_ref, own_ref, recv_ref, adv_first_ref, adv_rest_ref, parts_ref
):
    slots, rows, width = own_ref.shape
    fields = adv_first_ref.shape[1] + adv_rest_ref.shape[1]
    across = width // LANES
    members, _, held, _ = parts_ref.shape

    def store(row_tile, index, value):
        for l in range(across):
            tile = value[:, l * LANES : (l + 1) * LANES]
            row = (row_tile * across + l) * TILE
            for k in range(0, TILE, min(held, TILE)):
                chunk, at = divmod(row + k, held)
                parts_ref[chunk, index, at : at + min(held, TILE)] = tile[k : k + min(held, TILE)]

    lower = lax.axis_index("lat") == 0
    for t in range(rows // TILE):
        here = slice(t * TILE, (t + 1) * TILE)
        near = (t * TILE) % SMOOTH
        scores = []
        for s in range(slots):
            recv = recv_ref[s, near : near + TILE, :]
            at_this_edge = lower if t * TILE >= rows - SMOOTH else jnp.logical_not(lower)
            score = own_ref[s, here, :] + jnp.where(at_this_edge, recv, 0.0)
            scores.append(jnp.where(s < counts_ref[0:1, 0:1], score, -jnp.inf))
        peak = functools.reduce(jnp.maximum, scores)
        gains = [jnp.exp(score - peak) for score in scores]
        total = functools.reduce(jnp.add, gains)
        store(t, 0, peak + jnp.log(total))
        gains = [gain / total for gain in gains]
        for f in range(fields):
            mean = None
            for s in range(slots):
                ref = field_ref(adv_first_ref, adv_rest_ref, s, f)
                pair = slice(t // 2 * 2 * TILE, (t // 2 + 1) * 2 * TILE)
                value = ref[pair, :].astype(jnp.float32)[t % 2 * TILE : (t % 2 + 1) * TILE]
                term = gains[s] * value
                mean = term if mean is None else mean + term
            store(t, 1 + f, mean)


def weigh_kernel(
    counts_ref, own_ref, recv_ref, adv_first_ref, adv_rest_ref, *out_refs
):
    slots, rows, width = own_ref.shape
    fields = adv_first_ref.shape[1] + adv_rest_ref.shape[1]
    half = width // PAIR
    lower = lax.axis_index("lat") == 0
    member = lax.axis_index("mem")
    even_side = member % PAIR == 0
    for distance in range(LINE):
        tile = (member // PAIR) ^ distance
        here = pl.ds(pl.multiple_of(tile * TILE, TILE), TILE)
        near = pl.ds(pl.multiple_of(tile % 2 * TILE, TILE), TILE)
        pair = pl.ds(pl.multiple_of(tile // 2 * (2 * TILE), 2 * TILE), 2 * TILE)
        even_tile = tile % 2 == 0
        at_edge = lower == (tile * TILE >= rows - SMOOTH)
        keep_ref, send_ref = out_refs[distance], out_refs[LINE + distance]

        def store(index, value):
            left, right = value[:, 0:half], value[:, half:width]
            keep_ref[index] = jnp.where(even_side, left, right)
            send_ref[index] = jnp.where(even_side, right, left)

        scores = []
        for s in range(slots):
            score = own_ref[s, here, :] + jnp.where(at_edge, recv_ref[s, near, :], 0.0)
            scores.append(jnp.where(s < counts_ref[0:1, 0:1], score, -jnp.inf))
        peak = functools.reduce(jnp.maximum, scores)
        gains = [jnp.exp(score - peak) for score in scores]
        total = functools.reduce(jnp.add, gains)
        store(0, peak + jnp.log(total))
        gains = [gain / total for gain in gains]
        for f in range(fields):
            mean = None
            for s in range(slots):
                ref = field_ref(adv_first_ref, adv_rest_ref, s, f)
                value = ref[pair, :].astype(jnp.float32)
                term = gains[s] * jnp.where(even_tile, value[0:TILE], value[TILE:])
                mean = term if mean is None else mean + term
            store(1 + f, mean)


def merge_values(refs):
    peak = functools.reduce(jnp.maximum, [ref[0] for ref in refs])
    weights = [jnp.exp(ref[0] - peak) for ref in refs]
    total = functools.reduce(jnp.add, weights)
    shares = [weight / total for weight in weights]
    means = [
        functools.reduce(jnp.add, [share * ref[q] for share, ref in zip(shares, refs)])
        for q in range(1, refs[0].shape[0])
    ]
    return peak + jnp.log(total), means


def merge_kernel(*refs):
    out_ref = refs[-1]
    log_weight, means = merge_values(refs[:-1])
    out_ref[0] = log_weight
    for f, mean in enumerate(means):
        out_ref[1 + f] = mean


def finish_kernel(*refs):
    merged_ref = refs[-1]
    parts = refs[:-1]
    if len(parts) == 1:
        parts = [parts[0].at[d] for d in range(parts[0].shape[0])]
    for f, mean in enumerate(merge_values(parts)[1]):
        merged_ref[f] = mean


def relaxed(value, merged, factor, live):
    value = value.astype(jnp.float32)
    return jnp.where(live, value + factor * (merged - value), 0.0).astype(jnp.bfloat16)


def relax_all_kernel(
    counts_ref, relax_ref, adv_first_ref, adv_rest_ref, whole_ref, new_ref, mean_ref
):
    _, fields, rows, width = new_ref.shape
    across = width // LANES
    held = whole_ref.shape[2]

    def tile(f, row):
        if held >= TILE:
            return whole_ref[row // held, f, row % held : row % held + TILE]
        return jnp.concatenate([whole_ref[(row + k) // held, f] for k in range(0, TILE, held)], axis=0)

    for f in range(fields):
        merged = jnp.concatenate(
            [
                jnp.concatenate([tile(f, (t * across + l) * TILE) for l in range(across)], axis=1)
                for t in range(rows // TILE)
            ],
            axis=0,
        )
        mean_ref[f] = merged.astype(jnp.bfloat16)
        for s in range(new_ref.shape[0]):
            value = field_ref(adv_first_ref, adv_rest_ref, s, f)[...]
            new_ref[s, f] = relaxed(value, merged, relax_ref[f], s < counts_ref[0:1, 0:1])


def relax_kernel(counts_ref, relax_ref, adv_first_ref, adv_rest_ref, *refs):
    share_refs, (new_out, mean_out, merged_ref, new_ref, mean_ref, sems) = refs[:-6], refs[-6:]
    slots, fields, rows, width = new_ref.shape
    share_of = dict(zip(SHARE_ORDER, share_refs))
    member = lax.axis_index("mem")
    even_side = member % PAIR == 0
    copies = []
    for f in range(fields):
        for distance in range(LINE):
            tile = (member // PAIR) ^ distance
            same = share_of[PAIR * distance][f]
            other = share_of[PAIR * distance + 1][f]
            left = jnp.where(even_side, same, other)
            right = jnp.where(even_side, other, same)
            merged_ref[f, pl.ds(pl.multiple_of(tile * TILE, TILE), TILE), :] = jnp.concatenate(
                [left, right], axis=1
            )
        merged = merged_ref[f]
        mean_ref[f] = merged.astype(jnp.bfloat16)
        for s in range(slots):
            value = field_ref(adv_first_ref, adv_rest_ref, s, f)[...]
            new_ref[s, f] = relaxed(value, merged, relax_ref[f], s < counts_ref[0:1, 0:1])
        copies.append(pltpu.make_async_copy(new_ref.at[:, f], new_out.at[:, f], sems.at[0, f]))
        copies.append(pltpu.make_async_copy(mean_ref.at[f], mean_out.at[f], sems.at[1, f]))
        for copy in copies[-2:]:
            copy.start()
    for copy in copies:
        copy.wait()


def call(kernel, ins, outs, scratch=(), **cost):
    return pl.pallas_call(
        kernel,
        out_shape=[jax.ShapeDtypeStruct(shape, dtype) for shape, dtype in outs],
        in_specs=ins,
        out_specs=[VMEM] * len(outs),
        scratch_shapes=list(scratch),
        compiler_params=PARAMS,
        cost_estimate=pl.CostEstimate(**cost),
    )


def on_device(
    state, counts, east_wind, north_wind, obs_cells, obs_mask, obs_values, obs_error, relax
):
    slots, fields, rows, width = state.shape
    f32, bf16 = jnp.float32, jnp.bfloat16
    swap = [(0, 1), (1, 0)]
    (message,) = pl.pallas_call(
        edge_kernel,
        out_shape=[jax.ShapeDtypeStruct((slots * fields + 2, TILE, width), f32)],
        in_specs=[pl.BlockSpec(memory_space=pltpu.HBM)] * 3,
        out_specs=[VMEM],
        scratch_shapes=[
            pltpu.VMEM((slots, fields, 2 * TILE, width), bf16),
            pltpu.VMEM((2, 2 * TILE, width), f32),
            pltpu.SemaphoreType.DMA((3,)),
        ],
        compiler_params=pltpu.CompilerParams(vmem_limit_bytes=EDGE_VMEM),
        cost_estimate=pl.CostEstimate(
            flops=0, bytes_accessed=6 * slots * fields * TILE * width, transcendentals=0
        ),
    )(state, east_wind, north_wind)
    halo = lax.ppermute(message, "lat", swap)

    observations = obs_cells.shape[1]
    flat = [
        x.reshape(observations // LANES, LANES) for x in (obs_cells, obs_mask, obs_values, obs_error)
    ]
    acc_shape = (PARTS * 2 * rows, width // 2)
    all_steps = observations // (LANES * CHUNK_ROWS)
    begin_steps = min(BEGIN_STEPS, all_steps)
    observe_flops = 2 * PARTS * rows * width * LANES * CHUNK_ROWS
    terms, begun = call(
        functools.partial(begin_kernel, rows, width, begin_steps),
        [VMEM] * 4,
        [((PARTS + 2, observations // LANES, LANES), f32), (acc_shape, f32)],
        flops=observe_flops * begin_steps,
        bytes_accessed=16 * observations,
        transcendentals=observations,
    )(*flat)

    index = np.arange(rows)
    own = index[None, :] - index[:, None]
    upper_side = index[None, :] - (index[:SMOOTH, None] + rows)
    lower_side = index[None, :] - (index[rows - SMOOTH :, None] - rows)
    lat_kernel = jnp.asarray(
        kernel_matrix(np.concatenate([own, upper_side, lower_side])), dtype=f32
    )
    distance = np.abs(np.arange(width)[:, None] - np.arange(width)[None, :])
    lon_kernel = jnp.asarray(kernel_matrix(np.minimum(distance, width - distance)))

    advect_scratch = [
        pltpu.VMEM((5, rows + TILE, width), f32),
        pltpu.VMEM((2, slots, width // LANES, rows + 3 * TILE, LANES), f32),
    ]
    advect_flops = STEPS * 16 * slots * rows * width
    adv_first, own_scores, edge_scores = call(
        functools.partial(first_kernel, begin_steps),
        [VMEM] * 8,
        [
            ((slots, fields - LATER_FIELDS, rows, width), bf16),
            ((slots, rows, width), f32),
            ((slots, SMOOTH, width), f32),
        ],
        [pltpu.VMEM(acc_shape, f32)] + advect_scratch,
        flops=observe_flops * (all_steps - begin_steps) + advect_flops * (fields - LATER_FIELDS),
        bytes_accessed=4 * width * width,
        transcendentals=0,
    )(state, halo, east_wind, north_wind, terms, begun, lat_kernel, lon_kernel)
    received = lax.ppermute(edge_scores, "lat", swap)

    (adv_rest,) = call(
        rest_kernel,
        [VMEM] * 4,
        [((slots, LATER_FIELDS, rows, width), bf16)],
        advect_scratch,
        flops=advect_flops * LATER_FIELDS,
        bytes_accessed=4 * slots * fields * rows * width,
        transcendentals=0,
    )(state, halo, east_wind, north_wind)

    members = lax.axis_size("mem")
    counts = jnp.broadcast_to(jnp.clip(counts, 1, slots)[0], (TILE, LANES))
    factors = jnp.broadcast_to(relax[:, None, None], (fields, 1, width))
    quantities = fields + 1
    direct = (members, rows, width % (PAIR * LANES)) == (PAIR * LINE, LINE * TILE, 0)
    chunk = (TILE, width // PAIR) if direct else (rows * width // LANES // members, LANES)
    cells = chunk[0] * chunk[1]

    def weigh(kernel, outs):
        return call(
            kernel,
            [VMEM] * 5,
            outs,
            flops=4 * slots * fields * rows * width,
            bytes_accessed=4 * slots * fields * rows * width,
            transcendentals=slots * rows * width,
        )(counts, own_scores, received, adv_first, adv_rest)

    def merge(kernel, pieces, out):
        size = quantities * cells * (len(pieces) if direct else members)
        return call(
            kernel,
            [VMEM] * len(pieces),
            [out],
            flops=4 * size,
            bytes_accessed=4 * size,
            transcendentals=size // quantities,
        )(*pieces)[0]

    def swapped(x, offset):
        return lax.ppermute(x, "mem", [(m, m ^ offset) for m in range(members)])

    merged_chunk = ((fields,) + chunk, f32)
    new_shape, mean_shape = (slots, fields, rows, width), (fields, rows, width)
    outs = [(new_shape, bf16), (mean_shape, bf16)]
    if direct:
        piece = ((quantities,) + chunk, f32)
        parts = weigh(weigh_kernel, [piece] * (PAIR * LINE))
        paired = [None] * LINE
        for j in reversed(range(LINE)):
            paired[j] = merge(merge_kernel, [parts[j], swapped(parts[LINE + j], 1)], piece)
        pieces = [paired[0]] + [swapped(paired[j], PAIR * j) for j in range(1, LINE)]
        merged = merge(finish_kernel, pieces, merged_chunk)
        far = LINE - 1
        sent = {0: merged}
        for offset in SHARE_ORDER[1:]:
            through = offset ^ 1 if offset % PAIR and offset // PAIR < far else 0
            sent[offset] = swapped(sent[through], offset ^ through)
        size = slots * fields * rows * width
        new_state, mean = pl.pallas_call(
            relax_kernel,
            out_shape=[jax.ShapeDtypeStruct(*out) for out in outs],
            in_specs=[VMEM] * (4 + len(sent)),
            out_specs=[pl.BlockSpec(memory_space=pl.ANY)] * 2,
            scratch_shapes=[
                pltpu.VMEM((fields, rows, width), f32),
                pltpu.VMEM(new_shape, bf16),
                pltpu.VMEM(mean_shape, bf16),
                pltpu.SemaphoreType.DMA((2, fields)),
            ],
            compiler_params=PARAMS,
            cost_estimate=pl.CostEstimate(flops=4 * size, bytes_accessed=4 * size, transcendentals=0),
        )(counts, factors, adv_first, adv_rest, *[sent[i] for i in SHARE_ORDER])
    else:
        (parts,) = weigh(weigh_all_kernel, [((members, quantities) + chunk, f32)])
        got = lax.all_to_all(parts, "mem", 0, 0, tiled=True)
        whole = lax.all_gather(merge(finish_kernel, [got], merged_chunk), "mem")
        new_state, mean = call(
            relax_all_kernel,
            [VMEM] * 5,
            outs,
            flops=4 * slots * fields * rows * width,
            bytes_accessed=4 * slots * fields * rows * width,
            transcendentals=0,
        )(counts, factors, adv_first, adv_rest, whole)
    return (new_state, mean)


def solution(mesh):
    return jax.shard_map(
        on_device,
        mesh=mesh,
        in_specs=(
            P(("groups", "mem"), None, "lat", None),
            P(("groups", "mem")),
            P(("groups", "lat"), None),
            P(("groups", "lat"), None),
            P(("groups", "lat"), None),
            P(("groups", "lat"), None),
            P(("groups", "lat"), None),
            P(("groups", "lat"), None),
            P(),
        ),
        out_specs=(P(("groups", "mem"), None, "lat", None), P("groups", "lat", None)),
        check_vma=False,
    )
```

```python
import functools

import jax
import jax.numpy as jnp
import ml_dtypes
import numpy as np
from jax import lax
from jax.experimental import pallas as pl
from jax.experimental.pallas import tpu as pltpu
from jax.sharding import PartitionSpec as P

STEPS = 4
SMOOTH = 16
LOG_TWO_PI = 1.8378770664093453
LANES = 128
TILE = 8
PARTS = 5
CHUNK_ROWS = 32
PACK = 16
BEGIN_STEPS = 2
LATER_FIELDS = 1
PAIR = 2
LINE = 4
SHARE_ORDER = (0, 6, 7, 4, 1, 2, 3, 5)


VMEM = pl.BlockSpec(memory_space=pltpu.VMEM)
PARAMS = pltpu.CompilerParams(vmem_limit_bytes=24 * 1024 * 1024)
EDGE_VMEM = 63 * 1024 * 1024


def kernel_matrix(offset):
    values = np.exp(-((2.0 * offset.astype(np.float32) / SMOOTH) ** 2))
    return np.where(np.abs(offset) <= SMOOTH, values, 0.0).astype(np.float32)


def split_constant(matrix):
    parts = []
    for _ in range(3):
        parts.append(matrix.astype(ml_dtypes.bfloat16))
        matrix = matrix - parts[-1].astype(np.float32)
    return jnp.asarray(np.stack(parts))


def split_two(x):
    high = x.astype(jnp.bfloat16).astype(jnp.float32)
    return high, x - high


def spread_terms(cells_ref, mask_ref, values_ref, error_ref, rows_ref, rows, width):
    half = width // 2
    cells = cells_ref[...]
    used = mask_ref[...].astype(jnp.float32)
    values = values_ref[...]
    error = error_ref[...]
    inverse = used / (error * error)
    first = inverse * values
    second = first * values + used * (2.0 * jnp.log(error) + LOG_TWO_PI)
    row = cells // width
    column = cells % width
    high = (column // half * rows + row).astype(jnp.float32)
    low = (column % half).astype(jnp.float32)
    for k, x in enumerate(split_two(inverse) + split_two(first) + (second, high, low)):
        rows_ref[k] = x


def add_observations(step, size, rows_ref, acc_ref):
    highs, lows = acc_ref.shape[0] // PARTS, acc_ref.shape[1]

    def steps_of(count):
        base = lax.broadcasted_iota(jnp.int32, (PACK, LANES), 0)
        return [
            (base + PACK * i).astype(jnp.float32).astype(jnp.bfloat16) for i in range(count // PACK)
        ]

    high_iota, low_iota = steps_of(highs), steps_of(lows)
    zero = jnp.zeros((PACK, LANES), jnp.bfloat16)
    one = jnp.ones((PACK, LANES), jnp.bfloat16)
    here = pl.ds(pl.multiple_of(step * size, size), size)
    held = [rows_ref[k, here, :] for k in range(PARTS + 2)]
    left, right = [], []
    for r in range(size):
        spread = [
            jnp.broadcast_to(x[r : r + 1, :], (PACK, LANES)).astype(jnp.bfloat16) for x in held
        ]
        high_row, low_row = spread[PARTS:]
        hit = [iota == high_row for iota in high_iota]
        left.append(
            jnp.concatenate([jnp.where(h, part, zero) for part in spread[:PARTS] for h in hit], axis=0)
        )
        right.append(
            jnp.concatenate([jnp.where(iota == low_row, one, zero) for iota in low_iota], axis=0)
        )
    acc_ref[...] += lax.dot_general(
        jnp.concatenate(left, axis=1),
        jnp.concatenate(right, axis=1),
        (((1,), (1,)), ((), ())),
        preferred_element_type=jnp.float32,
    )


def grids_of(acc_ref, rows):
    highs = 2 * rows

    def part_sum(indices):
        total = acc_ref[pl.ds(indices[-1] * highs, highs), :]
        for i in indices[-2::-1]:
            total = total + acc_ref[pl.ds(i * highs, highs), :]
        return jnp.concatenate([total[0:rows], total[rows:highs]], axis=1)

    return [part_sum(indices) for indices in ((0, 1), (2, 3), (4,))]


def begin_kernel(rows, width, steps, cells_ref, mask_ref, values_ref, error_ref, rows_ref, acc_ref):
    spread_terms(cells_ref, mask_ref, values_ref, error_ref, rows_ref, rows, width)
    acc_ref[...] = jnp.zeros_like(acc_ref)

    def body(step, carry):
        add_observations(step, CHUNK_ROWS, rows_ref, acc_ref)
        return carry

    lax.fori_loop(0, steps, body, 0)


def wind_parts(east_ref, north_ref, wind_halo_ref):
    east = jnp.concatenate([east_ref[...], wind_halo_ref[0]], axis=0)
    north = jnp.concatenate([north_ref[...], wind_halo_ref[1]], axis=0)
    west, south = jnp.maximum(east, 0.0), jnp.maximum(north, 0.0)
    east, north = -jnp.minimum(east, 0.0), -jnp.minimum(north, 0.0)
    return 1.0 - west - east - south - north, west, east, south, north


def edge_kernel(state_in, east_in, north_in, out_ref, state_ref, wind_ref, sems):
    slots, fields, rows, width = state_in.shape
    place = lax.axis_index("lat")
    lower = place == 0
    here = pl.ds(pl.multiple_of((1 - place) * (rows - 2 * TILE), 2 * TILE), 2 * TILE)
    copies = [
        pltpu.make_async_copy(state_in.at[:, :, here], state_ref, sems.at[0]),
        pltpu.make_async_copy(east_in.at[here], wind_ref.at[0], sems.at[1]),
        pltpu.make_async_copy(north_in.at[here], wind_ref.at[1], sems.at[2]),
    ]
    for copy in copies:
        copy.start()
    low_row = lax.broadcasted_iota(jnp.int32, (TILE, width), 0) < TILE // 2
    keep = low_row != lower

    def edge(block):
        return jnp.where(keep, jnp.where(lower, block[TILE:], block[0:TILE]), 0.0)

    for copy in copies:
        copy.wait()
    for s in range(slots):
        for f in range(fields):
            out_ref[s * fields + f] = edge(state_ref[s, f].astype(jnp.float32))
    for i in range(2):
        out_ref[slots * fields + i] = edge(wind_ref[i])


def store_winds(east_ref, north_ref, halo_ref, count, winds_ref):
    for i, part in enumerate(wind_parts(east_ref, north_ref, halo_ref.at[pl.ds(count, 2)])):
        winds_ref[i] = part


def advect_field(state_ref, halo_ref, winds_ref, buffer_ref, f, adv_ref, place, as_written=False):
    slots, fields, rows, width = state_ref.shape
    across, band_tiles = width // LANES, rows // TILE
    tiles = band_tiles + 1
    lane = lax.broadcasted_iota(jnp.int32, (TILE, LANES), 1)
    first, last = lane == 0, lane == LANES - 1

    def columns(l):
        return slice(l * LANES, (l + 1) * LANES)

    def put(side, k, l, v, value):
        copies = [v + 1] + ([0] if v == tiles - 1 else []) + ([tiles + 1] if v == 0 else [])
        for at in copies:
            buffer_ref[side, k, l, at * TILE : (at + 1) * TILE, :] = value

    for k in range(slots):
        x = state_ref[k, f].astype(jnp.float32)
        halo = halo_ref[k * fields + f]
        for l in range(across):
            for v in range(band_tiles):
                put(0, k, l, v, x[v * TILE : (v + 1) * TILE, columns(l)])
            put(0, k, l, band_tiles, halo[:, columns(l)])

    done = [[] for _ in range(slots)]
    for step in range(STEPS):
        side = step % 2
        ends = step == STEPS - 1
        for v in range(band_tiles if ends else tiles):
            cells = []
            for k in range(slots):

                def row_tile(offset):
                    start = (v + 1) * TILE + offset
                    return [buffer_ref[side, k, l, start : start + TILE, :] for l in range(across)]

                x = row_tile(0)
                west = [pltpu.roll(value, 1, 1) for value in x]
                east = [pltpu.roll(value, LANES - 1, 1) for value in x]
                cells.append(
                    (
                        x,
                        [jnp.where(first, west[l - 1], west[l]) for l in range(across)],
                        [jnp.where(last, east[(l + 1) % across], east[l]) for l in range(across)],
                        row_tile(-1),
                        row_tile(1),
                    )
                )
            stepped = [[] for _ in range(slots)]
            for l in range(across):
                here = slice(v * TILE, (v + 1) * TILE)
                centre, *winds = [winds_ref[c, here, columns(l)] for c in range(5)]
                for k in range(slots):
                    x, west, east, south, north = [values[l] for values in cells[k]]
                    if as_written:
                        x = (
                            x
                            - winds[0] * (x - west)
                            + winds[1] * (east - x)
                            - winds[2] * (x - south)
                            + winds[3] * (north - x)
                        )
                    else:
                        x = (
                            centre * x
                            + winds[0] * west
                            + winds[1] * east
                            + winds[2] * south
                            + winds[3] * north
                        )
                    if ends:
                        stepped[k].append(x)
                    else:
                        put(1 - side, k, l, v, x)
            if ends:
                for k in range(slots):
                    done[k].append(jnp.concatenate(stepped[k], axis=1))
    for k in range(slots):
        for v in range(0, band_tiles, 2):
            block = jnp.concatenate(done[k][v : v + 2], axis=0)
            adv_ref[k, place, v * TILE : (v + 2) * TILE, :] = block.astype(jnp.bfloat16)


def parts_of(x):
    high = x.astype(jnp.bfloat16)
    rest = x - high.astype(jnp.float32)
    middle = rest.astype(jnp.bfloat16)
    return [high, middle, (rest - middle.astype(jnp.float32)).astype(jnp.bfloat16)]


def product(left, right):
    rows = left[0].shape[0]
    total = None
    for p in reversed(range(3)):
        pieces = jnp.dot(
            jnp.concatenate(left[: 3 - p], axis=0), right[p], preferred_element_type=jnp.float32
        )
        for q in reversed(range(3 - p)):
            term = pieces[q * rows : (q + 1) * rows]
            total = term if total is None else total + term
    return total


def first_kernel(
    steps, state_ref, halo_ref, east_ref, north_ref, terms_ref, acc_in_ref, lat_ref, lon_ref,
    adv_ref, own_ref, send_ref, acc_ref, winds_ref, buffer_ref,
):
    slots, fields, rows, width = state_ref.shape
    store_winds(east_ref, north_ref, halo_ref, slots * fields, winds_ref)
    acc_ref[...] = acc_in_ref[...]
    held = adv_ref.shape[1]
    total = terms_ref.shape[1] // CHUNK_ROWS

    def advect_next(f, as_written):
        advect_field(state_ref, halo_ref, winds_ref, buffer_ref, f, adv_ref, f, as_written)

    def both(as_written):
        def body(i, carry):
            add_observations(steps + i, CHUNK_ROWS, terms_ref, acc_ref)
            advect_next(i, as_written)
            return carry

        return body

    def observe(step, carry):
        add_observations(step, CHUNK_ROWS, terms_ref, acc_ref)
        return carry

    shared = min(held, total - steps)
    if shared:
        lax.fori_loop(0, 1, both(True), 0)
        lax.fori_loop(1, shared, both(False), 0)
    if steps + shared < total:
        lax.fori_loop(steps + shared, total, observe, 0)
    for f in range(shared, held):
        advect_next(f, f == 0)

    inverse, first, second = grids_of(acc_ref, rows)
    logliks = []
    for s in range(slots):
        value = adv_ref[s, 0].astype(jnp.float32)
        logliks.append(-0.5 * (inverse * value * value - 2.0 * first * value + second))
    count = slots * rows
    edge = count + jnp.where(lax.axis_index("lat") == 0, 0, slots * SMOOTH)
    edge = pl.ds(pl.multiple_of(edge, SMOOTH), slots * SMOOTH)
    lat_parts = [
        jnp.concatenate([lat_ref[p, 0:count], lat_ref[p, edge]], axis=0) for p in range(3)
    ]
    along = product(parts_of(jnp.concatenate(logliks, axis=0)), [lon_ref[p] for p in range(3)])
    scores = product(lat_parts, parts_of(along))
    for s in range(slots):
        own_ref[s] = scores[s * rows : (s + 1) * rows]
        send_ref[s] = scores[count + s * SMOOTH : count + (s + 1) * SMOOTH]


def rest_kernel(
    state_ref, halo_ref, east_ref, north_ref, adv_ref, winds_ref, buffer_ref
):
    slots, fields = state_ref.shape[:2]
    held = adv_ref.shape[1]
    store_winds(east_ref, north_ref, halo_ref, slots * fields, winds_ref)


    def body(i, carry):
        f = fields - held + i
        advect_field(state_ref, halo_ref, winds_ref, buffer_ref, f, adv_ref, i)
        return carry

    lax.fori_loop(0, held, body, 0)


def field_ref(adv_first_ref, adv_rest_ref, s, f):
    held = adv_first_ref.shape[1]
    return adv_first_ref.at[s, f] if f < held else adv_rest_ref.at[s, f - held]


def weigh_all_kernel(
    counts_ref, own_ref, recv_ref, adv_first_ref, adv_rest_ref, parts_ref
):
    slots, rows, width = own_ref.shape
    fields = adv_first_ref.shape[1] + adv_rest_ref.shape[1]
    across = width // LANES
    members, _, held, _ = parts_ref.shape

    def store(row_tile, index, value):
        for l in range(across):
            tile = value[:, l * LANES : (l + 1) * LANES]
            row = (row_tile * across + l) * TILE
            for k in range(0, TILE, min(held, TILE)):
                chunk, at = divmod(row + k, held)
                parts_ref[chunk, index, at : at + min(held, TILE)] = tile[k : k + min(held, TILE)]

    lower = lax.axis_index("lat") == 0
    for t in range(rows // TILE):
        here = slice(t * TILE, (t + 1) * TILE)
        near = (t * TILE) % SMOOTH
        scores = []
        for s in range(slots):
            recv = recv_ref[s, near : near + TILE, :]
            at_this_edge = lower if t * TILE >= rows - SMOOTH else jnp.logical_not(lower)
            score = own_ref[s, here, :] + jnp.where(at_this_edge, recv, 0.0)
            scores.append(jnp.where(s < counts_ref[0:1, 0:1], score, -jnp.inf))
        peak = functools.reduce(jnp.maximum, scores)
        gains = [jnp.exp(score - peak) for score in scores]
        total = functools.reduce(jnp.add, gains)
        store(t, 0, peak + jnp.log(total))
        gains = [gain / total for gain in gains]
        for f in range(fields):
            mean = None
            for s in range(slots):
                ref = field_ref(adv_first_ref, adv_rest_ref, s, f)
                pair = slice(t // 2 * 2 * TILE, (t // 2 + 1) * 2 * TILE)
                value = ref[pair, :].astype(jnp.float32)[t % 2 * TILE : (t % 2 + 1) * TILE]
                term = gains[s] * value
                mean = term if mean is None else mean + term
            store(t, 1 + f, mean)


def weigh_kernel(
    counts_ref, own_ref, recv_ref, adv_first_ref, adv_rest_ref, *out_refs
):
    slots, rows, width = own_ref.shape
    fields = adv_first_ref.shape[1] + adv_rest_ref.shape[1]
    half = width // PAIR
    lower = lax.axis_index("lat") == 0
    member = lax.axis_index("mem")
    even_side = member % PAIR == 0
    for distance in range(LINE):
        tile = (member // PAIR) ^ distance
        here = pl.ds(pl.multiple_of(tile * TILE, TILE), TILE)
        near = pl.ds(pl.multiple_of(tile % 2 * TILE, TILE), TILE)
        pair = pl.ds(pl.multiple_of(tile // 2 * (2 * TILE), 2 * TILE), 2 * TILE)
        even_tile = tile % 2 == 0
        at_edge = lower == (tile * TILE >= rows - SMOOTH)
        keep_ref, send_ref = out_refs[distance], out_refs[LINE + distance]

        def store(index, value):
            left, right = value[:, 0:half], value[:, half:width]
            keep_ref[index] = jnp.where(even_side, left, right)
            send_ref[index] = jnp.where(even_side, right, left)

        scores = []
        for s in range(slots):
            score = own_ref[s, here, :] + jnp.where(at_edge, recv_ref[s, near, :], 0.0)
            scores.append(jnp.where(s < counts_ref[0:1, 0:1], score, -jnp.inf))
        peak = functools.reduce(jnp.maximum, scores)
        gains = [jnp.exp(score - peak) for score in scores]
        total = functools.reduce(jnp.add, gains)
        store(0, peak + jnp.log(total))
        gains = [gain / total for gain in gains]
        for f in range(fields):
            mean = None
            for s in range(slots):
                ref = field_ref(adv_first_ref, adv_rest_ref, s, f)
                value = ref[pair, :].astype(jnp.float32)
                term = gains[s] * jnp.where(even_tile, value[0:TILE], value[TILE:])
                mean = term if mean is None else mean + term
            store(1 + f, mean)


def merge_values(refs):
    peak = functools.reduce(jnp.maximum, [ref[0] for ref in refs])
    weights = [jnp.exp(ref[0] - peak) for ref in refs]
    total = functools.reduce(jnp.add, weights)
    shares = [weight / total for weight in weights]
    means = [
        functools.reduce(jnp.add, [share * ref[q] for share, ref in zip(shares, refs)])
        for q in range(1, refs[0].shape[0])
    ]
    return peak + jnp.log(total), means


def merge_kernel(*refs):
    out_ref = refs[-1]
    log_weight, means = merge_values(refs[:-1])
    out_ref[0] = log_weight
    for f, mean in enumerate(means):
        out_ref[1 + f] = mean


def finish_kernel(*refs):
    merged_ref = refs[-1]
    parts = refs[:-1]
    if len(parts) == 1:
        parts = [parts[0].at[d] for d in range(parts[0].shape[0])]
    for f, mean in enumerate(merge_values(parts)[1]):
        merged_ref[f] = mean


def relaxed(value, merged, factor, live):
    value = value.astype(jnp.float32)
    return jnp.where(live, value + factor * (merged - value), 0.0).astype(jnp.bfloat16)


def relax_all_kernel(
    counts_ref, relax_ref, adv_first_ref, adv_rest_ref, whole_ref, new_ref, mean_ref
):
    _, fields, rows, width = new_ref.shape
    across = width // LANES
    held = whole_ref.shape[2]

    def tile(f, row):
        if held >= TILE:
            return whole_ref[row // held, f, row % held : row % held + TILE]
        return jnp.concatenate([whole_ref[(row + k) // held, f] for k in range(0, TILE, held)], axis=0)

    for f in range(fields):
        merged = jnp.concatenate(
            [
                jnp.concatenate([tile(f, (t * across + l) * TILE) for l in range(across)], axis=1)
                for t in range(rows // TILE)
            ],
            axis=0,
        )
        mean_ref[f] = merged.astype(jnp.bfloat16)
        for s in range(new_ref.shape[0]):
            value = field_ref(adv_first_ref, adv_rest_ref, s, f)[...]
            new_ref[s, f] = relaxed(value, merged, relax_ref[f], s < counts_ref[0:1, 0:1])


def relax_kernel(counts_ref, relax_ref, adv_first_ref, adv_rest_ref, *refs):
    share_refs, (new_out, mean_out, merged_ref, new_ref, mean_ref, sems) = refs[:-6], refs[-6:]
    slots, fields, rows, width = new_ref.shape
    share_of = dict(zip(SHARE_ORDER, share_refs))
    member = lax.axis_index("mem")
    even_side = member % PAIR == 0
    copies = []
    for f in range(fields):
        for distance in range(LINE):
            tile = (member // PAIR) ^ distance
            same = share_of[PAIR * distance][f]
            other = share_of[PAIR * distance + 1][f]
            left = jnp.where(even_side, same, other)
            right = jnp.where(even_side, other, same)
            merged_ref[f, pl.ds(pl.multiple_of(tile * TILE, TILE), TILE), :] = jnp.concatenate(
                [left, right], axis=1
            )
        merged = merged_ref[f]
        mean_ref[f] = merged.astype(jnp.bfloat16)
        for s in range(slots):
            value = field_ref(adv_first_ref, adv_rest_ref, s, f)[...]
            new_ref[s, f] = relaxed(value, merged, relax_ref[f], s < counts_ref[0:1, 0:1])
        copies.append(pltpu.make_async_copy(new_ref.at[:, f], new_out.at[:, f], sems.at[0, f]))
        copies.append(pltpu.make_async_copy(mean_ref.at[f], mean_out.at[f], sems.at[1, f]))
        for copy in copies[-2:]:
            copy.start()
    for copy in copies:
        copy.wait()


def call(kernel, ins, outs, scratch=(), **cost):
    return pl.pallas_call(
        kernel,
        out_shape=[jax.ShapeDtypeStruct(shape, dtype) for shape, dtype in outs],
        in_specs=ins,
        out_specs=[VMEM] * len(outs),
        scratch_shapes=list(scratch),
        compiler_params=PARAMS,
        cost_estimate=pl.CostEstimate(**cost),
    )


def on_device(
    state, counts, east_wind, north_wind, obs_cells, obs_mask, obs_values, obs_error, relax
):
    slots, fields, rows, width = state.shape
    f32, bf16 = jnp.float32, jnp.bfloat16
    swap = [(0, 1), (1, 0)]
    (message,) = pl.pallas_call(
        edge_kernel,
        out_shape=[jax.ShapeDtypeStruct((slots * fields + 2, TILE, width), f32)],
        in_specs=[pl.BlockSpec(memory_space=pltpu.HBM)] * 3,
        out_specs=[VMEM],
        scratch_shapes=[
            pltpu.VMEM((slots, fields, 2 * TILE, width), bf16),
            pltpu.VMEM((2, 2 * TILE, width), f32),
            pltpu.SemaphoreType.DMA((3,)),
        ],
        compiler_params=pltpu.CompilerParams(vmem_limit_bytes=EDGE_VMEM),
        cost_estimate=pl.CostEstimate(
            flops=0, bytes_accessed=6 * slots * fields * TILE * width, transcendentals=0
        ),
    )(state, east_wind, north_wind)
    halo = lax.ppermute(message, "lat", swap)

    observations = obs_cells.shape[1]
    flat = [
        x.reshape(observations // LANES, LANES) for x in (obs_cells, obs_mask, obs_values, obs_error)
    ]
    acc_shape = (PARTS * 2 * rows, width // 2)
    all_steps = observations // (LANES * CHUNK_ROWS)
    begin_steps = min(BEGIN_STEPS, all_steps)
    observe_flops = 2 * PARTS * rows * width * LANES * CHUNK_ROWS
    terms, begun = call(
        functools.partial(begin_kernel, rows, width, begin_steps),
        [VMEM] * 4,
        [((PARTS + 2, observations // LANES, LANES), f32), (acc_shape, f32)],
        flops=observe_flops * begin_steps,
        bytes_accessed=16 * observations,
        transcendentals=observations,
    )(*flat)

    index = np.arange(rows)
    own = index[None, :] - index[:, None]
    upper_side = index[None, :] - (index[:SMOOTH, None] + rows)
    lower_side = index[None, :] - (index[rows - SMOOTH :, None] - rows)
    same_slot = np.eye(slots, dtype=np.float32)
    lat_kernel = split_constant(
        np.concatenate(
            [np.kron(same_slot, kernel_matrix(x)) for x in (own, upper_side, lower_side)]
        )
    )
    distance = np.abs(np.arange(width)[:, None] - np.arange(width)[None, :])
    lon_kernel = split_constant(kernel_matrix(np.minimum(distance, width - distance)))

    advect_scratch = [
        pltpu.VMEM((5, rows + TILE, width), f32),
        pltpu.VMEM((2, slots, width // LANES, rows + 3 * TILE, LANES), f32),
    ]
    advect_flops = STEPS * 16 * slots * rows * width
    adv_first, own_scores, edge_scores = call(
        functools.partial(first_kernel, begin_steps),
        [VMEM] * 8,
        [
            ((slots, fields - LATER_FIELDS, rows, width), bf16),
            ((slots, rows, width), f32),
            ((slots, SMOOTH, width), f32),
        ],
        [pltpu.VMEM(acc_shape, f32)] + advect_scratch,
        flops=observe_flops * (all_steps - begin_steps) + advect_flops * (fields - LATER_FIELDS),
        bytes_accessed=4 * width * width,
        transcendentals=0,
    )(state, halo, east_wind, north_wind, terms, begun, lat_kernel, lon_kernel)
    received = lax.ppermute(edge_scores, "lat", swap)

    (adv_rest,) = call(
        rest_kernel,
        [VMEM] * 4,
        [((slots, LATER_FIELDS, rows, width), bf16)],
        advect_scratch,
        flops=advect_flops * LATER_FIELDS,
        bytes_accessed=4 * slots * fields * rows * width,
        transcendentals=0,
    )(state, halo, east_wind, north_wind)

    members = lax.axis_size("mem")
    counts = jnp.broadcast_to(jnp.clip(counts, 1, slots)[0], (TILE, LANES))
    factors = jnp.broadcast_to(relax[:, None, None], (fields, 1, width))
    quantities = fields + 1
    direct = (members, rows, width % (PAIR * LANES)) == (PAIR * LINE, LINE * TILE, 0)
    chunk = (TILE, width // PAIR) if direct else (rows * width // LANES // members, LANES)
    cells = chunk[0] * chunk[1]

    def weigh(kernel, outs):
        return call(
            kernel,
            [VMEM] * 5,
            outs,
            flops=4 * slots * fields * rows * width,
            bytes_accessed=4 * slots * fields * rows * width,
            transcendentals=slots * rows * width,
        )(counts, own_scores, received, adv_first, adv_rest)

    def merge(kernel, pieces, out):
        size = quantities * cells * (len(pieces) if direct else members)
        return call(
            kernel,
            [VMEM] * len(pieces),
            [out],
            flops=4 * size,
            bytes_accessed=4 * size,
            transcendentals=size // quantities,
        )(*pieces)[0]

    def swapped(x, offset):
        return lax.ppermute(x, "mem", [(m, m ^ offset) for m in range(members)])

    merged_chunk = ((fields,) + chunk, f32)
    new_shape, mean_shape = (slots, fields, rows, width), (fields, rows, width)
    outs = [(new_shape, bf16), (mean_shape, bf16)]
    if direct:
        piece = ((quantities,) + chunk, f32)
        parts = weigh(weigh_kernel, [piece] * (PAIR * LINE))
        paired = [None] * LINE
        for j in reversed(range(LINE)):
            paired[j] = merge(merge_kernel, [parts[j], swapped(parts[LINE + j], 1)], piece)
        pieces = [paired[0]] + [swapped(paired[j], PAIR * j) for j in range(1, LINE)]
        merged = merge(finish_kernel, pieces, merged_chunk)
        far = LINE - 1
        sent = {0: merged}
        for offset in SHARE_ORDER[1:]:
            through = offset ^ 1 if offset % PAIR and offset // PAIR < far else 0
            sent[offset] = swapped(sent[through], offset ^ through)
        size = slots * fields * rows * width
        new_state, mean = pl.pallas_call(
            relax_kernel,
            out_shape=[jax.ShapeDtypeStruct(*out) for out in outs],
            in_specs=[VMEM] * (4 + len(sent)),
            out_specs=[pl.BlockSpec(memory_space=pl.ANY)] * 2,
            scratch_shapes=[
                pltpu.VMEM((fields, rows, width), f32),
                pltpu.VMEM(new_shape, bf16),
                pltpu.VMEM(mean_shape, bf16),
                pltpu.SemaphoreType.DMA((2, fields)),
            ],
            compiler_params=PARAMS,
            cost_estimate=pl.CostEstimate(flops=4 * size, bytes_accessed=4 * size, transcendentals=0),
        )(counts, factors, adv_first, adv_rest, *[sent[i] for i in SHARE_ORDER])
    else:
        (parts,) = weigh(weigh_all_kernel, [((members, quantities) + chunk, f32)])
        got = lax.all_to_all(parts, "mem", 0, 0, tiled=True)
        whole = lax.all_gather(merge(finish_kernel, [got], merged_chunk), "mem")
        new_state, mean = call(
            relax_all_kernel,
            [VMEM] * 5,
            outs,
            flops=4 * slots * fields * rows * width,
            bytes_accessed=4 * slots * fields * rows * width,
            transcendentals=0,
        )(counts, factors, adv_first, adv_rest, whole)
    return (new_state, mean)


def solution(mesh):
    return jax.shard_map(
        on_device,
        mesh=mesh,
        in_specs=(
            P(("groups", "mem"), None, "lat", None),
            P(("groups", "mem")),
            P(("groups", "lat"), None),
            P(("groups", "lat"), None),
            P(("groups", "lat"), None),
            P(("groups", "lat"), None),
            P(("groups", "lat"), None),
            P(("groups", "lat"), None),
            P(),
        ),
        out_specs=(P(("groups", "mem"), None, "lat", None), P("groups", "lat", None)),
        check_vma=False,
    )
```

```python
import functools

import jax
import jax.numpy as jnp
import ml_dtypes
import numpy as np
from jax import lax
from jax.experimental import pallas as pl
from jax.experimental.pallas import tpu as pltpu
from jax.sharding import PartitionSpec as P

STEPS = 4
SMOOTH = 16
LOG_TWO_PI = 1.8378770664093453
LANES = 128
TILE = 8
PARTS = 5
CHUNK_ROWS = 32
PACK = 16
BEGIN_STEPS = 2
LATER_FIELDS = 1
PAIR = 2
LINE = 4
SHARE_ORDER = (0, 6, 7, 2, 1, 4, 5, 3)


VMEM = pl.BlockSpec(memory_space=pltpu.VMEM)
PARAMS = pltpu.CompilerParams(vmem_limit_bytes=24 * 1024 * 1024)
EDGE_VMEM = 63 * 1024 * 1024


def kernel_matrix(offset):
    values = np.exp(-((2.0 * offset.astype(np.float32) / SMOOTH) ** 2))
    return np.where(np.abs(offset) <= SMOOTH, values, 0.0).astype(np.float32)


def split_constant(matrix):
    parts = []
    for _ in range(3):
        parts.append(matrix.astype(ml_dtypes.bfloat16))
        matrix = matrix - parts[-1].astype(np.float32)
    return jnp.asarray(np.stack(parts))


def split_two(x):
    high = x.astype(jnp.bfloat16).astype(jnp.float32)
    return high, x - high


def spread_terms(cells_ref, mask_ref, values_ref, error_ref, rows_ref, rows, width):
    half = width // 2
    cells = cells_ref[...]
    used = mask_ref[...].astype(jnp.float32)
    values = values_ref[...]
    error = error_ref[...]
    inverse = used / (error * error)
    first = inverse * values
    second = first * values + used * (2.0 * jnp.log(error) + LOG_TWO_PI)
    row = cells // width
    column = cells % width
    high = (column // half * rows + row).astype(jnp.float32)
    low = (column % half).astype(jnp.float32)
    for k, x in enumerate(split_two(inverse) + split_two(first) + (second, high, low)):
        rows_ref[k] = x


def add_observations(step, size, rows_ref, acc_ref):
    highs, lows = acc_ref.shape[0] // PARTS, acc_ref.shape[1]

    def steps_of(count):
        base = lax.broadcasted_iota(jnp.int32, (PACK, LANES), 0)
        return [
            (base + PACK * i).astype(jnp.float32).astype(jnp.bfloat16) for i in range(count // PACK)
        ]

    high_iota, low_iota = steps_of(highs), steps_of(lows)
    zero = jnp.zeros((PACK, LANES), jnp.bfloat16)
    one = jnp.ones((PACK, LANES), jnp.bfloat16)
    here = pl.ds(pl.multiple_of(step * size, size), size)
    held = [rows_ref[k, here, :] for k in range(PARTS + 2)]
    left, right = [], []
    for r in range(size):
        spread = [
            jnp.broadcast_to(x[r : r + 1, :], (PACK, LANES)).astype(jnp.bfloat16) for x in held
        ]
        high_row, low_row = spread[PARTS:]
        hit = [iota == high_row for iota in high_iota]
        left.append(
            jnp.concatenate([jnp.where(h, part, zero) for part in spread[:PARTS] for h in hit], axis=0)
        )
        right.append(
            jnp.concatenate([jnp.where(iota == low_row, one, zero) for iota in low_iota], axis=0)
        )
    acc_ref[...] += lax.dot_general(
        jnp.concatenate(left, axis=1),
        jnp.concatenate(right, axis=1),
        (((1,), (1,)), ((), ())),
        preferred_element_type=jnp.float32,
    )


def grids_of(acc_ref, rows):
    highs = 2 * rows

    def part_sum(indices):
        total = acc_ref[pl.ds(indices[-1] * highs, highs), :]
        for i in indices[-2::-1]:
            total = total + acc_ref[pl.ds(i * highs, highs), :]
        return jnp.concatenate([total[0:rows], total[rows:highs]], axis=1)

    return [part_sum(indices) for indices in ((0, 1), (2, 3), (4,))]


def begin_kernel(rows, width, steps, cells_ref, mask_ref, values_ref, error_ref, rows_ref, acc_ref):
    spread_terms(cells_ref, mask_ref, values_ref, error_ref, rows_ref, rows, width)
    acc_ref[...] = jnp.zeros_like(acc_ref)

    def body(step, carry):
        add_observations(step, CHUNK_ROWS, rows_ref, acc_ref)
        return carry

    lax.fori_loop(0, steps, body, 0)


def wind_parts(east_ref, north_ref, wind_halo_ref):
    east = jnp.concatenate([east_ref[...], wind_halo_ref[0]], axis=0)
    north = jnp.concatenate([north_ref[...], wind_halo_ref[1]], axis=0)
    west, south = jnp.maximum(east, 0.0), jnp.maximum(north, 0.0)
    east, north = -jnp.minimum(east, 0.0), -jnp.minimum(north, 0.0)
    return 1.0 - west - east - south - north, west, east, south, north


def edge_kernel(state_in, east_in, north_in, out_ref, state_ref, wind_ref, sems):
    slots, fields, rows, width = state_in.shape
    place = lax.axis_index("lat")
    lower = place == 0
    here = pl.ds(pl.multiple_of((1 - place) * (rows - 2 * TILE), 2 * TILE), 2 * TILE)
    copies = [
        pltpu.make_async_copy(state_in.at[:, :, here], state_ref, sems.at[0]),
        pltpu.make_async_copy(east_in.at[here], wind_ref.at[0], sems.at[1]),
        pltpu.make_async_copy(north_in.at[here], wind_ref.at[1], sems.at[2]),
    ]
    for copy in copies:
        copy.start()
    low_row = lax.broadcasted_iota(jnp.int32, (TILE, width), 0) < TILE // 2
    keep = low_row != lower

    def edge(block):
        return jnp.where(keep, jnp.where(lower, block[TILE:], block[0:TILE]), 0.0)

    for copy in copies:
        copy.wait()
    for s in range(slots):
        for f in range(fields):
            out_ref[s * fields + f] = edge(state_ref[s, f].astype(jnp.float32))
    for i in range(2):
        out_ref[slots * fields + i] = edge(wind_ref[i])


def store_winds(east_ref, north_ref, halo_ref, count, winds_ref):
    for i, part in enumerate(wind_parts(east_ref, north_ref, halo_ref.at[pl.ds(count, 2)])):
        winds_ref[i] = part


def advect_field(state_ref, halo_ref, winds_ref, buffer_ref, f, adv_ref, place, as_written=False):
    slots, fields, rows, width = state_ref.shape
    across, band_tiles = width // LANES, rows // TILE
    tiles = band_tiles + 1
    lane = lax.broadcasted_iota(jnp.int32, (TILE, LANES), 1)
    first, last = lane == 0, lane == LANES - 1

    def columns(l):
        return slice(l * LANES, (l + 1) * LANES)

    def put(side, k, l, v, value):
        copies = [v + 1] + ([0] if v == tiles - 1 else []) + ([tiles + 1] if v == 0 else [])
        for at in copies:
            buffer_ref[side, k, l, at * TILE : (at + 1) * TILE, :] = value

    for k in range(slots):
        x = state_ref[k, f].astype(jnp.float32)
        halo = halo_ref[k * fields + f]
        for l in range(across):
            for v in range(band_tiles):
                put(0, k, l, v, x[v * TILE : (v + 1) * TILE, columns(l)])
            put(0, k, l, band_tiles, halo[:, columns(l)])

    done = [[] for _ in range(slots)]
    for step in range(STEPS):
        side = step % 2
        ends = step == STEPS - 1
        for v in range(band_tiles if ends else tiles):
            cells = []
            for k in range(slots):

                def row_tile(offset):
                    start = (v + 1) * TILE + offset
                    return [buffer_ref[side, k, l, start : start + TILE, :] for l in range(across)]

                x = row_tile(0)
                west = [pltpu.roll(value, 1, 1) for value in x]
                east = [pltpu.roll(value, LANES - 1, 1) for value in x]
                cells.append(
                    (
                        x,
                        [jnp.where(first, west[l - 1], west[l]) for l in range(across)],
                        [jnp.where(last, east[(l + 1) % across], east[l]) for l in range(across)],
                        row_tile(-1),
                        row_tile(1),
                    )
                )
            stepped = [[] for _ in range(slots)]
            for l in range(across):
                here = slice(v * TILE, (v + 1) * TILE)
                centre, *winds = [winds_ref[c, here, columns(l)] for c in range(5)]
                for k in range(slots):
                    x, west, east, south, north = [values[l] for values in cells[k]]
                    if as_written:
                        x = (
                            x
                            - winds[0] * (x - west)
                            + winds[1] * (east - x)
                            - winds[2] * (x - south)
                            + winds[3] * (north - x)
                        )
                    else:
                        x = (
                            centre * x
                            + winds[0] * west
                            + winds[1] * east
                            + winds[2] * south
                            + winds[3] * north
                        )
                    if ends:
                        stepped[k].append(x)
                    else:
                        put(1 - side, k, l, v, x)
            if ends:
                for k in range(slots):
                    done[k].append(jnp.concatenate(stepped[k], axis=1))
    for k in range(slots):
        for v in range(0, band_tiles, 2):
            block = jnp.concatenate(done[k][v : v + 2], axis=0)
            adv_ref[k, place, v * TILE : (v + 2) * TILE, :] = block.astype(jnp.bfloat16)


def parts_of(x):
    high = x.astype(jnp.bfloat16)
    rest = x - high.astype(jnp.float32)
    middle = rest.astype(jnp.bfloat16)
    return [high, middle, (rest - middle.astype(jnp.float32)).astype(jnp.bfloat16)]


def product(left, right):
    rows = left[0].shape[0]
    total = None
    for p in reversed(range(3)):
        pieces = jnp.dot(
            jnp.concatenate(left[: 3 - p], axis=0), right[p], preferred_element_type=jnp.float32
        )
        for q in reversed(range(3 - p)):
            term = pieces[q * rows : (q + 1) * rows]
            total = term if total is None else total + term
    return total


def first_kernel(
    steps, state_ref, halo_ref, east_ref, north_ref, terms_ref, acc_in_ref, lat_ref, lon_ref,
    adv_ref, own_ref, send_ref, acc_ref, winds_ref, buffer_ref,
):
    slots, fields, rows, width = state_ref.shape
    store_winds(east_ref, north_ref, halo_ref, slots * fields, winds_ref)
    acc_ref[...] = acc_in_ref[...]
    held = adv_ref.shape[1]
    total = terms_ref.shape[1] // CHUNK_ROWS

    def advect_next(f, as_written):
        advect_field(state_ref, halo_ref, winds_ref, buffer_ref, f, adv_ref, f, as_written)

    def both(as_written):
        def body(i, carry):
            add_observations(steps + i, CHUNK_ROWS, terms_ref, acc_ref)
            advect_next(i, as_written)
            return carry

        return body

    def observe(step, carry):
        add_observations(step, CHUNK_ROWS, terms_ref, acc_ref)
        return carry

    shared = min(held, total - steps)
    if shared:
        lax.fori_loop(0, 1, both(True), 0)
        lax.fori_loop(1, shared, both(False), 0)
    if steps + shared < total:
        lax.fori_loop(steps + shared, total, observe, 0)
    for f in range(shared, held):
        advect_next(f, f == 0)

    inverse, first, second = grids_of(acc_ref, rows)
    logliks = []
    for s in range(slots):
        value = adv_ref[s, 0].astype(jnp.float32)
        logliks.append(-0.5 * (inverse * value * value - 2.0 * first * value + second))
    count = slots * rows
    edge = count + jnp.where(lax.axis_index("lat") == 0, 0, slots * SMOOTH)
    edge = pl.ds(pl.multiple_of(edge, SMOOTH), slots * SMOOTH)
    lat_parts = [
        jnp.concatenate([lat_ref[p, 0:count], lat_ref[p, edge]], axis=0) for p in range(3)
    ]
    along = product(parts_of(jnp.concatenate(logliks, axis=0)), [lon_ref[p] for p in range(3)])
    scores = product(lat_parts, parts_of(along))
    for s in range(slots):
        own_ref[s] = scores[s * rows : (s + 1) * rows]
        send_ref[s] = scores[count + s * SMOOTH : count + (s + 1) * SMOOTH]


def rest_kernel(
    state_ref, halo_ref, east_ref, north_ref, adv_ref, winds_ref, buffer_ref
):
    slots, fields = state_ref.shape[:2]
    held = adv_ref.shape[1]
    store_winds(east_ref, north_ref, halo_ref, slots * fields, winds_ref)


    def body(i, carry):
        f = fields - held + i
        advect_field(state_ref, halo_ref, winds_ref, buffer_ref, f, adv_ref, i)
        return carry

    lax.fori_loop(0, held, body, 0)


def field_ref(adv_first_ref, adv_rest_ref, s, f):
    held = adv_first_ref.shape[1]
    return adv_first_ref.at[s, f] if f < held else adv_rest_ref.at[s, f - held]


def weigh_all_kernel(
    counts_ref, own_ref, recv_ref, adv_first_ref, adv_rest_ref, parts_ref
):
    slots, rows, width = own_ref.shape
    fields = adv_first_ref.shape[1] + adv_rest_ref.shape[1]
    across = width // LANES
    members, _, held, _ = parts_ref.shape

    def store(row_tile, index, value):
        for l in range(across):
            tile = value[:, l * LANES : (l + 1) * LANES]
            row = (row_tile * across + l) * TILE
            for k in range(0, TILE, min(held, TILE)):
                chunk, at = divmod(row + k, held)
                parts_ref[chunk, index, at : at + min(held, TILE)] = tile[k : k + min(held, TILE)]

    lower = lax.axis_index("lat") == 0
    for t in range(rows // TILE):
        here = slice(t * TILE, (t + 1) * TILE)
        near = (t * TILE) % SMOOTH
        scores = []
        for s in range(slots):
            recv = recv_ref[s, near : near + TILE, :]
            at_this_edge = lower if t * TILE >= rows - SMOOTH else jnp.logical_not(lower)
            score = own_ref[s, here, :] + jnp.where(at_this_edge, recv, 0.0)
            scores.append(jnp.where(s < counts_ref[0:1, 0:1], score, -jnp.inf))
        peak = functools.reduce(jnp.maximum, scores)
        gains = [jnp.exp(score - peak) for score in scores]
        total = functools.reduce(jnp.add, gains)
        store(t, 0, peak + jnp.log(total))
        gains = [gain / total for gain in gains]
        for f in range(fields):
            mean = None
            for s in range(slots):
                ref = field_ref(adv_first_ref, adv_rest_ref, s, f)
                pair = slice(t // 2 * 2 * TILE, (t // 2 + 1) * 2 * TILE)
                value = ref[pair, :].astype(jnp.float32)[t % 2 * TILE : (t % 2 + 1) * TILE]
                term = gains[s] * value
                mean = term if mean is None else mean + term
            store(t, 1 + f, mean)


def weigh_kernel(
    counts_ref, own_ref, recv_ref, adv_first_ref, adv_rest_ref, *out_refs
):
    slots, rows, width = own_ref.shape
    fields = adv_first_ref.shape[1] + adv_rest_ref.shape[1]
    half = width // PAIR
    lower = lax.axis_index("lat") == 0
    member = lax.axis_index("mem")
    even_side = member % PAIR == 0
    for distance in range(LINE):
        tile = (member // PAIR) ^ distance
        here = pl.ds(pl.multiple_of(tile * TILE, TILE), TILE)
        near = pl.ds(pl.multiple_of(tile % 2 * TILE, TILE), TILE)
        pair = pl.ds(pl.multiple_of(tile // 2 * (2 * TILE), 2 * TILE), 2 * TILE)
        even_tile = tile % 2 == 0
        at_edge = lower == (tile * TILE >= rows - SMOOTH)
        keep_ref, send_ref = out_refs[distance], out_refs[LINE + distance]

        def store(index, value):
            left, right = value[:, 0:half], value[:, half:width]
            keep_ref[index] = jnp.where(even_side, left, right)
            send_ref[index] = jnp.where(even_side, right, left)

        scores = []
        for s in range(slots):
            score = own_ref[s, here, :] + jnp.where(at_edge, recv_ref[s, near, :], 0.0)
            scores.append(jnp.where(s < counts_ref[0:1, 0:1], score, -jnp.inf))
        peak = functools.reduce(jnp.maximum, scores)
        gains = [jnp.exp(score - peak) for score in scores]
        total = functools.reduce(jnp.add, gains)
        store(0, peak + jnp.log(total))
        gains = [gain / total for gain in gains]
        for f in range(fields):
            mean = None
            for s in range(slots):
                ref = field_ref(adv_first_ref, adv_rest_ref, s, f)
                value = ref[pair, :].astype(jnp.float32)
                term = gains[s] * jnp.where(even_tile, value[0:TILE], value[TILE:])
                mean = term if mean is None else mean + term
            store(1 + f, mean)


def merge_values(refs):
    peak = functools.reduce(jnp.maximum, [ref[0] for ref in refs])
    weights = [jnp.exp(ref[0] - peak) for ref in refs]
    total = functools.reduce(jnp.add, weights)
    shares = [weight / total for weight in weights]
    means = [
        functools.reduce(jnp.add, [share * ref[q] for share, ref in zip(shares, refs)])
        for q in range(1, refs[0].shape[0])
    ]
    return peak + jnp.log(total), means


def merge_kernel(*refs):
    out_ref = refs[-1]
    log_weight, means = merge_values(refs[:-1])
    out_ref[0] = log_weight
    for f, mean in enumerate(means):
        out_ref[1 + f] = mean


def finish_kernel(*refs):
    merged_ref = refs[-1]
    parts = refs[:-1]
    if len(parts) == 1:
        parts = [parts[0].at[d] for d in range(parts[0].shape[0])]
    for f, mean in enumerate(merge_values(parts)[1]):
        merged_ref[f] = mean


def relaxed(value, merged, factor, live):
    value = value.astype(jnp.float32)
    return jnp.where(live, value + factor * (merged - value), 0.0).astype(jnp.bfloat16)


def relax_all_kernel(
    counts_ref, relax_ref, adv_first_ref, adv_rest_ref, whole_ref, new_ref, mean_ref
):
    _, fields, rows, width = new_ref.shape
    across = width // LANES
    held = whole_ref.shape[2]

    def tile(f, row):
        if held >= TILE:
            return whole_ref[row // held, f, row % held : row % held + TILE]
        return jnp.concatenate([whole_ref[(row + k) // held, f] for k in range(0, TILE, held)], axis=0)

    for f in range(fields):
        merged = jnp.concatenate(
            [
                jnp.concatenate([tile(f, (t * across + l) * TILE) for l in range(across)], axis=1)
                for t in range(rows // TILE)
            ],
            axis=0,
        )
        mean_ref[f] = merged.astype(jnp.bfloat16)
        for s in range(new_ref.shape[0]):
            value = field_ref(adv_first_ref, adv_rest_ref, s, f)[...]
            new_ref[s, f] = relaxed(value, merged, relax_ref[f], s < counts_ref[0:1, 0:1])


def relax_kernel(counts_ref, relax_ref, adv_first_ref, adv_rest_ref, *refs):
    share_refs, (new_out, mean_out, merged_ref, new_ref, mean_ref, sems) = refs[:-6], refs[-6:]
    slots, fields, rows, width = new_ref.shape
    share_of = dict(zip(SHARE_ORDER, share_refs))
    member = lax.axis_index("mem")
    even_side = member % PAIR == 0
    copies = []
    for f in range(fields):
        for distance in range(LINE):
            tile = (member // PAIR) ^ distance
            same = share_of[PAIR * distance][f]
            other = share_of[PAIR * distance + 1][f]
            left = jnp.where(even_side, same, other)
            right = jnp.where(even_side, other, same)
            merged_ref[f, pl.ds(pl.multiple_of(tile * TILE, TILE), TILE), :] = jnp.concatenate(
                [left, right], axis=1
            )
        merged = merged_ref[f]
        mean_ref[f] = merged.astype(jnp.bfloat16)
        for s in range(slots):
            value = field_ref(adv_first_ref, adv_rest_ref, s, f)[...]
            new_ref[s, f] = relaxed(value, merged, relax_ref[f], s < counts_ref[0:1, 0:1])
        copies.append(pltpu.make_async_copy(new_ref.at[:, f], new_out.at[:, f], sems.at[0, f]))
        copies.append(pltpu.make_async_copy(mean_ref.at[f], mean_out.at[f], sems.at[1, f]))
        for copy in copies[-2:]:
            copy.start()
    for copy in copies:
        copy.wait()


def call(kernel, ins, outs, scratch=(), **cost):
    return pl.pallas_call(
        kernel,
        out_shape=[jax.ShapeDtypeStruct(shape, dtype) for shape, dtype in outs],
        in_specs=ins,
        out_specs=[VMEM] * len(outs),
        scratch_shapes=list(scratch),
        compiler_params=PARAMS,
        cost_estimate=pl.CostEstimate(**cost),
    )


def on_device(
    state, counts, east_wind, north_wind, obs_cells, obs_mask, obs_values, obs_error, relax
):
    slots, fields, rows, width = state.shape
    f32, bf16 = jnp.float32, jnp.bfloat16
    swap = [(0, 1), (1, 0)]
    (message,) = pl.pallas_call(
        edge_kernel,
        out_shape=[jax.ShapeDtypeStruct((slots * fields + 2, TILE, width), f32)],
        in_specs=[pl.BlockSpec(memory_space=pltpu.HBM)] * 3,
        out_specs=[VMEM],
        scratch_shapes=[
            pltpu.VMEM((slots, fields, 2 * TILE, width), bf16),
            pltpu.VMEM((2, 2 * TILE, width), f32),
            pltpu.SemaphoreType.DMA((3,)),
        ],
        compiler_params=pltpu.CompilerParams(vmem_limit_bytes=EDGE_VMEM),
        cost_estimate=pl.CostEstimate(
            flops=0, bytes_accessed=6 * slots * fields * TILE * width, transcendentals=0
        ),
    )(state, east_wind, north_wind)
    halo = lax.ppermute(message, "lat", swap)

    observations = obs_cells.shape[1]
    flat = [
        x.reshape(observations // LANES, LANES) for x in (obs_cells, obs_mask, obs_values, obs_error)
    ]
    acc_shape = (PARTS * 2 * rows, width // 2)
    all_steps = observations // (LANES * CHUNK_ROWS)
    begin_steps = min(BEGIN_STEPS, all_steps)
    observe_flops = 2 * PARTS * rows * width * LANES * CHUNK_ROWS
    terms, begun = call(
        functools.partial(begin_kernel, rows, width, begin_steps),
        [VMEM] * 4,
        [((PARTS + 2, observations // LANES, LANES), f32), (acc_shape, f32)],
        flops=observe_flops * begin_steps,
        bytes_accessed=16 * observations,
        transcendentals=observations,
    )(*flat)

    index = np.arange(rows)
    own = index[None, :] - index[:, None]
    upper_side = index[None, :] - (index[:SMOOTH, None] + rows)
    lower_side = index[None, :] - (index[rows - SMOOTH :, None] - rows)
    same_slot = np.eye(slots, dtype=np.float32)
    lat_kernel = split_constant(
        np.concatenate(
            [np.kron(same_slot, kernel_matrix(x)) for x in (own, upper_side, lower_side)]
        )
    )
    distance = np.abs(np.arange(width)[:, None] - np.arange(width)[None, :])
    lon_kernel = split_constant(kernel_matrix(np.minimum(distance, width - distance)))

    advect_scratch = [
        pltpu.VMEM((5, rows + TILE, width), f32),
        pltpu.VMEM((2, slots, width // LANES, rows + 3 * TILE, LANES), f32),
    ]
    advect_flops = STEPS * 16 * slots * rows * width
    adv_first, own_scores, edge_scores = call(
        functools.partial(first_kernel, begin_steps),
        [VMEM] * 8,
        [
            ((slots, fields - LATER_FIELDS, rows, width), bf16),
            ((slots, rows, width), f32),
            ((slots, SMOOTH, width), f32),
        ],
        [pltpu.VMEM(acc_shape, f32)] + advect_scratch,
        flops=observe_flops * (all_steps - begin_steps) + advect_flops * (fields - LATER_FIELDS),
        bytes_accessed=4 * width * width,
        transcendentals=0,
    )(state, halo, east_wind, north_wind, terms, begun, lat_kernel, lon_kernel)
    received = lax.ppermute(edge_scores, "lat", swap)

    (adv_rest,) = call(
        rest_kernel,
        [VMEM] * 4,
        [((slots, LATER_FIELDS, rows, width), bf16)],
        advect_scratch,
        flops=advect_flops * LATER_FIELDS,
        bytes_accessed=4 * slots * fields * rows * width,
        transcendentals=0,
    )(state, halo, east_wind, north_wind)

    members = lax.axis_size("mem")
    counts = jnp.broadcast_to(jnp.clip(counts, 1, slots)[0], (TILE, LANES))
    factors = jnp.broadcast_to(relax[:, None, None], (fields, 1, width))
    quantities = fields + 1
    direct = (members, rows, width % (PAIR * LANES)) == (PAIR * LINE, LINE * TILE, 0)
    chunk = (TILE, width // PAIR) if direct else (rows * width // LANES // members, LANES)
    cells = chunk[0] * chunk[1]

    def weigh(kernel, outs):
        return call(
            kernel,
            [VMEM] * 5,
            outs,
            flops=4 * slots * fields * rows * width,
            bytes_accessed=4 * slots * fields * rows * width,
            transcendentals=slots * rows * width,
        )(counts, own_scores, received, adv_first, adv_rest)

    def merge(kernel, pieces, out):
        size = quantities * cells * (len(pieces) if direct else members)
        return call(
            kernel,
            [VMEM] * len(pieces),
            [out],
            flops=4 * size,
            bytes_accessed=4 * size,
            transcendentals=size // quantities,
        )(*pieces)[0]

    def swapped(x, offset):
        return lax.ppermute(x, "mem", [(m, m ^ offset) for m in range(members)])

    merged_chunk = ((fields,) + chunk, f32)
    new_shape, mean_shape = (slots, fields, rows, width), (fields, rows, width)
    outs = [(new_shape, bf16), (mean_shape, bf16)]
    if direct:
        piece = ((quantities,) + chunk, f32)
        parts = weigh(weigh_kernel, [piece] * (PAIR * LINE))
        paired = [None] * LINE
        for j in reversed(range(LINE)):
            paired[j] = merge(merge_kernel, [parts[j], swapped(parts[LINE + j], 1)], piece)
        pieces = [paired[0]] + [swapped(paired[j], PAIR * j) for j in range(1, LINE)]
        merged = merge(finish_kernel, pieces, merged_chunk)
        far = LINE - 1
        sent = {0: merged}
        for offset in SHARE_ORDER[1:]:
            through = offset ^ 1 if offset % PAIR and offset // PAIR < far else 0
            sent[offset] = swapped(sent[through], offset ^ through)
        size = slots * fields * rows * width
        new_state, mean = pl.pallas_call(
            relax_kernel,
            out_shape=[jax.ShapeDtypeStruct(*out) for out in outs],
            in_specs=[VMEM] * (4 + len(sent)),
            out_specs=[pl.BlockSpec(memory_space=pl.ANY)] * 2,
            scratch_shapes=[
                pltpu.VMEM((fields, rows, width), f32),
                pltpu.VMEM(new_shape, bf16),
                pltpu.VMEM(mean_shape, bf16),
                pltpu.SemaphoreType.DMA((2, fields)),
            ],
            compiler_params=PARAMS,
            cost_estimate=pl.CostEstimate(flops=4 * size, bytes_accessed=4 * size, transcendentals=0),
        )(counts, factors, adv_first, adv_rest, *[sent[i] for i in SHARE_ORDER])
    else:
        (parts,) = weigh(weigh_all_kernel, [((members, quantities) + chunk, f32)])
        got = lax.all_to_all(parts, "mem", 0, 0, tiled=True)
        whole = lax.all_gather(merge(finish_kernel, [got], merged_chunk), "mem")
        new_state, mean = call(
            relax_all_kernel,
            [VMEM] * 5,
            outs,
            flops=4 * slots * fields * rows * width,
            bytes_accessed=4 * slots * fields * rows * width,
            transcendentals=0,
        )(counts, factors, adv_first, adv_rest, whole)
    return (new_state, mean)


def solution(mesh):
    return jax.shard_map(
        on_device,
        mesh=mesh,
        in_specs=(
            P(("groups", "mem"), None, "lat", None),
            P(("groups", "mem")),
            P(("groups", "lat"), None),
            P(("groups", "lat"), None),
            P(("groups", "lat"), None),
            P(("groups", "lat"), None),
            P(("groups", "lat"), None),
            P(("groups", "lat"), None),
            P(),
        ),
        out_specs=(P(("groups", "mem"), None, "lat", None), P("groups", "lat", None)),
        check_vma=False,
    )
```

```python
import functools

import jax
import jax.numpy as jnp
import ml_dtypes
import numpy as np
from jax import lax
from jax.experimental import pallas as pl
from jax.experimental.pallas import tpu as pltpu
from jax.sharding import PartitionSpec as P

STEPS = 4
SMOOTH = 16
LOG_TWO_PI = 1.8378770664093453
LANES = 128
TILE = 8
PARTS = 5
CHUNK_ROWS = 32
PACK = 16
BEGIN_STEPS = 2
LATER_FIELDS = 1
PAIR = 2
LINE = 4
SHARE_ORDER = (0, 6, 7, 2, 1, 4, 5, 3)


VMEM = pl.BlockSpec(memory_space=pltpu.VMEM)
PARAMS = pltpu.CompilerParams(vmem_limit_bytes=24 * 1024 * 1024)
EDGE_VMEM = 63 * 1024 * 1024


def kernel_matrix(offset):
    values = np.exp(-((2.0 * offset.astype(np.float32) / SMOOTH) ** 2))
    return np.where(np.abs(offset) <= SMOOTH, values, 0.0).astype(np.float32)


def split_constant(matrix):
    parts = []
    for _ in range(3):
        parts.append(matrix.astype(ml_dtypes.bfloat16))
        matrix = matrix - parts[-1].astype(np.float32)
    return jnp.asarray(np.stack(parts))


def split_two(x):
    high = x.astype(jnp.bfloat16).astype(jnp.float32)
    return high, x - high


def spread_terms(cells_ref, mask_ref, values_ref, error_ref, rows_ref, rows, width):
    half = width // 2
    cells = cells_ref[...]
    used = mask_ref[...].astype(jnp.float32)
    values = values_ref[...]
    error = error_ref[...]
    inverse = used / (error * error)
    first = inverse * values
    second = first * values + used * (2.0 * jnp.log(error) + LOG_TWO_PI)
    row = cells // width
    column = cells % width
    high = (column // half * rows + row).astype(jnp.float32)
    low = (column % half).astype(jnp.float32)
    for k, x in enumerate(split_two(inverse) + split_two(first) + (second, high, low)):
        rows_ref[k] = x


def add_observations(step, size, rows_ref, acc_ref):
    highs, lows = acc_ref.shape[0] // PARTS, acc_ref.shape[1]

    def steps_of(count):
        base = lax.broadcasted_iota(jnp.int32, (PACK, LANES), 0)
        return [
            (base + PACK * i).astype(jnp.float32).astype(jnp.bfloat16) for i in range(count // PACK)
        ]

    high_iota, low_iota = steps_of(highs), steps_of(lows)
    zero = jnp.zeros((PACK, LANES), jnp.bfloat16)
    one = jnp.ones((PACK, LANES), jnp.bfloat16)
    here = pl.ds(pl.multiple_of(step * size, size), size)
    held = [rows_ref[k, here, :] for k in range(PARTS + 2)]
    left, right = [], []
    for r in range(size):
        spread = [
            jnp.broadcast_to(x[r : r + 1, :], (PACK, LANES)).astype(jnp.bfloat16) for x in held
        ]
        high_row, low_row = spread[PARTS:]
        hit = [iota == high_row for iota in high_iota]
        left.append(
            jnp.concatenate([jnp.where(h, part, zero) for part in spread[:PARTS] for h in hit], axis=0)
        )
        right.append(
            jnp.concatenate([jnp.where(iota == low_row, one, zero) for iota in low_iota], axis=0)
        )
    acc_ref[...] += lax.dot_general(
        jnp.concatenate(left, axis=1),
        jnp.concatenate(right, axis=1),
        (((1,), (1,)), ((), ())),
        preferred_element_type=jnp.float32,
    )


def grids_of(acc_ref, rows):
    highs = 2 * rows

    def part_sum(indices):
        total = acc_ref[pl.ds(indices[-1] * highs, highs), :]
        for i in indices[-2::-1]:
            total = total + acc_ref[pl.ds(i * highs, highs), :]
        return jnp.concatenate([total[0:rows], total[rows:highs]], axis=1)

    return [part_sum(indices) for indices in ((0, 1), (2, 3), (4,))]


def begin_kernel(rows, width, steps, cells_ref, mask_ref, values_ref, error_ref, rows_ref, acc_ref):
    spread_terms(cells_ref, mask_ref, values_ref, error_ref, rows_ref, rows, width)
    acc_ref[...] = jnp.zeros_like(acc_ref)

    def body(step, carry):
        add_observations(step, CHUNK_ROWS, rows_ref, acc_ref)
        return carry

    lax.fori_loop(0, steps, body, 0)


def wind_parts(east_ref, north_ref, wind_halo_ref):
    east = jnp.concatenate([east_ref[...], wind_halo_ref[0]], axis=0)
    north = jnp.concatenate([north_ref[...], wind_halo_ref[1]], axis=0)
    west, south = jnp.maximum(east, 0.0), jnp.maximum(north, 0.0)
    east, north = -jnp.minimum(east, 0.0), -jnp.minimum(north, 0.0)
    return 1.0 - west - east - south - north, west, east, south, north


def edge_kernel(state_in, east_in, north_in, out_ref, state_ref, wind_ref, sems):
    slots, fields, rows, width = state_in.shape
    place = lax.axis_index("lat")
    lower = place == 0
    here = pl.ds(pl.multiple_of((1 - place) * (rows - 2 * TILE), 2 * TILE), 2 * TILE)
    copies = [
        pltpu.make_async_copy(state_in.at[:, :, here], state_ref, sems.at[0]),
        pltpu.make_async_copy(east_in.at[here], wind_ref.at[0], sems.at[1]),
        pltpu.make_async_copy(north_in.at[here], wind_ref.at[1], sems.at[2]),
    ]
    for copy in copies:
        copy.start()
    low_row = lax.broadcasted_iota(jnp.int32, (TILE, width), 0) < TILE // 2
    keep = low_row != lower

    def edge(block):
        return jnp.where(keep, jnp.where(lower, block[TILE:], block[0:TILE]), 0.0)

    for copy in copies:
        copy.wait()
    for s in range(slots):
        for f in range(fields):
            out_ref[s * fields + f] = edge(state_ref[s, f].astype(jnp.float32))
    for i in range(2):
        out_ref[slots * fields + i] = edge(wind_ref[i])


def store_winds(east_ref, north_ref, halo_ref, count, winds_ref):
    for i, part in enumerate(wind_parts(east_ref, north_ref, halo_ref.at[pl.ds(count, 2)])):
        winds_ref[i] = part


def advect_field(state_ref, halo_ref, winds_ref, buffer_ref, f, adv_ref, place, as_written=False):
    slots, fields, rows, width = state_ref.shape
    across, band_tiles = width // LANES, rows // TILE
    tiles = band_tiles + 1
    lane = lax.broadcasted_iota(jnp.int32, (TILE, LANES), 1)
    first, last = lane == 0, lane == LANES - 1

    def columns(l):
        return slice(l * LANES, (l + 1) * LANES)

    def put(side, k, l, v, value):
        copies = [v + 1] + ([0] if v == tiles - 1 else []) + ([tiles + 1] if v == 0 else [])
        for at in copies:
            buffer_ref[side, k, l, at * TILE : (at + 1) * TILE, :] = value

    for k in range(slots):
        x = state_ref[k, f].astype(jnp.float32)
        halo = halo_ref[k * fields + f]
        for l in range(across):
            for v in range(band_tiles):
                put(0, k, l, v, x[v * TILE : (v + 1) * TILE, columns(l)])
            put(0, k, l, band_tiles, halo[:, columns(l)])

    done = [[] for _ in range(slots)]
    for step in range(STEPS):
        side = step % 2
        ends = step == STEPS - 1
        for v in range(band_tiles if ends else tiles):
            cells = []
            for k in range(slots):

                def row_tile(offset):
                    start = (v + 1) * TILE + offset
                    return [buffer_ref[side, k, l, start : start + TILE, :] for l in range(across)]

                x = row_tile(0)
                west = [pltpu.roll(value, 1, 1) for value in x]
                east = [pltpu.roll(value, LANES - 1, 1) for value in x]
                cells.append(
                    (
                        x,
                        [jnp.where(first, west[l - 1], west[l]) for l in range(across)],
                        [jnp.where(last, east[(l + 1) % across], east[l]) for l in range(across)],
                        row_tile(-1),
                        row_tile(1),
                    )
                )
            stepped = [[] for _ in range(slots)]
            for l in range(across):
                here = slice(v * TILE, (v + 1) * TILE)
                centre, *winds = [winds_ref[c, here, columns(l)] for c in range(5)]
                for k in range(slots):
                    x, west, east, south, north = [values[l] for values in cells[k]]
                    if as_written:
                        x = (
                            x
                            - winds[0] * (x - west)
                            + winds[1] * (east - x)
                            - winds[2] * (x - south)
                            + winds[3] * (north - x)
                        )
                    else:
                        x = (
                            centre * x
                            + winds[0] * west
                            + winds[1] * east
                            + winds[2] * south
                            + winds[3] * north
                        )
                    if ends:
                        stepped[k].append(x)
                    else:
                        put(1 - side, k, l, v, x)
            if ends:
                for k in range(slots):
                    done[k].append(jnp.concatenate(stepped[k], axis=1))
    for k in range(slots):
        for v in range(0, band_tiles, 2):
            block = jnp.concatenate(done[k][v : v + 2], axis=0)
            adv_ref[k, place, v * TILE : (v + 2) * TILE, :] = block.astype(jnp.bfloat16)


def parts_of(x):
    high = x.astype(jnp.bfloat16)
    rest = x - high.astype(jnp.float32)
    middle = rest.astype(jnp.bfloat16)
    return [high, middle, (rest - middle.astype(jnp.float32)).astype(jnp.bfloat16)]


def product(left, right):
    rows = left[0].shape[0]
    total = None
    for p in reversed(range(3)):
        pieces = jnp.dot(
            jnp.concatenate(left[: 3 - p], axis=0), right[p], preferred_element_type=jnp.float32
        )
        for q in reversed(range(3 - p)):
            term = pieces[q * rows : (q + 1) * rows]
            total = term if total is None else total + term
    return total


def first_kernel(
    steps, state_ref, halo_ref, east_ref, north_ref, terms_ref, acc_in_ref, lat_ref, lon_ref,
    adv_ref, own_ref, send_ref, acc_ref, winds_ref, buffer_ref,
):
    slots, fields, rows, width = state_ref.shape
    store_winds(east_ref, north_ref, halo_ref, slots * fields, winds_ref)
    acc_ref[...] = acc_in_ref[...]
    held = adv_ref.shape[1]
    total = terms_ref.shape[1] // CHUNK_ROWS

    def advect_next(f, as_written):
        advect_field(state_ref, halo_ref, winds_ref, buffer_ref, f, adv_ref, f, as_written)

    def both(as_written):
        def body(i, carry):
            add_observations(steps + i, CHUNK_ROWS, terms_ref, acc_ref)
            advect_next(i, as_written)
            return carry

        return body

    def observe(step, carry):
        add_observations(step, CHUNK_ROWS, terms_ref, acc_ref)
        return carry

    shared = min(held, total - steps)
    if shared:
        lax.fori_loop(0, 1, both(True), 0)
        lax.fori_loop(1, shared, both(False), 0)
    if steps + shared < total:
        lax.fori_loop(steps + shared, total, observe, 0)
    for f in range(shared, held):
        advect_next(f, f == 0)

    inverse, first, second = grids_of(acc_ref, rows)
    logliks = []
    for s in range(slots):
        value = adv_ref[s, 0].astype(jnp.float32)
        logliks.append(-0.5 * (inverse * value * value - 2.0 * first * value + second))
    count = slots * rows
    edge = count + jnp.where(lax.axis_index("lat") == 0, 0, slots * SMOOTH)
    edge = pl.ds(pl.multiple_of(edge, SMOOTH), slots * SMOOTH)
    lat_parts = [
        jnp.concatenate([lat_ref[p, 0:count], lat_ref[p, edge]], axis=0) for p in range(3)
    ]
    along = product(parts_of(jnp.concatenate(logliks, axis=0)), [lon_ref[p] for p in range(3)])
    scores = product(lat_parts, parts_of(along))
    for s in range(slots):
        own_ref[s] = scores[s * rows : (s + 1) * rows]
        send_ref[s] = scores[count + s * SMOOTH : count + (s + 1) * SMOOTH]


def rest_kernel(
    state_ref, halo_ref, east_ref, north_ref, adv_ref, winds_ref, buffer_ref
):
    slots, fields = state_ref.shape[:2]
    held = adv_ref.shape[1]
    store_winds(east_ref, north_ref, halo_ref, slots * fields, winds_ref)


    def body(i, carry):
        f = fields - held + i
        advect_field(state_ref, halo_ref, winds_ref, buffer_ref, f, adv_ref, i)
        return carry

    lax.fori_loop(0, held, body, 0)


def field_ref(adv_first_ref, adv_rest_ref, s, f):
    held = adv_first_ref.shape[1]
    return adv_first_ref.at[s, f] if f < held else adv_rest_ref.at[s, f - held]


def weigh_all_kernel(
    counts_ref, own_ref, recv_ref, adv_first_ref, adv_rest_ref, parts_ref
):
    slots, rows, width = own_ref.shape
    fields = adv_first_ref.shape[1] + adv_rest_ref.shape[1]
    across = width // LANES
    members, _, held, _ = parts_ref.shape

    def store(row_tile, index, value):
        for l in range(across):
            tile = value[:, l * LANES : (l + 1) * LANES]
            row = (row_tile * across + l) * TILE
            for k in range(0, TILE, min(held, TILE)):
                chunk, at = divmod(row + k, held)
                parts_ref[chunk, index, at : at + min(held, TILE)] = tile[k : k + min(held, TILE)]

    lower = lax.axis_index("lat") == 0
    for t in range(rows // TILE):
        here = slice(t * TILE, (t + 1) * TILE)
        near = (t * TILE) % SMOOTH
        scores = []
        for s in range(slots):
            recv = recv_ref[s, near : near + TILE, :]
            at_this_edge = lower if t * TILE >= rows - SMOOTH else jnp.logical_not(lower)
            score = own_ref[s, here, :] + jnp.where(at_this_edge, recv, 0.0)
            scores.append(jnp.where(s < counts_ref[0:1, 0:1], score, -jnp.inf))
        peak = functools.reduce(jnp.maximum, scores)
        gains = [jnp.exp(score - peak) for score in scores]
        total = functools.reduce(jnp.add, gains)
        store(t, 0, peak + jnp.log(total))
        gains = [gain / total for gain in gains]
        for f in range(fields):
            mean = None
            for s in range(slots):
                ref = field_ref(adv_first_ref, adv_rest_ref, s, f)
                pair = slice(t // 2 * 2 * TILE, (t // 2 + 1) * 2 * TILE)
                value = ref[pair, :].astype(jnp.float32)[t % 2 * TILE : (t % 2 + 1) * TILE]
                term = gains[s] * value
                mean = term if mean is None else mean + term
            store(t, 1 + f, mean)


def weigh_kernel(
    counts_ref, own_ref, recv_ref, adv_first_ref, adv_rest_ref, *out_refs
):
    slots, rows, width = own_ref.shape
    fields = adv_first_ref.shape[1] + adv_rest_ref.shape[1]
    half = width // PAIR
    lower = lax.axis_index("lat") == 0
    member = lax.axis_index("mem")
    even_side = member % PAIR == 0
    for distance in range(LINE):
        tile = (member // PAIR) ^ distance
        here = pl.ds(pl.multiple_of(tile * TILE, TILE), TILE)
        near = pl.ds(pl.multiple_of(tile % 2 * TILE, TILE), TILE)
        pair = pl.ds(pl.multiple_of(tile // 2 * (2 * TILE), 2 * TILE), 2 * TILE)
        even_tile = tile % 2 == 0
        at_edge = lower == (tile * TILE >= rows - SMOOTH)
        keep_ref, send_ref = out_refs[distance], out_refs[LINE + distance]

        def store(index, value):
            left, right = value[:, 0:half], value[:, half:width]
            keep_ref[index] = jnp.where(even_side, left, right)
            send_ref[index] = jnp.where(even_side, right, left)

        scores = []
        for s in range(slots):
            score = own_ref[s, here, :] + jnp.where(at_edge, recv_ref[s, near, :], 0.0)
            scores.append(jnp.where(s < counts_ref[0:1, 0:1], score, -jnp.inf))
        peak = functools.reduce(jnp.maximum, scores)
        gains = [jnp.exp(score - peak) for score in scores]
        total = functools.reduce(jnp.add, gains)
        store(0, peak + jnp.log(total))
        gains = [gain / total for gain in gains]
        for f in range(fields):
            mean = None
            for s in range(slots):
                ref = field_ref(adv_first_ref, adv_rest_ref, s, f)
                value = ref[pair, :].astype(jnp.float32)
                term = gains[s] * jnp.where(even_tile, value[0:TILE], value[TILE:])
                mean = term if mean is None else mean + term
            store(1 + f, mean)


def merge_values(refs):
    peak = functools.reduce(jnp.maximum, [ref[0] for ref in refs])
    weights = [jnp.exp(ref[0] - peak) for ref in refs]
    total = functools.reduce(jnp.add, weights)
    shares = [weight / total for weight in weights]
    means = [
        functools.reduce(jnp.add, [share * ref[q] for share, ref in zip(shares, refs)])
        for q in range(1, refs[0].shape[0])
    ]
    return peak + jnp.log(total), means


def merge_kernel(*refs):
    out_ref = refs[-1]
    log_weight, means = merge_values(refs[:-1])
    out_ref[0] = log_weight
    for f, mean in enumerate(means):
        out_ref[1 + f] = mean


def finish_kernel(*refs):
    merged_ref = refs[-1]
    parts = refs[:-1]
    if len(parts) == 1:
        parts = [parts[0].at[d] for d in range(parts[0].shape[0])]
    for f, mean in enumerate(merge_values(parts)[1]):
        merged_ref[f] = mean


def relaxed(value, merged, factor, live):
    value = value.astype(jnp.float32)
    return jnp.where(live, value + factor * (merged - value), 0.0).astype(jnp.bfloat16)


def relax_all_kernel(
    counts_ref, relax_ref, adv_first_ref, adv_rest_ref, whole_ref, new_ref, mean_ref
):
    _, fields, rows, width = new_ref.shape
    across = width // LANES
    held = whole_ref.shape[2]

    def tile(f, row):
        if held >= TILE:
            return whole_ref[row // held, f, row % held : row % held + TILE]
        return jnp.concatenate([whole_ref[(row + k) // held, f] for k in range(0, TILE, held)], axis=0)

    for f in range(fields):
        merged = jnp.concatenate(
            [
                jnp.concatenate([tile(f, (t * across + l) * TILE) for l in range(across)], axis=1)
                for t in range(rows // TILE)
            ],
            axis=0,
        )
        mean_ref[f] = merged.astype(jnp.bfloat16)
        for s in range(new_ref.shape[0]):
            value = field_ref(adv_first_ref, adv_rest_ref, s, f)[...]
            new_ref[s, f] = relaxed(value, merged, relax_ref[f], s < counts_ref[0:1, 0:1])


def relax_kernel(counts_ref, relax_ref, adv_first_ref, adv_rest_ref, *refs):
    share_refs, (new_out, mean_out, merged_ref, new_ref, mean_ref, sems) = refs[:-6], refs[-6:]
    slots, fields, rows, width = new_ref.shape
    share_of = dict(zip(SHARE_ORDER, share_refs))
    lower = lax.axis_index("lat") == 0
    member = lax.axis_index("mem")
    even_side = member % PAIR == 0
    copies = []
    for f in range(fields):
        for distance in range(LINE):
            tile = (member // PAIR) ^ distance
            same = share_of[PAIR * distance][f]
            other = share_of[PAIR * distance + 1][f]
            if distance == LINE - 1:
                other = jnp.where(lower, other, share_refs[-1][f])
            left = jnp.where(even_side, same, other)
            right = jnp.where(even_side, other, same)
            merged_ref[f, pl.ds(pl.multiple_of(tile * TILE, TILE), TILE), :] = jnp.concatenate(
                [left, right], axis=1
            )
        merged = merged_ref[f]
        mean_ref[f] = merged.astype(jnp.bfloat16)
        for s in range(slots):
            value = field_ref(adv_first_ref, adv_rest_ref, s, f)[...]
            new_ref[s, f] = relaxed(value, merged, relax_ref[f], s < counts_ref[0:1, 0:1])
        copies.append(pltpu.make_async_copy(new_ref.at[:, f], new_out.at[:, f], sems.at[0, f]))
        copies.append(pltpu.make_async_copy(mean_ref.at[f], mean_out.at[f], sems.at[1, f]))
        for copy in copies[-2:]:
            copy.start()
    for copy in copies:
        copy.wait()


def call(kernel, ins, outs, scratch=(), **cost):
    return pl.pallas_call(
        kernel,
        out_shape=[jax.ShapeDtypeStruct(shape, dtype) for shape, dtype in outs],
        in_specs=ins,
        out_specs=[VMEM] * len(outs),
        scratch_shapes=list(scratch),
        compiler_params=PARAMS,
        cost_estimate=pl.CostEstimate(**cost),
    )


def on_device(
    state, counts, east_wind, north_wind, obs_cells, obs_mask, obs_values, obs_error, relax
):
    slots, fields, rows, width = state.shape
    f32, bf16 = jnp.float32, jnp.bfloat16
    swap = [(0, 1), (1, 0)]
    (message,) = pl.pallas_call(
        edge_kernel,
        out_shape=[jax.ShapeDtypeStruct((slots * fields + 2, TILE, width), f32)],
        in_specs=[pl.BlockSpec(memory_space=pltpu.HBM)] * 3,
        out_specs=[VMEM],
        scratch_shapes=[
            pltpu.VMEM((slots, fields, 2 * TILE, width), bf16),
            pltpu.VMEM((2, 2 * TILE, width), f32),
            pltpu.SemaphoreType.DMA((3,)),
        ],
        compiler_params=pltpu.CompilerParams(vmem_limit_bytes=EDGE_VMEM),
        cost_estimate=pl.CostEstimate(
            flops=0, bytes_accessed=6 * slots * fields * TILE * width, transcendentals=0
        ),
    )(state, east_wind, north_wind)
    halo = lax.ppermute(message, "lat", swap)

    observations = obs_cells.shape[1]
    flat = [
        x.reshape(observations // LANES, LANES) for x in (obs_cells, obs_mask, obs_values, obs_error)
    ]
    acc_shape = (PARTS * 2 * rows, width // 2)
    all_steps = observations // (LANES * CHUNK_ROWS)
    begin_steps = min(BEGIN_STEPS, all_steps)
    observe_flops = 2 * PARTS * rows * width * LANES * CHUNK_ROWS
    terms, begun = call(
        functools.partial(begin_kernel, rows, width, begin_steps),
        [VMEM] * 4,
        [((PARTS + 2, observations // LANES, LANES), f32), (acc_shape, f32)],
        flops=observe_flops * begin_steps,
        bytes_accessed=16 * observations,
        transcendentals=observations,
    )(*flat)

    index = np.arange(rows)
    own = index[None, :] - index[:, None]
    upper_side = index[None, :] - (index[:SMOOTH, None] + rows)
    lower_side = index[None, :] - (index[rows - SMOOTH :, None] - rows)
    same_slot = np.eye(slots, dtype=np.float32)
    lat_kernel = split_constant(
        np.concatenate(
            [np.kron(same_slot, kernel_matrix(x)) for x in (own, upper_side, lower_side)]
        )
    )
    distance = np.abs(np.arange(width)[:, None] - np.arange(width)[None, :])
    lon_kernel = split_constant(kernel_matrix(np.minimum(distance, width - distance)))

    advect_scratch = [
        pltpu.VMEM((5, rows + TILE, width), f32),
        pltpu.VMEM((2, slots, width // LANES, rows + 3 * TILE, LANES), f32),
    ]
    advect_flops = STEPS * 16 * slots * rows * width
    adv_first, own_scores, edge_scores = call(
        functools.partial(first_kernel, begin_steps),
        [VMEM] * 8,
        [
            ((slots, fields - LATER_FIELDS, rows, width), bf16),
            ((slots, rows, width), f32),
            ((slots, SMOOTH, width), f32),
        ],
        [pltpu.VMEM(acc_shape, f32)] + advect_scratch,
        flops=observe_flops * (all_steps - begin_steps) + advect_flops * (fields - LATER_FIELDS),
        bytes_accessed=4 * width * width,
        transcendentals=0,
    )(state, halo, east_wind, north_wind, terms, begun, lat_kernel, lon_kernel)
    received = lax.ppermute(edge_scores, "lat", swap)

    (adv_rest,) = call(
        rest_kernel,
        [VMEM] * 4,
        [((slots, LATER_FIELDS, rows, width), bf16)],
        advect_scratch,
        flops=advect_flops * LATER_FIELDS,
        bytes_accessed=4 * slots * fields * rows * width,
        transcendentals=0,
    )(state, halo, east_wind, north_wind)

    members = lax.axis_size("mem")
    counts = jnp.broadcast_to(jnp.clip(counts, 1, slots)[0], (TILE, LANES))
    factors = jnp.broadcast_to(relax[:, None, None], (fields, 1, width))
    quantities = fields + 1
    direct = (members, rows, width % (PAIR * LANES)) == (PAIR * LINE, LINE * TILE, 0)
    chunk = (TILE, width // PAIR) if direct else (rows * width // LANES // members, LANES)
    cells = chunk[0] * chunk[1]

    def weigh(kernel, outs):
        return call(
            kernel,
            [VMEM] * 5,
            outs,
            flops=4 * slots * fields * rows * width,
            bytes_accessed=4 * slots * fields * rows * width,
            transcendentals=slots * rows * width,
        )(counts, own_scores, received, adv_first, adv_rest)

    def merge(kernel, pieces, out):
        size = quantities * cells * (len(pieces) if direct else members)
        return call(
            kernel,
            [VMEM] * len(pieces),
            [out],
            flops=4 * size,
            bytes_accessed=4 * size,
            transcendentals=size // quantities,
        )(*pieces)[0]

    def swapped(x, offset):
        return lax.ppermute(x, "mem", [(m, m ^ offset) for m in range(members)])

    def swapped_on(band, x, offset):
        pairs = [(2 * m + band, 2 * (m ^ offset) + band) for m in range(members)]
        return lax.ppermute(x, ("mem", "lat"), pairs)

    merged_chunk = ((fields,) + chunk, f32)
    new_shape, mean_shape = (slots, fields, rows, width), (fields, rows, width)
    outs = [(new_shape, bf16), (mean_shape, bf16)]
    if direct:
        piece = ((quantities,) + chunk, f32)
        parts = weigh(weigh_kernel, [piece] * (PAIR * LINE))
        paired = [None] * LINE
        for j in reversed(range(LINE)):
            paired[j] = merge(merge_kernel, [parts[j], swapped(parts[LINE + j], 1)], piece)
        pieces = [paired[0]] + [swapped(paired[j], PAIR * j) for j in range(1, LINE)]
        merged = merge(finish_kernel, pieces, merged_chunk)
        far = PAIR * (LINE - 1)
        sent = {0: merged}
        for offset in SHARE_ORDER[1:]:
            if offset == far + 1:
                sent[offset] = swapped_on(0, merged, offset)
            else:
                through = offset ^ 1 if offset % PAIR and offset < far else 0
                sent[offset] = swapped(sent[through], offset ^ through)
        forwarded = swapped_on(1, sent[far], 1)
        shares = [sent[i] for i in SHARE_ORDER] + [forwarded]
        size = slots * fields * rows * width
        new_state, mean = pl.pallas_call(
            relax_kernel,
            out_shape=[jax.ShapeDtypeStruct(*out) for out in outs],
            in_specs=[VMEM] * (4 + len(shares)),
            out_specs=[pl.BlockSpec(memory_space=pl.ANY)] * 2,
            scratch_shapes=[
                pltpu.VMEM((fields, rows, width), f32),
                pltpu.VMEM(new_shape, bf16),
                pltpu.VMEM(mean_shape, bf16),
                pltpu.SemaphoreType.DMA((2, fields)),
            ],
            compiler_params=PARAMS,
            cost_estimate=pl.CostEstimate(flops=4 * size, bytes_accessed=4 * size, transcendentals=0),
        )(counts, factors, adv_first, adv_rest, *shares)
    else:
        (parts,) = weigh(weigh_all_kernel, [((members, quantities) + chunk, f32)])
        got = lax.all_to_all(parts, "mem", 0, 0, tiled=True)
        whole = lax.all_gather(merge(finish_kernel, [got], merged_chunk), "mem")
        new_state, mean = call(
            relax_all_kernel,
            [VMEM] * 5,
            outs,
            flops=4 * slots * fields * rows * width,
            bytes_accessed=4 * slots * fields * rows * width,
            transcendentals=0,
        )(counts, factors, adv_first, adv_rest, whole)
    return (new_state, mean)


def solution(mesh):
    return jax.shard_map(
        on_device,
        mesh=mesh,
        in_specs=(
            P(("groups", "mem"), None, "lat", None),
            P(("groups", "mem")),
            P(("groups", "lat"), None),
            P(("groups", "lat"), None),
            P(("groups", "lat"), None),
            P(("groups", "lat"), None),
            P(("groups", "lat"), None),
            P(("groups", "lat"), None),
            P(),
        ),
        out_specs=(P(("groups", "mem"), None, "lat", None), P("groups", "lat", None)),
        check_vma=False,
    )
```

```python
import functools

import jax
import jax.numpy as jnp
import ml_dtypes
import numpy as np
from jax import lax
from jax.experimental import pallas as pl
from jax.experimental.pallas import tpu as pltpu
from jax.sharding import PartitionSpec as P

STEPS = 4
SMOOTH = 16
LOG_TWO_PI = 1.8378770664093453
LANES = 128
TILE = 8
PARTS = 5
CHUNK_ROWS = 32
PACK = 16
BEGIN_STEPS = 1
LATER_FIELDS = 1
PAIR = 2
LINE = 4
SHARE_ORDER = (0, 6, 7, 2, 1, 4, 5, 3)


VMEM = pl.BlockSpec(memory_space=pltpu.VMEM)
PARAMS = pltpu.CompilerParams(vmem_limit_bytes=24 * 1024 * 1024)
EDGE_VMEM = 63 * 1024 * 1024


def kernel_matrix(offset):
    values = np.exp(-((2.0 * offset.astype(np.float32) / SMOOTH) ** 2))
    return np.where(np.abs(offset) <= SMOOTH, values, 0.0).astype(np.float32)


def split_constant(matrix):
    parts = []
    for _ in range(3):
        parts.append(matrix.astype(ml_dtypes.bfloat16))
        matrix = matrix - parts[-1].astype(np.float32)
    return jnp.asarray(np.stack(parts))


def split_two(x):
    high = x.astype(jnp.bfloat16).astype(jnp.float32)
    return high, x - high


def spread_terms(cells_ref, mask_ref, values_ref, error_ref, rows_ref, rows, width):
    half = width // 2
    cells = cells_ref[...]
    used = mask_ref[...].astype(jnp.float32)
    values = values_ref[...]
    error = error_ref[...]
    inverse = used / (error * error)
    first = inverse * values
    second = first * values + used * (2.0 * jnp.log(error) + LOG_TWO_PI)
    row = cells // width
    column = cells % width
    high = (column // half * rows + row).astype(jnp.float32)
    low = (column % half).astype(jnp.float32)
    for k, x in enumerate(split_two(inverse) + split_two(first) + (second, high, low)):
        rows_ref[k] = x


def add_observations(step, size, rows_ref, acc_ref):
    highs, lows = acc_ref.shape[0] // PARTS, acc_ref.shape[1]

    def steps_of(count):
        base = lax.broadcasted_iota(jnp.int32, (PACK, LANES), 0)
        return [
            (base + PACK * i).astype(jnp.float32).astype(jnp.bfloat16) for i in range(count // PACK)
        ]

    high_iota, low_iota = steps_of(highs), steps_of(lows)
    zero = jnp.zeros((PACK, LANES), jnp.bfloat16)
    one = jnp.ones((PACK, LANES), jnp.bfloat16)
    here = pl.ds(pl.multiple_of(step * size, size), size)
    held = [rows_ref[k, here, :] for k in range(PARTS + 2)]
    left, right = [], []
    for r in range(size):
        spread = [
            jnp.broadcast_to(x[r : r + 1, :], (PACK, LANES)).astype(jnp.bfloat16) for x in held
        ]
        high_row, low_row = spread[PARTS:]
        hit = [iota == high_row for iota in high_iota]
        left.append(
            jnp.concatenate([jnp.where(h, part, zero) for part in spread[:PARTS] for h in hit], axis=0)
        )
        right.append(
            jnp.concatenate([jnp.where(iota == low_row, one, zero) for iota in low_iota], axis=0)
        )
    acc_ref[...] += lax.dot_general(
        jnp.concatenate(left, axis=1),
        jnp.concatenate(right, axis=1),
        (((1,), (1,)), ((), ())),
        preferred_element_type=jnp.float32,
    )


def grids_of(acc_ref, rows):
    highs = 2 * rows

    def part_sum(indices):
        total = acc_ref[pl.ds(indices[-1] * highs, highs), :]
        for i in indices[-2::-1]:
            total = total + acc_ref[pl.ds(i * highs, highs), :]
        return jnp.concatenate([total[0:rows], total[rows:highs]], axis=1)

    return [part_sum(indices) for indices in ((0, 1), (2, 3), (4,))]


def begin_kernel(rows, width, steps, cells_ref, mask_ref, values_ref, error_ref, rows_ref, acc_ref):
    spread_terms(cells_ref, mask_ref, values_ref, error_ref, rows_ref, rows, width)
    acc_ref[...] = jnp.zeros_like(acc_ref)

    def body(step, carry):
        add_observations(step, CHUNK_ROWS, rows_ref, acc_ref)
        return carry

    lax.fori_loop(0, steps, body, 0)


def wind_parts(east_ref, north_ref, wind_halo_ref):
    east = jnp.concatenate([east_ref[...], wind_halo_ref[0]], axis=0)
    north = jnp.concatenate([north_ref[...], wind_halo_ref[1]], axis=0)
    west, south = jnp.maximum(east, 0.0), jnp.maximum(north, 0.0)
    east, north = -jnp.minimum(east, 0.0), -jnp.minimum(north, 0.0)
    return 1.0 - west - east - south - north, west, east, south, north


def edge_kernel(state_in, east_in, north_in, out_ref, state_ref, wind_ref, sems):
    slots, fields, rows, width = state_in.shape
    place = lax.axis_index("lat")
    lower = place == 0
    here = pl.ds(pl.multiple_of((1 - place) * (rows - 2 * TILE), 2 * TILE), 2 * TILE)
    copies = [
        pltpu.make_async_copy(state_in.at[:, :, here], state_ref, sems.at[0]),
        pltpu.make_async_copy(east_in.at[here], wind_ref.at[0], sems.at[1]),
        pltpu.make_async_copy(north_in.at[here], wind_ref.at[1], sems.at[2]),
    ]
    for copy in copies:
        copy.start()
    low_row = lax.broadcasted_iota(jnp.int32, (TILE, width), 0) < TILE // 2
    keep = low_row != lower

    def edge(block):
        return jnp.where(keep, jnp.where(lower, block[TILE:], block[0:TILE]), 0.0)

    for copy in copies:
        copy.wait()
    for s in range(slots):
        for f in range(fields):
            out_ref[s * fields + f] = edge(state_ref[s, f].astype(jnp.float32))
    for i in range(2):
        out_ref[slots * fields + i] = edge(wind_ref[i])


def store_winds(east_ref, north_ref, halo_ref, count, winds_ref):
    for i, part in enumerate(wind_parts(east_ref, north_ref, halo_ref.at[pl.ds(count, 2)])):
        winds_ref[i] = part


def advect_field(state_ref, halo_ref, winds_ref, buffer_ref, f, adv_ref, place, as_written=False):
    slots, fields, rows, width = state_ref.shape
    across, band_tiles = width // LANES, rows // TILE
    tiles = band_tiles + 1
    lane = lax.broadcasted_iota(jnp.int32, (TILE, LANES), 1)
    first, last = lane == 0, lane == LANES - 1

    def columns(l):
        return slice(l * LANES, (l + 1) * LANES)

    def put(side, k, l, v, value):
        copies = [v + 1] + ([0] if v == tiles - 1 else []) + ([tiles + 1] if v == 0 else [])
        for at in copies:
            buffer_ref[side, k, l, at * TILE : (at + 1) * TILE, :] = value

    for k in range(slots):
        x = state_ref[k, f].astype(jnp.float32)
        halo = halo_ref[k * fields + f]
        for l in range(across):
            for v in range(band_tiles):
                put(0, k, l, v, x[v * TILE : (v + 1) * TILE, columns(l)])
            put(0, k, l, band_tiles, halo[:, columns(l)])

    done = [[] for _ in range(slots)]
    for step in range(STEPS):
        side = step % 2
        ends = step == STEPS - 1
        for v in range(band_tiles if ends else tiles):
            cells = []
            for k in range(slots):

                def row_tile(offset):
                    start = (v + 1) * TILE + offset
                    return [buffer_ref[side, k, l, start : start + TILE, :] for l in range(across)]

                x = row_tile(0)
                west = [pltpu.roll(value, 1, 1) for value in x]
                east = [pltpu.roll(value, LANES - 1, 1) for value in x]
                cells.append(
                    (
                        x,
                        [jnp.where(first, west[l - 1], west[l]) for l in range(across)],
                        [jnp.where(last, east[(l + 1) % across], east[l]) for l in range(across)],
                        row_tile(-1),
                        row_tile(1),
                    )
                )
            stepped = [[] for _ in range(slots)]
            for l in range(across):
                here = slice(v * TILE, (v + 1) * TILE)
                centre, *winds = [winds_ref[c, here, columns(l)] for c in range(5)]
                for k in range(slots):
                    x, west, east, south, north = [values[l] for values in cells[k]]
                    if as_written:
                        x = (
                            x
                            - winds[0] * (x - west)
                            + winds[1] * (east - x)
                            - winds[2] * (x - south)
                            + winds[3] * (north - x)
                        )
                    else:
                        x = (
                            centre * x
                            + winds[0] * west
                            + winds[1] * east
                            + winds[2] * south
                            + winds[3] * north
                        )
                    if ends:
                        stepped[k].append(x)
                    else:
                        put(1 - side, k, l, v, x)
            if ends:
                for k in range(slots):
                    done[k].append(jnp.concatenate(stepped[k], axis=1))
    for k in range(slots):
        for v in range(0, band_tiles, 2):
            block = jnp.concatenate(done[k][v : v + 2], axis=0)
            adv_ref[k, place, v * TILE : (v + 2) * TILE, :] = block.astype(jnp.bfloat16)


def parts_of(x):
    high = x.astype(jnp.bfloat16)
    rest = x - high.astype(jnp.float32)
    middle = rest.astype(jnp.bfloat16)
    return [high, middle, (rest - middle.astype(jnp.float32)).astype(jnp.bfloat16)]


def product(left, right):
    rows = left[0].shape[0]
    total = None
    for p in reversed(range(3)):
        pieces = jnp.dot(
            jnp.concatenate(left[: 3 - p], axis=0), right[p], preferred_element_type=jnp.float32
        )
        for q in reversed(range(3 - p)):
            term = pieces[q * rows : (q + 1) * rows]
            total = term if total is None else total + term
    return total


def first_kernel(
    steps, state_ref, halo_ref, east_ref, north_ref, terms_ref, acc_in_ref, lat_ref, lon_ref,
    adv_ref, own_ref, send_ref, acc_ref, winds_ref, buffer_ref,
):
    slots, fields, rows, width = state_ref.shape
    store_winds(east_ref, north_ref, halo_ref, slots * fields, winds_ref)
    acc_ref[...] = acc_in_ref[...]
    held = adv_ref.shape[1]
    total = terms_ref.shape[1] // CHUNK_ROWS

    def advect_next(f, as_written):
        advect_field(state_ref, halo_ref, winds_ref, buffer_ref, f, adv_ref, f, as_written)

    def both(as_written):
        def body(i, carry):
            add_observations(steps + i, CHUNK_ROWS, terms_ref, acc_ref)
            advect_next(i, as_written)
            return carry

        return body

    def observe(step, carry):
        add_observations(step, CHUNK_ROWS, terms_ref, acc_ref)
        return carry

    shared = min(held, total - steps)
    if shared:
        lax.fori_loop(0, 1, both(True), 0)
        lax.fori_loop(1, shared, both(False), 0)
    if steps + shared < total:
        lax.fori_loop(steps + shared, total, observe, 0)
    for f in range(shared, held):
        advect_next(f, f == 0)

    inverse, first, second = grids_of(acc_ref, rows)
    logliks = []
    for s in range(slots):
        value = adv_ref[s, 0].astype(jnp.float32)
        logliks.append(-0.5 * (inverse * value * value - 2.0 * first * value + second))
    count = slots * rows
    edge = count + jnp.where(lax.axis_index("lat") == 0, 0, slots * SMOOTH)
    edge = pl.ds(pl.multiple_of(edge, SMOOTH), slots * SMOOTH)
    lat_parts = [
        jnp.concatenate([lat_ref[p, 0:count], lat_ref[p, edge]], axis=0) for p in range(3)
    ]
    along = product(parts_of(jnp.concatenate(logliks, axis=0)), [lon_ref[p] for p in range(3)])
    scores = product(lat_parts, parts_of(along))
    for s in range(slots):
        own_ref[s] = scores[s * rows : (s + 1) * rows]
        send_ref[s] = scores[count + s * SMOOTH : count + (s + 1) * SMOOTH]


def rest_kernel(
    state_ref, halo_ref, east_ref, north_ref, adv_ref, winds_ref, buffer_ref
):
    slots, fields = state_ref.shape[:2]
    held = adv_ref.shape[1]
    store_winds(east_ref, north_ref, halo_ref, slots * fields, winds_ref)


    def body(i, carry):
        f = fields - held + i
        advect_field(state_ref, halo_ref, winds_ref, buffer_ref, f, adv_ref, i)
        return carry

    lax.fori_loop(0, held, body, 0)


def field_ref(adv_first_ref, adv_rest_ref, s, f):
    held = adv_first_ref.shape[1]
    return adv_first_ref.at[s, f] if f < held else adv_rest_ref.at[s, f - held]


def weigh_all_kernel(
    counts_ref, own_ref, recv_ref, adv_first_ref, adv_rest_ref, parts_ref
):
    slots, rows, width = own_ref.shape
    fields = adv_first_ref.shape[1] + adv_rest_ref.shape[1]
    across = width // LANES
    members, _, held, _ = parts_ref.shape

    def store(row_tile, index, value):
        for l in range(across):
            tile = value[:, l * LANES : (l + 1) * LANES]
            row = (row_tile * across + l) * TILE
            for k in range(0, TILE, min(held, TILE)):
                chunk, at = divmod(row + k, held)
                parts_ref[chunk, index, at : at + min(held, TILE)] = tile[k : k + min(held, TILE)]

    lower = lax.axis_index("lat") == 0
    for t in range(rows // TILE):
        here = slice(t * TILE, (t + 1) * TILE)
        near = (t * TILE) % SMOOTH
        scores = []
        for s in range(slots):
            recv = recv_ref[s, near : near + TILE, :]
            at_this_edge = lower if t * TILE >= rows - SMOOTH else jnp.logical_not(lower)
            score = own_ref[s, here, :] + jnp.where(at_this_edge, recv, 0.0)
            scores.append(jnp.where(s < counts_ref[0:1, 0:1], score, -jnp.inf))
        peak = functools.reduce(jnp.maximum, scores)
        gains = [jnp.exp(score - peak) for score in scores]
        total = functools.reduce(jnp.add, gains)
        store(t, 0, peak + jnp.log(total))
        gains = [gain / total for gain in gains]
        for f in range(fields):
            mean = None
            for s in range(slots):
                ref = field_ref(adv_first_ref, adv_rest_ref, s, f)
                pair = slice(t // 2 * 2 * TILE, (t // 2 + 1) * 2 * TILE)
                value = ref[pair, :].astype(jnp.float32)[t % 2 * TILE : (t % 2 + 1) * TILE]
                term = gains[s] * value
                mean = term if mean is None else mean + term
            store(t, 1 + f, mean)


def weigh_kernel(
    counts_ref, own_ref, recv_ref, adv_first_ref, adv_rest_ref, *out_refs
):
    slots, rows, width = own_ref.shape
    fields = adv_first_ref.shape[1] + adv_rest_ref.shape[1]
    half = width // PAIR
    lower = lax.axis_index("lat") == 0
    member = lax.axis_index("mem")
    even_side = member % PAIR == 0
    for distance in range(LINE):
        tile = (member // PAIR) ^ distance
        here = pl.ds(pl.multiple_of(tile * TILE, TILE), TILE)
        near = pl.ds(pl.multiple_of(tile % 2 * TILE, TILE), TILE)
        pair = pl.ds(pl.multiple_of(tile // 2 * (2 * TILE), 2 * TILE), 2 * TILE)
        even_tile = tile % 2 == 0
        at_edge = lower == (tile * TILE >= rows - SMOOTH)
        keep_ref, send_ref = out_refs[distance], out_refs[LINE + distance]

        def store(index, value):
            left, right = value[:, 0:half], value[:, half:width]
            keep_ref[index] = jnp.where(even_side, left, right)
            send_ref[index] = jnp.where(even_side, right, left)

        scores = []
        for s in range(slots):
            score = own_ref[s, here, :] + jnp.where(at_edge, recv_ref[s, near, :], 0.0)
            scores.append(jnp.where(s < counts_ref[0:1, 0:1], score, -jnp.inf))
        peak = functools.reduce(jnp.maximum, scores)
        gains = [jnp.exp(score - peak) for score in scores]
        total = functools.reduce(jnp.add, gains)
        store(0, peak + jnp.log(total))
        gains = [gain / total for gain in gains]
        for f in range(fields):
            mean = None
            for s in range(slots):
                ref = field_ref(adv_first_ref, adv_rest_ref, s, f)
                value = ref[pair, :].astype(jnp.float32)
                term = gains[s] * jnp.where(even_tile, value[0:TILE], value[TILE:])
                mean = term if mean is None else mean + term
            store(1 + f, mean)


def merge_values(refs):
    peak = functools.reduce(jnp.maximum, [ref[0] for ref in refs])
    weights = [jnp.exp(ref[0] - peak) for ref in refs]
    total = functools.reduce(jnp.add, weights)
    shares = [weight / total for weight in weights]
    means = [
        functools.reduce(jnp.add, [share * ref[q] for share, ref in zip(shares, refs)])
        for q in range(1, refs[0].shape[0])
    ]
    return peak + jnp.log(total), means


def merge_kernel(*refs):
    out_ref = refs[-1]
    log_weight, means = merge_values(refs[:-1])
    out_ref[0] = log_weight
    for f, mean in enumerate(means):
        out_ref[1 + f] = mean


def finish_kernel(*refs):
    merged_ref = refs[-1]
    parts = refs[:-1]
    if len(parts) == 1:
        parts = [parts[0].at[d] for d in range(parts[0].shape[0])]
    for f, mean in enumerate(merge_values(parts)[1]):
        merged_ref[f] = mean


def relaxed(value, merged, factor, live):
    value = value.astype(jnp.float32)
    return jnp.where(live, value + factor * (merged - value), 0.0).astype(jnp.bfloat16)


def relax_all_kernel(
    counts_ref, relax_ref, adv_first_ref, adv_rest_ref, whole_ref, new_ref, mean_ref
):
    _, fields, rows, width = new_ref.shape
    across = width // LANES
    held = whole_ref.shape[2]

    def tile(f, row):
        if held >= TILE:
            return whole_ref[row // held, f, row % held : row % held + TILE]
        return jnp.concatenate([whole_ref[(row + k) // held, f] for k in range(0, TILE, held)], axis=0)

    for f in range(fields):
        merged = jnp.concatenate(
            [
                jnp.concatenate([tile(f, (t * across + l) * TILE) for l in range(across)], axis=1)
                for t in range(rows // TILE)
            ],
            axis=0,
        )
        mean_ref[f] = merged.astype(jnp.bfloat16)
        for s in range(new_ref.shape[0]):
            value = field_ref(adv_first_ref, adv_rest_ref, s, f)[...]
            new_ref[s, f] = relaxed(value, merged, relax_ref[f], s < counts_ref[0:1, 0:1])


def relax_kernel(counts_ref, relax_ref, adv_first_ref, adv_rest_ref, *refs):
    share_refs, (new_out, mean_out, merged_ref, new_ref, mean_ref, sems) = refs[:-6], refs[-6:]
    slots, fields, rows, width = new_ref.shape
    share_of = dict(zip(SHARE_ORDER, share_refs))
    member = lax.axis_index("mem")
    even_side = member % PAIR == 0
    copies = []
    for f in range(fields):
        for distance in range(LINE):
            tile = (member // PAIR) ^ distance
            same = share_of[PAIR * distance][f]
            other = share_of[PAIR * distance + 1][f]
            left = jnp.where(even_side, same, other)
            right = jnp.where(even_side, other, same)
            merged_ref[f, pl.ds(pl.multiple_of(tile * TILE, TILE), TILE), :] = jnp.concatenate(
                [left, right], axis=1
            )
        merged = merged_ref[f]
        mean_ref[f] = merged.astype(jnp.bfloat16)
        for s in range(slots):
            value = field_ref(adv_first_ref, adv_rest_ref, s, f)[...]
            new_ref[s, f] = relaxed(value, merged, relax_ref[f], s < counts_ref[0:1, 0:1])
        copies.append(pltpu.make_async_copy(new_ref.at[:, f], new_out.at[:, f], sems.at[0, f]))
        copies.append(pltpu.make_async_copy(mean_ref.at[f], mean_out.at[f], sems.at[1, f]))
        for copy in copies[-2:]:
            copy.start()
    for copy in copies:
        copy.wait()


def call(kernel, ins, outs, scratch=(), **cost):
    return pl.pallas_call(
        kernel,
        out_shape=[jax.ShapeDtypeStruct(shape, dtype) for shape, dtype in outs],
        in_specs=ins,
        out_specs=[VMEM] * len(outs),
        scratch_shapes=list(scratch),
        compiler_params=PARAMS,
        cost_estimate=pl.CostEstimate(**cost),
    )


def on_device(
    state, counts, east_wind, north_wind, obs_cells, obs_mask, obs_values, obs_error, relax
):
    slots, fields, rows, width = state.shape
    f32, bf16 = jnp.float32, jnp.bfloat16
    swap = [(0, 1), (1, 0)]
    (message,) = pl.pallas_call(
        edge_kernel,
        out_shape=[jax.ShapeDtypeStruct((slots * fields + 2, TILE, width), f32)],
        in_specs=[pl.BlockSpec(memory_space=pltpu.HBM)] * 3,
        out_specs=[VMEM],
        scratch_shapes=[
            pltpu.VMEM((slots, fields, 2 * TILE, width), bf16),
            pltpu.VMEM((2, 2 * TILE, width), f32),
            pltpu.SemaphoreType.DMA((3,)),
        ],
        compiler_params=pltpu.CompilerParams(vmem_limit_bytes=EDGE_VMEM),
        cost_estimate=pl.CostEstimate(
            flops=0, bytes_accessed=6 * slots * fields * TILE * width, transcendentals=0
        ),
    )(state, east_wind, north_wind)
    halo = lax.ppermute(message, "lat", swap)

    observations = obs_cells.shape[1]
    flat = [
        x.reshape(observations // LANES, LANES) for x in (obs_cells, obs_mask, obs_values, obs_error)
    ]
    acc_shape = (PARTS * 2 * rows, width // 2)
    all_steps = observations // (LANES * CHUNK_ROWS)
    begin_steps = min(BEGIN_STEPS, all_steps)
    observe_flops = 2 * PARTS * rows * width * LANES * CHUNK_ROWS
    terms, begun = call(
        functools.partial(begin_kernel, rows, width, begin_steps),
        [VMEM] * 4,
        [((PARTS + 2, observations // LANES, LANES), f32), (acc_shape, f32)],
        flops=observe_flops * begin_steps,
        bytes_accessed=16 * observations,
        transcendentals=observations,
    )(*flat)

    index = np.arange(rows)
    own = index[None, :] - index[:, None]
    upper_side = index[None, :] - (index[:SMOOTH, None] + rows)
    lower_side = index[None, :] - (index[rows - SMOOTH :, None] - rows)
    same_slot = np.eye(slots, dtype=np.float32)
    lat_kernel = split_constant(
        np.concatenate(
            [np.kron(same_slot, kernel_matrix(x)) for x in (own, upper_side, lower_side)]
        )
    )
    distance = np.abs(np.arange(width)[:, None] - np.arange(width)[None, :])
    lon_kernel = split_constant(kernel_matrix(np.minimum(distance, width - distance)))

    advect_scratch = [
        pltpu.VMEM((5, rows + TILE, width), f32),
        pltpu.VMEM((2, slots, width // LANES, rows + 3 * TILE, LANES), f32),
    ]
    advect_flops = STEPS * 16 * slots * rows * width
    adv_first, own_scores, edge_scores = call(
        functools.partial(first_kernel, begin_steps),
        [VMEM] * 8,
        [
            ((slots, fields - LATER_FIELDS, rows, width), bf16),
            ((slots, rows, width), f32),
            ((slots, SMOOTH, width), f32),
        ],
        [pltpu.VMEM(acc_shape, f32)] + advect_scratch,
        flops=observe_flops * (all_steps - begin_steps) + advect_flops * (fields - LATER_FIELDS),
        bytes_accessed=4 * width * width,
        transcendentals=0,
    )(state, halo, east_wind, north_wind, terms, begun, lat_kernel, lon_kernel)
    received = lax.ppermute(edge_scores, "lat", swap)

    (adv_rest,) = call(
        rest_kernel,
        [VMEM] * 4,
        [((slots, LATER_FIELDS, rows, width), bf16)],
        advect_scratch,
        flops=advect_flops * LATER_FIELDS,
        bytes_accessed=4 * slots * fields * rows * width,
        transcendentals=0,
    )(state, halo, east_wind, north_wind)

    members = lax.axis_size("mem")
    counts = jnp.broadcast_to(jnp.clip(counts, 1, slots)[0], (TILE, LANES))
    factors = jnp.broadcast_to(relax[:, None, None], (fields, 1, width))
    quantities = fields + 1
    direct = (members, rows, width % (PAIR * LANES)) == (PAIR * LINE, LINE * TILE, 0)
    chunk = (TILE, width // PAIR) if direct else (rows * width // LANES // members, LANES)
    cells = chunk[0] * chunk[1]

    def weigh(kernel, outs):
        return call(
            kernel,
            [VMEM] * 5,
            outs,
            flops=4 * slots * fields * rows * width,
            bytes_accessed=4 * slots * fields * rows * width,
            transcendentals=slots * rows * width,
        )(counts, own_scores, received, adv_first, adv_rest)

    def merge(kernel, pieces, out):
        size = quantities * cells * (len(pieces) if direct else members)
        return call(
            kernel,
            [VMEM] * len(pieces),
            [out],
            flops=4 * size,
            bytes_accessed=4 * size,
            transcendentals=size // quantities,
        )(*pieces)[0]

    def swapped(x, offset):
        return lax.ppermute(x, "mem", [(m, m ^ offset) for m in range(members)])

    merged_chunk = ((fields,) + chunk, f32)
    new_shape, mean_shape = (slots, fields, rows, width), (fields, rows, width)
    outs = [(new_shape, bf16), (mean_shape, bf16)]
    if direct:
        piece = ((quantities,) + chunk, f32)
        parts = weigh(weigh_kernel, [piece] * (PAIR * LINE))
        paired = [None] * LINE
        for j in reversed(range(LINE)):
            paired[j] = merge(merge_kernel, [parts[j], swapped(parts[LINE + j], 1)], piece)
        pieces = [paired[0]] + [swapped(paired[j], PAIR * j) for j in range(1, LINE)]
        merged = merge(finish_kernel, pieces, merged_chunk)
        far = LINE - 1
        sent = {0: merged}
        for offset in SHARE_ORDER[1:]:
            through = offset ^ 1 if offset % PAIR and offset // PAIR < far else 0
            sent[offset] = swapped(sent[through], offset ^ through)
        size = slots * fields * rows * width
        new_state, mean = pl.pallas_call(
            relax_kernel,
            out_shape=[jax.ShapeDtypeStruct(*out) for out in outs],
            in_specs=[VMEM] * (4 + len(sent)),
            out_specs=[pl.BlockSpec(memory_space=pl.ANY)] * 2,
            scratch_shapes=[
                pltpu.VMEM((fields, rows, width), f32),
                pltpu.VMEM(new_shape, bf16),
                pltpu.VMEM(mean_shape, bf16),
                pltpu.SemaphoreType.DMA((2, fields)),
            ],
            compiler_params=PARAMS,
            cost_estimate=pl.CostEstimate(flops=4 * size, bytes_accessed=4 * size, transcendentals=0),
        )(counts, factors, adv_first, adv_rest, *[sent[i] for i in SHARE_ORDER])
    else:
        (parts,) = weigh(weigh_all_kernel, [((members, quantities) + chunk, f32)])
        got = lax.all_to_all(parts, "mem", 0, 0, tiled=True)
        whole = lax.all_gather(merge(finish_kernel, [got], merged_chunk), "mem")
        new_state, mean = call(
            relax_all_kernel,
            [VMEM] * 5,
            outs,
            flops=4 * slots * fields * rows * width,
            bytes_accessed=4 * slots * fields * rows * width,
            transcendentals=0,
        )(counts, factors, adv_first, adv_rest, whole)
    return (new_state, mean)


def solution(mesh):
    return jax.shard_map(
        on_device,
        mesh=mesh,
        in_specs=(
            P(("groups", "mem"), None, "lat", None),
            P(("groups", "mem")),
            P(("groups", "lat"), None),
            P(("groups", "lat"), None),
            P(("groups", "lat"), None),
            P(("groups", "lat"), None),
            P(("groups", "lat"), None),
            P(("groups", "lat"), None),
            P(),
        ),
        out_specs=(P(("groups", "mem"), None, "lat", None), P("groups", "lat", None)),
        check_vma=False,
    )
```

```python
import functools

import jax
import jax.numpy as jnp
import ml_dtypes
import numpy as np
from jax import lax
from jax.experimental import pallas as pl
from jax.experimental.pallas import tpu as pltpu
from jax.sharding import PartitionSpec as P

STEPS = 4
SMOOTH = 16
LOG_TWO_PI = 1.8378770664093453
LANES = 128
TILE = 8
PARTS = 5
CHUNK_ROWS = 32
PACK = 16
BEGIN_STEPS = 2
LATER_FIELDS = 1
PAIR = 2
LINE = 4
SHARE_ORDER = (0, 6, 7, 2, 1, 4, 5, 3)


VMEM = pl.BlockSpec(memory_space=pltpu.VMEM)
PARAMS = pltpu.CompilerParams(vmem_limit_bytes=24 * 1024 * 1024)
EDGE_VMEM = 63 * 1024 * 1024


def kernel_matrix(offset):
    values = np.exp(-((2.0 * offset.astype(np.float32) / SMOOTH) ** 2))
    return np.where(np.abs(offset) <= SMOOTH, values, 0.0).astype(np.float32)


def split_constant(matrix):
    parts = []
    for _ in range(3):
        parts.append(matrix.astype(ml_dtypes.bfloat16))
        matrix = matrix - parts[-1].astype(np.float32)
    return jnp.asarray(np.stack(parts))


def split_two(x):
    high = x.astype(jnp.bfloat16).astype(jnp.float32)
    return high, x - high


def spread_terms(cells_ref, mask_ref, values_ref, error_ref, rows_ref, rows, width):
    half = width // 2
    cells = cells_ref[...]
    used = mask_ref[...].astype(jnp.float32)
    values = values_ref[...]
    error = error_ref[...]
    inverse = used / (error * error)
    first = inverse * values
    second = first * values + used * (2.0 * jnp.log(error) + LOG_TWO_PI)
    row = cells // width
    column = cells % width
    high = (column // half * rows + row).astype(jnp.float32)
    low = (column % half).astype(jnp.float32)
    for k, x in enumerate(split_two(inverse) + split_two(first) + (second, high, low)):
        rows_ref[k] = x


def add_observations(step, size, rows_ref, acc_ref):
    highs, lows = acc_ref.shape[0] // PARTS, acc_ref.shape[1]

    def steps_of(count):
        base = lax.broadcasted_iota(jnp.int32, (PACK, LANES), 0)
        return [
            (base + PACK * i).astype(jnp.float32).astype(jnp.bfloat16) for i in range(count // PACK)
        ]

    high_iota, low_iota = steps_of(highs), steps_of(lows)
    zero = jnp.zeros((PACK, LANES), jnp.bfloat16)
    one = jnp.ones((PACK, LANES), jnp.bfloat16)
    here = pl.ds(pl.multiple_of(step * size, size), size)
    held = [rows_ref[k, here, :] for k in range(PARTS + 2)]
    left, right = [], []
    for r in range(size):
        spread = [
            jnp.broadcast_to(x[r : r + 1, :], (PACK, LANES)).astype(jnp.bfloat16) for x in held
        ]
        high_row, low_row = spread[PARTS:]
        hit = [iota == high_row for iota in high_iota]
        left.append(
            jnp.concatenate([jnp.where(h, part, zero) for part in spread[:PARTS] for h in hit], axis=0)
        )
        right.append(
            jnp.concatenate([jnp.where(iota == low_row, one, zero) for iota in low_iota], axis=0)
        )
    acc_ref[...] += lax.dot_general(
        jnp.concatenate(left, axis=1),
        jnp.concatenate(right, axis=1),
        (((1,), (1,)), ((), ())),
        preferred_element_type=jnp.float32,
    )


def grids_of(acc_ref, rows):
    highs = 2 * rows

    def part_sum(indices):
        total = acc_ref[pl.ds(indices[-1] * highs, highs), :]
        for i in indices[-2::-1]:
            total = total + acc_ref[pl.ds(i * highs, highs), :]
        return jnp.concatenate([total[0:rows], total[rows:highs]], axis=1)

    return [part_sum(indices) for indices in ((0, 1), (2, 3), (4,))]


def begin_kernel(rows, width, steps, cells_ref, mask_ref, values_ref, error_ref, rows_ref, acc_ref):
    spread_terms(cells_ref, mask_ref, values_ref, error_ref, rows_ref, rows, width)
    acc_ref[...] = jnp.zeros_like(acc_ref)

    def body(step, carry):
        add_observations(step, CHUNK_ROWS, rows_ref, acc_ref)
        return carry

    lax.fori_loop(0, steps, body, 0)


def wind_parts(east_ref, north_ref, wind_halo_ref):
    east = jnp.concatenate([east_ref[...], wind_halo_ref[0]], axis=0)
    north = jnp.concatenate([north_ref[...], wind_halo_ref[1]], axis=0)
    west, south = jnp.maximum(east, 0.0), jnp.maximum(north, 0.0)
    east, north = -jnp.minimum(east, 0.0), -jnp.minimum(north, 0.0)
    return 1.0 - west - east - south - north, west, east, south, north


def edge_kernel(state_in, east_in, north_in, out_ref, state_ref, wind_ref, sems):
    slots, fields, rows, width = state_in.shape
    place = lax.axis_index("lat")
    lower = place == 0
    here = pl.ds(pl.multiple_of((1 - place) * (rows - 2 * TILE), 2 * TILE), 2 * TILE)
    copies = [
        pltpu.make_async_copy(state_in.at[:, :, here], state_ref, sems.at[0]),
        pltpu.make_async_copy(east_in.at[here], wind_ref.at[0], sems.at[1]),
        pltpu.make_async_copy(north_in.at[here], wind_ref.at[1], sems.at[2]),
    ]
    for copy in copies:
        copy.start()
    low_row = lax.broadcasted_iota(jnp.int32, (TILE, width), 0) < TILE // 2
    keep = low_row != lower

    def edge(block):
        return jnp.where(keep, jnp.where(lower, block[TILE:], block[0:TILE]), 0.0)

    for copy in copies:
        copy.wait()
    for s in range(slots):
        for f in range(fields):
            out_ref[s * fields + f] = edge(state_ref[s, f].astype(jnp.float32))
    for i in range(2):
        out_ref[slots * fields + i] = edge(wind_ref[i])


def store_winds(east_ref, north_ref, halo_ref, count, winds_ref):
    for i, part in enumerate(wind_parts(east_ref, north_ref, halo_ref.at[pl.ds(count, 2)])):
        winds_ref[i] = part


def advect_field(state_ref, halo_ref, winds_ref, buffer_ref, f, adv_ref, place, as_written=False):
    slots, fields, rows, width = state_ref.shape
    across, band_tiles = width // LANES, rows // TILE
    tiles = band_tiles + 1
    lane = lax.broadcasted_iota(jnp.int32, (TILE, LANES), 1)
    first, last = lane == 0, lane == LANES - 1

    def columns(l):
        return slice(l * LANES, (l + 1) * LANES)

    def put(side, k, l, v, value):
        copies = [v + 1] + ([0] if v == tiles - 1 else []) + ([tiles + 1] if v == 0 else [])
        for at in copies:
            buffer_ref[side, k, l, at * TILE : (at + 1) * TILE, :] = value

    for k in range(slots):
        x = state_ref[k, f].astype(jnp.float32)
        halo = halo_ref[k * fields + f]
        for l in range(across):
            for v in range(band_tiles):
                put(0, k, l, v, x[v * TILE : (v + 1) * TILE, columns(l)])
            put(0, k, l, band_tiles, halo[:, columns(l)])

    done = [[] for _ in range(slots)]
    for step in range(STEPS):
        side = step % 2
        ends = step == STEPS - 1
        for v in range(band_tiles if ends else tiles):
            cells = []
            for k in range(slots):

                def row_tile(offset):
                    start = (v + 1) * TILE + offset
                    return [buffer_ref[side, k, l, start : start + TILE, :] for l in range(across)]

                x = row_tile(0)
                west = [pltpu.roll(value, 1, 1) for value in x]
                east = [pltpu.roll(value, LANES - 1, 1) for value in x]
                cells.append(
                    (
                        x,
                        [jnp.where(first, west[l - 1], west[l]) for l in range(across)],
                        [jnp.where(last, east[(l + 1) % across], east[l]) for l in range(across)],
                        row_tile(-1),
                        row_tile(1),
                    )
                )
            stepped = [[] for _ in range(slots)]
            for l in range(across):
                here = slice(v * TILE, (v + 1) * TILE)
                centre, *winds = [winds_ref[c, here, columns(l)] for c in range(5)]
                for k in range(slots):
                    x, west, east, south, north = [values[l] for values in cells[k]]
                    if as_written:
                        x = (
                            x
                            - winds[0] * (x - west)
                            + winds[1] * (east - x)
                            - winds[2] * (x - south)
                            + winds[3] * (north - x)
                        )
                    else:
                        x = (
                            centre * x
                            + winds[0] * west
                            + winds[1] * east
                            + winds[2] * south
                            + winds[3] * north
                        )
                    if ends:
                        stepped[k].append(x)
                    else:
                        put(1 - side, k, l, v, x)
            if ends:
                for k in range(slots):
                    done[k].append(jnp.concatenate(stepped[k], axis=1))
    for k in range(slots):
        for v in range(0, band_tiles, 2):
            block = jnp.concatenate(done[k][v : v + 2], axis=0)
            adv_ref[k, place, v * TILE : (v + 2) * TILE, :] = block.astype(jnp.bfloat16)


def parts_of(x):
    high = x.astype(jnp.bfloat16)
    rest = x - high.astype(jnp.float32)
    middle = rest.astype(jnp.bfloat16)
    return [high, middle, (rest - middle.astype(jnp.float32)).astype(jnp.bfloat16)]


def product(left, right):
    rows = left[0].shape[0]
    total = None
    for p in reversed(range(3)):
        pieces = jnp.dot(
            jnp.concatenate(left[: 3 - p], axis=0), right[p], preferred_element_type=jnp.float32
        )
        for q in reversed(range(3 - p)):
            term = pieces[q * rows : (q + 1) * rows]
            total = term if total is None else total + term
    return total


def first_kernel(
    steps, state_ref, halo_ref, east_ref, north_ref, terms_ref, acc_in_ref, lat_ref, lon_ref,
    adv_ref, own_ref, send_ref, acc_ref, winds_ref, buffer_ref,
):
    slots, fields, rows, width = state_ref.shape
    store_winds(east_ref, north_ref, halo_ref, slots * fields, winds_ref)
    acc_ref[...] = acc_in_ref[...]
    held = adv_ref.shape[1]
    total = terms_ref.shape[1] // CHUNK_ROWS

    def advect_next(f, as_written):
        advect_field(state_ref, halo_ref, winds_ref, buffer_ref, f, adv_ref, f, as_written)

    def both(as_written):
        def body(i, carry):
            add_observations(steps + i, CHUNK_ROWS, terms_ref, acc_ref)
            advect_next(i, as_written)
            return carry

        return body

    def observe(step, carry):
        add_observations(step, CHUNK_ROWS, terms_ref, acc_ref)
        return carry

    shared = min(held, total - steps)
    if shared:
        lax.fori_loop(0, 1, both(True), 0)
        lax.fori_loop(1, shared, both(False), 0)
    if steps + shared < total:
        lax.fori_loop(steps + shared, total, observe, 0)
    for f in range(shared, held):
        advect_next(f, f == 0)

    inverse, first, second = grids_of(acc_ref, rows)
    logliks = []
    for s in range(slots):
        value = adv_ref[s, 0].astype(jnp.float32)
        logliks.append(-0.5 * (inverse * value * value - 2.0 * first * value + second))
    count = slots * rows
    edge = count + jnp.where(lax.axis_index("lat") == 0, 0, slots * SMOOTH)
    edge = pl.ds(pl.multiple_of(edge, SMOOTH), slots * SMOOTH)
    lat_parts = [
        jnp.concatenate([lat_ref[p, 0:count], lat_ref[p, edge]], axis=0) for p in range(3)
    ]
    along = product(parts_of(jnp.concatenate(logliks, axis=0)), [lon_ref[p] for p in range(3)])
    scores = product(lat_parts, parts_of(along))
    for s in range(slots):
        own_ref[s] = scores[s * rows : (s + 1) * rows]
        send_ref[s] = scores[count + s * SMOOTH : count + (s + 1) * SMOOTH]


def rest_kernel(
    state_ref, halo_ref, east_ref, north_ref, adv_ref, winds_ref, buffer_ref
):
    slots, fields = state_ref.shape[:2]
    held = adv_ref.shape[1]
    store_winds(east_ref, north_ref, halo_ref, slots * fields, winds_ref)


    def body(i, carry):
        f = fields - held + i
        advect_field(state_ref, halo_ref, winds_ref, buffer_ref, f, adv_ref, i)
        return carry

    lax.fori_loop(0, held, body, 0)


def field_ref(adv_first_ref, adv_rest_ref, s, f):
    held = adv_first_ref.shape[1]
    return adv_first_ref.at[s, f] if f < held else adv_rest_ref.at[s, f - held]


def weigh_all_kernel(
    counts_ref, own_ref, recv_ref, adv_first_ref, adv_rest_ref, parts_ref
):
    slots, rows, width = own_ref.shape
    fields = adv_first_ref.shape[1] + adv_rest_ref.shape[1]
    across = width // LANES
    members, _, held, _ = parts_ref.shape

    def store(row_tile, index, value):
        for l in range(across):
            tile = value[:, l * LANES : (l + 1) * LANES]
            row = (row_tile * across + l) * TILE
            for k in range(0, TILE, min(held, TILE)):
                chunk, at = divmod(row + k, held)
                parts_ref[chunk, index, at : at + min(held, TILE)] = tile[k : k + min(held, TILE)]

    lower = lax.axis_index("lat") == 0
    for t in range(rows // TILE):
        here = slice(t * TILE, (t + 1) * TILE)
        near = (t * TILE) % SMOOTH
        scores = []
        for s in range(slots):
            recv = recv_ref[s, near : near + TILE, :]
            at_this_edge = lower if t * TILE >= rows - SMOOTH else jnp.logical_not(lower)
            score = own_ref[s, here, :] + jnp.where(at_this_edge, recv, 0.0)
            scores.append(jnp.where(s < counts_ref[0:1, 0:1], score, -jnp.inf))
        peak = functools.reduce(jnp.maximum, scores)
        gains = [jnp.exp(score - peak) for score in scores]
        total = functools.reduce(jnp.add, gains)
        store(t, 0, peak + jnp.log(total))
        scale = 1.0 / total
        gains = [gain * scale for gain in gains]
        for f in range(fields):
            mean = None
            for s in range(slots):
                ref = field_ref(adv_first_ref, adv_rest_ref, s, f)
                pair = slice(t // 2 * 2 * TILE, (t // 2 + 1) * 2 * TILE)
                value = ref[pair, :].astype(jnp.float32)[t % 2 * TILE : (t % 2 + 1) * TILE]
                term = gains[s] * value
                mean = term if mean is None else mean + term
            store(t, 1 + f, mean)


def weigh_kernel(
    counts_ref, own_ref, recv_ref, adv_first_ref, adv_rest_ref, *out_refs
):
    slots, rows, width = own_ref.shape
    fields = adv_first_ref.shape[1] + adv_rest_ref.shape[1]
    half = width // PAIR
    lower = lax.axis_index("lat") == 0
    member = lax.axis_index("mem")
    even_side = member % PAIR == 0
    for distance in range(LINE):
        tile = (member // PAIR) ^ distance
        here = pl.ds(pl.multiple_of(tile * TILE, TILE), TILE)
        near = pl.ds(pl.multiple_of(tile % 2 * TILE, TILE), TILE)
        pair = pl.ds(pl.multiple_of(tile // 2 * (2 * TILE), 2 * TILE), 2 * TILE)
        even_tile = tile % 2 == 0
        at_edge = lower == (tile * TILE >= rows - SMOOTH)
        keep_ref, send_ref = out_refs[distance], out_refs[LINE + distance]

        def store(index, value):
            left, right = value[:, 0:half], value[:, half:width]
            keep_ref[index] = jnp.where(even_side, left, right)
            send_ref[index] = jnp.where(even_side, right, left)

        scores = []
        for s in range(slots):
            score = own_ref[s, here, :] + jnp.where(at_edge, recv_ref[s, near, :], 0.0)
            scores.append(jnp.where(s < counts_ref[0:1, 0:1], score, -jnp.inf))
        peak = functools.reduce(jnp.maximum, scores)
        gains = [jnp.exp(score - peak) for score in scores]
        total = functools.reduce(jnp.add, gains)
        store(0, peak + jnp.log(total))
        scale = 1.0 / total
        gains = [gain * scale for gain in gains]
        for f in range(fields):
            mean = None
            for s in range(slots):
                ref = field_ref(adv_first_ref, adv_rest_ref, s, f)
                value = ref[pair, :].astype(jnp.float32)
                term = gains[s] * jnp.where(even_tile, value[0:TILE], value[TILE:])
                mean = term if mean is None else mean + term
            store(1 + f, mean)


def merge_values(refs):
    peak = functools.reduce(jnp.maximum, [ref[0] for ref in refs])
    weights = [jnp.exp(ref[0] - peak) for ref in refs]
    total = functools.reduce(jnp.add, weights)
    scale = 1.0 / total
    shares = [weight * scale for weight in weights]
    means = [
        functools.reduce(jnp.add, [share * ref[q] for share, ref in zip(shares, refs)])
        for q in range(1, refs[0].shape[0])
    ]
    return peak + jnp.log(total), means


def merge_kernel(*refs):
    out_ref = refs[-1]
    log_weight, means = merge_values(refs[:-1])
    out_ref[0] = log_weight
    for f, mean in enumerate(means):
        out_ref[1 + f] = mean


def finish_kernel(*refs):
    merged_ref = refs[-1]
    parts = refs[:-1]
    if len(parts) == 1:
        parts = [parts[0].at[d] for d in range(parts[0].shape[0])]
    for f, mean in enumerate(merge_values(parts)[1]):
        merged_ref[f] = mean


def relaxed(value, merged, factor, live):
    value = value.astype(jnp.float32)
    return jnp.where(live, value + factor * (merged - value), 0.0).astype(jnp.bfloat16)


def relax_all_kernel(
    counts_ref, relax_ref, adv_first_ref, adv_rest_ref, whole_ref, new_ref, mean_ref
):
    _, fields, rows, width = new_ref.shape
    across = width // LANES
    held = whole_ref.shape[2]

    def tile(f, row):
        if held >= TILE:
            return whole_ref[row // held, f, row % held : row % held + TILE]
        return jnp.concatenate([whole_ref[(row + k) // held, f] for k in range(0, TILE, held)], axis=0)

    for f in range(fields):
        merged = jnp.concatenate(
            [
                jnp.concatenate([tile(f, (t * across + l) * TILE) for l in range(across)], axis=1)
                for t in range(rows // TILE)
            ],
            axis=0,
        )
        mean_ref[f] = merged.astype(jnp.bfloat16)
        for s in range(new_ref.shape[0]):
            value = field_ref(adv_first_ref, adv_rest_ref, s, f)[...]
            new_ref[s, f] = relaxed(value, merged, relax_ref[f], s < counts_ref[0:1, 0:1])


def relax_kernel(counts_ref, relax_ref, adv_first_ref, adv_rest_ref, *refs):
    share_refs, (new_out, mean_out, merged_ref, new_ref, mean_ref, sems) = refs[:-6], refs[-6:]
    slots, fields, rows, width = new_ref.shape
    share_of = dict(zip(SHARE_ORDER, share_refs))
    member = lax.axis_index("mem")
    even_side = member % PAIR == 0
    copies = []
    for f in range(fields):
        for distance in range(LINE):
            tile = (member // PAIR) ^ distance
            same = share_of[PAIR * distance][f]
            other = share_of[PAIR * distance + 1][f]
            left = jnp.where(even_side, same, other)
            right = jnp.where(even_side, other, same)
            merged_ref[f, pl.ds(pl.multiple_of(tile * TILE, TILE), TILE), :] = jnp.concatenate(
                [left, right], axis=1
            )
        merged = merged_ref[f]
        mean_ref[f] = merged.astype(jnp.bfloat16)
        for s in range(slots):
            value = field_ref(adv_first_ref, adv_rest_ref, s, f)[...]
            new_ref[s, f] = relaxed(value, merged, relax_ref[f], s < counts_ref[0:1, 0:1])
        copies.append(pltpu.make_async_copy(new_ref.at[:, f], new_out.at[:, f], sems.at[0, f]))
        copies.append(pltpu.make_async_copy(mean_ref.at[f], mean_out.at[f], sems.at[1, f]))
        for copy in copies[-2:]:
            copy.start()
    for copy in copies:
        copy.wait()


def call(kernel, ins, outs, scratch=(), **cost):
    return pl.pallas_call(
        kernel,
        out_shape=[jax.ShapeDtypeStruct(shape, dtype) for shape, dtype in outs],
        in_specs=ins,
        out_specs=[VMEM] * len(outs),
        scratch_shapes=list(scratch),
        compiler_params=PARAMS,
        cost_estimate=pl.CostEstimate(**cost),
    )


def on_device(
    state, counts, east_wind, north_wind, obs_cells, obs_mask, obs_values, obs_error, relax
):
    slots, fields, rows, width = state.shape
    f32, bf16 = jnp.float32, jnp.bfloat16
    swap = [(0, 1), (1, 0)]
    (message,) = pl.pallas_call(
        edge_kernel,
        out_shape=[jax.ShapeDtypeStruct((slots * fields + 2, TILE, width), f32)],
        in_specs=[pl.BlockSpec(memory_space=pltpu.HBM)] * 3,
        out_specs=[VMEM],
        scratch_shapes=[
            pltpu.VMEM((slots, fields, 2 * TILE, width), bf16),
            pltpu.VMEM((2, 2 * TILE, width), f32),
            pltpu.SemaphoreType.DMA((3,)),
        ],
        compiler_params=pltpu.CompilerParams(vmem_limit_bytes=EDGE_VMEM),
        cost_estimate=pl.CostEstimate(
            flops=0, bytes_accessed=6 * slots * fields * TILE * width, transcendentals=0
        ),
    )(state, east_wind, north_wind)
    halo = lax.ppermute(message, "lat", swap)

    observations = obs_cells.shape[1]
    flat = [
        x.reshape(observations // LANES, LANES) for x in (obs_cells, obs_mask, obs_values, obs_error)
    ]
    acc_shape = (PARTS * 2 * rows, width // 2)
    all_steps = observations // (LANES * CHUNK_ROWS)
    begin_steps = min(BEGIN_STEPS, all_steps)
    observe_flops = 2 * PARTS * rows * width * LANES * CHUNK_ROWS
    terms, begun = call(
        functools.partial(begin_kernel, rows, width, begin_steps),
        [VMEM] * 4,
        [((PARTS + 2, observations // LANES, LANES), f32), (acc_shape, f32)],
        flops=observe_flops * begin_steps,
        bytes_accessed=16 * observations,
        transcendentals=observations,
    )(*flat)

    index = np.arange(rows)
    own = index[None, :] - index[:, None]
    upper_side = index[None, :] - (index[:SMOOTH, None] + rows)
    lower_side = index[None, :] - (index[rows - SMOOTH :, None] - rows)
    same_slot = np.eye(slots, dtype=np.float32)
    lat_kernel = split_constant(
        np.concatenate(
            [np.kron(same_slot, kernel_matrix(x)) for x in (own, upper_side, lower_side)]
        )
    )
    distance = np.abs(np.arange(width)[:, None] - np.arange(width)[None, :])
    lon_kernel = split_constant(kernel_matrix(np.minimum(distance, width - distance)))

    advect_scratch = [
        pltpu.VMEM((5, rows + TILE, width), f32),
        pltpu.VMEM((2, slots, width // LANES, rows + 3 * TILE, LANES), f32),
    ]
    advect_flops = STEPS * 16 * slots * rows * width
    adv_first, own_scores, edge_scores = call(
        functools.partial(first_kernel, begin_steps),
        [VMEM] * 8,
        [
            ((slots, fields - LATER_FIELDS, rows, width), bf16),
            ((slots, rows, width), f32),
            ((slots, SMOOTH, width), f32),
        ],
        [pltpu.VMEM(acc_shape, f32)] + advect_scratch,
        flops=observe_flops * (all_steps - begin_steps) + advect_flops * (fields - LATER_FIELDS),
        bytes_accessed=4 * width * width,
        transcendentals=0,
    )(state, halo, east_wind, north_wind, terms, begun, lat_kernel, lon_kernel)
    received = lax.ppermute(edge_scores, "lat", swap)

    (adv_rest,) = call(
        rest_kernel,
        [VMEM] * 4,
        [((slots, LATER_FIELDS, rows, width), bf16)],
        advect_scratch,
        flops=advect_flops * LATER_FIELDS,
        bytes_accessed=4 * slots * fields * rows * width,
        transcendentals=0,
    )(state, halo, east_wind, north_wind)

    members = lax.axis_size("mem")
    counts = jnp.broadcast_to(jnp.clip(counts, 1, slots)[0], (TILE, LANES))
    factors = jnp.broadcast_to(relax[:, None, None], (fields, 1, width))
    quantities = fields + 1
    direct = (members, rows, width % (PAIR * LANES)) == (PAIR * LINE, LINE * TILE, 0)
    chunk = (TILE, width // PAIR) if direct else (rows * width // LANES // members, LANES)
    cells = chunk[0] * chunk[1]

    def weigh(kernel, outs):
        return call(
            kernel,
            [VMEM] * 5,
            outs,
            flops=4 * slots * fields * rows * width,
            bytes_accessed=4 * slots * fields * rows * width,
            transcendentals=slots * rows * width,
        )(counts, own_scores, received, adv_first, adv_rest)

    def merge(kernel, pieces, out):
        size = quantities * cells * (len(pieces) if direct else members)
        return call(
            kernel,
            [VMEM] * len(pieces),
            [out],
            flops=4 * size,
            bytes_accessed=4 * size,
            transcendentals=size // quantities,
        )(*pieces)[0]

    def swapped(x, offset):
        return lax.ppermute(x, "mem", [(m, m ^ offset) for m in range(members)])

    merged_chunk = ((fields,) + chunk, f32)
    new_shape, mean_shape = (slots, fields, rows, width), (fields, rows, width)
    outs = [(new_shape, bf16), (mean_shape, bf16)]
    if direct:
        piece = ((quantities,) + chunk, f32)
        parts = weigh(weigh_kernel, [piece] * (PAIR * LINE))
        paired = [None] * LINE
        for j in reversed(range(LINE)):
            paired[j] = merge(merge_kernel, [parts[j], swapped(parts[LINE + j], 1)], piece)
        pieces = [paired[0]] + [swapped(paired[j], PAIR * j) for j in range(1, LINE)]
        merged = merge(finish_kernel, pieces, merged_chunk)
        far = LINE - 1
        sent = {0: merged}
        for offset in SHARE_ORDER[1:]:
            through = offset ^ 1 if offset % PAIR and offset // PAIR < far else 0
            sent[offset] = swapped(sent[through], offset ^ through)
        size = slots * fields * rows * width
        new_state, mean = pl.pallas_call(
            relax_kernel,
            out_shape=[jax.ShapeDtypeStruct(*out) for out in outs],
            in_specs=[VMEM] * (4 + len(sent)),
            out_specs=[pl.BlockSpec(memory_space=pl.ANY)] * 2,
            scratch_shapes=[
                pltpu.VMEM((fields, rows, width), f32),
                pltpu.VMEM(new_shape, bf16),
                pltpu.VMEM(mean_shape, bf16),
                pltpu.SemaphoreType.DMA((2, fields)),
            ],
            compiler_params=PARAMS,
            cost_estimate=pl.CostEstimate(flops=4 * size, bytes_accessed=4 * size, transcendentals=0),
        )(counts, factors, adv_first, adv_rest, *[sent[i] for i in SHARE_ORDER])
    else:
        (parts,) = weigh(weigh_all_kernel, [((members, quantities) + chunk, f32)])
        got = lax.all_to_all(parts, "mem", 0, 0, tiled=True)
        whole = lax.all_gather(merge(finish_kernel, [got], merged_chunk), "mem")
        new_state, mean = call(
            relax_all_kernel,
            [VMEM] * 5,
            outs,
            flops=4 * slots * fields * rows * width,
            bytes_accessed=4 * slots * fields * rows * width,
            transcendentals=0,
        )(counts, factors, adv_first, adv_rest, whole)
    return (new_state, mean)


def solution(mesh):
    return jax.shard_map(
        on_device,
        mesh=mesh,
        in_specs=(
            P(("groups", "mem"), None, "lat", None),
            P(("groups", "mem")),
            P(("groups", "lat"), None),
            P(("groups", "lat"), None),
            P(("groups", "lat"), None),
            P(("groups", "lat"), None),
            P(("groups", "lat"), None),
            P(("groups", "lat"), None),
            P(),
        ),
        out_specs=(P(("groups", "mem"), None, "lat", None), P("groups", "lat", None)),
        check_vma=False,
    )
```
